32 devices in a mesh: groups: 2 (over x), tile: 16 (over z, y, core).
Axes of the slice: x: 2, y: 2, z: 4, core: 2. Of those that a mesh axis runs over, the one named last changes fastest.
Arguments:
- t2_tiles: bfloat16 [3072, 128, 128], P(('groups', 'tile')), parts along dimension 0, may hold values from -6 to 6
- t2_row: int32 [3072], P(('groups', 'tile')), parts along dimension 0, may hold values from 0 to 15
- t2_col: int32 [3072], P(('groups', 'tile')), parts along dimension 0, may hold values from 0 to 63, as said below
- integrals: bfloat16 [128, 128, 1024], P(('groups', 'tile')), parts along dimension 0, may hold values from -0.21875 to 0.21875
Outputs:
- ladder: bfloat16 [512, 128, 1024], P(('groups', 'tile')), parts along dimension 0
The draws below stay inside these ranges and needn't reach their ends.
There are 2 independent parts, one for each index of `groups`. The reference program is written for one: setup_inputs(seed, part) draws one part's arguments, and reference() takes and returns one part's arrays. A program takes and returns all parts, laid end to end along the dimension named above; each array names one. Nothing has to cross between parts.
Inputs may be any that keep to these rules, and one draw needn't show every extreme that they name: `t2_col`: on each device the 96 tiles name exactly 32 distinct integral blocks, each by 3 tiles of distinct row blocks; integral block k belongs to device k // 4; each device names at most 2 blocks of any one device, and exactly 2 of some device.
All inputs are finite; a program needn't handle non-finite values.
Results may differ from the reference program's by a relative error of at most 0.001.
Values may be sent and summed in bfloat16 or wider, within the bound.
No kernel may reach another device: no remote copies, remote signals or barrier semaphores. Data moves between devices by JAX's collectives and lax.ppermute only.
A program may use at most 128 MiB of HBM per device.

```python
import jax
import jax.numpy as jnp
from jax import lax

RB = 128
CB = 128
W = 32
AB = 1024
PPD = 16
TPR = 6
REUSE = 3
KPD = 4
TPD = 96
NEED = 32
CAP = 2
KBLOCKS = 64
ROWBLOCKS = 256
TILES = 1536
N_TILE = 16


def tile_lists(key):
    device_total = TILES // TPD

    def one_device(device_key):
        owner_key, pick_key, row_key, order_key = jax.random.split(device_key, 4)
        local = jax.vmap(lambda single: jax.random.permutation(single, KPD)[:CAP])(jax.random.split(owner_key, device_total))
        candidates = (jnp.arange(device_total, dtype=jnp.int32)[:, None] * KPD + local.astype(jnp.int32)).reshape(-1)
        column_list = jax.random.permutation(pick_key, candidates)[:NEED]
        row_keys = jax.random.split(row_key, NEED)
        row_list = jax.vmap(lambda single: jax.random.permutation(single, PPD)[:REUSE])(row_keys).reshape(-1)
        column_list = jnp.repeat(column_list, REUSE)
        tile_order = jax.random.permutation(order_key, TPD)
        return (row_list[tile_order], column_list[tile_order])
    row_list, column_list = jax.vmap(one_device)(jax.random.split(key, device_total))
    return (row_list.reshape(-1).astype(jnp.int32), column_list.reshape(-1).astype(jnp.int32))


def draw_t2_row(key, part):
    return tile_lists(key)[0]


def draw_t2_col(key, part):
    return tile_lists(key)[1]


def block_levels(rng, dims, cuts, least, high):
    def one(dim, shards_of):
        heights = jax.random.uniform(jax.random.fold_in(jax.random.fold_in(rng, 6), dim), (shards_of,), jnp.float32, least / len(cuts), high / len(cuts))
        return jnp.repeat(jnp.exp(heights), dims[dim] // shards_of).reshape((-1,) + (1,) * (len(dims) - dim - 1))

    factor_of = one(*cuts[0])
    for cut in cuts[1:]:
        factor_of = factor_of * one(*cut)
    return factor_of


def noise(rng, extent, deviation, reach, pieces=(), kind=jnp.bfloat16):
    entries = jax.random.normal(rng, extent, jnp.float32) * deviation
    if len(pieces) > 0:
        entries = block_levels(rng, extent, pieces, -0.22, 0.18) * entries
    return jnp.clip(entries, min=-reach, max=reach).astype(kind)


def setup_inputs(seed: int = 0, part: int = 0) -> dict:
    key_list = jax.random.split(jax.random.key(seed), 5)
    part_keys = jax.random.split(jax.random.fold_in(key_list[4], part), 5)
    t2_tiles = noise(part_keys[0], (TILES, RB, CB), 1.0, 6.0, ((0, 16),))
    t2_row = draw_t2_row(jax.random.fold_in(jax.random.fold_in(key_list[4], part), 71), part)
    t2_col = draw_t2_col(jax.random.fold_in(jax.random.fold_in(key_list[4], part), 71), part)
    integrals = noise(part_keys[3], (KBLOCKS, CB, AB), (CB * TPR) ** -0.5, 0.21875, ((0, 16),))
    return dict(t2_tiles=t2_tiles, t2_row=t2_row, t2_col=t2_col, integrals=integrals)


def reference(t2_tiles, t2_row, t2_col, integrals):
    tile_data = t2_tiles.reshape(N_TILE, TPD, RB, CB)
    row_list = t2_row.reshape(N_TILE, TPD).astype(jnp.int32)
    column_list = t2_col.reshape(N_TILE, TPD).astype(jnp.int32)

    def per_device(inputs):
        amplitude, row_ids, column_ids = inputs
        blocks = integrals[column_ids].astype(jnp.float32)
        contrib = jnp.einsum("tij,tjc->tic", amplitude.astype(jnp.float32), blocks)
        onehot = (row_ids[None, :] == jnp.arange(PPD, dtype=jnp.int32)[:, None]).astype(jnp.float32)
        return jnp.einsum("pt,tic->pic", onehot, contrib)

    residual = lax.map(per_device, (tile_data, row_list, column_list)).reshape(ROWBLOCKS, RB, AB)
    mirror = jnp.roll(residual, ROWBLOCKS // 2, axis=0)
    flipped = mirror.reshape(ROWBLOCKS, RB, W, W).swapaxes(2, 3).reshape(ROWBLOCKS, RB, AB)
    return (residual + flipped).astype(jnp.bfloat16)
```

```python
import functools

import jax
import jax.numpy as jnp
from jax import lax
from jax.experimental import pallas as pl
from jax.experimental.pallas import tpu as pltpu
from jax.sharding import PartitionSpec as P

W = 32
PPD = 16
REUSE = 3
VMEM_LIMIT = 56 * 1024 * 1024


def sorted_order(t2_col):
    count = t2_col.shape[0]
    ids = jnp.arange(count, dtype=jnp.int32)
    before = (t2_col[None, :] < t2_col[:, None]) | (
        (t2_col[None, :] == t2_col[:, None]) & (ids[None, :] < ids[:, None])
    )
    rank = jnp.sum(before.astype(jnp.int32), axis=1)
    return jnp.sum(jnp.where(rank[None, :] == ids[:, None], ids[None, :], 0), axis=1)


def flip_matrix(width):
    columns = jnp.arange(width * width, dtype=jnp.int32)
    source = (columns % width) * width + columns // width
    return (columns[:, None] == source[None, :]).astype(jnp.bfloat16)


def own_kernel(rows, own_ids, far_ids, tiles_ref, block_ref, far_ref, perm_ref, sum_ref, flip_ref):
    step = pl.program_id(0)

    @pl.when(step == 0)
    def _():
        sum_ref[...] = jnp.zeros_like(sum_ref)

    reuse, height, depth = tiles_ref.shape
    product = jnp.dot(
        tiles_ref[...].reshape(reuse * height, depth), block_ref[0], preferred_element_type=jnp.float32
    )
    for part in range(reuse):
        row = rows[step * reuse + part]
        sum_ref[row] += product[part * height : (part + 1) * height]
    flip_ref[0] = jnp.dot(far_ref[0], perm_ref[...], preferred_element_type=jnp.float32).astype(jnp.bfloat16)


def own_part(rows, own_ids, far_ids, tiles, blocks, perm):
    need = own_ids.shape[0]
    height, depth = tiles.shape[1:]
    width = blocks.shape[2]
    return pl.pallas_call(
        own_kernel,
        grid_spec=pltpu.PrefetchScalarGridSpec(
            num_scalar_prefetch=3,
            grid=(need,),
            in_specs=[
                pl.BlockSpec((REUSE, height, depth), lambda j, rows, own, far: (j, 0, 0)),
                pl.BlockSpec((1, depth, width), lambda j, rows, own, far: (own[j], 0, 0)),
                pl.BlockSpec((1, depth, width), lambda j, rows, own, far: (far[j], 0, 0)),
                pl.BlockSpec((width, width), lambda j, rows, own, far: (0, 0)),
            ],
            out_specs=[
                pl.BlockSpec((PPD, height, width), lambda j, rows, own, far: (0, 0, 0)),
                pl.BlockSpec((1, depth, width), lambda j, rows, own, far: (j, 0, 0)),
            ],
        ),
        out_shape=[
            jax.ShapeDtypeStruct((PPD, height, width), jnp.float32),
            jax.ShapeDtypeStruct((need, depth, width), jnp.bfloat16),
        ],
        compiler_params=pltpu.CompilerParams(vmem_limit_bytes=VMEM_LIMIT),
        name="own_part",
    )(rows, own_ids, far_ids, tiles, blocks, blocks, perm)


def far_kernel(rows, tiles_ref, flip_ref, base_ref, out_ref, sum_ref):
    step = pl.program_id(0)

    @pl.when(step == 0)
    def _():
        sum_ref[...] = base_ref[...]

    reuse, height, depth = tiles_ref.shape
    product = jnp.dot(
        tiles_ref[...].reshape(reuse * height, depth), flip_ref[0], preferred_element_type=jnp.float32
    )
    for part in range(reuse):
        row = rows[step * reuse + part]
        sum_ref[row] += product[part * height : (part + 1) * height]

    @pl.when(step == pl.num_programs(0) - 1)
    def _():
        out_ref[...] = sum_ref[...].astype(out_ref.dtype)


def far_part(rows, tiles, flipped, base):
    need, depth, width = flipped.shape
    height = tiles.shape[1]
    whole = (PPD, height, width)
    return pl.pallas_call(
        far_kernel,
        grid_spec=pltpu.PrefetchScalarGridSpec(
            num_scalar_prefetch=1,
            grid=(need,),
            in_specs=[
                pl.BlockSpec((REUSE, height, depth), lambda j, rows: (j, 0, 0)),
                pl.BlockSpec((1, depth, width), lambda j, rows: (j, 0, 0)),
                pl.BlockSpec(whole, lambda j, rows: (0, 0, 0)),
            ],
            out_specs=pl.BlockSpec(whole, lambda j, rows: (0, 0, 0)),
            scratch_shapes=[pltpu.VMEM(whole, jnp.float32)],
        ),
        out_shape=jax.ShapeDtypeStruct(whole, jnp.bfloat16),
        compiler_params=pltpu.CompilerParams(vmem_limit_bytes=VMEM_LIMIT),
        name="far_part",
    )(rows, tiles, flipped, base)


def per_device(t2_tiles, t2_row, t2_col, integrals):
    peers = lax.axis_size("tile")
    opposite = [(source, (source + peers // 2) % peers) for source in range(peers)]
    order = sorted_order(t2_col)
    tiles = jnp.take(t2_tiles, order, axis=0)
    rows = jnp.take(t2_row, order)
    ids = jnp.take(t2_col, order)[::REUSE]
    need = ids.shape[0]
    notes = lax.ppermute(jnp.concatenate([rows, ids]), "tile", opposite)
    far_tiles = lax.ppermute(tiles, "tile", opposite)
    blocks = lax.all_gather(integrals, "tile", axis=0, tiled=True)
    far_rows, far_ids = notes[: REUSE * need], notes[REUSE * need :]
    base, flipped = own_part(rows, ids, far_ids, tiles, blocks, flip_matrix(W))
    return far_part(far_rows, far_tiles, flipped, base)


def solution(mesh):
    in_specs = (
        P(("groups", "tile"), None, None),
        P(("groups", "tile")),
        P(("groups", "tile")),
        P(("groups", "tile"), None, None),
    )
    out_specs = P(("groups", "tile"), None, None)
    return jax.shard_map(
        per_device, mesh=mesh, in_specs=in_specs, out_specs=out_specs, check_vma=False
    )
```

```python
import jax
import jax.numpy as jnp
from jax import lax
from jax.experimental import pallas as pl
from jax.experimental.pallas import tpu as pltpu
from jax.sharding import PartitionSpec as P

W = 32
PPD = 16
REUSE = 3
CAP = 2
LAST = 4
VMEM_LIMIT = 56 * 1024 * 1024


def sorted_order(t2_col):
    count = t2_col.shape[0]
    ids = jnp.arange(count, dtype=jnp.int32)
    before = (t2_col[None, :] < t2_col[:, None]) | (
        (t2_col[None, :] == t2_col[:, None]) & (ids[None, :] < ids[:, None])
    )
    rank = jnp.sum(before.astype(jnp.int32), axis=1)
    return jnp.sum(jnp.where(rank[None, :] == ids[:, None], ids[None, :], 0), axis=1)


def flip_matrix(width):
    columns = jnp.arange(width * width, dtype=jnp.int32)
    source = (columns % width) * width + columns // width
    return (columns[:, None] == source[None, :]).astype(jnp.bfloat16)


def tree_gather(shard):
    everyone = range(16)
    centre = [i for i in everyone if i // 4 in (1, 2)]

    def send(value, pairs):
        return lax.ppermute(value, "tile", pairs)

    across = [(i, i ^ 12) for i in centre]
    outward = [(i, i ^ 4) for i in centre]
    me = lax.axis_index("tile")
    z = me // 4
    in_centre = (z == 1) | (z == 2)
    near = send(shard, [(i, i ^ 4) for i in everyone])
    first_centre = send(shard, across)
    second_centre = send(near, across)
    first = jnp.where(in_centre, first_centre, send(first_centre, outward))
    second = jnp.where(in_centre, second_centre, send(second_centre, outward))
    line = [shard, near, first, second]
    other_line = [send(value, [(i, i ^ 2) for i in everyone]) for value in line]
    buffers = []
    for value in line + other_line:
        buffers += [value, send(value, [(i, i ^ 1) for i in everyone])]
    low = z < 2
    zs = [z, z ^ 1, jnp.where(low, 2, 1), jnp.where(low, 3, 0)]
    owners = [4 * zs[k] + ((me & 3) ^ (2 * y + c)) for y in (0, 1) for k in range(4) for c in (0, 1)]
    return buffers, jnp.stack(owners).astype(jnp.int32)


def own_kernel(slots, rows, own_ids, far_ids, owners, tiles_refs, buffer_refs, perm_ref, sum_ref, flip_ref,
               own_blocks, far_blocks, own_sems, far_sems):
    need = own_blocks.shape[0]
    local = buffer_refs[0].shape[0]

    def fetch(buffer_ref, ids, slot, landing, sems):
        offset = lax.rem(ids[slot], local)
        pltpu.make_async_copy(buffer_ref.at[offset], landing.at[slot], sems.at[slot]).start()

    if slots:
        for ids, landing, sems in ((own_ids, own_blocks, own_sems), (far_ids, far_blocks, far_sems)):
            for number, buffer_ref in enumerate(buffer_refs):
                for extra in range(slots):
                    fetch(buffer_ref, ids, owners[number] * slots + extra, landing, sems)
    else:
        for ids, landing, sems in ((own_ids, own_blocks, own_sems), (far_ids, far_blocks, far_sems)):

            @pl.loop(0, need)
            def _(slot):
                fetch(buffer_refs[0], ids, slot, landing, sems)

    sum_ref[...] = jnp.zeros_like(sum_ref)
    base = 0
    for tiles_ref in tiles_refs:
        count, height, depth = tiles_ref.shape

        @pl.loop(0, count // REUSE)
        def _(step, tiles_ref=tiles_ref, base=base):
            slot = base + step
            pltpu.make_async_copy(own_blocks.at[slot], own_blocks.at[slot], own_sems.at[slot]).wait()
            block = own_blocks[slot]
            for part in range(REUSE):
                row = rows[slot * REUSE + part]
                sum_ref[row] += jnp.dot(tiles_ref[step * REUSE + part], block, preferred_element_type=jnp.float32)

        base += count // REUSE

    @pl.loop(0, need)
    def _(slot):
        pltpu.make_async_copy(far_blocks.at[slot], far_blocks.at[slot], far_sems.at[slot]).wait()
        flip_ref[slot] = jnp.dot(
            far_blocks[slot], perm_ref[...], preferred_element_type=jnp.float32
        ).astype(jnp.bfloat16)


def own_part(slots, rows, own_ids, far_ids, owners, tiles, buffers, perm):
    need = own_ids.shape[0]
    height = tiles[0].shape[1]
    depth, width = buffers[0].shape[1:]

    def kernel(rows, own_ids, far_ids, owners, *refs):
        tiles_refs = refs[: len(tiles)]
        buffer_refs = refs[len(tiles) : len(tiles) + len(buffers)]
        own_kernel(slots, rows, own_ids, far_ids, owners, tiles_refs, buffer_refs, *refs[len(tiles) + len(buffers) :])

    vmem = pl.BlockSpec(memory_space=pltpu.VMEM)
    return pl.pallas_call(
        kernel,
        in_specs=[pl.BlockSpec(memory_space=pltpu.SMEM)] * 4
        + [vmem] * len(tiles)
        + [pl.BlockSpec(memory_space=pl.ANY)] * len(buffers)
        + [vmem],
        out_specs=[vmem, vmem],
        out_shape=[
            jax.ShapeDtypeStruct((PPD, height, width), jnp.float32),
            jax.ShapeDtypeStruct((need, depth, width), jnp.bfloat16),
        ],
        scratch_shapes=[
            pltpu.VMEM((need, depth, width), jnp.bfloat16),
            pltpu.VMEM((need, depth, width), jnp.bfloat16),
            pltpu.SemaphoreType.DMA((need,)),
            pltpu.SemaphoreType.DMA((need,)),
        ],
        compiler_params=pltpu.CompilerParams(vmem_limit_bytes=VMEM_LIMIT),
        name="own_part",
    )(rows, own_ids, far_ids, owners, *tiles, *buffers, perm)


def far_kernel(base, rows, tiles_ref, flip_ref, base_ref, out_ref, sum_ref):
    step = pl.program_id(0)

    @pl.when(step == 0)
    def _():
        sum_ref[...] = base_ref[...]

    for part in range(REUSE):
        row = rows[base + step * REUSE + part]
        sum_ref[row] += jnp.dot(tiles_ref[part], flip_ref[0], preferred_element_type=jnp.float32)

    @pl.when(step == pl.num_programs(0) - 1)
    def _():
        out_ref[...] = sum_ref[...].astype(out_ref.dtype)


def far_part(base, rows, tiles, flipped, total, dtype):
    depth, width = flipped.shape[1:]
    count, height = tiles.shape[:2]
    whole = (PPD, height, width)
    first = base // REUSE

    def kernel(*refs):
        far_kernel(base, *refs)

    return pl.pallas_call(
        kernel,
        grid_spec=pltpu.PrefetchScalarGridSpec(
            num_scalar_prefetch=1,
            grid=(count // REUSE,),
            in_specs=[
                pl.BlockSpec((REUSE, height, depth), lambda j, rows: (j, 0, 0)),
                pl.BlockSpec((1, depth, width), lambda j, rows: (first + j, 0, 0)),
                pl.BlockSpec(whole, lambda j, rows: (0, 0, 0), pipeline_mode=pl.Buffered(1)),
            ],
            out_specs=pl.BlockSpec(whole, lambda j, rows: (0, 0, 0), pipeline_mode=pl.Buffered(1)),
            scratch_shapes=[pltpu.VMEM(whole, jnp.float32)],
        ),
        out_shape=jax.ShapeDtypeStruct(whole, dtype),
        compiler_params=pltpu.CompilerParams(vmem_limit_bytes=VMEM_LIMIT),
        name="far_part",
    )(rows, tiles, flipped, total)


def per_device(t2_tiles, t2_row, t2_col, integrals):
    peers = lax.axis_size("tile")
    opposite = [(source, (source + peers // 2) % peers) for source in range(peers)]
    need = t2_col.shape[0] // REUSE
    if peers == 16 and need == CAP * peers:
        slots = CAP
        buffers, owners = tree_gather(integrals)
    else:
        slots = 0
        buffers = [lax.all_gather(integrals, "tile", axis=0, tiled=True)]
        owners = jnp.zeros((1,), jnp.int32)
    order = sorted_order(t2_col)
    rows = jnp.take(t2_row, order)
    ids = jnp.take(t2_col, order)[::REUSE]
    notes = lax.ppermute(jnp.concatenate([rows, ids]), "tile", opposite)
    far_rows, far_ids = notes[: REUSE * need], notes[REUSE * need :]
    cut = REUSE * (need - need // LAST)
    tiles = [jnp.take(t2_tiles, order[:cut], axis=0), jnp.take(t2_tiles, order[cut:], axis=0)]
    far_tiles = [lax.ppermute(part, "tile", opposite) for part in tiles]
    total, flipped = own_part(slots, rows, ids, far_ids, owners, tiles, buffers, flip_matrix(W))
    total = far_part(0, far_rows, far_tiles[0], flipped, total, jnp.float32)
    return far_part(cut, far_rows, far_tiles[1], flipped, total, jnp.bfloat16)


def solution(mesh):
    in_specs = (
        P(("groups", "tile"), None, None),
        P(("groups", "tile")),
        P(("groups", "tile")),
        P(("groups", "tile"), None, None),
    )
    out_specs = P(("groups", "tile"), None, None)
    return jax.shard_map(
        per_device, mesh=mesh, in_specs=in_specs, out_specs=out_specs, check_vma=False
    )
```

```python
import jax
import jax.numpy as jnp
from jax import lax
from jax.experimental import pallas as pl
from jax.experimental.pallas import tpu as pltpu
from jax.sharding import PartitionSpec as P

W = 32
PPD = 16
REUSE = 3
CAP = 2
LAST = 4
VMEM_LIMIT = 56 * 1024 * 1024


def sorted_order(t2_col):
    count = t2_col.shape[0]
    ids = jnp.arange(count, dtype=jnp.int32)
    before = (t2_col[None, :] < t2_col[:, None]) | (
        (t2_col[None, :] == t2_col[:, None]) & (ids[None, :] < ids[:, None])
    )
    rank = jnp.sum(before.astype(jnp.int32), axis=1)
    return jnp.sum(jnp.where(rank[None, :] == ids[:, None], ids[None, :], 0), axis=1)


def flip_matrix(width):
    columns = jnp.arange(width * width, dtype=jnp.int32)
    source = (columns % width) * width + columns // width
    return (columns[:, None] == source[None, :]).astype(jnp.bfloat16)


def together(*values):
    return lax.optimization_barrier(values)


def send(value, pairs):
    return lax.ppermute(value, "tile", pairs)


def flipped_bit(bit):
    return [(i, i ^ bit) for i in range(16)]


def staged_gather(shard, notes, tiles):
    centre = [i for i in range(16) if i // 4 in (1, 2)]
    across = [(i, i ^ 12) for i in centre]
    outward = [(i, i ^ 4) for i in centre]
    other_z, other_y, other_core, opposite = (flipped_bit(bit) for bit in (4, 2, 1, 8))
    me = lax.axis_index("tile")
    z = me // 4
    in_centre = (z == 1) | (z == 2)

    near = send(shard, other_z)
    first = send(shard, across)
    y_own = send(shard, other_y)
    c_own = send(shard, other_core)
    far_notes = send(notes, opposite)
    near, first, y_own, c_own, far_notes, *tiles = together(near, first, y_own, c_own, far_notes, *tiles)

    second = send(near, across)
    first = jnp.where(in_centre, first, send(first, outward))
    y_near = send(near, other_y)
    c_near = send(near, other_core)
    c_y_own = send(y_own, other_core)
    second, first, y_near, c_near, c_y_own, *tiles = together(second, first, y_near, c_near, c_y_own, *tiles)

    far_first = send(tiles[0], opposite)
    second = jnp.where(in_centre, second, send(second, outward))
    y_first = send(first, other_y)
    c_first = send(first, other_core)
    c_y_near = send(y_near, other_core)
    second, y_first, c_first, c_y_near, *tiles = together(second, y_first, c_first, c_y_near, *tiles)

    y_second = send(second, other_y)
    c_second = send(second, other_core)
    c_y_first = send(y_first, other_core)
    y_second, c_second, c_y_first, *tiles = together(y_second, c_second, c_y_first, *tiles)

    c_y_second = send(y_second, other_core)

    buffers = [shard, c_own, near, c_near, first, c_first, second, c_second]
    buffers += [y_own, c_y_own, y_near, c_y_near, y_first, c_y_first, y_second, c_y_second]
    low = z < 2
    zs = [z, z ^ 1, jnp.where(low, 2, 1), jnp.where(low, 3, 0)]
    owners = [4 * zs[k] + ((me & 3) ^ (2 * y + c)) for y in (0, 1) for k in range(4) for c in (0, 1)]
    return buffers, jnp.stack(owners).astype(jnp.int32), far_notes, tiles, far_first


def own_kernel(slots, rows, own_ids, far_ids, owners, tiles_refs, buffer_refs, perm_ref, sum_ref, flip_ref,
               own_blocks, far_blocks, own_sems, far_sems):
    need = own_blocks.shape[0]
    local = buffer_refs[0].shape[0]

    def fetch(buffer_ref, ids, slot, landing, sems):
        offset = lax.rem(ids[slot], local)
        pltpu.make_async_copy(buffer_ref.at[offset], landing.at[slot], sems.at[slot]).start()

    if slots:
        for ids, landing, sems in ((own_ids, own_blocks, own_sems), (far_ids, far_blocks, far_sems)):
            for number, buffer_ref in enumerate(buffer_refs):
                for extra in range(slots):
                    fetch(buffer_ref, ids, owners[number] * slots + extra, landing, sems)
    else:
        for ids, landing, sems in ((own_ids, own_blocks, own_sems), (far_ids, far_blocks, far_sems)):

            @pl.loop(0, need)
            def _(slot):
                fetch(buffer_refs[0], ids, slot, landing, sems)

    sum_ref[...] = jnp.zeros_like(sum_ref)
    base = 0
    for tiles_ref in tiles_refs:
        count, height, depth = tiles_ref.shape

        @pl.loop(0, count // REUSE)
        def _(step, tiles_ref=tiles_ref, base=base):
            slot = base + step
            pltpu.make_async_copy(own_blocks.at[slot], own_blocks.at[slot], own_sems.at[slot]).wait()
            block = own_blocks[slot]
            for part in range(REUSE):
                row = rows[slot * REUSE + part]
                sum_ref[row] += jnp.dot(tiles_ref[step * REUSE + part], block, preferred_element_type=jnp.float32)

        base += count // REUSE

    @pl.loop(0, need)
    def _(slot):
        pltpu.make_async_copy(far_blocks.at[slot], far_blocks.at[slot], far_sems.at[slot]).wait()
        flip_ref[slot] = jnp.dot(
            far_blocks[slot], perm_ref[...], preferred_element_type=jnp.float32
        ).astype(jnp.bfloat16)


def own_part(slots, rows, own_ids, far_ids, owners, tiles, buffers, perm):
    need = own_ids.shape[0]
    height = tiles[0].shape[1]
    depth, width = buffers[0].shape[1:]

    def kernel(rows, own_ids, far_ids, owners, *refs):
        tiles_refs = refs[: len(tiles)]
        buffer_refs = refs[len(tiles) : len(tiles) + len(buffers)]
        own_kernel(slots, rows, own_ids, far_ids, owners, tiles_refs, buffer_refs, *refs[len(tiles) + len(buffers) :])

    vmem = pl.BlockSpec(memory_space=pltpu.VMEM)
    return pl.pallas_call(
        kernel,
        in_specs=[pl.BlockSpec(memory_space=pltpu.SMEM)] * 4
        + [vmem] * len(tiles)
        + [pl.BlockSpec(memory_space=pl.ANY)] * len(buffers)
        + [vmem],
        out_specs=[vmem, vmem],
        out_shape=[
            jax.ShapeDtypeStruct((PPD, height, width), jnp.float32),
            jax.ShapeDtypeStruct((need, depth, width), jnp.bfloat16),
        ],
        scratch_shapes=[
            pltpu.VMEM((need, depth, width), jnp.bfloat16),
            pltpu.VMEM((need, depth, width), jnp.bfloat16),
            pltpu.SemaphoreType.DMA((need,)),
            pltpu.SemaphoreType.DMA((need,)),
        ],
        compiler_params=pltpu.CompilerParams(vmem_limit_bytes=VMEM_LIMIT),
        name="own_part",
    )(rows, own_ids, far_ids, owners, *tiles, *buffers, perm)


def far_kernel(base, rows, tiles_ref, flip_ref, base_ref, out_ref, sum_ref):
    step = pl.program_id(0)

    @pl.when(step == 0)
    def _():
        sum_ref[...] = base_ref[...]

    for part in range(REUSE):
        row = rows[base + step * REUSE + part]
        sum_ref[row] += jnp.dot(tiles_ref[part], flip_ref[0], preferred_element_type=jnp.float32)

    @pl.when(step == pl.num_programs(0) - 1)
    def _():
        out_ref[...] = sum_ref[...].astype(out_ref.dtype)


def far_part(base, rows, tiles, flipped, total, dtype):
    depth, width = flipped.shape[1:]
    count, height = tiles.shape[:2]
    whole = (PPD, height, width)
    first = base // REUSE

    def kernel(*refs):
        far_kernel(base, *refs)

    return pl.pallas_call(
        kernel,
        grid_spec=pltpu.PrefetchScalarGridSpec(
            num_scalar_prefetch=1,
            grid=(count // REUSE,),
            in_specs=[
                pl.BlockSpec((REUSE, height, depth), lambda j, rows: (j, 0, 0)),
                pl.BlockSpec((1, depth, width), lambda j, rows: (first + j, 0, 0)),
                pl.BlockSpec(whole, lambda j, rows: (0, 0, 0), pipeline_mode=pl.Buffered(1)),
            ],
            out_specs=pl.BlockSpec(whole, lambda j, rows: (0, 0, 0), pipeline_mode=pl.Buffered(1)),
            scratch_shapes=[pltpu.VMEM(whole, jnp.float32)],
        ),
        out_shape=jax.ShapeDtypeStruct(whole, dtype),
        compiler_params=pltpu.CompilerParams(vmem_limit_bytes=VMEM_LIMIT),
        name="far_part",
    )(rows, tiles, flipped, total)


def per_device(t2_tiles, t2_row, t2_col, integrals):
    peers = lax.axis_size("tile")
    count = t2_col.shape[0]
    need = count // REUSE
    opposite = [(source, (source + peers // 2) % peers) for source in range(peers)]
    order = sorted_order(t2_col)
    rows = jnp.take(t2_row, order)
    ids = jnp.take(t2_col, order)[::REUSE]
    cut = REUSE * (need - need // LAST)
    tiles = [jnp.take(t2_tiles, order[:cut], axis=0), jnp.take(t2_tiles, order[cut:], axis=0)]
    notes = jnp.concatenate([t2_row, t2_col])
    if peers == 16 and need == CAP * peers:
        slots = CAP
        buffers, owners, notes, tiles, far_first = staged_gather(integrals, notes, tiles)
    else:
        slots = 0
        buffers = [lax.all_gather(integrals, "tile", axis=0, tiled=True)]
        owners = jnp.zeros((1,), jnp.int32)
        notes = send(notes, opposite)
        far_first = send(tiles[0], opposite)
    far_order = sorted_order(notes[count:])
    far_rows = jnp.take(notes[:count], far_order)
    far_ids = jnp.take(notes[count:], far_order)[::REUSE]
    total, flipped = own_part(slots, rows, ids, far_ids, owners, tiles, buffers, flip_matrix(W))
    total, rest = together(total, tiles[1])
    far_rest = send(rest, opposite)
    total = far_part(0, far_rows, far_first, flipped, total, jnp.float32)
    return far_part(cut, far_rows, far_rest, flipped, total, jnp.bfloat16)


def solution(mesh):
    in_specs = (
        P(("groups", "tile"), None, None),
        P(("groups", "tile")),
        P(("groups", "tile")),
        P(("groups", "tile"), None, None),
    )
    out_specs = P(("groups", "tile"), None, None)
    return jax.shard_map(
        per_device, mesh=mesh, in_specs=in_specs, out_specs=out_specs, check_vma=False
    )
```

```python
import functools

import jax
import jax.numpy as jnp
from jax import lax
from jax.experimental import pallas as pl
from jax.experimental.pallas import tpu as pltpu
from jax.sharding import PartitionSpec as P

W = 32
PPD = 16
REUSE = 3
QUAD = 4
LAST = 8
COLUMNS = 256
MIB = 1024 * 1024
SMEM = pl.BlockSpec(memory_space=pltpu.SMEM)
VMEM = pl.BlockSpec(memory_space=pltpu.VMEM)
ANY = pl.BlockSpec(memory_space=pl.ANY)


def flip_matrix(width):
    columns = jnp.arange(width * width, dtype=jnp.int32)
    source = (columns % width) * width + columns // width
    return (columns[:, None] == source[None, :]).astype(jnp.bfloat16)


def tables_kernel(rows, cols, starts, tile_at, block_at, slots, cursor):
    count, total = rows.shape[0], slots.shape[0]

    @pl.loop(0, total)
    def _(block):
        slots[block] = 0

    for row in range(PPD):
        cursor[row] = 0

    @pl.loop(0, count)
    def _(tile):
        cursor[rows[tile]] += 1
        slots[cols[tile]] = 1

    place = jnp.int32(0)
    for row in range(PPD):
        size = cursor[row]
        starts[row] = place
        cursor[row] = place
        place += size
    starts[PPD] = place

    def number(block, used):
        named = slots[block]
        slots[block] = jnp.where(named > 0, used, -1)
        return used + named

    lax.fori_loop(0, total, number, jnp.int32(0))

    @pl.loop(0, count)
    def _(tile):
        row = rows[tile]
        position = cursor[row]
        cursor[row] = position + 1
        tile_at[position] = tile
        block_at[position] = slots[cols[tile]]


def tables(rows, cols, total):
    count = rows.shape[0]
    return pl.pallas_call(
        tables_kernel,
        in_specs=[SMEM] * 2,
        out_specs=[SMEM] * 4,
        out_shape=[jax.ShapeDtypeStruct((size,), jnp.int32) for size in (PPD + 1, count, count, total)],
        scratch_shapes=[pltpu.SMEM((PPD,), jnp.int32)],
        name="tables",
    )(rows, cols)


def sort_kernel(tile_at, tiles_ref, first_ref, rest_ref, first_sem, rest_sem):
    cut = first_ref.shape[0]

    @pl.loop(0, cut)
    def _(position):
        pltpu.make_async_copy(tiles_ref.at[tile_at[position]], first_ref.at[position], first_sem).start()

    @pl.loop(0, rest_ref.shape[0])
    def _(position):
        pltpu.make_async_copy(tiles_ref.at[tile_at[cut + position]], rest_ref.at[position], rest_sem).start()

    pltpu.make_async_copy(first_ref, first_ref, first_sem).wait()
    pltpu.make_async_copy(rest_ref, rest_ref, rest_sem).wait()


def sort_tiles(tile_at, tiles, cut):
    count, height, depth = tiles.shape
    return pl.pallas_call(
        sort_kernel,
        in_specs=[SMEM, ANY],
        out_specs=[ANY] * 2,
        out_shape=[jax.ShapeDtypeStruct((size, height, depth), tiles.dtype) for size in (cut, count - cut)],
        scratch_shapes=[pltpu.SemaphoreType.DMA] * 2,
        name="sort_tiles",
    )(tile_at, tiles)


def add_row(sum_ref, fresh, begin, end, tile_of, block_of):
    width = sum_ref.shape[1]

    @pl.loop(0, (end - begin + QUAD - 1) // QUAD)
    def _(turn):
        here = begin + turn * QUAD
        places = [jnp.minimum(here + part, end - 1) for part in range(QUAD)]
        left = [tile_of(places[0])]
        for part in range(1, QUAD):
            tile = tile_of(places[part])
            left.append(jnp.where(here + part < end, tile, jnp.zeros_like(tile)))
        left = jnp.concatenate(left, axis=1)
        for column in range(0, width, COLUMNS):
            window = pl.ds(column, COLUMNS)
            right = jnp.concatenate([block_of(place, window) for place in places], axis=0)
            product = jnp.dot(left, right, preferred_element_type=jnp.float32)
            if fresh:
                sum_ref[:, window] = jnp.where(turn == 0, 0.0, sum_ref[:, window]) + product
            else:
                sum_ref[:, window] += product


def own_kernel(counts, starts, tile_at, block_at, own_slots, far_slots, firsts, tiles_ref, perm_ref, *refs):
    pieces = refs[: len(counts)]
    sum_out, flip_out, own_blocks, far_blocks, sums, own_sems, far_sems, sum_sem, flip_sem = refs[len(counts) :]

    for slots, landing, sems in ((far_slots, far_blocks, far_sems), (own_slots, own_blocks, own_sems)):
        for number, (piece, count) in enumerate(zip(pieces, counts)):

            def fetch(offset, slots=slots, landing=landing, sems=sems, piece=piece, number=number):
                slot = slots[firsts[number] + offset]

                @pl.when(slot >= 0)
                def _():
                    pltpu.make_async_copy(piece.at[offset], landing.at[slot], sems.at[slot]).start()

            if count <= 8:
                for offset in range(count):
                    fetch(offset)
            else:
                pl.loop(0, count)(fetch)

    def arrived(landing, sems, slot):
        pltpu.make_async_copy(landing.at[slot], landing.at[slot], sems.at[slot]).wait()

    need = own_blocks.shape[0]

    @pl.loop(0, need)
    def _(slot):
        arrived(far_blocks, far_sems, slot)
        far_blocks[slot] = jnp.dot(
            far_blocks[slot], perm_ref[...], preferred_element_type=jnp.float32
        ).astype(jnp.bfloat16)
        pltpu.make_async_copy(far_blocks.at[slot], flip_out.at[slot], flip_sem).start()

    @pl.loop(0, need)
    def _(slot):
        arrived(own_blocks, own_sems, slot)

    @pl.loop(0, PPD)
    def _(row):
        begin, end = starts[row], starts[row + 1]

        @pl.when(begin == end)
        def _():
            sums[row] = jnp.zeros(sums.shape[1:], jnp.float32)

        add_row(
            sums.at[row],
            True,
            begin,
            end,
            lambda place: tiles_ref[tile_at[place]],
            lambda place, window: own_blocks[block_at[place], :, window],
        )
        pltpu.make_async_copy(sums.at[row], sum_out.at[row], sum_sem).start()

    pltpu.make_async_copy(far_blocks, flip_out, flip_sem).wait()
    pltpu.make_async_copy(sums, sum_out, sum_sem).wait()


def own_part(own_tables, far_slots, tiles, pieces, firsts):
    starts, tile_at, block_at, own_slots = own_tables
    count, height, _ = tiles.shape
    depth, width = pieces[0].shape[1:]
    need = count // REUSE
    counts = [piece.shape[0] for piece in pieces]
    return pl.pallas_call(
        functools.partial(own_kernel, counts),
        in_specs=[SMEM] * 6 + [VMEM] * 2 + [ANY] * len(pieces),
        out_specs=[ANY] * 2,
        out_shape=[
            jax.ShapeDtypeStruct((PPD, height, width), jnp.float32),
            jax.ShapeDtypeStruct((need, depth, width), jnp.bfloat16),
        ],
        scratch_shapes=[
            pltpu.VMEM((need, depth, width), jnp.bfloat16),
            pltpu.VMEM((need, depth, width), jnp.bfloat16),
            pltpu.VMEM((PPD, height, width), jnp.float32),
            pltpu.SemaphoreType.DMA((need,)),
            pltpu.SemaphoreType.DMA((need,)),
            pltpu.SemaphoreType.DMA,
            pltpu.SemaphoreType.DMA,
        ],
        compiler_params=pltpu.CompilerParams(vmem_limit_bytes=44 * MIB),
        name="own_part",
    )(starts, tile_at, block_at, own_slots, far_slots, firsts, tiles, flip_matrix(W), *pieces)


def far_first_kernel(starts, block_at, tiles_ref, sum_in, flip_in, sum_out, result, blocks, sums, rounded,
                     block_sem, row_sems, back_sem, out_sems):
    cut = tiles_ref.shape[0]
    pltpu.make_async_copy(flip_in, blocks, block_sem).start()
    for row in range(PPD):
        pltpu.make_async_copy(sum_in.at[row], sums.at[row], row_sems.at[row]).start()
    pltpu.make_async_copy(flip_in, blocks, block_sem).wait()

    @pl.loop(0, PPD)
    def _(row):
        pltpu.make_async_copy(sum_in.at[row], sums.at[row], row_sems.at[row]).wait()
        begin, stop = starts[row], starts[row + 1]
        end = jnp.minimum(stop, cut)
        add_row(
            sums.at[row],
            False,
            begin,
            end,
            lambda place: tiles_ref[place],
            lambda place, window: blocks[block_at[place], :, window],
        )

        @pl.when(stop <= cut)
        def _():
            rounded[row] = sums[row].astype(rounded.dtype)
            pltpu.make_async_copy(rounded.at[row], result.at[row], out_sems.at[row]).start()

        @pl.when((begin < cut) & (stop > cut))
        def _():
            copy = pltpu.make_async_copy(sums.at[row], sum_out.at[row], back_sem)
            copy.start()
            copy.wait()

    @pl.loop(0, PPD)
    def _(row):
        @pl.when(starts[row + 1] <= cut)
        def _():
            pltpu.make_async_copy(rounded.at[row], result.at[row], out_sems.at[row]).wait()


def far_first_part(far_tables, tiles, total, flipped):
    starts, _, block_at, _ = far_tables
    whole = total.shape
    return pl.pallas_call(
        far_first_kernel,
        in_specs=[SMEM] * 2 + [VMEM] + [ANY] * 2,
        out_specs=[ANY] * 2,
        out_shape=[jax.ShapeDtypeStruct(whole, jnp.float32), jax.ShapeDtypeStruct(whole, jnp.bfloat16)],
        input_output_aliases={3: 0},
        scratch_shapes=[
            pltpu.VMEM(flipped.shape, jnp.bfloat16),
            pltpu.VMEM(whole, jnp.float32),
            pltpu.VMEM(whole, jnp.bfloat16),
            pltpu.SemaphoreType.DMA,
            pltpu.SemaphoreType.DMA((PPD,)),
            pltpu.SemaphoreType.DMA,
            pltpu.SemaphoreType.DMA((PPD,)),
        ],
        compiler_params=pltpu.CompilerParams(vmem_limit_bytes=36 * MIB),
        name="far_first",
    )(starts, block_at, tiles, total, flipped)


def far_rest_kernel(cut, starts, block_at, tiles_ref, sum_in, flip_in, result_in, result, blocks, sums, rounded,
                    block_sem, row_sems, out_sems):
    del result_in
    count = tiles_ref.shape[0]

    @pl.loop(0, count)
    def _(number):
        pltpu.make_async_copy(flip_in.at[block_at[cut + number]], blocks.at[number], block_sem).start()

    def open_rows(action):
        @pl.loop(0, PPD)
        def _(row):
            @pl.when(starts[row + 1] > cut)
            def _():
                action(row)

    def load(row):
        return pltpu.make_async_copy(sum_in.at[row], sums.at[row], row_sems.at[row])

    def store(row):
        return pltpu.make_async_copy(rounded.at[row], result.at[row], out_sems.at[row])

    open_rows(lambda row: load(row).start())
    pltpu.make_async_copy(blocks, blocks, block_sem).wait()

    def finish(row):
        load(row).wait()
        add_row(
            sums.at[row],
            False,
            jnp.maximum(starts[row], cut),
            starts[row + 1],
            lambda place: tiles_ref[place - cut],
            lambda place, window: blocks[place - cut, :, window],
        )
        rounded[row] = sums[row].astype(rounded.dtype)
        store(row).start()

    open_rows(finish)
    open_rows(lambda row: store(row).wait())


def far_rest_part(far_tables, tiles, total, flipped, result):
    starts, _, block_at, _ = far_tables
    count = block_at.shape[0]
    whole = total.shape
    return pl.pallas_call(
        functools.partial(far_rest_kernel, count - tiles.shape[0]),
        in_specs=[SMEM] * 2 + [VMEM] + [ANY] * 3,
        out_specs=ANY,
        out_shape=jax.ShapeDtypeStruct(whole, result.dtype),
        input_output_aliases={5: 0},
        scratch_shapes=[
            pltpu.VMEM((tiles.shape[0],) + flipped.shape[1:], jnp.bfloat16),
            pltpu.VMEM(whole, jnp.float32),
            pltpu.VMEM(whole, jnp.bfloat16),
            pltpu.SemaphoreType.DMA,
            pltpu.SemaphoreType.DMA((PPD,)),
            pltpu.SemaphoreType.DMA((PPD,)),
        ],
        compiler_params=pltpu.CompilerParams(vmem_limit_bytes=36 * MIB),
        name="far_rest",
    )(starts, block_at, tiles, total, flipped, result)


def together(*values):
    return lax.optimization_barrier(values)


def send(value, pairs):
    return lax.ppermute(value, "tile", pairs)


def flipped_bit(bit):
    return [(i, i ^ bit) for i in range(16)]


def staged_gather(shard, notes, tiles):
    centre = [i for i in range(16) if i // 4 in (1, 2)]
    across = [(i, i ^ 12) for i in centre]
    outward = [(i, i ^ 4) for i in centre]
    other_z, other_y, other_core, opposite = (flipped_bit(bit) for bit in (4, 2, 1, 8))
    me = lax.axis_index("tile")
    z = me // 4
    in_centre = (z == 1) | (z == 2)

    near = send(shard, other_z)
    first = send(shard, across)
    y_own = send(shard, other_y)
    c_own = send(shard, other_core)
    far_notes = send(notes, opposite)
    near, first, y_own, c_own, far_notes, *tiles = together(near, first, y_own, c_own, far_notes, *tiles)

    second = send(near, across)
    first = jnp.where(in_centre, first, send(first, outward))
    y_near = send(near, other_y)
    c_near = send(near, other_core)
    c_y_own = send(y_own, other_core)
    second, first, y_near, c_near, c_y_own, *tiles = together(second, first, y_near, c_near, c_y_own, *tiles)

    far_first = send(tiles[0], opposite)
    second = jnp.where(in_centre, second, send(second, outward))
    y_first = send(first, other_y)
    c_first = send(first, other_core)
    c_y_near = send(y_near, other_core)
    second, y_first, c_first, c_y_near, *tiles = together(second, y_first, c_first, c_y_near, *tiles)

    y_second = send(second, other_y)
    c_second = send(second, other_core)
    c_y_first = send(y_first, other_core)
    y_second, c_second, c_y_first, *tiles = together(y_second, c_second, c_y_first, *tiles)

    half = y_second.shape[0] // 2
    c_y_second = [send(y_second[:half], other_core), send(y_second[half:], other_core)]

    buffers = [shard, c_own, near, c_near, first, c_first, second, c_second]
    buffers += [y_own, c_y_own, y_near, c_y_near, y_first, c_y_first, y_second, *c_y_second]
    low = z < 2
    zs = [z, z ^ 1, jnp.where(low, 2, 1), jnp.where(low, 3, 0)]
    owners = [4 * zs[k] + ((me & 3) ^ (2 * y + c)) for y in (0, 1) for k in range(4) for c in (0, 1)]
    local = shard.shape[0]
    firsts = [owner * local for owner in owners]
    firsts.append(firsts[-1] + half)
    return buffers, jnp.stack(firsts).astype(jnp.int32), far_notes, tiles, far_first


def per_device(t2_tiles, t2_row, t2_col, integrals):
    peers = lax.axis_size("tile")
    count = t2_col.shape[0]
    block_total = peers * integrals.shape[0]
    opposite = [(source, (source + peers // 2) % peers) for source in range(peers)]
    own_tables = tables(t2_row, t2_col, block_total)
    tiles = sort_tiles(own_tables[1], t2_tiles, count - count // LAST)
    notes = jnp.stack([t2_row, t2_col])
    if peers == 16:
        pieces, firsts, notes, tiles, far_first = staged_gather(integrals, notes, tiles)
    else:
        pieces = [lax.all_gather(integrals, "tile", axis=0, tiled=True)]
        firsts = jnp.zeros((1,), jnp.int32)
        notes = send(notes, opposite)
        far_first = send(tiles[0], opposite)
    far_tables = tables(notes[0], notes[1], block_total)
    total, flipped = own_part(own_tables, far_tables[3], t2_tiles, pieces, firsts)
    total, rest = together(total, tiles[1])
    far_rest = send(rest, opposite)
    total, result = far_first_part(far_tables, far_first, total, flipped)
    return far_rest_part(far_tables, far_rest, total, flipped, result)


def solution(mesh):
    in_specs = (
        P(("groups", "tile"), None, None),
        P(("groups", "tile")),
        P(("groups", "tile")),
        P(("groups", "tile"), None, None),
    )
    out_specs = P(("groups", "tile"), None, None)
    return jax.shard_map(
        per_device, mesh=mesh, in_specs=in_specs, out_specs=out_specs, check_vma=False
    )
```

```python
import functools

import jax
import jax.numpy as jnp
from jax import lax
from jax.experimental import pallas as pl
from jax.experimental.pallas import tpu as pltpu
from jax.sharding import PartitionSpec as P

W = 32
PPD = 16
REUSE = 3
QUAD = 4
SHARES = (22, 20)
COLUMNS = 256
MIB = 1024 * 1024
SMEM = pl.BlockSpec(memory_space=pltpu.SMEM)
VMEM = pl.BlockSpec(memory_space=pltpu.VMEM)
ANY = pl.BlockSpec(memory_space=pl.ANY)


def flip_matrix(width):
    columns = jnp.arange(width * width, dtype=jnp.int32)
    source = (columns % width) * width + columns // width
    return (columns[:, None] == source[None, :]).astype(jnp.bfloat16)


def tables_kernel(rows, cols, starts, tile_at, block_at, slots, cursor):
    count, total, groups = rows.shape[0], slots.shape[0], cursor.shape[0]

    @pl.loop(0, total)
    def _(block):
        slots[block] = 0

    for row in range(groups):
        cursor[row] = 0

    @pl.loop(0, count)
    def _(tile):
        cursor[rows[tile]] += 1
        slots[cols[tile]] = 1

    place = jnp.int32(0)
    for row in range(groups):
        size = cursor[row]
        starts[row] = place
        cursor[row] = place
        place += size
    starts[groups] = place

    def number(block, used):
        named = slots[block]
        slots[block] = jnp.where(named > 0, used, -1)
        return used + named

    lax.fori_loop(0, total, number, jnp.int32(0))

    @pl.loop(0, count)
    def _(tile):
        row = rows[tile]
        position = cursor[row]
        cursor[row] = position + 1
        tile_at[position] = tile
        block_at[position] = slots[cols[tile]]


def tables(rows, cols, total, groups=PPD):
    count = rows.shape[0]
    return pl.pallas_call(
        tables_kernel,
        in_specs=[SMEM] * 2,
        out_specs=[SMEM] * 4,
        out_shape=[jax.ShapeDtypeStruct((size,), jnp.int32) for size in (groups + 1, count, count, total)],
        scratch_shapes=[pltpu.SMEM((groups,), jnp.int32)],
        name="tables",
    )(rows, cols)


def sort_kernel(tile_at, tiles_ref, *refs):
    parts, sems = refs[: len(refs) // 2], refs[len(refs) // 2 :]
    base = 0
    for part, sem in zip(parts, sems):

        @pl.loop(0, part.shape[0])
        def _(number, part=part, sem=sem, base=base):
            pltpu.make_async_copy(tiles_ref.at[tile_at[base + number]], part.at[number], sem).start()

        base += part.shape[0]
    for part, sem in zip(parts, sems):
        pltpu.make_async_copy(part, part, sem).wait()


def sort_tiles(tile_at, tiles, sizes):
    return pl.pallas_call(
        sort_kernel,
        in_specs=[SMEM, ANY],
        out_specs=[VMEM] * len(sizes),
        out_shape=[jax.ShapeDtypeStruct((size,) + tiles.shape[1:], tiles.dtype) for size in sizes],
        scratch_shapes=[pltpu.SemaphoreType.DMA] * len(sizes),
        compiler_params=pltpu.CompilerParams(vmem_limit_bytes=16 * MIB),
        name="sort_tiles",
    )(tile_at, tiles)


def add_row(sum_ref, begin, end, tile_of, block_of):
    width = sum_ref.shape[1]

    @pl.loop(0, (end - begin + QUAD - 1) // QUAD)
    def _(turn):
        here = begin + turn * QUAD
        places = [jnp.minimum(here + part, end - 1) for part in range(QUAD)]
        left = [tile_of(places[0])]
        for part in range(1, QUAD):
            tile = tile_of(places[part])
            left.append(jnp.where(here + part < end, tile, jnp.zeros_like(tile)))
        left = jnp.concatenate(left, axis=1)
        for column in range(0, width, COLUMNS):
            window = pl.ds(column, COLUMNS)
            right = jnp.concatenate([block_of(place, window) for place in places], axis=0)
            sum_ref[:, window] += jnp.dot(left, right, preferred_element_type=jnp.float32)


def own_kernel(counts, group, fresh, starts, tile_at, block_at, own_slots, far_slots, firsts, tiles_ref, perm_ref, *refs):
    pieces = refs[: len(counts)]
    refs = refs[len(counts) :]
    if not fresh:
        sum_in, refs = refs[0], refs[2:]
    sum_out, flip_out, own_blocks, far_blocks, sums, own_list, far_list, own_sems, far_sems, row_sems = refs

    if not fresh:
        for row in range(PPD):
            pltpu.make_async_copy(sum_in.at[row], sums.at[row], row_sems.at[row]).start()

    def fetch(slots, landing, sems, fetched):
        found = jnp.int32(0)
        for number, (piece, count) in enumerate(zip(pieces, counts)):

            def one(offset, found, piece=piece, number=number):
                slot = slots[firsts[number] + offset]

                @pl.when(slot >= 0)
                def _():
                    fetched[found] = slot
                    pltpu.make_async_copy(piece.at[offset], landing.at[slot], sems.at[slot]).start()

                return found + (slot >= 0).astype(jnp.int32)

            found = lax.fori_loop(0, count, one, found)
        return found

    far_found = fetch(far_slots, far_blocks, far_sems, far_list)
    own_found = fetch(own_slots, own_blocks, own_sems, own_list)

    def arrived(landing, sems, slot):
        pltpu.make_async_copy(landing.at[slot], landing.at[slot], sems.at[slot]).wait()

    def flip_store(slot):
        return pltpu.make_async_copy(far_blocks.at[slot], flip_out.at[slot], far_sems.at[slot])

    @pl.loop(0, far_found)
    def _(number):
        slot = far_list[number]
        arrived(far_blocks, far_sems, slot)
        far_blocks[slot] = jnp.dot(
            far_blocks[slot], perm_ref[...], preferred_element_type=jnp.float32
        ).astype(jnp.bfloat16)
        flip_store(slot).start()

    @pl.loop(0, own_found)
    def _(number):
        arrived(own_blocks, own_sems, own_list[number])

    def store(row):
        return pltpu.make_async_copy(sums.at[row], sum_out.at[row], row_sems.at[row])

    @pl.loop(0, PPD)
    def _(row):
        if fresh:
            sums[row] = jnp.zeros(sums.shape[1:], jnp.float32)
        else:
            arrived(sums, row_sems, row)
        add_row(
            sums.at[row],
            starts[group + row],
            starts[group + row + 1],
            lambda place: tiles_ref[tile_at[place]],
            lambda place, window: own_blocks[block_at[place], :, window],
        )
        store(row).start()

    @pl.loop(0, far_found)
    def _(number):
        flip_store(far_list[number]).wait()

    @pl.loop(0, PPD)
    def _(row):
        store(row).wait()


def own_part(own_tables, far_slots, tiles, pieces, firsts, perm, group=0, earlier=()):
    starts, tile_at, block_at, own_slots = own_tables
    count, height, _ = tiles.shape
    depth, width = pieces[0].shape[1:]
    need = count // REUSE
    counts = [piece.shape[0] for piece in pieces]
    operands = 8 + len(pieces)
    return pl.pallas_call(
        functools.partial(own_kernel, counts, group, not earlier),
        in_specs=[SMEM] * 6 + [VMEM] * 2 + [ANY] * (len(pieces) + len(earlier)),
        out_specs=[ANY] * 2,
        out_shape=[
            jax.ShapeDtypeStruct((PPD, height, width), jnp.float32),
            jax.ShapeDtypeStruct((need, depth, width), jnp.bfloat16),
        ],
        input_output_aliases={operands: 0, operands + 1: 1} if earlier else {},
        scratch_shapes=[
            pltpu.VMEM((need, depth, width), jnp.bfloat16),
            pltpu.VMEM((need, depth, width), jnp.bfloat16),
            pltpu.VMEM((PPD, height, width), jnp.float32),
            pltpu.SMEM((need,), jnp.int32),
            pltpu.SMEM((need,), jnp.int32),
            pltpu.SemaphoreType.DMA((need,)),
            pltpu.SemaphoreType.DMA((need,)),
            pltpu.SemaphoreType.DMA((PPD,)),
        ],
        compiler_params=pltpu.CompilerParams(vmem_limit_bytes=56 * MIB),
        name="own_part",
    )(starts, tile_at, block_at, own_slots, far_slots, firsts, tiles, perm, *pieces, *earlier)


def far_kernel(base, starts, block_at, tiles_ref, sum_in, flip_in, *refs):
    if base:
        refs = refs[1:]
    sum_out, result, blocks, sums, rounded, block_sem, row_sems, out_sems = refs
    count = tiles_ref.shape[0]
    stop = base + count

    @pl.loop(0, count)
    def _(number):
        pltpu.make_async_copy(flip_in.at[block_at[base + number]], blocks.at[number], block_sem).start()

    def each_row(action):
        @pl.loop(0, PPD)
        def _(row):
            first, last = starts[row], starts[row + 1]

            @pl.when(((last > base) if base else True) & ((last <= stop) | (first < stop)))
            def _():
                action(row, last <= stop)

    def load(row):
        return pltpu.make_async_copy(sum_in.at[row], sums.at[row], row_sems.at[row])

    def store(row):
        return pltpu.make_async_copy(rounded.at[row], result.at[row], out_sems.at[row])

    def keep(row):
        return pltpu.make_async_copy(sums.at[row], sum_out.at[row], out_sems.at[row])

    each_row(lambda row, complete: load(row).start())
    pltpu.make_async_copy(blocks, blocks, block_sem).wait()

    def add(row, complete):
        load(row).wait()
        add_row(
            sums.at[row],
            jnp.maximum(starts[row], base),
            jnp.minimum(starts[row + 1], stop),
            lambda place: tiles_ref[place - base],
            lambda place, window: blocks[place - base, :, window],
        )

        @pl.when(complete)
        def _():
            rounded[row] = sums[row].astype(rounded.dtype)
            store(row).start()

        @pl.when(jnp.logical_not(complete))
        def _():
            keep(row).start()

    def finish(row, complete):
        pl.when(complete)(lambda: store(row).wait())
        pl.when(jnp.logical_not(complete))(lambda: keep(row).wait())

    each_row(add)
    each_row(finish)


def far_part(base, far_tables, tiles, flipped, total, result=None):
    starts, _, block_at, _ = far_tables
    whole = total.shape
    count = tiles.shape[0]
    given = [] if result is None else [result]
    aliases = {3: 0, 5: 1} if given else {3: 0}
    return pl.pallas_call(
        functools.partial(far_kernel, base),
        in_specs=[SMEM] * 2 + [VMEM] + [ANY] * (2 + len(given)),
        out_specs=[ANY] * 2,
        out_shape=[jax.ShapeDtypeStruct(whole, jnp.float32), jax.ShapeDtypeStruct(whole, jnp.bfloat16)],
        input_output_aliases=aliases,
        scratch_shapes=[
            pltpu.VMEM((count,) + flipped.shape[1:], jnp.bfloat16),
            pltpu.VMEM(whole, jnp.float32),
            pltpu.VMEM(whole, jnp.bfloat16),
            pltpu.SemaphoreType.DMA,
            pltpu.SemaphoreType.DMA((PPD,)),
            pltpu.SemaphoreType.DMA((PPD,)),
        ],
        compiler_params=pltpu.CompilerParams(vmem_limit_bytes=36 * MIB),
        name="far_part",
    )(starts, block_at, tiles, total, flipped, *given)


def together(*values):
    return lax.optimization_barrier(values)


def send(value, pairs):
    return lax.ppermute(value, "tile", pairs)


def flipped_bit(bit):
    return [(i, i ^ bit) for i in range(16)]


def staged_part(tiles, rows, cols, shard):
    local = shard.shape[0]
    block_total = 16 * local
    centre = [i for i in range(16) if i // 4 in (1, 2)]
    across = [(i, i ^ 12) for i in centre]
    outward = [(i, i ^ 4) for i in centre]
    other_z, other_y, other_core, opposite = (flipped_bit(bit) for bit in (4, 2, 1, 8))
    me = lax.axis_index("tile")
    z = me // 4
    in_centre = (z == 1) | (z == 2)
    zs = [z, z ^ 1, jnp.where(z < 2, 2, 1), jnp.where(z < 2, 3, 0)]

    def owner(k, bits):
        return 4 * zs[k] + ((me & 3) ^ bits)

    def first_blocks(owners):
        return jnp.stack([value * local for value in owners]).astype(jnp.int32)

    col_owner = cols // local
    late = (col_owner // 4 == zs[3]) | (col_owner == owner(2, 3))
    keys = rows + PPD * late.astype(jnp.int32)

    near = send(shard, other_z)
    first = send(shard, across)
    y_own = send(shard, other_y)
    c_own = send(shard, other_core)
    notes = send(jnp.stack([rows, cols]), opposite)
    order = tables(rows, cols, block_total)[1]
    sizes = tile_parts(tiles.shape[0])
    parts = sort_tiles(order, tiles, sizes)
    near, first, y_own, c_own, notes, *parts = together(near, first, y_own, c_own, notes, *parts)

    far_parts = [send(parts[0], opposite)]
    second = send(near, across)
    first = jnp.where(in_centre, first, send(first, outward))
    y_near = send(near, other_y)
    c_near = send(near, other_core)
    c_y_own = send(y_own, other_core)
    own_tables = tables(keys, cols, block_total, 2 * PPD)
    far_tables = tables(notes[0], notes[1], block_total)
    second, first, y_near, c_near, c_y_own, *rest = together(
        second, first, y_near, c_near, c_y_own, *parts[1:], *own_tables, *far_tables
    )
    parts, own_tables, far_tables = rest[: len(parts) - 1], rest[-8:-4], rest[-4:]

    second = jnp.where(in_centre, second, send(second, outward))
    y_first = send(first, other_y)
    c_first = send(first, other_core)
    c_y_near = send(y_near, other_core)
    second, y_first, c_first, c_y_near, far_parts[0] = together(second, y_first, c_first, c_y_near, far_parts[0])

    far_parts.append(send(parts[0], opposite))
    y_second = send(second, other_y)
    c_second = send(second, other_core)
    c_y_first = send(y_first, other_core)
    perm = flip_matrix(W)
    pieces = [shard, c_own, near, c_near, first, c_first, y_own, c_y_own, y_near, c_y_near, y_first]
    owners = [owner(k, y + core) for y in (0, 2) for k in range(3) for core in (0, 1)][:11]
    early = own_part(own_tables, far_tables[3], tiles, pieces, first_blocks(owners), perm)
    y_second, c_second, c_y_first, *early = together(y_second, c_second, c_y_first, *early)

    c_y_second = send(y_second, other_core)
    pieces = [c_y_first, second, c_second, y_second, c_y_second]
    owners = [owner(2, 3)] + [owner(3, bits) for bits in range(4)]
    total, flipped = own_part(own_tables, far_tables[3], tiles, pieces, first_blocks(owners), perm, PPD, early)
    far_parts.append(send(parts[1], opposite))
    return far_products(far_tables, far_parts, flipped, total)


def tile_parts(count):
    sizes = [count * share // 48 for share in SHARES]
    return sizes + [count - sum(sizes)]


def far_products(far_tables, far_parts, flipped, total):
    base, result = 0, None
    for part in far_parts:
        total, result = far_part(base, far_tables, part, flipped, total, result)
        base += part.shape[0]
    return result


def per_device(t2_tiles, t2_row, t2_col, integrals):
    peers = lax.axis_size("tile")
    if peers == 16:
        return staged_part(t2_tiles, t2_row, t2_col, integrals)
    block_total = peers * integrals.shape[0]
    opposite = [(source, (source + peers // 2) % peers) for source in range(peers)]
    own_tables = tables(t2_row, t2_col, block_total)
    parts = sort_tiles(own_tables[1], t2_tiles, tile_parts(t2_tiles.shape[0]))
    notes = send(jnp.stack([t2_row, t2_col]), opposite)
    far_parts = [send(part, opposite) for part in parts]
    blocks = lax.all_gather(integrals, "tile", axis=0, tiled=True)
    far_tables = tables(notes[0], notes[1], block_total)
    firsts = jnp.zeros((1,), jnp.int32)
    total, flipped = own_part(own_tables, far_tables[3], t2_tiles, [blocks], firsts, flip_matrix(W))
    return far_products(far_tables, far_parts, flipped, total)


def solution(mesh):
    in_specs = (
        P(("groups", "tile"), None, None),
        P(("groups", "tile")),
        P(("groups", "tile")),
        P(("groups", "tile"), None, None),
    )
    out_specs = P(("groups", "tile"), None, None)
    return jax.shard_map(
        per_device, mesh=mesh, in_specs=in_specs, out_specs=out_specs, check_vma=False
    )
```

```python
import functools

import jax
import jax.numpy as jnp
from jax import lax
from jax.experimental import pallas as pl
from jax.experimental.pallas import tpu as pltpu
from jax.sharding import PartitionSpec as P

W = 32
PPD = 16
REUSE = 3
QUAD = 4
SHARES = (24, 18)
COLUMNS = 256
MIB = 1024 * 1024
SMEM = pl.BlockSpec(memory_space=pltpu.SMEM)
VMEM = pl.BlockSpec(memory_space=pltpu.VMEM)
ANY = pl.BlockSpec(memory_space=pl.ANY)


def flip_matrix(width):
    columns = jnp.arange(width * width, dtype=jnp.int32)
    source = (columns % width) * width + columns // width
    return (columns[:, None] == source[None, :]).astype(jnp.bfloat16)


def tables_kernel(rows, cols, starts, tile_at, block_at, slots, cursor):
    count, total, groups = rows.shape[0], slots.shape[0], cursor.shape[0]

    @pl.loop(0, total)
    def _(block):
        slots[block] = 0

    for row in range(groups):
        cursor[row] = 0

    @pl.loop(0, count)
    def _(tile):
        cursor[rows[tile]] += 1
        slots[cols[tile]] = 1

    place = jnp.int32(0)
    for row in range(groups):
        size = cursor[row]
        starts[row] = place
        cursor[row] = place
        place += size
    starts[groups] = place

    def number(block, used):
        named = slots[block]
        slots[block] = jnp.where(named > 0, used, -1)
        return used + named

    lax.fori_loop(0, total, number, jnp.int32(0))

    @pl.loop(0, count)
    def _(tile):
        row = rows[tile]
        position = cursor[row]
        cursor[row] = position + 1
        tile_at[position] = tile
        block_at[position] = slots[cols[tile]]


def tables(rows, cols, total, groups=PPD):
    count = rows.shape[0]
    return pl.pallas_call(
        tables_kernel,
        in_specs=[SMEM] * 2,
        out_specs=[SMEM] * 4,
        out_shape=[jax.ShapeDtypeStruct((size,), jnp.int32) for size in (groups + 1, count, count, total)],
        scratch_shapes=[pltpu.SMEM((groups,), jnp.int32)],
        name="tables",
    )(rows, cols)


def sort_kernel(tile_at, tiles_ref, *refs):
    parts, sems = refs[: len(refs) // 2], refs[len(refs) // 2 :]
    base = 0
    for part, sem in zip(parts, sems):
        base %= tile_at.shape[0]

        @pl.loop(0, part.shape[0])
        def _(number, part=part, sem=sem, base=base):
            pltpu.make_async_copy(tiles_ref.at[tile_at[base + number]], part.at[number], sem).start()

        base += part.shape[0]
    for part, sem in zip(parts, sems):
        pltpu.make_async_copy(part, part, sem).wait()


def sort_tiles(tile_at, tiles, sizes):
    return pl.pallas_call(
        sort_kernel,
        in_specs=[SMEM, ANY],
        out_specs=[VMEM] * len(sizes),
        out_shape=[jax.ShapeDtypeStruct((size,) + tiles.shape[1:], tiles.dtype) for size in sizes],
        scratch_shapes=[pltpu.SemaphoreType.DMA] * len(sizes),
        compiler_params=pltpu.CompilerParams(vmem_limit_bytes=16 * MIB),
        name="sort_tiles",
    )(tile_at, tiles)


def add_row(sum_ref, begin, end, tile_of, block_of):
    width = sum_ref.shape[1]

    @pl.loop(0, (end - begin + QUAD - 1) // QUAD)
    def _(turn):
        here = begin + turn * QUAD
        places = [jnp.minimum(here + part, end - 1) for part in range(QUAD)]
        left = [tile_of(places[0])]
        for part in range(1, QUAD):
            tile = tile_of(places[part])
            left.append(jnp.where(here + part < end, tile, jnp.zeros_like(tile)))
        left = jnp.concatenate(left, axis=1)
        for column in range(0, width, COLUMNS):
            window = pl.ds(column, COLUMNS)
            right = jnp.concatenate([block_of(place, window) for place in places], axis=0)
            sum_ref[:, window] += jnp.dot(left, right, preferred_element_type=jnp.float32)


def own_kernel(counts, group, fresh, starts, tile_at, block_at, own_slots, far_slots, firsts, tiles_ref, perm_ref, *refs):
    pieces = refs[: len(counts)]
    refs = refs[len(counts) :]
    if not fresh:
        sum_in, refs = refs[0], refs[2:]
    sum_out, flip_out, own_blocks, far_blocks, sums, own_list, far_list, own_sems, far_sems, row_sems = refs

    if not fresh:
        for row in range(PPD):
            pltpu.make_async_copy(sum_in.at[row], sums.at[row], row_sems.at[row]).start()

    def fetch(slots, landing, sems, fetched):
        found = jnp.int32(0)
        for number, (piece, count) in enumerate(zip(pieces, counts)):

            def one(offset, found, piece=piece, number=number):
                slot = slots[firsts[number] + offset]

                @pl.when(slot >= 0)
                def _():
                    fetched[found] = slot
                    pltpu.make_async_copy(piece.at[offset], landing.at[slot], sems.at[slot]).start()

                return found + (slot >= 0).astype(jnp.int32)

            found = lax.fori_loop(0, count, one, found)
        return found

    far_found = fetch(far_slots, far_blocks, far_sems, far_list)
    own_found = fetch(own_slots, own_blocks, own_sems, own_list)

    def arrived(landing, sems, slot):
        pltpu.make_async_copy(landing.at[slot], landing.at[slot], sems.at[slot]).wait()

    def flip_store(slot):
        return pltpu.make_async_copy(far_blocks.at[slot], flip_out.at[slot], far_sems.at[slot])

    @pl.loop(0, far_found)
    def _(number):
        slot = far_list[number]
        arrived(far_blocks, far_sems, slot)
        far_blocks[slot] = jnp.dot(
            far_blocks[slot], perm_ref[...], preferred_element_type=jnp.float32
        ).astype(jnp.bfloat16)
        flip_store(slot).start()

    @pl.loop(0, own_found)
    def _(number):
        arrived(own_blocks, own_sems, own_list[number])

    def store(row):
        return pltpu.make_async_copy(sums.at[row], sum_out.at[row], row_sems.at[row])

    @pl.loop(0, PPD)
    def _(row):
        if fresh:
            sums[row] = jnp.zeros(sums.shape[1:], jnp.float32)
        else:
            arrived(sums, row_sems, row)
        add_row(
            sums.at[row],
            starts[group + row],
            starts[group + row + 1],
            lambda place: tiles_ref[tile_at[place]],
            lambda place, window: own_blocks[block_at[place], :, window],
        )
        store(row).start()

    @pl.loop(0, far_found)
    def _(number):
        flip_store(far_list[number]).wait()

    @pl.loop(0, PPD)
    def _(row):
        store(row).wait()


def own_part(own_tables, far_slots, tiles, pieces, firsts, perm, group=0, earlier=()):
    starts, tile_at, block_at, own_slots = own_tables
    count, height, _ = tiles.shape
    depth, width = pieces[0].shape[1:]
    need = count // REUSE
    counts = [piece.shape[0] for piece in pieces]
    operands = 8 + len(pieces)
    return pl.pallas_call(
        functools.partial(own_kernel, counts, group, not earlier),
        in_specs=[SMEM] * 6 + [VMEM] * 2 + [ANY] * (len(pieces) + len(earlier)),
        out_specs=[ANY] * 2,
        out_shape=[
            jax.ShapeDtypeStruct((PPD, height, width), jnp.float32),
            jax.ShapeDtypeStruct((need, depth, width), jnp.bfloat16),
        ],
        input_output_aliases={operands: 0, operands + 1: 1} if earlier else {},
        scratch_shapes=[
            pltpu.VMEM((need, depth, width), jnp.bfloat16),
            pltpu.VMEM((need, depth, width), jnp.bfloat16),
            pltpu.VMEM((PPD, height, width), jnp.float32),
            pltpu.SMEM((need,), jnp.int32),
            pltpu.SMEM((need,), jnp.int32),
            pltpu.SemaphoreType.DMA((need,)),
            pltpu.SemaphoreType.DMA((need,)),
            pltpu.SemaphoreType.DMA((PPD,)),
        ],
        compiler_params=pltpu.CompilerParams(vmem_limit_bytes=56 * MIB),
        name="own_part",
    )(starts, tile_at, block_at, own_slots, far_slots, firsts, tiles, perm, *pieces, *earlier)


def far_kernel(base, sources, starts, block_at, chosen, *refs):
    tile_refs, refs = refs[:sources], refs[sources:]
    sum_in, flip_in = refs[:2]
    refs = refs[3:] if base else refs[2:]
    sum_out, result, tiles_ref, blocks, sums, rounded, tile_sem, block_sem, row_sems, out_sems = refs
    count = tiles_ref.shape[0]
    stop = base + count

    for number, source in enumerate(tile_refs):

        @pl.when(chosen[0] == number)
        def _(source=source):
            begin = base if source.shape[0] > count else 0
            pltpu.make_async_copy(source.at[pl.ds(begin, count)], tiles_ref, tile_sem).start()

    @pl.loop(0, count)
    def _(number):
        pltpu.make_async_copy(flip_in.at[block_at[base + number]], blocks.at[number], block_sem).start()

    def each_row(action):
        @pl.loop(0, PPD)
        def _(row):
            first, last = starts[row], starts[row + 1]

            @pl.when(((last > base) if base else True) & ((last <= stop) | (first < stop)))
            def _():
                action(row, last <= stop)

    def load(row):
        return pltpu.make_async_copy(sum_in.at[row], sums.at[row], row_sems.at[row])

    def store(row):
        return pltpu.make_async_copy(rounded.at[row], result.at[row], out_sems.at[row])

    def keep(row):
        return pltpu.make_async_copy(sums.at[row], sum_out.at[row], out_sems.at[row])

    each_row(lambda row, complete: load(row).start())
    pltpu.make_async_copy(tiles_ref, tiles_ref, tile_sem).wait()
    pltpu.make_async_copy(blocks, blocks, block_sem).wait()

    def add(row, complete):
        load(row).wait()
        add_row(
            sums.at[row],
            jnp.maximum(starts[row], base),
            jnp.minimum(starts[row + 1], stop),
            lambda place: tiles_ref[place - base],
            lambda place, window: blocks[place - base, :, window],
        )

        @pl.when(complete)
        def _():
            rounded[row] = sums[row].astype(rounded.dtype)
            store(row).start()

        @pl.when(jnp.logical_not(complete))
        def _():
            keep(row).start()

    def finish(row, complete):
        pl.when(complete)(lambda: store(row).wait())
        pl.when(jnp.logical_not(complete))(lambda: keep(row).wait())

    each_row(add)
    each_row(finish)


def far_part(base, far_tables, chosen, sources, flipped, total, result=None):
    starts, _, block_at, _ = far_tables
    whole = total.shape
    tiles_shape = sources[-1].shape
    given = [] if result is None else [result]
    operand = 3 + len(sources)
    aliases = {operand: 0, operand + 2: 1} if given else {operand: 0}
    return pl.pallas_call(
        functools.partial(far_kernel, base, len(sources)),
        in_specs=[SMEM] * 3 + [ANY] * (len(sources) + 2 + len(given)),
        out_specs=[ANY] * 2,
        out_shape=[jax.ShapeDtypeStruct(whole, jnp.float32), jax.ShapeDtypeStruct(whole, jnp.bfloat16)],
        input_output_aliases=aliases,
        scratch_shapes=[
            pltpu.VMEM(tiles_shape, jnp.bfloat16),
            pltpu.VMEM(tiles_shape[:1] + flipped.shape[1:], jnp.bfloat16),
            pltpu.VMEM(whole, jnp.float32),
            pltpu.VMEM(whole, jnp.bfloat16),
            pltpu.SemaphoreType.DMA,
            pltpu.SemaphoreType.DMA,
            pltpu.SemaphoreType.DMA((PPD,)),
            pltpu.SemaphoreType.DMA((PPD,)),
        ],
        compiler_params=pltpu.CompilerParams(vmem_limit_bytes=36 * MIB),
        name="far_part",
    )(starts, block_at, chosen, *sources, total, flipped, *given)


def together(*values):
    return lax.optimization_barrier(values)


def send(value, pairs):
    return lax.ppermute(value, "tile", pairs)


def flipped_bit(bit):
    return [(i, i ^ bit) for i in range(16)]


def staged_part(tiles, rows, cols, shard):
    local = shard.shape[0]
    block_total = 16 * local
    centre = [i for i in range(16) if i // 4 in (1, 2)]
    across = [(i, i ^ 12) for i in centre]
    outward = [(i, i ^ 4) for i in centre]
    from_ends = [(i, i ^ 8) for i in range(16) if i not in centre]
    from_centre = [(i, i ^ 8) for i in centre]
    other_z, other_y, other_core, opposite = (flipped_bit(bit) for bit in (4, 2, 1, 8))
    me = lax.axis_index("tile")
    z = me // 4
    in_centre = (z == 1) | (z == 2)
    zs = [z, z ^ 1, jnp.where(z < 2, 2, 1), jnp.where(z < 2, 3, 0)]

    def owner(k, bits):
        return 4 * zs[k] + ((me & 3) ^ bits)

    def first_blocks(owners):
        return jnp.stack([value * local for value in owners]).astype(jnp.int32)

    col_owner = cols // local
    late = (col_owner // 4 == zs[3]) | (col_owner == owner(2, 3))
    keys = rows + PPD * late.astype(jnp.int32)

    near = send(shard, other_z)
    first = send(shard, across)
    y_own = send(shard, other_y)
    c_own = send(shard, other_core)
    notes = send(jnp.stack([rows, cols]), opposite)
    order = tables(rows, cols, block_total)[1]
    sizes = [tiles.shape[0]] + tile_parts(tiles.shape[0])
    whole, *parts = sort_tiles(order, tiles, sizes)
    near, first, y_own, c_own, notes, whole, *parts = together(near, first, y_own, c_own, notes, whole, *parts)

    second = send(near, across)
    first = jnp.where(in_centre, first, send(first, outward))
    y_near = send(near, other_y)
    c_near = send(near, other_core)
    c_y_own = send(y_own, other_core)
    own_tables = tables(keys, cols, block_total, 2 * PPD)
    far_tables = tables(notes[0], notes[1], block_total)
    second, first, y_near, c_near, c_y_own, whole, *rest = together(
        second, first, y_near, c_near, c_y_own, whole, *parts, *own_tables, *far_tables
    )
    parts, own_tables, far_tables = rest[: len(parts)], rest[-8:-4], rest[-4:]

    far_whole = send(whole, from_ends)
    far_parts = [send(part, from_centre) for part in parts]
    second = jnp.where(in_centre, second, send(second, outward))
    y_first = send(first, other_y)
    c_first = send(first, other_core)
    c_y_near = send(y_near, other_core)
    second, y_first, c_first, c_y_near = together(second, y_first, c_first, c_y_near)

    y_second = send(second, other_y)
    c_second = send(second, other_core)
    c_y_first = send(y_first, other_core)
    perm = flip_matrix(W)
    pieces = [shard, c_own, near, c_near, first, c_first, y_own, c_y_own, y_near, c_y_near, y_first]
    owners = [owner(k, y + core) for y in (0, 2) for k in range(3) for core in (0, 1)][:11]
    early = own_part(own_tables, far_tables[3], tiles, pieces, first_blocks(owners), perm)
    y_second, c_second, c_y_first, *early = together(y_second, c_second, c_y_first, *early)

    c_y_second = send(y_second, other_core)
    pieces = [c_y_first, second, c_second, y_second, c_y_second]
    owners = [owner(2, 3)] + [owner(3, bits) for bits in range(4)]
    total, flipped = own_part(own_tables, far_tables[3], tiles, pieces, first_blocks(owners), perm, PPD, early)
    chosen = in_centre.astype(jnp.int32).reshape(1)
    return far_products(far_tables, 1 - chosen, [[far_whole, part] for part in far_parts], flipped, total)


def tile_parts(count):
    sizes = [count * share // 48 for share in SHARES]
    return sizes + [count - sum(sizes)]


def far_products(far_tables, chosen, far_parts, flipped, total):
    base, result = 0, None
    for sources in far_parts:
        total, result = far_part(base, far_tables, chosen, sources, flipped, total, result)
        base += sources[-1].shape[0]
    return result


def per_device(t2_tiles, t2_row, t2_col, integrals):
    peers = lax.axis_size("tile")
    if peers == 16:
        return staged_part(t2_tiles, t2_row, t2_col, integrals)
    block_total = peers * integrals.shape[0]
    opposite = [(source, (source + peers // 2) % peers) for source in range(peers)]
    own_tables = tables(t2_row, t2_col, block_total)
    parts = sort_tiles(own_tables[1], t2_tiles, tile_parts(t2_tiles.shape[0]))
    notes = send(jnp.stack([t2_row, t2_col]), opposite)
    far_parts = [send(part, opposite) for part in parts]
    blocks = lax.all_gather(integrals, "tile", axis=0, tiled=True)
    far_tables = tables(notes[0], notes[1], block_total)
    zero = jnp.zeros((1,), jnp.int32)
    total, flipped = own_part(own_tables, far_tables[3], t2_tiles, [blocks], zero, flip_matrix(W))
    return far_products(far_tables, zero, [[part] for part in far_parts], flipped, total)


def solution(mesh):
    in_specs = (
        P(("groups", "tile"), None, None),
        P(("groups", "tile")),
        P(("groups", "tile")),
        P(("groups", "tile"), None, None),
    )
    out_specs = P(("groups", "tile"), None, None)
    return jax.shard_map(
        per_device, mesh=mesh, in_specs=in_specs, out_specs=out_specs, check_vma=False
    )
```

```python
import functools

import jax
import jax.numpy as jnp
from jax import lax
from jax.experimental import pallas as pl
from jax.experimental.pallas import tpu as pltpu
from jax.sharding import PartitionSpec as P

W = 32
PPD = 16
REUSE = 3
QUAD = 4
SHARES = (24, 18)
COLUMNS = 256
MIB = 1024 * 1024
SMEM = pl.BlockSpec(memory_space=pltpu.SMEM)
VMEM = pl.BlockSpec(memory_space=pltpu.VMEM)
ANY = pl.BlockSpec(memory_space=pl.ANY)


def flip_matrix(width):
    columns = jnp.arange(width * width, dtype=jnp.int32)
    source = (columns % width) * width + columns // width
    return (columns[:, None] == source[None, :]).astype(jnp.bfloat16)


def tables_kernel(rows, cols, starts, tile_at, block_at, slots, cursor):
    count, total, groups = rows.shape[0], slots.shape[0], cursor.shape[0]

    @pl.loop(0, total)
    def _(block):
        slots[block] = 0

    for row in range(groups):
        cursor[row] = 0

    @pl.loop(0, count)
    def _(tile):
        cursor[rows[tile]] += 1
        slots[cols[tile]] = 1

    place = jnp.int32(0)
    for row in range(groups):
        size = cursor[row]
        starts[row] = place
        cursor[row] = place
        place += size
    starts[groups] = place

    def number(block, used):
        named = slots[block]
        slots[block] = jnp.where(named > 0, used, -1)
        return used + named

    lax.fori_loop(0, total, number, jnp.int32(0))

    @pl.loop(0, count)
    def _(tile):
        row = rows[tile]
        position = cursor[row]
        cursor[row] = position + 1
        tile_at[position] = tile
        block_at[position] = slots[cols[tile]]


def tables(rows, cols, total, groups=PPD):
    count = rows.shape[0]
    return pl.pallas_call(
        tables_kernel,
        in_specs=[SMEM] * 2,
        out_specs=[SMEM] * 4,
        out_shape=[jax.ShapeDtypeStruct((size,), jnp.int32) for size in (groups + 1, count, count, total)],
        scratch_shapes=[pltpu.SMEM((groups,), jnp.int32)],
        name="tables",
    )(rows, cols)


def window(ref, tile):
    depth = ref.shape[1]
    across = ref.shape[2] // depth
    if across == 1:
        return ref.at[tile]
    return ref.at[lax.div(tile, across), :, pl.ds(pl.multiple_of(lax.rem(tile, across) * depth, depth), depth)]


def sort_kernel(choices, tile_at, chosen, tiles_ref, *refs):
    parts, sems = refs[: len(refs) // 2], refs[len(refs) // 2 :]
    begin = {choice: 0 for choice in choices}
    for choice, part, sem in zip(choices, parts, sems):
        base = begin[choice]
        count = part.shape[0] * part.shape[2] // tiles_ref.shape[2]
        begin[choice] += count

        @pl.when(chosen[0] == choice)
        def _(part=part, sem=sem, base=base, count=count):
            @pl.loop(0, count)
            def _(number):
                pltpu.make_async_copy(tiles_ref.at[tile_at[base + number]], window(part, number), sem).start()

    for choice, part, sem in zip(choices, parts, sems):

        @pl.when(chosen[0] == choice)
        def _(part=part, sem=sem):
            pltpu.make_async_copy(part, part, sem).wait()


def sort_tiles(tile_at, chosen, tiles, choices, shapes):
    return pl.pallas_call(
        functools.partial(sort_kernel, choices),
        in_specs=[SMEM] * 2 + [ANY],
        out_specs=[VMEM] * len(shapes),
        out_shape=[jax.ShapeDtypeStruct(shape, tiles.dtype) for shape in shapes],
        scratch_shapes=[pltpu.SemaphoreType.DMA] * len(shapes),
        compiler_params=pltpu.CompilerParams(vmem_limit_bytes=16 * MIB),
        name="sort_tiles",
    )(tile_at, chosen, tiles)


def add_row(sum_ref, begin, end, tile_of, block_of):
    width = sum_ref.shape[1]

    @pl.loop(0, (end - begin + QUAD - 1) // QUAD)
    def _(turn):
        here = begin + turn * QUAD
        places = [jnp.minimum(here + part, end - 1) for part in range(QUAD)]
        left = [tile_of(places[0])]
        for part in range(1, QUAD):
            tile = tile_of(places[part])
            left.append(jnp.where(here + part < end, tile, jnp.zeros_like(tile)))
        left = jnp.concatenate(left, axis=1)
        for column in range(0, width, COLUMNS):
            window = pl.ds(column, COLUMNS)
            right = jnp.concatenate([block_of(place, window) for place in places], axis=0)
            sum_ref[:, window] += jnp.dot(left, right, preferred_element_type=jnp.float32)


def own_kernel(counts, group, fresh, starts, tile_at, block_at, own_slots, far_slots, firsts, tiles_ref, perm_ref, *refs):
    pieces = refs[: len(counts)]
    refs = refs[len(counts) :]
    if not fresh:
        sum_in, refs = refs[0], refs[2:]
    sum_out, flip_out, own_blocks, far_blocks, sums, own_list, far_list, own_sems, far_sems, row_sems = refs

    if not fresh:
        for row in range(PPD):
            pltpu.make_async_copy(sum_in.at[row], sums.at[row], row_sems.at[row]).start()

    def fetch(slots, landing, sems, fetched):
        found = jnp.int32(0)
        for number, (piece, count) in enumerate(zip(pieces, counts)):

            def one(offset, found, piece=piece, number=number):
                slot = slots[firsts[number] + offset]

                @pl.when(slot >= 0)
                def _():
                    fetched[found] = slot
                    pltpu.make_async_copy(piece.at[offset], landing.at[slot], sems.at[slot]).start()

                return found + (slot >= 0).astype(jnp.int32)

            found = lax.fori_loop(0, count, one, found)
        return found

    far_found = fetch(far_slots, far_blocks, far_sems, far_list)
    own_found = fetch(own_slots, own_blocks, own_sems, own_list)

    def arrived(landing, sems, slot):
        pltpu.make_async_copy(landing.at[slot], landing.at[slot], sems.at[slot]).wait()

    def flip_store(slot):
        return pltpu.make_async_copy(far_blocks.at[slot], flip_out.at[slot], far_sems.at[slot])

    @pl.loop(0, far_found)
    def _(number):
        slot = far_list[number]
        arrived(far_blocks, far_sems, slot)
        far_blocks[slot] = jnp.dot(
            far_blocks[slot], perm_ref[...], preferred_element_type=jnp.float32
        ).astype(jnp.bfloat16)
        flip_store(slot).start()

    @pl.loop(0, own_found)
    def _(number):
        arrived(own_blocks, own_sems, own_list[number])

    def store(row):
        return pltpu.make_async_copy(sums.at[row], sum_out.at[row], row_sems.at[row])

    @pl.loop(0, PPD)
    def _(row):
        if fresh:
            sums[row] = jnp.zeros(sums.shape[1:], jnp.float32)
        else:
            arrived(sums, row_sems, row)
        add_row(
            sums.at[row],
            starts[group + row],
            starts[group + row + 1],
            lambda place: tiles_ref[tile_at[place]],
            lambda place, window: own_blocks[block_at[place], :, window],
        )
        store(row).start()

    @pl.loop(0, far_found)
    def _(number):
        flip_store(far_list[number]).wait()

    @pl.loop(0, PPD)
    def _(row):
        store(row).wait()


def own_part(own_tables, far_slots, tiles, pieces, firsts, perm, group=0, earlier=()):
    starts, tile_at, block_at, own_slots = own_tables
    count, height, _ = tiles.shape
    depth, width = pieces[0].shape[1:]
    need = count // REUSE
    counts = [piece.shape[0] for piece in pieces]
    operands = 8 + len(pieces)
    return pl.pallas_call(
        functools.partial(own_kernel, counts, group, not earlier),
        in_specs=[SMEM] * 6 + [VMEM] * 2 + [ANY] * (len(pieces) + len(earlier)),
        out_specs=[ANY] * 2,
        out_shape=[
            jax.ShapeDtypeStruct((PPD, height, width), jnp.float32),
            jax.ShapeDtypeStruct((need, depth, width), jnp.bfloat16),
        ],
        input_output_aliases={operands: 0, operands + 1: 1} if earlier else {},
        scratch_shapes=[
            pltpu.VMEM((need, depth, width), jnp.bfloat16),
            pltpu.VMEM((need, depth, width), jnp.bfloat16),
            pltpu.VMEM((PPD, height, width), jnp.float32),
            pltpu.SMEM((need,), jnp.int32),
            pltpu.SMEM((need,), jnp.int32),
            pltpu.SemaphoreType.DMA((need,)),
            pltpu.SemaphoreType.DMA((need,)),
            pltpu.SemaphoreType.DMA((PPD,)),
        ],
        compiler_params=pltpu.CompilerParams(vmem_limit_bytes=56 * MIB),
        name="own_part",
    )(starts, tile_at, block_at, own_slots, far_slots, firsts, tiles, perm, *pieces, *earlier)


def far_kernel(base, segments, starts, block_at, chosen, *refs):
    tile_refs, refs = refs[: len(segments)], refs[len(segments) :]
    sum_in, flip_in = refs[:2]
    refs = refs[3:] if base else refs[2:]
    sum_out, result, tiles_ref, blocks, sums, rounded, tile_sem, block_sem, row_sems, out_sems = refs
    count = tiles_ref.shape[0]
    stop = base + count

    for source, (choice, begin) in zip(tile_refs, segments):
        held = source.shape[0] * source.shape[2] // tiles_ref.shape[2]
        low, high = max(begin, base), min(begin + held, stop)

        @pl.when(chosen[0] == choice)
        def _(source=source, begin=begin, low=low, high=high):
            if source.shape[2] == tiles_ref.shape[2]:
                here, there = source.at[pl.ds(low - begin, high - low)], tiles_ref.at[pl.ds(low - base, high - low)]
                pltpu.make_async_copy(here, there, tile_sem).start()
            else:

                @pl.loop(low, high)
                def _(place):
                    pltpu.make_async_copy(window(source, place - begin), tiles_ref.at[place - base], tile_sem).start()

    @pl.loop(0, count)
    def _(number):
        pltpu.make_async_copy(flip_in.at[block_at[base + number]], blocks.at[number], block_sem).start()

    def each_row(action):
        @pl.loop(0, PPD)
        def _(row):
            first, last = starts[row], starts[row + 1]

            @pl.when(((last > base) if base else True) & ((last <= stop) | (first < stop)))
            def _():
                action(row, last <= stop)

    def load(row):
        return pltpu.make_async_copy(sum_in.at[row], sums.at[row], row_sems.at[row])

    def store(row):
        return pltpu.make_async_copy(rounded.at[row], result.at[row], out_sems.at[row])

    def keep(row):
        return pltpu.make_async_copy(sums.at[row], sum_out.at[row], out_sems.at[row])

    each_row(lambda row, complete: load(row).start())
    pltpu.make_async_copy(tiles_ref, tiles_ref, tile_sem).wait()
    pltpu.make_async_copy(blocks, blocks, block_sem).wait()

    def add(row, complete):
        load(row).wait()
        add_row(
            sums.at[row],
            jnp.maximum(starts[row], base),
            jnp.minimum(starts[row + 1], stop),
            lambda place: tiles_ref[place - base],
            lambda place, window: blocks[place - base, :, window],
        )

        @pl.when(complete)
        def _():
            rounded[row] = sums[row].astype(rounded.dtype)
            store(row).start()

        @pl.when(jnp.logical_not(complete))
        def _():
            keep(row).start()

    def finish(row, complete):
        pl.when(complete)(lambda: store(row).wait())
        pl.when(jnp.logical_not(complete))(lambda: keep(row).wait())

    each_row(add)
    each_row(finish)


def far_part(base, count, far_tables, chosen, sources, flipped, total, result=None):
    starts, _, block_at, _ = far_tables
    whole = total.shape
    given = [] if result is None else [result]
    held = [array.size // (whole[1] * flipped.shape[1]) for _, _, array in sources]
    used = [
        (source[:2], source[2])
        for source, size in zip(sources, held)
        if source[1] < base + count and source[1] + size > base
    ]
    operand = 3 + len(used)
    aliases = {operand: 0, operand + 2: 1} if given else {operand: 0}
    return pl.pallas_call(
        functools.partial(far_kernel, base, [segment for segment, _ in used]),
        in_specs=[SMEM] * 3 + [ANY] * (len(used) + 2 + len(given)),
        out_specs=[ANY] * 2,
        out_shape=[jax.ShapeDtypeStruct(whole, jnp.float32), jax.ShapeDtypeStruct(whole, jnp.bfloat16)],
        input_output_aliases=aliases,
        scratch_shapes=[
            pltpu.VMEM((count, whole[1], flipped.shape[1]), jnp.bfloat16),
            pltpu.VMEM((count,) + flipped.shape[1:], jnp.bfloat16),
            pltpu.VMEM(whole, jnp.float32),
            pltpu.VMEM(whole, jnp.bfloat16),
            pltpu.SemaphoreType.DMA,
            pltpu.SemaphoreType.DMA,
            pltpu.SemaphoreType.DMA((PPD,)),
            pltpu.SemaphoreType.DMA((PPD,)),
        ],
        compiler_params=pltpu.CompilerParams(vmem_limit_bytes=36 * MIB),
        name="far_part",
    )(starts, block_at, chosen, *[array for _, array in used], total, flipped, *given)


def together(*values):
    return lax.optimization_barrier(values)


def send(value, pairs):
    return lax.ppermute(value, "tile", pairs)


def flipped_bit(bit):
    return [(i, i ^ bit) for i in range(16)]


def staged_part(tiles, rows, cols, shard):
    local = shard.shape[0]
    block_total = 16 * local
    centre = [i for i in range(16) if i // 4 in (1, 2)]
    across = [(i, i ^ 12) for i in centre]
    from_ends = [(i, i ^ 8) for i in range(16) if i not in centre]
    from_centre = [(i, i ^ 8) for i in centre]
    around = [(i, i ^ 4) for i in centre] + from_ends
    other_z, other_y, other_core, opposite = (flipped_bit(bit) for bit in (4, 2, 1, 8))
    me = lax.axis_index("tile")
    z = me // 4
    in_centre = (z == 1) | (z == 2)
    at_end = 1 - in_centre.astype(jnp.int32).reshape(1)
    zs = [z, z ^ 1, jnp.where(z < 2, 2, 1), jnp.where(z < 2, 3, 0)]

    def owner(k, bits):
        return 4 * zs[k] + ((me & 3) ^ bits)

    def first_blocks(firsts):
        return jnp.stack(firsts).astype(jnp.int32)

    col_owner = cols // local
    late = (col_owner // 4 == zs[3]) | (col_owner == owner(2, 3))
    keys = rows + PPD * late.astype(jnp.int32)

    near = send(shard, other_z)
    first = send(shard, across)
    y_own = send(shard, other_y)
    c_own = send(shard, other_core)
    notes = send(jnp.stack([rows, cols]), opposite)
    order = tables(rows, cols, block_total)[1]
    count = tiles.shape[0]
    step = shard.size // tiles[0].size
    sizes = tile_parts(count)
    shapes = [shard.shape] * 2 + [(size,) + tiles.shape[1:] for size in [count - 2 * step] + sizes]
    parts = sort_tiles(order, at_end, tiles, [1, 1, 1, 0, 0, 0], shapes)
    near, first, y_own, c_own, notes, *parts = together(near, first, y_own, c_own, notes, *parts)

    outer = send(jnp.where(in_centre, first, parts[0]), around)
    second = send(near, across)
    y_near = send(near, other_y)
    c_near = send(near, other_core)
    c_y_own = send(y_own, other_core)
    own_tables = tables(keys, cols, block_total, 2 * PPD)
    far_tables = tables(notes[0], notes[1], block_total)
    far_ends = [outer]
    first = jnp.where(in_centre, first, outer)
    second, first, y_near, c_near, c_y_own, *rest = together(
        second, first, y_near, c_near, c_y_own, *parts[1:], *own_tables, *far_tables
    )
    parts, own_tables, far_tables = rest[:5], rest[5:9], rest[9:]

    outer = send(jnp.where(in_centre, second, parts[0]), around)
    far_ends += [outer, send(parts[1], from_ends)]
    y_first = send(first, other_y)
    c_first = send(first, other_core)
    c_y_near = send(y_near, other_core)
    halves = (slice(0, local // 2), slice(local // 2, None))
    second = [jnp.where(in_centre, second[half], outer[half]) for half in halves]
    *second, y_first, c_first, c_y_near = together(*second, y_first, c_first, c_y_near)

    far_centre = [send(part, from_centre) for part in parts[2:]]
    y_second = [send(half, other_y) for half in second]
    perm = flip_matrix(W)
    pieces = [shard, c_own, near, c_near, first, c_first, y_own, c_y_own, y_near, c_y_near, y_first]
    firsts = [owner(k, y + core) * local for y in (0, 2) for k in range(3) for core in (0, 1)][:11]
    early = own_part(own_tables, far_tables[3], tiles, pieces, first_blocks(firsts), perm)
    *y_second, y_first, far_ends[2], total, flipped = together(*y_second, y_first, far_ends[2], *early)

    c_y_first = send(y_first, other_core)
    c_second = [send(half, other_core) for half in second]
    c_y_second = [send(half, other_core) for half in y_second]
    pieces = [c_y_first, *second, *c_second, *y_second, *c_y_second]
    firsts = [owner(2, 3) * local] + [owner(3, bits) * local + half for bits in range(4) for half in (0, local // 2)]
    total, flipped = own_part(own_tables, far_tables[3], tiles, pieces, first_blocks(firsts), perm, PPD, (total, flipped))

    sources = [(0, step * number, array) for number, array in enumerate(far_ends)]
    sources += [(1, sum(sizes[:number]), array) for number, array in enumerate(far_centre)]
    return far_products(far_tables, at_end, sources, sizes, flipped, total)


def tile_parts(count):
    sizes = [count * share // 48 for share in SHARES]
    return sizes + [count - sum(sizes)]


def far_products(far_tables, chosen, sources, sizes, flipped, total):
    base, result = 0, None
    for size in sizes:
        total, result = far_part(base, size, far_tables, chosen, sources, flipped, total, result)
        base += size
    return result


def per_device(t2_tiles, t2_row, t2_col, integrals):
    peers = lax.axis_size("tile")
    if peers == 16:
        return staged_part(t2_tiles, t2_row, t2_col, integrals)
    block_total = peers * integrals.shape[0]
    opposite = [(source, (source + peers // 2) % peers) for source in range(peers)]
    own_tables = tables(t2_row, t2_col, block_total)
    sizes = tile_parts(t2_tiles.shape[0])
    zero = jnp.zeros((1,), jnp.int32)
    parts = sort_tiles(own_tables[1], zero, t2_tiles, [0] * 3, [(size,) + t2_tiles.shape[1:] for size in sizes])
    notes = send(jnp.stack([t2_row, t2_col]), opposite)
    sources = [(0, sum(sizes[:number]), send(part, opposite)) for number, part in enumerate(parts)]
    blocks = lax.all_gather(integrals, "tile", axis=0, tiled=True)
    far_tables = tables(notes[0], notes[1], block_total)
    total, flipped = own_part(own_tables, far_tables[3], t2_tiles, [blocks], zero, flip_matrix(W))
    return far_products(far_tables, zero, sources, sizes, flipped, total)


def solution(mesh):
    in_specs = (
        P(("groups", "tile"), None, None),
        P(("groups", "tile")),
        P(("groups", "tile")),
        P(("groups", "tile"), None, None),
    )
    out_specs = P(("groups", "tile"), None, None)
    return jax.shard_map(
        per_device, mesh=mesh, in_specs=in_specs, out_specs=out_specs, check_vma=False
    )
```

```python
import functools

import jax
import jax.numpy as jnp
from jax import lax
from jax.experimental import pallas as pl
from jax.experimental.pallas import tpu as pltpu
from jax.sharding import PartitionSpec as P

W = 32
PPD = 16
REUSE = 3
SHARES = (24, 18)
COLUMNS = 512
MIB = 1024 * 1024
SMEM = pl.BlockSpec(memory_space=pltpu.SMEM)
VMEM = pl.BlockSpec(memory_space=pltpu.VMEM)
ANY = pl.BlockSpec(memory_space=pl.ANY)


def flip_matrix(width):
    columns = jnp.arange(width * width, dtype=jnp.int32)
    source = (columns % width) * width + columns // width
    return (columns[:, None] == source[None, :]).astype(jnp.bfloat16)


def tables_kernel(rows, cols, starts, tile_at, block_at, slots, cursor):
    count, total, groups = rows.shape[0], slots.shape[0], cursor.shape[0]

    @pl.loop(0, total)
    def _(block):
        slots[block] = 0

    for row in range(groups):
        cursor[row] = 0

    @pl.loop(0, count)
    def _(tile):
        cursor[rows[tile]] += 1
        slots[cols[tile]] = 1

    place = jnp.int32(0)
    for row in range(groups):
        size = cursor[row]
        starts[row] = place
        cursor[row] = place
        place += size
    starts[groups] = place

    def number(block, used):
        named = slots[block]
        slots[block] = jnp.where(named > 0, used, -1)
        return used + named

    lax.fori_loop(0, total, number, jnp.int32(0))

    @pl.loop(0, count)
    def _(tile):
        row = rows[tile]
        position = cursor[row]
        cursor[row] = position + 1
        tile_at[position] = tile
        block_at[position] = slots[cols[tile]]


def tables(rows, cols, total, groups=PPD):
    count = rows.shape[0]
    return pl.pallas_call(
        tables_kernel,
        in_specs=[SMEM] * 2,
        out_specs=[SMEM] * 4,
        out_shape=[jax.ShapeDtypeStruct((size,), jnp.int32) for size in (groups + 1, count, count, total)],
        scratch_shapes=[pltpu.SMEM((groups,), jnp.int32)],
        name="tables",
    )(rows, cols)


def window(ref, tile):
    depth = ref.shape[1]
    across = ref.shape[2] // depth
    if across == 1:
        return ref.at[tile]
    return ref.at[lax.div(tile, across), :, pl.ds(pl.multiple_of(lax.rem(tile, across) * depth, depth), depth)]


def sort_kernel(choices, tile_at, chosen, tiles_ref, *refs):
    parts, sems = refs[: len(refs) // 2], refs[len(refs) // 2 :]
    begin = {choice: 0 for choice in choices}
    for choice, part, sem in zip(choices, parts, sems):
        base = begin[choice]
        count = part.shape[0] * part.shape[2] // tiles_ref.shape[2]
        begin[choice] += count

        @pl.when(chosen[0] == choice)
        def _(part=part, sem=sem, base=base, count=count):
            @pl.loop(0, count)
            def _(number):
                pltpu.make_async_copy(tiles_ref.at[tile_at[base + number]], window(part, number), sem).start()

    for choice, part, sem in zip(choices, parts, sems):

        @pl.when(chosen[0] == choice)
        def _(part=part, sem=sem):
            pltpu.make_async_copy(part, part, sem).wait()


def sort_tiles(tile_at, chosen, tiles, choices, shapes):
    return pl.pallas_call(
        functools.partial(sort_kernel, choices),
        in_specs=[SMEM] * 2 + [ANY],
        out_specs=[VMEM] * len(shapes),
        out_shape=[jax.ShapeDtypeStruct(shape, tiles.dtype) for shape in shapes],
        scratch_shapes=[pltpu.SemaphoreType.DMA] * len(shapes),
        compiler_params=pltpu.CompilerParams(vmem_limit_bytes=16 * MIB),
        name="sort_tiles",
    )(tile_at, chosen, tiles)


def add_row(sum_ref, begin, end, depth, ready, tile_of, block_of):
    width = sum_ref.shape[1]

    @pl.loop(0, (end - begin + depth - 1) // depth)
    def _(turn):
        here = begin + turn * depth
        places = [jnp.minimum(here + part, end - 1) for part in range(depth)]
        left = []
        for part, place in enumerate(places):
            inside = here + part < end
            pl.when(inside)(functools.partial(ready, place))
            tile = tile_of(place)
            left.append(jnp.where(inside, tile, jnp.zeros_like(tile)))
        left = jnp.concatenate(left, axis=1)
        for column in range(0, width, COLUMNS):
            window = pl.ds(column, COLUMNS)
            right = jnp.concatenate([block_of(place, window) for place in places], axis=0)
            sum_ref[:, window] += jnp.dot(left, right, preferred_element_type=jnp.float32)


def own_kernel(counts, group, fresh, starts, tile_at, block_at, own_slots, far_slots, firsts, tiles_ref, perm_ref, *refs):
    pieces = refs[: len(counts)]
    refs = refs[len(counts) :]
    if not fresh:
        sum_in, refs = refs[0], refs[2:]
    sum_out, flip_out, own_blocks, far_blocks, sums, own_list, far_list, own_sems, far_sems, row_sems = refs

    if not fresh:
        for row in range(PPD):
            pltpu.make_async_copy(sum_in.at[row], sums.at[row], row_sems.at[row]).start()

    def fetch(slots, landing, sems, fetched):
        found = jnp.int32(0)
        for number, (piece, count) in enumerate(zip(pieces, counts)):

            def one(offset, found, piece=piece, number=number):
                slot = slots[firsts[number] + offset]

                @pl.when(slot >= 0)
                def _():
                    fetched[found] = slot
                    pltpu.make_async_copy(piece.at[offset], landing.at[slot], sems.at[slot]).start()

                return found + (slot >= 0).astype(jnp.int32)

            found = lax.fori_loop(0, count, one, found)
        return found

    far_found = fetch(far_slots, far_blocks, far_sems, far_list)
    own_found = fetch(own_slots, own_blocks, own_sems, own_list)

    def arrived(landing, sems, slot):
        pltpu.make_async_copy(landing.at[slot], landing.at[slot], sems.at[slot]).wait()

    def flip_store(slot):
        return pltpu.make_async_copy(far_blocks.at[slot], flip_out.at[slot], far_sems.at[slot])

    @pl.loop(0, far_found)
    def _(number):
        slot = far_list[number]
        arrived(far_blocks, far_sems, slot)
        far_blocks[slot] = jnp.dot(
            far_blocks[slot], perm_ref[...], preferred_element_type=jnp.float32
        ).astype(jnp.bfloat16)
        flip_store(slot).start()

    @pl.loop(0, own_found)
    def _(number):
        arrived(own_blocks, own_sems, own_list[number])

    def store(row):
        return pltpu.make_async_copy(sums.at[row], sum_out.at[row], row_sems.at[row])

    @pl.loop(0, PPD)
    def _(row):
        if fresh:
            sums[row] = jnp.zeros(sums.shape[1:], jnp.float32)
        else:
            arrived(sums, row_sems, row)
        add_row(
            sums.at[row],
            starts[group + row],
            starts[group + row + 1],
            4 if fresh else 2,
            lambda place: None,
            lambda place: tiles_ref[tile_at[place]],
            lambda place, window: own_blocks[block_at[place], :, window],
        )
        store(row).start()

    @pl.loop(0, far_found)
    def _(number):
        flip_store(far_list[number]).wait()

    @pl.loop(0, PPD)
    def _(row):
        store(row).wait()


def own_part(own_tables, far_slots, tiles, pieces, firsts, perm, group=0, earlier=()):
    starts, tile_at, block_at, own_slots = own_tables
    count, height, _ = tiles.shape
    depth, width = pieces[0].shape[1:]
    need = count // REUSE
    counts = [piece.shape[0] for piece in pieces]
    operands = 8 + len(pieces)
    return pl.pallas_call(
        functools.partial(own_kernel, counts, group, not earlier),
        in_specs=[SMEM] * 6 + [VMEM] * 2 + [ANY] * (len(pieces) + len(earlier)),
        out_specs=[ANY] * 2,
        out_shape=[
            jax.ShapeDtypeStruct((PPD, height, width), jnp.float32),
            jax.ShapeDtypeStruct((need, depth, width), jnp.bfloat16),
        ],
        input_output_aliases={operands: 0, operands + 1: 1} if earlier else {},
        scratch_shapes=[
            pltpu.VMEM((need, depth, width), jnp.bfloat16),
            pltpu.VMEM((need, depth, width), jnp.bfloat16),
            pltpu.VMEM((PPD, height, width), jnp.float32),
            pltpu.SMEM((need,), jnp.int32),
            pltpu.SMEM((need,), jnp.int32),
            pltpu.SemaphoreType.DMA((need,)),
            pltpu.SemaphoreType.DMA((need,)),
            pltpu.SemaphoreType.DMA((PPD,)),
        ],
        compiler_params=pltpu.CompilerParams(vmem_limit_bytes=56 * MIB),
        name="own_part",
    )(starts, tile_at, block_at, own_slots, far_slots, firsts, tiles, perm, *pieces, *earlier)


def far_kernel(base, segments, starts, block_at, chosen, *refs):
    tile_refs, refs = refs[: len(segments)], refs[len(segments) :]
    sum_in, flip_in = refs[:2]
    refs = refs[3:] if base else refs[2:]
    sum_out, result, tiles_ref, blocks, sums, rounded, tile_sem, block_sems, row_sems, out_sems = refs
    count = tiles_ref.shape[0]
    stop = base + count

    for source, (choice, begin) in zip(tile_refs, segments):
        held = source.shape[0] * source.shape[2] // tiles_ref.shape[2]
        low, high = max(begin, base), min(begin + held, stop)

        @pl.when(chosen[0] == choice)
        def _(source=source, begin=begin, low=low, high=high):
            if source.shape[2] == tiles_ref.shape[2]:
                here, there = source.at[pl.ds(low - begin, high - low)], tiles_ref.at[pl.ds(low - base, high - low)]
                pltpu.make_async_copy(here, there, tile_sem).start()
            else:

                @pl.loop(low, high)
                def _(place):
                    pltpu.make_async_copy(window(source, place - begin), tiles_ref.at[place - base], tile_sem).start()

    @pl.loop(0, count)
    def _(number):
        pltpu.make_async_copy(flip_in.at[block_at[base + number]], blocks.at[number], block_sems.at[number]).start()

    def each_row(action):
        @pl.loop(0, PPD)
        def _(row):
            first, last = starts[row], starts[row + 1]

            @pl.when(((last > base) if base else True) & ((last <= stop) | (first < stop)))
            def _():
                action(row, last <= stop)

    def load(row):
        return pltpu.make_async_copy(sum_in.at[row], sums.at[row], row_sems.at[row])

    def store(row):
        return pltpu.make_async_copy(rounded.at[row], result.at[row], out_sems.at[row])

    def keep(row):
        return pltpu.make_async_copy(sums.at[row], sum_out.at[row], out_sems.at[row])

    each_row(lambda row, complete: load(row).start())
    pltpu.make_async_copy(tiles_ref, tiles_ref, tile_sem).wait()

    def ready(place):
        block = blocks.at[place - base]
        pltpu.make_async_copy(block, block, block_sems.at[place - base]).wait()

    def add(row, complete):
        load(row).wait()
        add_row(
            sums.at[row],
            jnp.maximum(starts[row], base),
            jnp.minimum(starts[row + 1], stop),
            4,
            ready,
            lambda place: tiles_ref[place - base],
            lambda place, window: blocks[place - base, :, window],
        )

        @pl.when(complete)
        def _():
            rounded[row] = sums[row].astype(rounded.dtype)
            store(row).start()

        @pl.when(jnp.logical_not(complete))
        def _():
            keep(row).start()

    def finish(row, complete):
        pl.when(complete)(lambda: store(row).wait())
        pl.when(jnp.logical_not(complete))(lambda: keep(row).wait())

    each_row(add)
    each_row(finish)


def far_part(base, count, far_tables, chosen, sources, flipped, total, result=None):
    starts, _, block_at, _ = far_tables
    whole = total.shape
    given = [] if result is None else [result]
    held = [array.size // (whole[1] * flipped.shape[1]) for _, _, array in sources]
    used = [
        (source[:2], source[2])
        for source, size in zip(sources, held)
        if source[1] < base + count and source[1] + size > base
    ]
    operand = 3 + len(used)
    aliases = {operand: 0, operand + 2: 1} if given else {operand: 0}
    return pl.pallas_call(
        functools.partial(far_kernel, base, [segment for segment, _ in used]),
        in_specs=[SMEM] * 3 + [ANY] * (len(used) + 2 + len(given)),
        out_specs=[ANY] * 2,
        out_shape=[jax.ShapeDtypeStruct(whole, jnp.float32), jax.ShapeDtypeStruct(whole, jnp.bfloat16)],
        input_output_aliases=aliases,
        scratch_shapes=[
            pltpu.VMEM((count, whole[1], flipped.shape[1]), jnp.bfloat16),
            pltpu.VMEM((count,) + flipped.shape[1:], jnp.bfloat16),
            pltpu.VMEM(whole, jnp.float32),
            pltpu.VMEM(whole, jnp.bfloat16),
            pltpu.SemaphoreType.DMA,
            pltpu.SemaphoreType.DMA((count,)),
            pltpu.SemaphoreType.DMA((PPD,)),
            pltpu.SemaphoreType.DMA((PPD,)),
        ],
        compiler_params=pltpu.CompilerParams(vmem_limit_bytes=56 * MIB),
        name="far_part",
    )(starts, block_at, chosen, *[array for _, array in used], total, flipped, *given)


def together(*values):
    return lax.optimization_barrier(values)


def send(value, pairs):
    return lax.ppermute(value, "tile", pairs)


def flipped_bit(bit):
    return [(i, i ^ bit) for i in range(16)]


def staged_part(tiles, rows, cols, shard):
    local = shard.shape[0]
    block_total = 16 * local
    centre = [i for i in range(16) if i // 4 in (1, 2)]
    across = [(i, i ^ 12) for i in centre]
    from_ends = [(i, i ^ 8) for i in range(16) if i not in centre]
    from_centre = [(i, i ^ 8) for i in centre]
    around = [(i, i ^ 4) for i in centre] + from_ends
    other_z, other_y, other_core, opposite = (flipped_bit(bit) for bit in (4, 2, 1, 8))
    me = lax.axis_index("tile")
    z = me // 4
    in_centre = (z == 1) | (z == 2)
    at_end = 1 - in_centre.astype(jnp.int32).reshape(1)
    zs = [z, z ^ 1, jnp.where(z < 2, 2, 1), jnp.where(z < 2, 3, 0)]

    def owner(k, bits):
        return 4 * zs[k] + ((me & 3) ^ bits)

    def first_blocks(firsts):
        return jnp.stack(firsts).astype(jnp.int32)

    col_owner = cols // local
    late = (col_owner // 4 == zs[3]) | (col_owner == owner(2, 3))
    keys = rows + PPD * late.astype(jnp.int32)

    near = send(shard, other_z)
    first = send(shard, across)
    notes, later = together(jnp.stack([rows, cols]), shard)
    y_own = send(later, other_y)
    c_own = send(later, other_core)
    notes = send(notes, opposite)
    order = tables(rows, cols, block_total)[1]
    count = tiles.shape[0]
    step = shard.size // tiles[0].size
    sizes = tile_parts(count)
    shapes = [shard.shape] * 2 + [(size,) + tiles.shape[1:] for size in [count - 2 * step] + sizes]
    parts = sort_tiles(order, at_end, tiles, [1, 1, 1, 0, 0, 0], shapes)
    near, first, y_own, c_own, notes, *parts = together(near, first, y_own, c_own, notes, *parts)

    outer = send(jnp.where(in_centre, first, parts[0]), around)
    second = send(near, across)
    y_near = send(near, other_y)
    c_near = send(near, other_core)
    c_y_own = send(y_own, other_core)
    own_tables = tables(keys, cols, block_total, 2 * PPD)
    far_tables = tables(notes[0], notes[1], block_total)
    far_ends = [outer]
    first = jnp.where(in_centre, first, outer)
    second, first, y_near, c_near, c_y_own, *rest = together(
        second, first, y_near, c_near, c_y_own, *parts[1:], *own_tables, *far_tables
    )
    parts, own_tables, far_tables = rest[:5], rest[5:9], rest[9:]

    outer = send(jnp.where(in_centre, second, parts[0]), around)
    far_ends += [outer, send(parts[1], from_ends)]
    y_first = send(first, other_y)
    c_first = send(first, other_core)
    c_y_near = send(y_near, other_core)
    halves = (slice(0, local // 2), slice(local // 2, None))
    second = [jnp.where(in_centre, second[half], outer[half]) for half in halves]
    *second, y_first, c_first, c_y_near = together(*second, y_first, c_first, c_y_near)

    far_centre = [send(parts[2], from_centre)]
    y_second = [send(half, other_y) for half in second]
    perm = flip_matrix(W)
    pieces = [shard, c_own, near, c_near, first, c_first, y_own, c_y_own, y_near, c_y_near, y_first]
    firsts = [owner(k, y + core) * local for y in (0, 2) for k in range(3) for core in (0, 1)][:11]
    early = own_part(own_tables, far_tables[3], tiles, pieces, first_blocks(firsts), perm)
    y_second[0], y_second[1], second[0], second[1], y_first, total, flipped, *parts = together(
        *y_second, *second, y_first, *early, *parts[3:]
    )
    far_centre += [send(part, from_centre) for part in parts]
    *y_second, far_ends[2] = together(*y_second, far_ends[2])

    c_y_first = send(y_first, other_core)
    c_second = [send(half, other_core) for half in second]
    c_y_second = [send(half, other_core) for half in y_second]
    pieces = [c_y_first, *second, *c_second, *y_second, *c_y_second]
    firsts = [owner(2, 3) * local] + [owner(3, bits) * local + half for bits in range(4) for half in (0, local // 2)]
    total, flipped = own_part(own_tables, far_tables[3], tiles, pieces, first_blocks(firsts), perm, PPD, (total, flipped))

    sources = [(0, step * number, array) for number, array in enumerate(far_ends)]
    sources += [(1, sum(sizes[:number]), array) for number, array in enumerate(far_centre)]
    return far_products(far_tables, at_end, sources, sizes, flipped, total)


def tile_parts(count):
    sizes = [count * share // 48 for share in SHARES]
    return sizes + [count - sum(sizes)]


def far_products(far_tables, chosen, sources, sizes, flipped, total):
    base, result = 0, None
    for size in sizes:
        total, result = far_part(base, size, far_tables, chosen, sources, flipped, total, result)
        base += size
    return result


def per_device(t2_tiles, t2_row, t2_col, integrals):
    peers = lax.axis_size("tile")
    if peers == 16:
        return staged_part(t2_tiles, t2_row, t2_col, integrals)
    block_total = peers * integrals.shape[0]
    opposite = [(source, (source + peers // 2) % peers) for source in range(peers)]
    own_tables = tables(t2_row, t2_col, block_total)
    sizes = tile_parts(t2_tiles.shape[0])
    zero = jnp.zeros((1,), jnp.int32)
    parts = sort_tiles(own_tables[1], zero, t2_tiles, [0] * 3, [(size,) + t2_tiles.shape[1:] for size in sizes])
    notes = send(jnp.stack([t2_row, t2_col]), opposite)
    sources = [(0, sum(sizes[:number]), send(part, opposite)) for number, part in enumerate(parts)]
    blocks = lax.all_gather(integrals, "tile", axis=0, tiled=True)
    far_tables = tables(notes[0], notes[1], block_total)
    total, flipped = own_part(own_tables, far_tables[3], t2_tiles, [blocks], zero, flip_matrix(W))
    return far_products(far_tables, zero, sources, sizes, flipped, total)


def solution(mesh):
    in_specs = (
        P(("groups", "tile"), None, None),
        P(("groups", "tile")),
        P(("groups", "tile")),
        P(("groups", "tile"), None, None),
    )
    out_specs = P(("groups", "tile"), None, None)
    return jax.shard_map(
        per_device, mesh=mesh, in_specs=in_specs, out_specs=out_specs, check_vma=False
    )
```

```python
import functools

import jax
import jax.numpy as jnp
from jax import lax
from jax.experimental import pallas as pl
from jax.experimental.pallas import tpu as pltpu
from jax.sharding import PartitionSpec as P

W = 32
PPD = 16
REUSE = 3
SHARES = (24, 18)
COLUMNS = 256
MIB = 1024 * 1024
SMEM = pl.BlockSpec(memory_space=pltpu.SMEM)
VMEM = pl.BlockSpec(memory_space=pltpu.VMEM)
ANY = pl.BlockSpec(memory_space=pl.ANY)


def flip_matrix(width):
    columns = jnp.arange(width * width, dtype=jnp.int32)
    source = (columns % width) * width + columns // width
    return (columns[:, None] == source[None, :]).astype(jnp.bfloat16)


def tables_kernel(rows, cols, starts, tile_at, block_at, slots, cursor):
    count, total, groups = rows.shape[0], slots.shape[0], cursor.shape[0]

    @pl.loop(0, total)
    def _(block):
        slots[block] = 0

    for row in range(groups):
        cursor[row] = 0

    @pl.loop(0, count)
    def _(tile):
        cursor[rows[tile]] += 1
        slots[cols[tile]] = 1

    place = jnp.int32(0)
    for row in range(groups):
        size = cursor[row]
        starts[row] = place
        cursor[row] = place
        place += size
    starts[groups] = place

    def number(block, used):
        named = slots[block]
        slots[block] = jnp.where(named > 0, used, -1)
        return used + named

    lax.fori_loop(0, total, number, jnp.int32(0))

    @pl.loop(0, count)
    def _(tile):
        row = rows[tile]
        position = cursor[row]
        cursor[row] = position + 1
        tile_at[position] = tile
        block_at[position] = slots[cols[tile]]


def tables(rows, cols, total, groups=PPD):
    count = rows.shape[0]
    return pl.pallas_call(
        tables_kernel,
        in_specs=[SMEM] * 2,
        out_specs=[SMEM] * 4,
        out_shape=[jax.ShapeDtypeStruct((size,), jnp.int32) for size in (groups + 1, count, count, total)],
        scratch_shapes=[pltpu.SMEM((groups,), jnp.int32)],
        name="tables",
    )(rows, cols)


def window(ref, tile):
    depth = ref.shape[1]
    across = ref.shape[2] // depth
    if across == 1:
        return ref.at[tile]
    return ref.at[lax.div(tile, across), :, pl.ds(pl.multiple_of(lax.rem(tile, across) * depth, depth), depth)]


def sort_kernel(choices, tile_at, chosen, tiles_ref, *refs):
    parts, sems = refs[: len(refs) // 2], refs[len(refs) // 2 :]
    begin = {choice: 0 for choice in choices}
    for choice, part, sem in zip(choices, parts, sems):
        base = begin[choice]
        count = part.shape[0] * part.shape[2] // tiles_ref.shape[2]
        begin[choice] += count

        @pl.when(chosen[0] == choice)
        def _(part=part, sem=sem, base=base, count=count):
            @pl.loop(0, count)
            def _(number):
                pltpu.make_async_copy(tiles_ref.at[tile_at[base + number]], window(part, number), sem).start()

    for choice, part, sem in zip(choices, parts, sems):

        @pl.when(chosen[0] == choice)
        def _(part=part, sem=sem):
            pltpu.make_async_copy(part, part, sem).wait()


def sort_tiles(tile_at, chosen, tiles, choices, shapes):
    return pl.pallas_call(
        functools.partial(sort_kernel, choices),
        in_specs=[SMEM] * 2 + [ANY],
        out_specs=[VMEM] * len(shapes),
        out_shape=[jax.ShapeDtypeStruct(shape, tiles.dtype) for shape in shapes],
        scratch_shapes=[pltpu.SemaphoreType.DMA] * len(shapes),
        compiler_params=pltpu.CompilerParams(vmem_limit_bytes=16 * MIB),
        name="sort_tiles",
    )(tile_at, chosen, tiles)


def add_row(sum_ref, begin, end, depth, tile_of, block_of):
    width = sum_ref.shape[1]

    @pl.loop(0, (end - begin + depth - 1) // depth)
    def _(turn):
        here = begin + turn * depth
        places = [jnp.minimum(here + part, end - 1) for part in range(depth)]
        left = [tile_of(places[0])]
        for part in range(1, depth):
            tile = tile_of(places[part])
            left.append(jnp.where(here + part < end, tile, jnp.zeros_like(tile)))
        left = jnp.concatenate(left, axis=1)
        for column in range(0, width, COLUMNS):
            window = pl.ds(column, COLUMNS)
            right = jnp.concatenate([block_of(place, window) for place in places], axis=0)
            sum_ref[:, window] += jnp.dot(left, right, preferred_element_type=jnp.float32)


def own_kernel(counts, group, fresh, starts, tile_at, block_at, own_slots, far_slots, firsts, tiles_ref, perm_ref, *refs):
    pieces = refs[: len(counts)]
    refs = refs[len(counts) :]
    if not fresh:
        sum_in, refs = refs[0], refs[2:]
    sum_out, flip_out, own_blocks, far_blocks, sums, own_list, far_list, own_sems, far_sems, row_sems = refs

    def fetch(slots, landing, sems, fetched):
        found = jnp.int32(0)
        for number, (piece, count) in enumerate(zip(pieces, counts)):

            def one(offset, found, piece=piece, number=number):
                slot = slots[firsts[number] + offset]

                @pl.when(slot >= 0)
                def _():
                    fetched[found] = slot
                    pltpu.make_async_copy(piece.at[offset], landing.at[slot], sems.at[slot]).start()

                return found + (slot >= 0).astype(jnp.int32)

            found = lax.fori_loop(0, count, one, found)
        return found

    far_found = fetch(far_slots, far_blocks, far_sems, far_list)
    own_found = fetch(own_slots, own_blocks, own_sems, own_list)
    if not fresh:
        for row in range(PPD):
            pltpu.make_async_copy(sum_in.at[row], sums.at[row], row_sems.at[row]).start()

    def arrived(landing, sems, slot):
        pltpu.make_async_copy(landing.at[slot], landing.at[slot], sems.at[slot]).wait()

    def flip_store(slot):
        return pltpu.make_async_copy(far_blocks.at[slot], flip_out.at[slot], far_sems.at[slot])

    @pl.loop(0, far_found)
    def _(number):
        slot = far_list[number]
        arrived(far_blocks, far_sems, slot)
        far_blocks[slot] = jnp.dot(
            far_blocks[slot], perm_ref[...], preferred_element_type=jnp.float32
        ).astype(jnp.bfloat16)
        flip_store(slot).start()

    @pl.loop(0, own_found)
    def _(number):
        arrived(own_blocks, own_sems, own_list[number])

    def store(row):
        return pltpu.make_async_copy(sums.at[row], sum_out.at[row], row_sems.at[row])

    @pl.loop(0, PPD)
    def _(row):
        if fresh:
            sums[row] = jnp.zeros(sums.shape[1:], jnp.float32)
        else:
            arrived(sums, row_sems, row)
        add_row(
            sums.at[row],
            starts[group + row],
            starts[group + row + 1],
            4 if fresh else 2,
            lambda place: tiles_ref[tile_at[place]],
            lambda place, window: own_blocks[block_at[place], :, window],
        )
        store(row).start()

    @pl.loop(0, far_found)
    def _(number):
        flip_store(far_list[number]).wait()

    @pl.loop(0, PPD)
    def _(row):
        store(row).wait()


def own_part(own_tables, far_slots, tiles, pieces, firsts, perm, group=0, earlier=()):
    starts, tile_at, block_at, own_slots = own_tables
    count, height, _ = tiles.shape
    depth, width = pieces[0].shape[1:]
    need = count // REUSE
    counts = [piece.shape[0] for piece in pieces]
    operands = 8 + len(pieces)
    return pl.pallas_call(
        functools.partial(own_kernel, counts, group, not earlier),
        in_specs=[SMEM] * 6 + [VMEM] * 2 + [ANY] * (len(pieces) + len(earlier)),
        out_specs=[ANY] * 2,
        out_shape=[
            jax.ShapeDtypeStruct((PPD, height, width), jnp.float32),
            jax.ShapeDtypeStruct((need, depth, width), jnp.bfloat16),
        ],
        input_output_aliases={operands: 0, operands + 1: 1} if earlier else {},
        scratch_shapes=[
            pltpu.VMEM((need, depth, width), jnp.bfloat16),
            pltpu.VMEM((need, depth, width), jnp.bfloat16),
            pltpu.VMEM((PPD, height, width), jnp.float32),
            pltpu.SMEM((need,), jnp.int32),
            pltpu.SMEM((need,), jnp.int32),
            pltpu.SemaphoreType.DMA((need,)),
            pltpu.SemaphoreType.DMA((need,)),
            pltpu.SemaphoreType.DMA((PPD,)),
        ],
        compiler_params=pltpu.CompilerParams(vmem_limit_bytes=56 * MIB),
        name="own_part",
    )(starts, tile_at, block_at, own_slots, far_slots, firsts, tiles, perm, *pieces, *earlier)


def far_kernel(base, segments, starts, block_at, chosen, *refs):
    tile_refs, refs = refs[: len(segments)], refs[len(segments) :]
    sum_in, flip_in = refs[:2]
    refs = refs[3:] if base else refs[2:]
    sum_out, result, tiles_ref, blocks, sums, rounded, tile_sem, block_sems, row_sems, out_sems = refs
    count = tiles_ref.shape[0]
    stop = base + count

    for source, (choice, begin) in zip(tile_refs, segments):
        held = source.shape[0] * source.shape[2] // tiles_ref.shape[2]
        low, high = max(begin, base), min(begin + held, stop)

        @pl.when(chosen[0] == choice)
        def _(source=source, begin=begin, low=low, high=high):
            if source.shape[2] == tiles_ref.shape[2]:
                here, there = source.at[pl.ds(low - begin, high - low)], tiles_ref.at[pl.ds(low - base, high - low)]
                pltpu.make_async_copy(here, there, tile_sem).start()
            else:

                @pl.loop(low, high)
                def _(place):
                    pltpu.make_async_copy(window(source, place - begin), tiles_ref.at[place - base], tile_sem).start()

    @pl.loop(0, count)
    def _(number):
        pltpu.make_async_copy(flip_in.at[block_at[base + number]], blocks.at[number], block_sems.at[number]).start()

    def each_row(action):
        @pl.loop(0, PPD)
        def _(row):
            first, last = starts[row], starts[row + 1]

            @pl.when(((last > base) if base else True) & ((last <= stop) | (first < stop)))
            def _():
                action(row, last <= stop)

    def load(row):
        return pltpu.make_async_copy(sum_in.at[row], sums.at[row], row_sems.at[row])

    def store(row):
        return pltpu.make_async_copy(rounded.at[row], result.at[row], out_sems.at[row])

    def keep(row):
        return pltpu.make_async_copy(sums.at[row], sum_out.at[row], out_sems.at[row])

    each_row(lambda row, complete: load(row).start())
    pltpu.make_async_copy(tiles_ref, tiles_ref, tile_sem).wait()


    def add(row, complete):
        begin, end = jnp.maximum(starts[row], base), jnp.minimum(starts[row + 1], stop)
        load(row).wait()

        @pl.loop(0, end - begin)
        def _(number):
            block = blocks.at[begin - base + number]
            pltpu.make_async_copy(block, block, block_sems.at[begin - base + number]).wait()

        add_row(
            sums.at[row],
            begin,
            end,
            4,
            lambda place: tiles_ref[place - base],
            lambda place, window: blocks[place - base, :, window],
        )

        @pl.when(complete)
        def _():
            rounded[row] = sums[row].astype(rounded.dtype)
            store(row).start()

        @pl.when(jnp.logical_not(complete))
        def _():
            keep(row).start()

    def finish(row, complete):
        pl.when(complete)(lambda: store(row).wait())
        pl.when(jnp.logical_not(complete))(lambda: keep(row).wait())

    each_row(add)
    each_row(finish)


def far_part(base, count, far_tables, chosen, sources, flipped, total, result=None):
    starts, _, block_at, _ = far_tables
    whole = total.shape
    given = [] if result is None else [result]
    held = [array.size // (whole[1] * flipped.shape[1]) for _, _, array in sources]
    used = [
        (source[:2], source[2])
        for source, size in zip(sources, held)
        if source[1] < base + count and source[1] + size > base
    ]
    operand = 3 + len(used)
    aliases = {operand: 0, operand + 2: 1} if given else {operand: 0}
    return pl.pallas_call(
        functools.partial(far_kernel, base, [segment for segment, _ in used]),
        in_specs=[SMEM] * 3 + [ANY] * (len(used) + 2 + len(given)),
        out_specs=[ANY] * 2,
        out_shape=[jax.ShapeDtypeStruct(whole, jnp.float32), jax.ShapeDtypeStruct(whole, jnp.bfloat16)],
        input_output_aliases=aliases,
        scratch_shapes=[
            pltpu.VMEM((count, whole[1], flipped.shape[1]), jnp.bfloat16),
            pltpu.VMEM((count,) + flipped.shape[1:], jnp.bfloat16),
            pltpu.VMEM(whole, jnp.float32),
            pltpu.VMEM(whole, jnp.bfloat16),
            pltpu.SemaphoreType.DMA,
            pltpu.SemaphoreType.DMA((count,)),
            pltpu.SemaphoreType.DMA((PPD,)),
            pltpu.SemaphoreType.DMA((PPD,)),
        ],
        compiler_params=pltpu.CompilerParams(vmem_limit_bytes=56 * MIB),
        name="far_part",
    )(starts, block_at, chosen, *[array for _, array in used], total, flipped, *given)


def together(*values):
    return lax.optimization_barrier(values)


def send(value, pairs):
    return lax.ppermute(value, "tile", pairs)


def flipped_bit(bit):
    return [(i, i ^ bit) for i in range(16)]


def staged_part(tiles, rows, cols, shard):
    local = shard.shape[0]
    block_total = 16 * local
    centre = [i for i in range(16) if i // 4 in (1, 2)]
    across = [(i, i ^ 12) for i in centre]
    from_ends = [(i, i ^ 8) for i in range(16) if i not in centre]
    from_centre = [(i, i ^ 8) for i in centre]
    around = [(i, i ^ 4) for i in centre] + from_ends
    around_crossed = [(i, i ^ 4) for i in centre] + [(i, i ^ 9) for i, _ in from_ends]
    other_z, other_y, other_core, opposite = (flipped_bit(bit) for bit in (4, 2, 1, 8))
    me = lax.axis_index("tile")
    z = me // 4
    in_centre = (z == 1) | (z == 2)
    at_end = 1 - in_centre.astype(jnp.int32).reshape(1)
    zs = [z, z ^ 1, jnp.where(z < 2, 2, 1), jnp.where(z < 2, 3, 0)]

    def owner(k, bits):
        return 4 * zs[k] + ((me & 3) ^ bits)

    def first_blocks(firsts):
        return jnp.stack(firsts).astype(jnp.int32)

    col_owner = cols // local
    late = (col_owner // 4 == zs[3]) | (col_owner == owner(2, 3))
    keys = rows + PPD * late.astype(jnp.int32)

    near = send(shard, other_z)
    first = send(shard, across)
    notes = send(jnp.stack([rows, cols]), opposite)
    order = tables(rows, cols, block_total)[1]
    c_own = send(shard, other_core)
    count = tiles.shape[0]
    step = shard.size // tiles[0].size
    sizes = tile_parts(count)
    shapes = [shard.shape] * 2 + [(size,) + tiles.shape[1:] for size in [count - 2 * step] + sizes]
    parts = sort_tiles(order, at_end, tiles, [1, 1, 1, 0, 0, 0], shapes)
    near, first, c_own, notes, *parts = together(near, first, c_own, notes, *parts)

    outer = send(jnp.where(in_centre, first, parts[0]), around)
    second = send(jnp.where(in_centre, near, parts[1]), across + [(i, i ^ 1) for i, _ in from_ends])
    y_own = send(shard, other_y)
    y_near = send(near, other_y)
    c_near = send(near, other_core)
    own_tables = tables(keys, cols, block_total, 2 * PPD)
    far_tables = tables(notes[0], notes[1], block_total)
    perm = flip_matrix(W)
    far_ends = [outer]
    first = jnp.where(in_centre, first, outer)
    second, first, y_own, y_near, c_near, perm, *rest = together(
        second, first, y_own, y_near, c_near, perm, *parts[2:], *own_tables, *far_tables
    )
    parts, own_tables, far_tables = rest[:4], rest[4:8], rest[8:]

    outer = send(second, around_crossed)
    y_first = send(first, other_y)
    c_first = send(first, other_core)
    c_y_own = send(y_own, other_core)
    c_y_near = send(y_near, other_core)
    tiles_last, c_first = together(parts[0], c_first)
    far_ends += [outer, send(tiles_last, from_ends)]
    halves = (slice(0, local // 2), slice(local // 2, None))
    second = [jnp.where(in_centre, second[half], outer[half]) for half in halves]
    *second, y_first, c_first, c_y_own, c_y_near = together(*second, y_first, c_first, c_y_own, c_y_near)

    far_centre = [send(parts[1], from_centre)]
    y_second = [send(half, other_y) for half in second]
    pieces = [shard, c_own, near, c_near, first, c_first, y_own, c_y_own, y_near, c_y_near, y_first]
    firsts = [owner(k, y + core) * local for y in (0, 2) for k in range(3) for core in (0, 1)][:11]
    early = own_part(own_tables, far_tables[3], tiles, pieces, first_blocks(firsts), perm)
    y_second[0], y_second[1], second[0], second[1], y_first, total, flipped, *parts = together(
        *y_second, *second, y_first, *early, *parts[2:]
    )
    far_centre += [send(part, from_centre) for part in parts]
    *y_second, far_ends[2] = together(*y_second, far_ends[2])

    c_y_first = send(y_first, other_core)
    c_second = [send(half, other_core) for half in second]
    c_y_second = [send(half, other_core) for half in y_second]
    pieces = [c_y_first, *second, *c_second, *y_second, *c_y_second]
    firsts = [owner(2, 3) * local] + [owner(3, bits) * local + half for bits in range(4) for half in (0, local // 2)]
    total, flipped = own_part(own_tables, far_tables[3], tiles, pieces, first_blocks(firsts), perm, PPD, (total, flipped))

    sources = [(0, step * number, array) for number, array in enumerate(far_ends)]
    sources += [(1, sum(sizes[:number]), array) for number, array in enumerate(far_centre)]
    return far_products(far_tables, at_end, sources, sizes, flipped, total)


def tile_parts(count):
    sizes = [count * share // 48 for share in SHARES]
    return sizes + [count - sum(sizes)]


def far_products(far_tables, chosen, sources, sizes, flipped, total):
    base, result = 0, None
    for size in sizes:
        total, result = far_part(base, size, far_tables, chosen, sources, flipped, total, result)
        base += size
    return result


def per_device(t2_tiles, t2_row, t2_col, integrals):
    peers = lax.axis_size("tile")
    if peers == 16:
        return staged_part(t2_tiles, t2_row, t2_col, integrals)
    block_total = peers * integrals.shape[0]
    opposite = [(source, (source + peers // 2) % peers) for source in range(peers)]
    own_tables = tables(t2_row, t2_col, block_total)
    sizes = tile_parts(t2_tiles.shape[0])
    zero = jnp.zeros((1,), jnp.int32)
    parts = sort_tiles(own_tables[1], zero, t2_tiles, [0] * 3, [(size,) + t2_tiles.shape[1:] for size in sizes])
    notes = send(jnp.stack([t2_row, t2_col]), opposite)
    sources = [(0, sum(sizes[:number]), send(part, opposite)) for number, part in enumerate(parts)]
    blocks = lax.all_gather(integrals, "tile", axis=0, tiled=True)
    far_tables = tables(notes[0], notes[1], block_total)
    total, flipped = own_part(own_tables, far_tables[3], t2_tiles, [blocks], zero, flip_matrix(W))
    return far_products(far_tables, zero, sources, sizes, flipped, total)


def solution(mesh):
    in_specs = (
        P(("groups", "tile"), None, None),
        P(("groups", "tile")),
        P(("groups", "tile")),
        P(("groups", "tile"), None, None),
    )
    out_specs = P(("groups", "tile"), None, None)
    return jax.shard_map(
        per_device, mesh=mesh, in_specs=in_specs, out_specs=out_specs, check_vma=False
    )
```

```python
import functools

import jax
import jax.numpy as jnp
from jax import lax
from jax.experimental import pallas as pl
from jax.experimental.pallas import tpu as pltpu
from jax.sharding import PartitionSpec as P

W = 32
PPD = 16
REUSE = 3
SHARES = (30, 12)
COLUMNS = 256
MIB = 1024 * 1024
SMEM = pl.BlockSpec(memory_space=pltpu.SMEM)
VMEM = pl.BlockSpec(memory_space=pltpu.VMEM)
ANY = pl.BlockSpec(memory_space=pl.ANY)


def flip_matrix(width):
    columns = jnp.arange(width * width, dtype=jnp.int32)
    source = (columns % width) * width + columns // width
    return (columns[:, None] == source[None, :]).astype(jnp.bfloat16)


def tables_kernel(rows, cols, starts, tile_at, block_at, slots, cursor):
    count, total, groups = rows.shape[0], slots.shape[0], cursor.shape[0]

    @pl.loop(0, total)
    def _(block):
        slots[block] = 0

    for row in range(groups):
        cursor[row] = 0

    @pl.loop(0, count)
    def _(tile):
        cursor[rows[tile]] += 1
        slots[cols[tile]] = 1

    place = jnp.int32(0)
    for row in range(groups):
        size = cursor[row]
        starts[row] = place
        cursor[row] = place
        place += size
    starts[groups] = place

    def number(block, used):
        named = slots[block]
        slots[block] = jnp.where(named > 0, used, -1)
        return used + named

    lax.fori_loop(0, total, number, jnp.int32(0))

    @pl.loop(0, count)
    def _(tile):
        row = rows[tile]
        position = cursor[row]
        cursor[row] = position + 1
        tile_at[position] = tile
        block_at[position] = slots[cols[tile]]


def tables(rows, cols, total, groups=PPD):
    count = rows.shape[0]
    return pl.pallas_call(
        tables_kernel,
        in_specs=[SMEM] * 2,
        out_specs=[SMEM] * 4,
        out_shape=[jax.ShapeDtypeStruct((size,), jnp.int32) for size in (groups + 1, count, count, total)],
        scratch_shapes=[pltpu.SMEM((groups,), jnp.int32)],
        name="tables",
    )(rows, cols)


def window(ref, tile):
    depth = ref.shape[1]
    across = ref.shape[2] // depth
    if across == 1:
        return ref.at[tile]
    return ref.at[lax.div(tile, across), :, pl.ds(pl.multiple_of(lax.rem(tile, across) * depth, depth), depth)]


def sort_kernel(choices, tile_at, chosen, tiles_ref, *refs):
    parts, sems = refs[: len(refs) // 2], refs[len(refs) // 2 :]
    begin = {choice: 0 for choice in choices}
    for choice, part, sem in zip(choices, parts, sems):
        base = begin[choice]
        count = part.shape[0] * part.shape[2] // tiles_ref.shape[2]
        begin[choice] += count

        @pl.when(chosen[0] == choice)
        def _(part=part, sem=sem, base=base, count=count):
            @pl.loop(0, count)
            def _(number):
                pltpu.make_async_copy(tiles_ref.at[tile_at[base + number]], window(part, number), sem).start()

    for choice, part, sem in zip(choices, parts, sems):

        @pl.when(chosen[0] == choice)
        def _(part=part, sem=sem):
            pltpu.make_async_copy(part, part, sem).wait()


def sort_tiles(tile_at, chosen, tiles, choices, shapes):
    return pl.pallas_call(
        functools.partial(sort_kernel, choices),
        in_specs=[SMEM] * 2 + [ANY],
        out_specs=[VMEM] * len(shapes),
        out_shape=[jax.ShapeDtypeStruct(shape, tiles.dtype) for shape in shapes],
        scratch_shapes=[pltpu.SemaphoreType.DMA] * len(shapes),
        compiler_params=pltpu.CompilerParams(vmem_limit_bytes=16 * MIB),
        name="sort_tiles",
    )(tile_at, chosen, tiles)


def add_row(sum_ref, begin, end, depth, tile_of, block_of):
    width = sum_ref.shape[1]

    @pl.loop(0, (end - begin + depth - 1) // depth)
    def _(turn):
        here = begin + turn * depth
        places = [jnp.minimum(here + part, end - 1) for part in range(depth)]
        left = [tile_of(places[0])]
        for part in range(1, depth):
            tile = tile_of(places[part])
            left.append(jnp.where(here + part < end, tile, jnp.zeros_like(tile)))
        left = jnp.concatenate(left, axis=1)
        for column in range(0, width, COLUMNS):
            window = pl.ds(column, COLUMNS)
            right = jnp.concatenate([block_of(place, window) for place in places], axis=0)
            sum_ref[:, window] += jnp.dot(left, right, preferred_element_type=jnp.float32)


def own_kernel(counts, group, fresh, starts, tile_at, block_at, own_slots, far_slots, firsts, tiles_ref, perm_ref, *refs):
    pieces = refs[: len(counts)]
    refs = refs[len(counts) :]
    if not fresh:
        sum_in, refs = refs[0], refs[2:]
    sum_out, flip_out, own_blocks, far_blocks, sums, own_list, far_list, own_sems, far_sems, row_sems = refs

    def fetch(slots, landing, sems, fetched):
        found = jnp.int32(0)
        for number, (piece, count) in enumerate(zip(pieces, counts)):

            def one(offset, found, piece=piece, number=number):
                slot = slots[firsts[number] + offset]

                @pl.when(slot >= 0)
                def _():
                    fetched[found] = slot
                    pltpu.make_async_copy(piece.at[offset], landing.at[slot], sems.at[slot]).start()

                return found + (slot >= 0).astype(jnp.int32)

            found = lax.fori_loop(0, count, one, found)
        return found

    far_found = fetch(far_slots, far_blocks, far_sems, far_list)
    own_found = fetch(own_slots, own_blocks, own_sems, own_list)
    if not fresh:
        for row in range(PPD):
            pltpu.make_async_copy(sum_in.at[row], sums.at[row], row_sems.at[row]).start()

    def arrived(landing, sems, slot):
        pltpu.make_async_copy(landing.at[slot], landing.at[slot], sems.at[slot]).wait()

    def flip_store(slot):
        return pltpu.make_async_copy(far_blocks.at[slot], flip_out.at[slot], far_sems.at[slot])

    @pl.loop(0, far_found)
    def _(number):
        slot = far_list[number]
        arrived(far_blocks, far_sems, slot)
        far_blocks[slot] = jnp.dot(
            far_blocks[slot], perm_ref[...], preferred_element_type=jnp.float32
        ).astype(jnp.bfloat16)
        flip_store(slot).start()

    @pl.loop(0, own_found)
    def _(number):
        arrived(own_blocks, own_sems, own_list[number])

    def store(row):
        return pltpu.make_async_copy(sums.at[row], sum_out.at[row], row_sems.at[row])

    @pl.loop(0, PPD)
    def _(row):
        if fresh:
            sums[row] = jnp.zeros(sums.shape[1:], jnp.float32)
        else:
            arrived(sums, row_sems, row)
        add_row(
            sums.at[row],
            starts[group + row],
            starts[group + row + 1],
            4 if fresh else 2,
            lambda place: tiles_ref[tile_at[place]],
            lambda place, window: own_blocks[block_at[place], :, window],
        )
        store(row).start()

    @pl.loop(0, far_found)
    def _(number):
        flip_store(far_list[number]).wait()

    @pl.loop(0, PPD)
    def _(row):
        store(row).wait()


def own_part(own_tables, far_slots, tiles, pieces, firsts, perm, group=0, earlier=()):
    starts, tile_at, block_at, own_slots = own_tables
    count, height, _ = tiles.shape
    depth, width = pieces[0].shape[1:]
    need = count // REUSE
    counts = [piece.shape[0] for piece in pieces]
    operands = 8 + len(pieces)
    return pl.pallas_call(
        functools.partial(own_kernel, counts, group, not earlier),
        in_specs=[SMEM] * 6 + [VMEM] * 2 + [ANY] * (len(pieces) + len(earlier)),
        out_specs=[ANY] * 2,
        out_shape=[
            jax.ShapeDtypeStruct((PPD, height, width), jnp.float32),
            jax.ShapeDtypeStruct((need, depth, width), jnp.bfloat16),
        ],
        input_output_aliases={operands: 0, operands + 1: 1} if earlier else {},
        scratch_shapes=[
            pltpu.VMEM((need, depth, width), jnp.bfloat16),
            pltpu.VMEM((need, depth, width), jnp.bfloat16),
            pltpu.VMEM((PPD, height, width), jnp.float32),
            pltpu.SMEM((need,), jnp.int32),
            pltpu.SMEM((need,), jnp.int32),
            pltpu.SemaphoreType.DMA((need,)),
            pltpu.SemaphoreType.DMA((need,)),
            pltpu.SemaphoreType.DMA((PPD,)),
        ],
        compiler_params=pltpu.CompilerParams(vmem_limit_bytes=56 * MIB),
        name="own_part",
    )(starts, tile_at, block_at, own_slots, far_slots, firsts, tiles, perm, *pieces, *earlier)


def far_kernel(base, segments, starts, block_at, chosen, *refs):
    tile_refs, refs = refs[: len(segments)], refs[len(segments) :]
    sum_in, flip_in = refs[:2]
    refs = refs[3:] if base else refs[2:]
    sum_out, result, tiles_ref, blocks, sums, rounded, tile_sem, block_sems, row_sems, out_sems = refs
    count = tiles_ref.shape[0]
    stop = base + count

    for source, (choice, begin) in zip(tile_refs, segments):
        held = source.shape[0] * source.shape[2] // tiles_ref.shape[2]
        low, high = max(begin, base), min(begin + held, stop)

        @pl.when(chosen[0] == choice)
        def _(source=source, begin=begin, low=low, high=high):
            if source.shape[2] == tiles_ref.shape[2]:
                here, there = source.at[pl.ds(low - begin, high - low)], tiles_ref.at[pl.ds(low - base, high - low)]
                pltpu.make_async_copy(here, there, tile_sem).start()
            else:

                @pl.loop(low, high)
                def _(place):
                    pltpu.make_async_copy(window(source, place - begin), tiles_ref.at[place - base], tile_sem).start()

    @pl.loop(0, count)
    def _(number):
        pltpu.make_async_copy(flip_in.at[block_at[base + number]], blocks.at[number], block_sems.at[number]).start()

    def each_row(action):
        @pl.loop(0, PPD)
        def _(row):
            first, last = starts[row], starts[row + 1]

            @pl.when(((last > base) if base else True) & ((last <= stop) | (first < stop)))
            def _():
                action(row, last <= stop)

    def load(row):
        return pltpu.make_async_copy(sum_in.at[row], sums.at[row], row_sems.at[row])

    def store(row):
        return pltpu.make_async_copy(rounded.at[row], result.at[row], out_sems.at[row])

    def keep(row):
        return pltpu.make_async_copy(sums.at[row], sum_out.at[row], out_sems.at[row])

    each_row(lambda row, complete: load(row).start())
    pltpu.make_async_copy(tiles_ref, tiles_ref, tile_sem).wait()


    def add(row, complete):
        begin, end = jnp.maximum(starts[row], base), jnp.minimum(starts[row + 1], stop)
        load(row).wait()

        @pl.loop(0, end - begin)
        def _(number):
            block = blocks.at[begin - base + number]
            pltpu.make_async_copy(block, block, block_sems.at[begin - base + number]).wait()

        add_row(
            sums.at[row],
            begin,
            end,
            4,
            lambda place: tiles_ref[place - base],
            lambda place, window: blocks[place - base, :, window],
        )

        @pl.when(complete)
        def _():
            rounded[row] = sums[row].astype(rounded.dtype)
            store(row).start()

        @pl.when(jnp.logical_not(complete))
        def _():
            keep(row).start()

    def finish(row, complete):
        pl.when(complete)(lambda: store(row).wait())
        pl.when(jnp.logical_not(complete))(lambda: keep(row).wait())

    each_row(add)
    each_row(finish)


def far_part(base, count, far_tables, chosen, sources, flipped, total, result=None):
    starts, _, block_at, _ = far_tables
    whole = total.shape
    given = [] if result is None else [result]
    held = [array.size // (whole[1] * flipped.shape[1]) for _, _, array in sources]
    used = [
        (source[:2], source[2])
        for source, size in zip(sources, held)
        if source[1] < base + count and source[1] + size > base
    ]
    operand = 3 + len(used)
    aliases = {operand: 0, operand + 2: 1} if given else {operand: 0}
    return pl.pallas_call(
        functools.partial(far_kernel, base, [segment for segment, _ in used]),
        in_specs=[SMEM] * 3 + [ANY] * (len(used) + 2 + len(given)),
        out_specs=[ANY] * 2,
        out_shape=[jax.ShapeDtypeStruct(whole, jnp.float32), jax.ShapeDtypeStruct(whole, jnp.bfloat16)],
        input_output_aliases=aliases,
        scratch_shapes=[
            pltpu.VMEM((count, whole[1], flipped.shape[1]), jnp.bfloat16),
            pltpu.VMEM((count,) + flipped.shape[1:], jnp.bfloat16),
            pltpu.VMEM(whole, jnp.float32),
            pltpu.VMEM(whole, jnp.bfloat16),
            pltpu.SemaphoreType.DMA,
            pltpu.SemaphoreType.DMA((count,)),
            pltpu.SemaphoreType.DMA((PPD,)),
            pltpu.SemaphoreType.DMA((PPD,)),
        ],
        compiler_params=pltpu.CompilerParams(vmem_limit_bytes=40 * MIB),
        name="far_part",
    )(starts, block_at, chosen, *[array for _, array in used], total, flipped, *given)


def together(*values):
    return lax.optimization_barrier(values)


def send(value, pairs):
    return lax.ppermute(value, "tile", pairs)


def flipped_bit(bit):
    return [(i, i ^ bit) for i in range(16)]


def staged_part(tiles, rows, cols, shard):
    local = shard.shape[0]
    block_total = 16 * local
    centre = [i for i in range(16) if i // 4 in (1, 2)]
    across = [(i, i ^ 12) for i in centre]
    from_ends = [(i, i ^ 8) for i in range(16) if i not in centre]
    from_centre = [(i, i ^ 8) for i in centre]
    around = [(i, i ^ 4) for i in centre] + from_ends
    around_crossed = [(i, i ^ 4) for i in centre] + [(i, i ^ 9) for i, _ in from_ends]
    other_z, other_y, other_core, opposite = (flipped_bit(bit) for bit in (4, 2, 1, 8))
    me = lax.axis_index("tile")
    z = me // 4
    in_centre = (z == 1) | (z == 2)
    at_end = 1 - in_centre.astype(jnp.int32).reshape(1)
    zs = [z, z ^ 1, jnp.where(z < 2, 2, 1), jnp.where(z < 2, 3, 0)]

    def owner(k, bits):
        return 4 * zs[k] + ((me & 3) ^ bits)

    def first_blocks(firsts):
        return jnp.stack(firsts).astype(jnp.int32)

    col_owner = cols // local
    late = (col_owner // 4 == zs[3]) | (col_owner == owner(2, 3))
    keys = rows + PPD * late.astype(jnp.int32)

    near = send(shard, other_z)
    first = send(shard, across)
    notes = send(jnp.stack([rows, cols]), opposite)
    order = tables(rows, cols, block_total)[1]
    c_own = send(shard, other_core)
    count = tiles.shape[0]
    step = shard.size // tiles[0].size
    sizes = tile_parts(count)
    shapes = [shard.shape] * 2 + [(size,) + tiles.shape[1:] for size in [count - 2 * step] + sizes]
    parts = sort_tiles(order, at_end, tiles, [1, 1, 1, 0, 0, 0], shapes)
    first, *parts = together(first, *parts)

    outer = send(jnp.where(in_centre, first, parts[0]), around)
    near, c_own, notes, *parts = together(near, c_own, notes, *parts)
    second = send(jnp.where(in_centre, near, parts[1]), across + [(i, i ^ 1) for i, _ in from_ends])
    y_own = send(shard, other_y)
    y_near = send(near, other_y)
    c_near = send(near, other_core)
    own_tables = tables(keys, cols, block_total, 2 * PPD)
    far_tables = tables(notes[0], notes[1], block_total)
    perm = flip_matrix(W)
    far_ends = [outer]
    first = jnp.where(in_centre, first, outer)
    second, first, y_own, y_near, c_near, perm, *rest = together(
        second, first, y_own, y_near, c_near, perm, *parts[2:], *own_tables, *far_tables
    )
    parts, own_tables, far_tables = rest[:4], rest[4:8], rest[8:]

    outer = send(second, around_crossed)
    y_first = send(first, other_y)
    c_first = send(first, other_core)
    c_y_own = send(y_own, other_core)
    c_y_near = send(y_near, other_core)
    tiles_last, c_first = together(parts[0], c_first)
    far_ends += [outer, send(tiles_last, from_ends)]
    halves = (slice(0, local // 2), slice(local // 2, None))
    second = [jnp.where(in_centre, second[half], outer[half]) for half in halves]
    *second, y_first, c_first, c_y_own, c_y_near = together(*second, y_first, c_first, c_y_own, c_y_near)

    far_centre = [send(parts[1], from_centre)]
    y_second = [send(half, other_y) for half in second]
    pieces = [shard, c_own, near, c_near, first, c_first, y_own, c_y_own, y_near, c_y_near, y_first]
    firsts = [owner(k, y + core) * local for y in (0, 2) for k in range(3) for core in (0, 1)][:11]
    early = own_part(own_tables, far_tables[3], tiles, pieces, first_blocks(firsts), perm)
    y_second[0], y_second[1], second[0], second[1], y_first, total, flipped, *parts = together(
        *y_second, *second, y_first, *early, *parts[2:]
    )
    far_centre += [send(part, from_centre) for part in parts]
    *y_second, far_ends[2] = together(*y_second, far_ends[2])

    c_y_first = send(y_first, other_core)
    c_second = [send(half, other_core) for half in second]
    c_y_second = [send(half, other_core) for half in y_second]
    pieces = [c_y_first, *second, *c_second, *y_second, *c_y_second]
    firsts = [owner(2, 3) * local] + [owner(3, bits) * local + half for bits in range(4) for half in (0, local // 2)]
    total, flipped = own_part(own_tables, far_tables[3], tiles, pieces, first_blocks(firsts), perm, PPD, (total, flipped))

    sources = [(0, step * number, array) for number, array in enumerate(far_ends)]
    sources += [(1, sum(sizes[:number]), array) for number, array in enumerate(far_centre)]
    return far_products(far_tables, at_end, sources, sizes, flipped, total)


def tile_parts(count):
    sizes = [count * share // 48 for share in SHARES]
    return sizes + [count - sum(sizes)]


def far_products(far_tables, chosen, sources, sizes, flipped, total):
    base, result = 0, None
    for size in sizes:
        total, result = far_part(base, size, far_tables, chosen, sources, flipped, total, result)
        base += size
    return result


def per_device(t2_tiles, t2_row, t2_col, integrals):
    peers = lax.axis_size("tile")
    if peers == 16:
        return staged_part(t2_tiles, t2_row, t2_col, integrals)
    block_total = peers * integrals.shape[0]
    opposite = [(source, (source + peers // 2) % peers) for source in range(peers)]
    own_tables = tables(t2_row, t2_col, block_total)
    sizes = tile_parts(t2_tiles.shape[0])
    zero = jnp.zeros((1,), jnp.int32)
    parts = sort_tiles(own_tables[1], zero, t2_tiles, [0] * 3, [(size,) + t2_tiles.shape[1:] for size in sizes])
    notes = send(jnp.stack([t2_row, t2_col]), opposite)
    sources = [(0, sum(sizes[:number]), send(part, opposite)) for number, part in enumerate(parts)]
    blocks = lax.all_gather(integrals, "tile", axis=0, tiled=True)
    far_tables = tables(notes[0], notes[1], block_total)
    total, flipped = own_part(own_tables, far_tables[3], t2_tiles, [blocks], zero, flip_matrix(W))
    return far_products(far_tables, zero, sources, sizes, flipped, total)


def solution(mesh):
    in_specs = (
        P(("groups", "tile"), None, None),
        P(("groups", "tile")),
        P(("groups", "tile")),
        P(("groups", "tile"), None, None),
    )
    out_specs = P(("groups", "tile"), None, None)
    return jax.shard_map(
        per_device, mesh=mesh, in_specs=in_specs, out_specs=out_specs, check_vma=False
    )
```

```python
import functools

import jax
import jax.numpy as jnp
from jax import lax
from jax.experimental import pallas as pl
from jax.experimental.pallas import tpu as pltpu
from jax.sharding import PartitionSpec as P

W = 32
PPD = 16
REUSE = 3
SHARES = (30, 12)
COLUMNS = 256
MIB = 1024 * 1024
SMEM = pl.BlockSpec(memory_space=pltpu.SMEM)
VMEM = pl.BlockSpec(memory_space=pltpu.VMEM)
ANY = pl.BlockSpec(memory_space=pl.ANY)


def flip_matrix(width):
    columns = jnp.arange(width * width, dtype=jnp.int32)
    source = (columns % width) * width + columns // width
    return (columns[:, None] == source[None, :]).astype(jnp.bfloat16)


def tables_kernel(rows, cols, starts, tile_at, block_at, slots, cursor):
    count, total, groups = rows.shape[0], slots.shape[0], cursor.shape[0]

    @pl.loop(0, total)
    def _(block):
        slots[block] = 0

    for row in range(groups):
        cursor[row] = 0

    @pl.loop(0, count)
    def _(tile):
        cursor[rows[tile]] += 1
        slots[cols[tile]] = 1

    place = jnp.int32(0)
    for row in range(groups):
        size = cursor[row]
        starts[row] = place
        cursor[row] = place
        place += size
    starts[groups] = place

    def number(block, used):
        named = slots[block]
        slots[block] = jnp.where(named > 0, used, -1)
        return used + named

    lax.fori_loop(0, total, number, jnp.int32(0))

    @pl.loop(0, count)
    def _(tile):
        row = rows[tile]
        position = cursor[row]
        cursor[row] = position + 1
        tile_at[position] = tile
        block_at[position] = slots[cols[tile]]


def tables(rows, cols, total, groups=PPD):
    count = rows.shape[0]
    return pl.pallas_call(
        tables_kernel,
        in_specs=[SMEM] * 2,
        out_specs=[SMEM] * 4,
        out_shape=[jax.ShapeDtypeStruct((size,), jnp.int32) for size in (groups + 1, count, count, total)],
        scratch_shapes=[pltpu.SMEM((groups,), jnp.int32)],
        name="tables",
    )(rows, cols)


def window(ref, tile):
    depth = ref.shape[1]
    across = ref.shape[2] // depth
    if across == 1:
        return ref.at[tile]
    return ref.at[lax.div(tile, across), :, pl.ds(pl.multiple_of(lax.rem(tile, across) * depth, depth), depth)]


def sort_kernel(choices, tile_at, chosen, tiles_ref, *refs):
    parts, sems = refs[: len(refs) // 2], refs[len(refs) // 2 :]
    begin = {choice: 0 for choice in choices}
    for choice, part, sem in zip(choices, parts, sems):
        base = begin[choice]
        count = part.shape[0] * part.shape[2] // tiles_ref.shape[2]
        begin[choice] += count

        @pl.when(chosen[0] == choice)
        def _(part=part, sem=sem, base=base, count=count):
            @pl.loop(0, count)
            def _(number):
                pltpu.make_async_copy(tiles_ref.at[tile_at[base + number]], window(part, number), sem).start()

    for choice, part, sem in zip(choices, parts, sems):

        @pl.when(chosen[0] == choice)
        def _(part=part, sem=sem):
            pltpu.make_async_copy(part, part, sem).wait()


def sort_tiles(tile_at, chosen, tiles, choices, shapes):
    return pl.pallas_call(
        functools.partial(sort_kernel, choices),
        in_specs=[SMEM] * 2 + [ANY],
        out_specs=[VMEM] * len(shapes),
        out_shape=[jax.ShapeDtypeStruct(shape, tiles.dtype) for shape in shapes],
        scratch_shapes=[pltpu.SemaphoreType.DMA] * len(shapes),
        compiler_params=pltpu.CompilerParams(vmem_limit_bytes=16 * MIB),
        name="sort_tiles",
    )(tile_at, chosen, tiles)


def payload_kernel(at_end, tiles_ref, received, payload, sem):
    del received

    @pl.when(at_end[0] == 1)
    def _():
        copy = pltpu.make_async_copy(tiles_ref, payload, sem)
        copy.start()
        copy.wait()


def payload_of(at_end, tiles, received):
    return pl.pallas_call(
        payload_kernel,
        in_specs=[SMEM, VMEM, ANY],
        out_specs=ANY,
        out_shape=jax.ShapeDtypeStruct(received.shape, received.dtype),
        input_output_aliases={2: 0},
        scratch_shapes=[pltpu.SemaphoreType.DMA],
        compiler_params=pltpu.CompilerParams(vmem_limit_bytes=4 * MIB),
        name="payload",
    )(at_end, tiles, received)


def add_row(sum_ref, begin, end, depth, tile_of, block_of):
    width = sum_ref.shape[1]

    @pl.loop(0, (end - begin + depth - 1) // depth)
    def _(turn):
        here = begin + turn * depth
        places = [jnp.minimum(here + part, end - 1) for part in range(depth)]
        left = [tile_of(places[0])]
        for part in range(1, depth):
            tile = tile_of(places[part])
            left.append(jnp.where(here + part < end, tile, jnp.zeros_like(tile)))
        left = jnp.concatenate(left, axis=1)
        for column in range(0, width, COLUMNS):
            window = pl.ds(column, COLUMNS)
            right = jnp.concatenate([block_of(place, window) for place in places], axis=0)
            sum_ref[:, window] += jnp.dot(left, right, preferred_element_type=jnp.float32)


def own_kernel(counts, group, fresh, starts, tile_at, block_at, own_slots, far_slots, firsts, tiles_ref, perm_ref, *refs):
    pieces = refs[: len(counts)]
    refs = refs[len(counts) :]
    if not fresh:
        sum_in, refs = refs[0], refs[2:]
    sum_out, flip_out, own_blocks, far_blocks, sums, own_list, far_list, own_sems, far_sems, row_sems = refs

    def fetch(slots, landing, sems, fetched):
        found = jnp.int32(0)
        for number, (piece, count) in enumerate(zip(pieces, counts)):

            def one(offset, found, piece=piece, number=number):
                slot = slots[firsts[number] + offset]

                @pl.when(slot >= 0)
                def _():
                    fetched[found] = slot
                    pltpu.make_async_copy(piece.at[offset], landing.at[slot], sems.at[slot]).start()

                return found + (slot >= 0).astype(jnp.int32)

            found = lax.fori_loop(0, count, one, found)
        return found

    far_found = fetch(far_slots, far_blocks, far_sems, far_list)
    own_found = fetch(own_slots, own_blocks, own_sems, own_list)
    if not fresh:
        for row in range(PPD):
            pltpu.make_async_copy(sum_in.at[row], sums.at[row], row_sems.at[row]).start()

    def arrived(landing, sems, slot):
        pltpu.make_async_copy(landing.at[slot], landing.at[slot], sems.at[slot]).wait()

    def flip_store(slot):
        return pltpu.make_async_copy(far_blocks.at[slot], flip_out.at[slot], far_sems.at[slot])

    @pl.loop(0, far_found)
    def _(number):
        slot = far_list[number]
        arrived(far_blocks, far_sems, slot)
        far_blocks[slot] = jnp.dot(
            far_blocks[slot], perm_ref[...], preferred_element_type=jnp.float32
        ).astype(jnp.bfloat16)
        flip_store(slot).start()

    @pl.loop(0, own_found)
    def _(number):
        arrived(own_blocks, own_sems, own_list[number])

    def store(row):
        return pltpu.make_async_copy(sums.at[row], sum_out.at[row], row_sems.at[row])

    @pl.loop(0, PPD)
    def _(row):
        if fresh:
            sums[row] = jnp.zeros(sums.shape[1:], jnp.float32)
        else:
            arrived(sums, row_sems, row)
        add_row(
            sums.at[row],
            starts[group + row],
            starts[group + row + 1],
            4 if fresh else 2,
            lambda place: tiles_ref[tile_at[place]],
            lambda place, window: own_blocks[block_at[place], :, window],
        )
        store(row).start()

    @pl.loop(0, far_found)
    def _(number):
        flip_store(far_list[number]).wait()

    @pl.loop(0, PPD)
    def _(row):
        store(row).wait()


def own_part(own_tables, far_slots, tiles, pieces, firsts, perm, group=0, earlier=()):
    starts, tile_at, block_at, own_slots = own_tables
    count, height, _ = tiles.shape
    depth, width = pieces[0].shape[1:]
    need = count // REUSE
    counts = [piece.shape[0] for piece in pieces]
    operands = 8 + len(pieces)
    return pl.pallas_call(
        functools.partial(own_kernel, counts, group, not earlier),
        in_specs=[SMEM] * 6 + [VMEM] * 2 + [ANY] * (len(pieces) + len(earlier)),
        out_specs=[ANY] * 2,
        out_shape=[
            jax.ShapeDtypeStruct((PPD, height, width), jnp.float32),
            jax.ShapeDtypeStruct((need, depth, width), jnp.bfloat16),
        ],
        input_output_aliases={operands: 0, operands + 1: 1} if earlier else {},
        scratch_shapes=[
            pltpu.VMEM((need, depth, width), jnp.bfloat16),
            pltpu.VMEM((need, depth, width), jnp.bfloat16),
            pltpu.VMEM((PPD, height, width), jnp.float32),
            pltpu.SMEM((need,), jnp.int32),
            pltpu.SMEM((need,), jnp.int32),
            pltpu.SemaphoreType.DMA((need,)),
            pltpu.SemaphoreType.DMA((need,)),
            pltpu.SemaphoreType.DMA((PPD,)),
        ],
        compiler_params=pltpu.CompilerParams(vmem_limit_bytes=56 * MIB),
        name="own_part",
    )(starts, tile_at, block_at, own_slots, far_slots, firsts, tiles, perm, *pieces, *earlier)


def far_kernel(base, segments, starts, block_at, chosen, *refs):
    tile_refs, refs = refs[: len(segments)], refs[len(segments) :]
    sum_in, flip_in = refs[:2]
    refs = refs[3:] if base else refs[2:]
    sum_out, result, tiles_ref, blocks, sums, rounded, tile_sem, block_sems, row_sems, out_sems = refs
    count = tiles_ref.shape[0]
    stop = base + count

    for source, (choice, begin) in zip(tile_refs, segments):
        held = source.shape[0] * source.shape[2] // tiles_ref.shape[2]
        low, high = max(begin, base), min(begin + held, stop)

        @pl.when(chosen[0] == choice)
        def _(source=source, begin=begin, low=low, high=high):
            if source.shape[2] == tiles_ref.shape[2]:
                here, there = source.at[pl.ds(low - begin, high - low)], tiles_ref.at[pl.ds(low - base, high - low)]
                pltpu.make_async_copy(here, there, tile_sem).start()
            else:

                @pl.loop(low, high)
                def _(place):
                    pltpu.make_async_copy(window(source, place - begin), tiles_ref.at[place - base], tile_sem).start()

    @pl.loop(0, count)
    def _(number):
        pltpu.make_async_copy(flip_in.at[block_at[base + number]], blocks.at[number], block_sems.at[number]).start()

    def each_row(action):
        @pl.loop(0, PPD)
        def _(row):
            first, last = starts[row], starts[row + 1]

            @pl.when(((last > base) if base else True) & ((last <= stop) | (first < stop)))
            def _():
                action(row, last <= stop)

    def load(row):
        return pltpu.make_async_copy(sum_in.at[row], sums.at[row], row_sems.at[row])

    def store(row):
        return pltpu.make_async_copy(rounded.at[row], result.at[row], out_sems.at[row])

    def keep(row):
        return pltpu.make_async_copy(sums.at[row], sum_out.at[row], out_sems.at[row])

    each_row(lambda row, complete: load(row).start())
    pltpu.make_async_copy(tiles_ref, tiles_ref, tile_sem).wait()


    def add(row, complete):
        begin, end = jnp.maximum(starts[row], base), jnp.minimum(starts[row + 1], stop)
        load(row).wait()

        @pl.loop(0, end - begin)
        def _(number):
            block = blocks.at[begin - base + number]
            pltpu.make_async_copy(block, block, block_sems.at[begin - base + number]).wait()

        add_row(
            sums.at[row],
            begin,
            end,
            4,
            lambda place: tiles_ref[place - base],
            lambda place, window: blocks[place - base, :, window],
        )

        @pl.when(complete)
        def _():
            rounded[row] = sums[row].astype(rounded.dtype)
            store(row).start()

        @pl.when(jnp.logical_not(complete))
        def _():
            keep(row).start()

    def finish(row, complete):
        pl.when(complete)(lambda: store(row).wait())
        pl.when(jnp.logical_not(complete))(lambda: keep(row).wait())

    each_row(add)
    each_row(finish)


def far_part(base, count, far_tables, chosen, sources, flipped, total, result=None):
    starts, _, block_at, _ = far_tables
    whole = total.shape
    given = [] if result is None else [result]
    held = [array.size // (whole[1] * flipped.shape[1]) for _, _, array in sources]
    used = [
        (source[:2], source[2])
        for source, size in zip(sources, held)
        if source[1] < base + count and source[1] + size > base
    ]
    operand = 3 + len(used)
    aliases = {operand: 0, operand + 2: 1} if given else {operand: 0}
    return pl.pallas_call(
        functools.partial(far_kernel, base, [segment for segment, _ in used]),
        in_specs=[SMEM] * 3 + [ANY] * (len(used) + 2 + len(given)),
        out_specs=[ANY] * 2,
        out_shape=[jax.ShapeDtypeStruct(whole, jnp.float32), jax.ShapeDtypeStruct(whole, jnp.bfloat16)],
        input_output_aliases=aliases,
        scratch_shapes=[
            pltpu.VMEM((count, whole[1], flipped.shape[1]), jnp.bfloat16),
            pltpu.VMEM((count,) + flipped.shape[1:], jnp.bfloat16),
            pltpu.VMEM(whole, jnp.float32),
            pltpu.VMEM(whole, jnp.bfloat16),
            pltpu.SemaphoreType.DMA,
            pltpu.SemaphoreType.DMA((count,)),
            pltpu.SemaphoreType.DMA((PPD,)),
            pltpu.SemaphoreType.DMA((PPD,)),
        ],
        compiler_params=pltpu.CompilerParams(vmem_limit_bytes=40 * MIB),
        name="far_part",
    )(starts, block_at, chosen, *[array for _, array in used], total, flipped, *given)


def together(*values):
    return lax.optimization_barrier(values)


def send(value, pairs):
    return lax.ppermute(value, "tile", pairs)


def flipped_bit(bit):
    return [(i, i ^ bit) for i in range(16)]


def staged_part(tiles, rows, cols, shard):
    local = shard.shape[0]
    block_total = 16 * local
    centre = [i for i in range(16) if i // 4 in (1, 2)]
    across = [(i, i ^ 12) for i in centre]
    from_ends = [(i, i ^ 8) for i in range(16) if i not in centre]
    from_centre = [(i, i ^ 8) for i in centre]
    around = [(i, i ^ 4) for i in centre] + from_ends
    other_z, other_y, other_core, opposite = (flipped_bit(bit) for bit in (4, 2, 1, 8))
    me = lax.axis_index("tile")
    z = me // 4
    in_centre = (z == 1) | (z == 2)
    at_end = 1 - in_centre.astype(jnp.int32).reshape(1)
    zs = [z, z ^ 1, jnp.where(z < 2, 2, 1), jnp.where(z < 2, 3, 0)]

    def owner(k, bits):
        return 4 * zs[k] + ((me & 3) ^ bits)

    def first_blocks(firsts):
        return jnp.stack(firsts).astype(jnp.int32)

    col_owner = cols // local
    late = (col_owner // 4 == zs[3]) | (col_owner == owner(2, 3))
    keys = rows + PPD * late.astype(jnp.int32)

    near = send(shard, other_z)
    first = send(shard, across)
    notes = send(jnp.stack([rows, cols]), opposite)
    order = tables(rows, cols, block_total)[1]
    c_own = send(shard, other_core)
    count = tiles.shape[0]
    step = shard.size // tiles[0].size
    sizes = tile_parts(count)
    shapes = [shard.shape] * 2 + [(size,) + tiles.shape[1:] for size in [count - 2 * step] + sizes]
    parts = sort_tiles(order, at_end, tiles, [1, 1, 1, 0, 0, 0], shapes)
    first, *parts = together(first, *parts)

    first = payload_of(at_end, parts[0], first)
    outer = send(first, around)
    near, c_own, *parts = together(near, c_own, *parts)
    second = send(near, across)
    y_own = send(shard, other_y)
    y_near = send(near, other_y)
    c_near = send(near, other_core)
    own_tables = tables(keys, cols, block_total, 2 * PPD)
    perm = flip_matrix(W)
    far_ends = [outer]
    first = jnp.where(in_centre, first, outer)
    second, first, y_own, y_near, c_near, perm, notes, *rest = together(
        second, first, y_own, y_near, c_near, perm, notes, *parts[1:], *own_tables
    )
    parts, own_tables = rest[1:5], rest[5:]

    second = payload_of(at_end, rest[0], second)
    outer = send(second, around)
    y_first = send(first, other_y)
    c_first = send(first, other_core)
    c_y_own = send(y_own, other_core)
    c_y_near = send(y_near, other_core)
    tiles_last, c_first = together(parts[0], c_first)
    far_ends += [outer, send(tiles_last, from_ends)]
    halves = (slice(0, local // 2), slice(local // 2, None))
    second = [jnp.where(in_centre, second[half], outer[half]) for half in halves]
    far_tables = tables(notes[0], notes[1], block_total)
    second[0], second[1], y_first, c_first, c_y_own, c_y_near, *far_tables = together(
        *second, y_first, c_first, c_y_own, c_y_near, *far_tables
    )

    far_centre = [send(parts[1], from_centre)]
    y_second = [send(half, other_y) for half in second]
    pieces = [shard, c_own, near, c_near, first, c_first, y_own, c_y_own, y_near, c_y_near, y_first]
    firsts = [owner(k, y + core) * local for y in (0, 2) for k in range(3) for core in (0, 1)][:11]
    early = own_part(own_tables, far_tables[3], tiles, pieces, first_blocks(firsts), perm)
    y_second[0], y_second[1], second[0], second[1], y_first, total, flipped, *parts = together(
        *y_second, *second, y_first, *early, *parts[2:]
    )
    far_centre += [send(part, from_centre) for part in parts]
    *y_second, far_ends[2] = together(*y_second, far_ends[2])

    c_y_first = send(y_first, other_core)
    c_second = [send(half, other_core) for half in second]
    c_y_second = [send(half, other_core) for half in y_second]
    pieces = [c_y_first, *second, *c_second, *y_second, *c_y_second]
    firsts = [owner(2, 3) * local] + [owner(3, bits) * local + half for bits in range(4) for half in (0, local // 2)]
    total, flipped = own_part(own_tables, far_tables[3], tiles, pieces, first_blocks(firsts), perm, PPD, (total, flipped))

    sources = [(0, step * number, array) for number, array in enumerate(far_ends)]
    sources += [(1, sum(sizes[:number]), array) for number, array in enumerate(far_centre)]
    return far_products(far_tables, at_end, sources, sizes, flipped, total)


def tile_parts(count):
    sizes = [count * share // 48 for share in SHARES]
    return sizes + [count - sum(sizes)]


def far_products(far_tables, chosen, sources, sizes, flipped, total):
    base, result = 0, None
    for size in sizes:
        total, result = far_part(base, size, far_tables, chosen, sources, flipped, total, result)
        base += size
    return result


def per_device(t2_tiles, t2_row, t2_col, integrals):
    peers = lax.axis_size("tile")
    if peers == 16:
        return staged_part(t2_tiles, t2_row, t2_col, integrals)
    block_total = peers * integrals.shape[0]
    opposite = [(source, (source + peers // 2) % peers) for source in range(peers)]
    own_tables = tables(t2_row, t2_col, block_total)
    sizes = tile_parts(t2_tiles.shape[0])
    zero = jnp.zeros((1,), jnp.int32)
    parts = sort_tiles(own_tables[1], zero, t2_tiles, [0] * 3, [(size,) + t2_tiles.shape[1:] for size in sizes])
    notes = send(jnp.stack([t2_row, t2_col]), opposite)
    sources = [(0, sum(sizes[:number]), send(part, opposite)) for number, part in enumerate(parts)]
    blocks = lax.all_gather(integrals, "tile", axis=0, tiled=True)
    far_tables = tables(notes[0], notes[1], block_total)
    total, flipped = own_part(own_tables, far_tables[3], t2_tiles, [blocks], zero, flip_matrix(W))
    return far_products(far_tables, zero, sources, sizes, flipped, total)


def solution(mesh):
    in_specs = (
        P(("groups", "tile"), None, None),
        P(("groups", "tile")),
        P(("groups", "tile")),
        P(("groups", "tile"), None, None),
    )
    out_specs = P(("groups", "tile"), None, None)
    return jax.shard_map(
        per_device, mesh=mesh, in_specs=in_specs, out_specs=out_specs, check_vma=False
    )
```

```python
import functools

import jax
import jax.numpy as jnp
from jax import lax
from jax.experimental import pallas as pl
from jax.experimental.pallas import tpu as pltpu
from jax.sharding import PartitionSpec as P

W = 32
PPD = 16
REUSE = 3
SHARES = (30, 12)
COLUMNS = 256
MIB = 1024 * 1024
SMEM = pl.BlockSpec(memory_space=pltpu.SMEM)
VMEM = pl.BlockSpec(memory_space=pltpu.VMEM)
ANY = pl.BlockSpec(memory_space=pl.ANY)


def flip_matrix(width):
    columns = jnp.arange(width * width, dtype=jnp.int32)
    source = (columns % width) * width + columns // width
    return (columns[:, None] == source[None, :]).astype(jnp.bfloat16)


def tables_kernel(rows, cols, starts, tile_at, block_at, slots, cursor):
    count, total, groups = rows.shape[0], slots.shape[0], cursor.shape[0]

    @pl.loop(0, total)
    def _(block):
        slots[block] = 0

    for row in range(groups):
        cursor[row] = 0

    @pl.loop(0, count)
    def _(tile):
        cursor[rows[tile]] += 1
        slots[cols[tile]] = 1

    place = jnp.int32(0)
    for row in range(groups):
        size = cursor[row]
        starts[row] = place
        cursor[row] = place
        place += size
    starts[groups] = place

    def number(block, used):
        named = slots[block]
        slots[block] = jnp.where(named > 0, used, -1)
        return used + named

    lax.fori_loop(0, total, number, jnp.int32(0))

    @pl.loop(0, count)
    def _(tile):
        row = rows[tile]
        position = cursor[row]
        cursor[row] = position + 1
        tile_at[position] = tile
        block_at[position] = slots[cols[tile]]


def tables(rows, cols, total, groups=PPD):
    count = rows.shape[0]
    return pl.pallas_call(
        tables_kernel,
        in_specs=[SMEM] * 2,
        out_specs=[SMEM] * 4,
        out_shape=[jax.ShapeDtypeStruct((size,), jnp.int32) for size in (groups + 1, count, count, total)],
        scratch_shapes=[pltpu.SMEM((groups,), jnp.int32)],
        name="tables",
    )(rows, cols)


def window(ref, tile):
    depth = ref.shape[1]
    across = ref.shape[2] // depth
    if across == 1:
        return ref.at[tile]
    return ref.at[lax.div(tile, across), :, pl.ds(pl.multiple_of(lax.rem(tile, across) * depth, depth), depth)]


def sort_kernel(choices, tile_at, chosen, tiles_ref, *refs):
    parts, sems = refs[: len(refs) // 2], refs[len(refs) // 2 :]
    begin = {choice: 0 for choice in choices}
    for choice, part, sem in zip(choices, parts, sems):
        base = begin[choice]
        count = part.shape[0] * part.shape[2] // tiles_ref.shape[2]
        begin[choice] += count

        @pl.when(chosen[0] == choice)
        def _(part=part, sem=sem, base=base, count=count):
            @pl.loop(0, count)
            def _(number):
                pltpu.make_async_copy(tiles_ref.at[tile_at[base + number]], window(part, number), sem).start()

    for choice, part, sem in zip(choices, parts, sems):

        @pl.when(chosen[0] == choice)
        def _(part=part, sem=sem):
            pltpu.make_async_copy(part, part, sem).wait()


def sort_tiles(tile_at, chosen, tiles, choices, shapes):
    return pl.pallas_call(
        functools.partial(sort_kernel, choices),
        in_specs=[SMEM] * 2 + [ANY],
        out_specs=[VMEM] * len(shapes),
        out_shape=[jax.ShapeDtypeStruct(shape, tiles.dtype) for shape in shapes],
        scratch_shapes=[pltpu.SemaphoreType.DMA] * len(shapes),
        compiler_params=pltpu.CompilerParams(vmem_limit_bytes=16 * MIB),
        name="sort_tiles",
    )(tile_at, chosen, tiles)


def payload_kernel(at_end, tiles_ref, received, payload, sem):
    del received

    @pl.when(at_end[0] == 1)
    def _():
        copy = pltpu.make_async_copy(tiles_ref, payload, sem)
        copy.start()
        copy.wait()


def payload_of(at_end, tiles, received):
    return pl.pallas_call(
        payload_kernel,
        in_specs=[SMEM, VMEM, ANY],
        out_specs=ANY,
        out_shape=jax.ShapeDtypeStruct(received.shape, received.dtype),
        input_output_aliases={2: 0},
        scratch_shapes=[pltpu.SemaphoreType.DMA],
        compiler_params=pltpu.CompilerParams(vmem_limit_bytes=4 * MIB),
        name="payload",
    )(at_end, tiles, received)


def add_row(sum_ref, begin, end, depth, tile_of, block_of):
    width = sum_ref.shape[1]

    @pl.loop(0, (end - begin + depth - 1) // depth)
    def _(turn):
        here = begin + turn * depth
        places = [jnp.minimum(here + part, end - 1) for part in range(depth)]
        left = [tile_of(places[0])]
        for part in range(1, depth):
            tile = tile_of(places[part])
            left.append(jnp.where(here + part < end, tile, jnp.zeros_like(tile)))
        left = jnp.concatenate(left, axis=1)
        for column in range(0, width, COLUMNS):
            window = pl.ds(column, COLUMNS)
            right = jnp.concatenate([block_of(place, window) for place in places], axis=0)
            sum_ref[:, window] += jnp.dot(left, right, preferred_element_type=jnp.float32)


def own_kernel(counts, group, fresh, starts, tile_at, block_at, own_slots, far_slots, firsts, tiles_ref, perm_ref, *refs):
    pieces = refs[: len(counts)]
    refs = refs[len(counts) :]
    if not fresh:
        sum_in, refs = refs[0], refs[2:]
    sum_out, flip_out, own_blocks, far_blocks, sums, own_list, far_list, own_sems, far_sems, row_sems = refs

    def fetch(slots, landing, sems, fetched):
        found = jnp.int32(0)
        for number, (piece, count) in enumerate(zip(pieces, counts)):

            def one(offset, found, piece=piece, number=number):
                slot = slots[firsts[number] + offset]

                @pl.when(slot >= 0)
                def _():
                    fetched[found] = slot
                    pltpu.make_async_copy(piece.at[offset], landing.at[slot], sems.at[slot]).start()

                return found + (slot >= 0).astype(jnp.int32)

            found = lax.fori_loop(0, count, one, found)
        return found

    far_found = fetch(far_slots, far_blocks, far_sems, far_list)
    own_found = fetch(own_slots, own_blocks, own_sems, own_list)
    if not fresh:
        for row in range(PPD):
            pltpu.make_async_copy(sum_in.at[row], sums.at[row], row_sems.at[row]).start()

    def arrived(landing, sems, slot):
        pltpu.make_async_copy(landing.at[slot], landing.at[slot], sems.at[slot]).wait()

    def flip_store(slot):
        return pltpu.make_async_copy(far_blocks.at[slot], flip_out.at[slot], far_sems.at[slot])

    @pl.loop(0, far_found)
    def _(number):
        slot = far_list[number]
        arrived(far_blocks, far_sems, slot)
        far_blocks[slot] = jnp.dot(
            far_blocks[slot], perm_ref[...], preferred_element_type=jnp.float32
        ).astype(jnp.bfloat16)
        flip_store(slot).start()

    @pl.loop(0, own_found)
    def _(number):
        arrived(own_blocks, own_sems, own_list[number])

    def store(row):
        return pltpu.make_async_copy(sums.at[row], sum_out.at[row], row_sems.at[row])

    @pl.loop(0, PPD)
    def _(row):
        if fresh:
            sums[row] = jnp.zeros(sums.shape[1:], jnp.float32)
        else:
            arrived(sums, row_sems, row)
        add_row(
            sums.at[row],
            starts[group + row],
            starts[group + row + 1],
            4 if fresh else 2,
            lambda place: tiles_ref[tile_at[place]],
            lambda place, window: own_blocks[block_at[place], :, window],
        )
        store(row).start()

    @pl.loop(0, far_found)
    def _(number):
        flip_store(far_list[number]).wait()

    @pl.loop(0, PPD)
    def _(row):
        store(row).wait()


def own_part(own_tables, far_slots, tiles, pieces, firsts, perm, group=0, earlier=()):
    starts, tile_at, block_at, own_slots = own_tables
    count, height, _ = tiles.shape
    depth, width = pieces[0].shape[1:]
    need = count // REUSE
    counts = [piece.shape[0] for piece in pieces]
    operands = 8 + len(pieces)
    return pl.pallas_call(
        functools.partial(own_kernel, counts, group, not earlier),
        in_specs=[SMEM] * 6 + [VMEM] * 2 + [ANY] * (len(pieces) + len(earlier)),
        out_specs=[ANY] * 2,
        out_shape=[
            jax.ShapeDtypeStruct((PPD, height, width), jnp.float32),
            jax.ShapeDtypeStruct((need, depth, width), jnp.bfloat16),
        ],
        input_output_aliases={operands: 0, operands + 1: 1} if earlier else {},
        scratch_shapes=[
            pltpu.VMEM((need, depth, width), jnp.bfloat16),
            pltpu.VMEM((need, depth, width), jnp.bfloat16),
            pltpu.VMEM((PPD, height, width), jnp.float32),
            pltpu.SMEM((need,), jnp.int32),
            pltpu.SMEM((need,), jnp.int32),
            pltpu.SemaphoreType.DMA((need,)),
            pltpu.SemaphoreType.DMA((need,)),
            pltpu.SemaphoreType.DMA((PPD,)),
        ],
        compiler_params=pltpu.CompilerParams(vmem_limit_bytes=56 * MIB),
        name="own_part",
    )(starts, tile_at, block_at, own_slots, far_slots, firsts, tiles, perm, *pieces, *earlier)


def far_kernel(base, segments, starts, block_at, chosen, *refs):
    tile_refs, refs = refs[: len(segments)], refs[len(segments) :]
    sum_in, flip_in = refs[:2]
    refs = refs[3:] if base else refs[2:]
    sum_out, result, tiles_ref, blocks, sums, rounded, tile_sem, block_sems, row_sems, out_sems = refs
    count = tiles_ref.shape[0]
    stop = base + count

    for source, (choice, begin) in zip(tile_refs, segments):
        held = source.shape[0] * source.shape[2] // tiles_ref.shape[2]
        low, high = max(begin, base), min(begin + held, stop)

        @pl.when(chosen[0] == choice)
        def _(source=source, begin=begin, low=low, high=high):
            if source.shape[2] == tiles_ref.shape[2]:
                here, there = source.at[pl.ds(low - begin, high - low)], tiles_ref.at[pl.ds(low - base, high - low)]
                pltpu.make_async_copy(here, there, tile_sem).start()
            else:

                @pl.loop(low, high)
                def _(place):
                    pltpu.make_async_copy(window(source, place - begin), tiles_ref.at[place - base], tile_sem).start()

    @pl.loop(0, count)
    def _(number):
        pltpu.make_async_copy(flip_in.at[block_at[base + number]], blocks.at[number], block_sems.at[number]).start()

    def each_row(action):
        @pl.loop(0, PPD)
        def _(row):
            first, last = starts[row], starts[row + 1]

            @pl.when(((last > base) if base else True) & ((last <= stop) | (first < stop)))
            def _():
                action(row, last <= stop)

    def load(row):
        return pltpu.make_async_copy(sum_in.at[row], sums.at[row], row_sems.at[row])

    def store(row):
        return pltpu.make_async_copy(rounded.at[row], result.at[row], out_sems.at[row])

    def keep(row):
        return pltpu.make_async_copy(sums.at[row], sum_out.at[row], out_sems.at[row])

    each_row(lambda row, complete: load(row).start())
    pltpu.make_async_copy(tiles_ref, tiles_ref, tile_sem).wait()


    def add(row, complete):
        begin, end = jnp.maximum(starts[row], base), jnp.minimum(starts[row + 1], stop)
        load(row).wait()

        @pl.loop(0, end - begin)
        def _(number):
            block = blocks.at[begin - base + number]
            pltpu.make_async_copy(block, block, block_sems.at[begin - base + number]).wait()

        add_row(
            sums.at[row],
            begin,
            end,
            4,
            lambda place: tiles_ref[place - base],
            lambda place, window: blocks[place - base, :, window],
        )

        @pl.when(complete)
        def _():
            rounded[row] = sums[row].astype(rounded.dtype)
            store(row).start()

        @pl.when(jnp.logical_not(complete))
        def _():
            keep(row).start()

    def finish(row, complete):
        pl.when(complete)(lambda: store(row).wait())
        pl.when(jnp.logical_not(complete))(lambda: keep(row).wait())

    each_row(add)
    each_row(finish)


def far_part(base, count, far_tables, chosen, sources, flipped, total, result=None):
    starts, _, block_at, _ = far_tables
    whole = total.shape
    given = [] if result is None else [result]
    held = [array.size // (whole[1] * flipped.shape[1]) for _, _, array in sources]
    used = [
        (source[:2], source[2])
        for source, size in zip(sources, held)
        if source[1] < base + count and source[1] + size > base
    ]
    operand = 3 + len(used)
    aliases = {operand: 0, operand + 2: 1} if given else {operand: 0}
    return pl.pallas_call(
        functools.partial(far_kernel, base, [segment for segment, _ in used]),
        in_specs=[SMEM] * 3 + [ANY] * (len(used) + 2 + len(given)),
        out_specs=[ANY] * 2,
        out_shape=[jax.ShapeDtypeStruct(whole, jnp.float32), jax.ShapeDtypeStruct(whole, jnp.bfloat16)],
        input_output_aliases=aliases,
        scratch_shapes=[
            pltpu.VMEM((count, whole[1], flipped.shape[1]), jnp.bfloat16),
            pltpu.VMEM((count,) + flipped.shape[1:], jnp.bfloat16),
            pltpu.VMEM(whole, jnp.float32),
            pltpu.VMEM(whole, jnp.bfloat16),
            pltpu.SemaphoreType.DMA,
            pltpu.SemaphoreType.DMA((count,)),
            pltpu.SemaphoreType.DMA((PPD,)),
            pltpu.SemaphoreType.DMA((PPD,)),
        ],
        compiler_params=pltpu.CompilerParams(vmem_limit_bytes=40 * MIB),
        name="far_part",
    )(starts, block_at, chosen, *[array for _, array in used], total, flipped, *given)


def together(*values):
    return lax.optimization_barrier(values)


def send(value, pairs):
    return lax.ppermute(value, "tile", pairs)


def flipped_bit(bit):
    return [(i, i ^ bit) for i in range(16)]


def staged_part(tiles, rows, cols, shard):
    local = shard.shape[0]
    block_total = 16 * local
    centre = [i for i in range(16) if i // 4 in (1, 2)]
    across = [(i, i ^ 12) for i in centre]
    from_ends = [(i, i ^ 8) for i in range(16) if i not in centre]
    from_centre = [(i, i ^ 8) for i in centre]
    around = [(i, i ^ 4) for i in centre] + from_ends
    other_z, other_y, other_core = (flipped_bit(bit) for bit in (4, 2, 1))
    me = lax.axis_index("tile")
    z = me // 4
    in_centre = (z == 1) | (z == 2)
    at_end = 1 - in_centre.astype(jnp.int32).reshape(1)
    zs = [z, z ^ 1, jnp.where(z < 2, 2, 1), jnp.where(z < 2, 3, 0)]

    def owner(k, bits):
        return 4 * zs[k] + ((me & 3) ^ bits)

    def first_blocks(firsts):
        return jnp.stack(firsts).astype(jnp.int32)

    col_owner = cols // local
    late = (col_owner // 4 == zs[3]) | (col_owner == owner(2, 3))
    keys = rows + PPD * late.astype(jnp.int32)

    near = send(shard, other_z)
    first = send(shard, across)
    notes = lax.all_gather(jnp.stack([rows, cols]), "tile")
    order = tables(rows, cols, block_total)[1]
    c_own = send(shard, other_core)
    y_own = send(shard, other_y)
    count = tiles.shape[0]
    step = shard.size // tiles[0].size
    sizes = tile_parts(count)
    shapes = [shard.shape] * 2 + [(size,) + tiles.shape[1:] for size in [count - 2 * step] + sizes]
    parts = sort_tiles(order, at_end, tiles, [1, 1, 1, 0, 0, 0], shapes)
    first, *parts = together(first, *parts)

    first = payload_of(at_end, parts[0], first)
    outer = send(first, around)
    near, c_own, y_own, *parts = together(near, c_own, y_own, *parts)
    second = send(near, across)
    y_near = send(near, other_y)
    c_near = send(near, other_core)
    own_tables = tables(keys, cols, block_total, 2 * PPD)
    perm = flip_matrix(W)
    far_ends = [outer]
    first = jnp.where(in_centre, first, outer)
    second, tiles_next = together(second, parts[1])
    second = payload_of(at_end, tiles_next, second)
    outer = send(second, around)
    first, y_own, y_near, c_near, perm, notes, *rest = together(
        first, y_own, y_near, c_near, perm, notes, *parts[2:], *own_tables
    )
    parts, own_tables = rest[:4], rest[4:]
    y_first = send(first, other_y)
    c_first = send(first, other_core)
    c_y_own = send(y_own, other_core)
    c_y_near = send(y_near, other_core)
    tiles_last, c_first = together(parts[0], c_first)
    far_ends += [outer, send(tiles_last, from_ends)]
    halves = (slice(0, local // 2), slice(local // 2, None))
    second = [jnp.where(in_centre, second[half], outer[half]) for half in halves]
    notes = lax.dynamic_index_in_dim(notes, me ^ 8, keepdims=False)
    far_tables = tables(notes[0], notes[1], block_total)
    second[0], second[1], y_first, c_first, c_y_own, c_y_near, *far_tables = together(
        *second, y_first, c_first, c_y_own, c_y_near, *far_tables
    )

    far_centre = [send(parts[1], from_centre)]
    y_second = [send(half, other_y) for half in second]
    pieces = [shard, c_own, near, c_near, first, c_first, y_own, c_y_own, y_near, c_y_near, y_first]
    firsts = [owner(k, y + core) * local for y in (0, 2) for k in range(3) for core in (0, 1)][:11]
    early = own_part(own_tables, far_tables[3], tiles, pieces, first_blocks(firsts), perm)
    y_second[0], y_second[1], second[0], second[1], y_first, total, flipped, *parts = together(
        *y_second, *second, y_first, *early, *parts[2:]
    )
    far_centre += [send(part, from_centre) for part in parts]
    *y_second, far_ends[2] = together(*y_second, far_ends[2])

    c_y_first = send(y_first, other_core)
    c_second = [send(half, other_core) for half in second]
    c_y_second = [send(half, other_core) for half in y_second]
    pieces = [c_y_first, *second, *c_second, *y_second, *c_y_second]
    firsts = [owner(2, 3) * local] + [owner(3, bits) * local + half for bits in range(4) for half in (0, local // 2)]
    total, flipped = own_part(own_tables, far_tables[3], tiles, pieces, first_blocks(firsts), perm, PPD, (total, flipped))

    sources = [(0, step * number, array) for number, array in enumerate(far_ends)]
    sources += [(1, sum(sizes[:number]), array) for number, array in enumerate(far_centre)]
    return far_products(far_tables, at_end, sources, sizes, flipped, total)


def tile_parts(count):
    sizes = [count * share // 48 for share in SHARES]
    return sizes + [count - sum(sizes)]


def far_products(far_tables, chosen, sources, sizes, flipped, total):
    base, result = 0, None
    for size in sizes:
        total, result = far_part(base, size, far_tables, chosen, sources, flipped, total, result)
        base += size
    return result


def per_device(t2_tiles, t2_row, t2_col, integrals):
    peers = lax.axis_size("tile")
    if peers == 16:
        return staged_part(t2_tiles, t2_row, t2_col, integrals)
    block_total = peers * integrals.shape[0]
    opposite = [(source, (source + peers // 2) % peers) for source in range(peers)]
    own_tables = tables(t2_row, t2_col, block_total)
    sizes = tile_parts(t2_tiles.shape[0])
    zero = jnp.zeros((1,), jnp.int32)
    parts = sort_tiles(own_tables[1], zero, t2_tiles, [0] * 3, [(size,) + t2_tiles.shape[1:] for size in sizes])
    notes = send(jnp.stack([t2_row, t2_col]), opposite)
    sources = [(0, sum(sizes[:number]), send(part, opposite)) for number, part in enumerate(parts)]
    blocks = lax.all_gather(integrals, "tile", axis=0, tiled=True)
    far_tables = tables(notes[0], notes[1], block_total)
    total, flipped = own_part(own_tables, far_tables[3], t2_tiles, [blocks], zero, flip_matrix(W))
    return far_products(far_tables, zero, sources, sizes, flipped, total)


def solution(mesh):
    in_specs = (
        P(("groups", "tile"), None, None),
        P(("groups", "tile")),
        P(("groups", "tile")),
        P(("groups", "tile"), None, None),
    )
    out_specs = P(("groups", "tile"), None, None)
    return jax.shard_map(
        per_device, mesh=mesh, in_specs=in_specs, out_specs=out_specs, check_vma=False
    )
```

```python
import functools

import jax
import jax.numpy as jnp
from jax import lax
from jax.experimental import pallas as pl
from jax.experimental.pallas import tpu as pltpu
from jax.sharding import PartitionSpec as P

W = 32
PPD = 16
REUSE = 3
SHARES = (30, 12)
COLUMNS = 256
MIB = 1024 * 1024
FAR_COST = 10**10
SMEM = pl.BlockSpec(memory_space=pltpu.SMEM)
VMEM = pl.BlockSpec(memory_space=pltpu.VMEM)
ANY = pl.BlockSpec(memory_space=pl.ANY)


def flip_matrix(width):
    columns = jnp.arange(width * width, dtype=jnp.int32)
    source = (columns % width) * width + columns // width
    return (columns[:, None] == source[None, :]).astype(jnp.bfloat16)


def tables_kernel(rows, cols, starts, tile_at, block_at, slots, cursor):
    count, total, groups = rows.shape[0], slots.shape[0], cursor.shape[0]

    @pl.loop(0, total)
    def _(block):
        slots[block] = 0

    for row in range(groups):
        cursor[row] = 0

    @pl.loop(0, count)
    def _(tile):
        cursor[rows[tile]] += 1
        slots[cols[tile]] = 1

    place = jnp.int32(0)
    for row in range(groups):
        size = cursor[row]
        starts[row] = place
        cursor[row] = place
        place += size
    starts[groups] = place

    def number(block, used):
        named = slots[block]
        slots[block] = jnp.where(named > 0, used, -1)
        return used + named

    lax.fori_loop(0, total, number, jnp.int32(0))

    @pl.loop(0, count)
    def _(tile):
        row = rows[tile]
        position = cursor[row]
        cursor[row] = position + 1
        tile_at[position] = tile
        block_at[position] = slots[cols[tile]]


def tables(rows, cols, total, groups=PPD, cost=0):
    count = rows.shape[0]
    return pl.pallas_call(
        tables_kernel,
        in_specs=[SMEM] * 2,
        out_specs=[SMEM] * 4,
        out_shape=[jax.ShapeDtypeStruct((size,), jnp.int32) for size in (groups + 1, count, count, total)],
        scratch_shapes=[pltpu.SMEM((groups,), jnp.int32)],
        cost_estimate=pl.CostEstimate(flops=cost, bytes_accessed=0, transcendentals=0) if cost else None,
        name="tables",
    )(rows, cols)


def window(ref, tile):
    depth = ref.shape[1]
    across = ref.shape[2] // depth
    if across == 1:
        return ref.at[tile]
    return ref.at[lax.div(tile, across), :, pl.ds(pl.multiple_of(lax.rem(tile, across) * depth, depth), depth)]


def sort_kernel(choices, tile_at, chosen, tiles_ref, *refs):
    parts, sems = refs[: len(refs) // 2], refs[len(refs) // 2 :]
    begin = {choice: 0 for choice in choices}
    for choice, part, sem in zip(choices, parts, sems):
        base = begin[choice]
        count = part.shape[0] * part.shape[2] // tiles_ref.shape[2]
        begin[choice] += count

        @pl.when(chosen[0] == choice)
        def _(part=part, sem=sem, base=base, count=count):
            @pl.loop(0, count)
            def _(number):
                pltpu.make_async_copy(tiles_ref.at[tile_at[base + number]], window(part, number), sem).start()

    for choice, part, sem in zip(choices, parts, sems):

        @pl.when(chosen[0] == choice)
        def _(part=part, sem=sem):
            pltpu.make_async_copy(part, part, sem).wait()


def sort_tiles(tile_at, chosen, tiles, choices, shapes):
    return pl.pallas_call(
        functools.partial(sort_kernel, choices),
        in_specs=[SMEM] * 2 + [ANY],
        out_specs=[VMEM] * len(shapes),
        out_shape=[jax.ShapeDtypeStruct(shape, tiles.dtype) for shape in shapes],
        scratch_shapes=[pltpu.SemaphoreType.DMA] * len(shapes),
        compiler_params=pltpu.CompilerParams(vmem_limit_bytes=16 * MIB),
        name="sort_tiles",
    )(tile_at, chosen, tiles)


def payload_kernel(at_end, tiles_ref, received, payload, sem):
    del received

    @pl.when(at_end[0] == 1)
    def _():
        copy = pltpu.make_async_copy(tiles_ref, payload, sem)
        copy.start()
        copy.wait()


def payload_of(at_end, tiles, received):
    return pl.pallas_call(
        payload_kernel,
        in_specs=[SMEM, VMEM, ANY],
        out_specs=ANY,
        out_shape=jax.ShapeDtypeStruct(received.shape, received.dtype),
        input_output_aliases={2: 0},
        scratch_shapes=[pltpu.SemaphoreType.DMA],
        compiler_params=pltpu.CompilerParams(vmem_limit_bytes=4 * MIB),
        name="payload",
    )(at_end, tiles, received)


def add_row(sum_ref, begin, end, depth, tile_of, block_of):
    width = sum_ref.shape[1]

    @pl.loop(0, (end - begin + depth - 1) // depth)
    def _(turn):
        here = begin + turn * depth
        places = [jnp.minimum(here + part, end - 1) for part in range(depth)]
        left = [tile_of(places[0])]
        for part in range(1, depth):
            tile = tile_of(places[part])
            left.append(jnp.where(here + part < end, tile, jnp.zeros_like(tile)))
        left = jnp.concatenate(left, axis=1)
        for column in range(0, width, COLUMNS):
            window = pl.ds(column, COLUMNS)
            right = jnp.concatenate([block_of(place, window) for place in places], axis=0)
            sum_ref[:, window] += jnp.dot(left, right, preferred_element_type=jnp.float32)


def own_kernel(counts, group, fresh, starts, tile_at, block_at, own_slots, far_slots, firsts, tiles_ref, perm_ref, *refs):
    pieces = refs[: len(counts)]
    refs = refs[len(counts) :]
    if not fresh:
        sum_in, refs = refs[0], refs[2:]
    sum_out, flip_out, own_blocks, far_blocks, sums, own_list, far_list, own_sems, far_sems, row_sems = refs

    def fetch(slots, landing, sems, fetched):
        found = jnp.int32(0)
        for number, (piece, count) in enumerate(zip(pieces, counts)):

            def one(offset, found, piece=piece, number=number):
                slot = slots[firsts[number] + offset]

                @pl.when(slot >= 0)
                def _():
                    fetched[found] = slot
                    pltpu.make_async_copy(piece.at[offset], landing.at[slot], sems.at[slot]).start()

                return found + (slot >= 0).astype(jnp.int32)

            found = lax.fori_loop(0, count, one, found)
        return found

    far_found = fetch(far_slots, far_blocks, far_sems, far_list)
    own_found = fetch(own_slots, own_blocks, own_sems, own_list)
    if not fresh:
        for row in range(PPD):
            pltpu.make_async_copy(sum_in.at[row], sums.at[row], row_sems.at[row]).start()

    def arrived(landing, sems, slot):
        pltpu.make_async_copy(landing.at[slot], landing.at[slot], sems.at[slot]).wait()

    def flip_store(slot):
        return pltpu.make_async_copy(far_blocks.at[slot], flip_out.at[slot], far_sems.at[slot])

    @pl.loop(0, far_found)
    def _(number):
        slot = far_list[number]
        arrived(far_blocks, far_sems, slot)
        far_blocks[slot] = jnp.dot(
            far_blocks[slot], perm_ref[...], preferred_element_type=jnp.float32
        ).astype(jnp.bfloat16)
        flip_store(slot).start()

    @pl.loop(0, own_found)
    def _(number):
        arrived(own_blocks, own_sems, own_list[number])

    def store(row):
        return pltpu.make_async_copy(sums.at[row], sum_out.at[row], row_sems.at[row])

    @pl.loop(0, PPD)
    def _(row):
        if fresh:
            sums[row] = jnp.zeros(sums.shape[1:], jnp.float32)
        else:
            arrived(sums, row_sems, row)
        add_row(
            sums.at[row],
            starts[group + row],
            starts[group + row + 1],
            4 if fresh else 2,
            lambda place: tiles_ref[tile_at[place]],
            lambda place, window: own_blocks[block_at[place], :, window],
        )
        store(row).start()

    @pl.loop(0, far_found)
    def _(number):
        flip_store(far_list[number]).wait()

    @pl.loop(0, PPD)
    def _(row):
        store(row).wait()


def own_part(own_tables, far_slots, tiles, pieces, firsts, perm, group=0, earlier=()):
    starts, tile_at, block_at, own_slots = own_tables
    count, height, _ = tiles.shape
    depth, width = pieces[0].shape[1:]
    need = count // REUSE
    counts = [piece.shape[0] for piece in pieces]
    operands = 8 + len(pieces)
    return pl.pallas_call(
        functools.partial(own_kernel, counts, group, not earlier),
        in_specs=[SMEM] * 6 + [VMEM] * 2 + [ANY] * (len(pieces) + len(earlier)),
        out_specs=[ANY] * 2,
        out_shape=[
            jax.ShapeDtypeStruct((PPD, height, width), jnp.float32),
            jax.ShapeDtypeStruct((need, depth, width), jnp.bfloat16),
        ],
        input_output_aliases={operands: 0, operands + 1: 1} if earlier else {},
        scratch_shapes=[
            pltpu.VMEM((need, depth, width), jnp.bfloat16),
            pltpu.VMEM((need, depth, width), jnp.bfloat16),
            pltpu.VMEM((PPD, height, width), jnp.float32),
            pltpu.SMEM((need,), jnp.int32),
            pltpu.SMEM((need,), jnp.int32),
            pltpu.SemaphoreType.DMA((need,)),
            pltpu.SemaphoreType.DMA((need,)),
            pltpu.SemaphoreType.DMA((PPD,)),
        ],
        compiler_params=pltpu.CompilerParams(vmem_limit_bytes=56 * MIB),
        name="own_part",
    )(starts, tile_at, block_at, own_slots, far_slots, firsts, tiles, perm, *pieces, *earlier)


def far_kernel(base, segments, starts, block_at, chosen, *refs):
    tile_refs, refs = refs[: len(segments)], refs[len(segments) :]
    sum_in, flip_in = refs[:2]
    refs = refs[3:] if base else refs[2:]
    sum_out, result, tiles_ref, blocks, sums, rounded, tile_sem, block_sems, row_sems, out_sems = refs
    count = tiles_ref.shape[0]
    stop = base + count

    for source, (choice, begin) in zip(tile_refs, segments):
        held = source.shape[0] * source.shape[2] // tiles_ref.shape[2]
        low, high = max(begin, base), min(begin + held, stop)

        @pl.when(chosen[0] == choice)
        def _(source=source, begin=begin, low=low, high=high):
            if source.shape[2] == tiles_ref.shape[2]:
                here, there = source.at[pl.ds(low - begin, high - low)], tiles_ref.at[pl.ds(low - base, high - low)]
                pltpu.make_async_copy(here, there, tile_sem).start()
            else:

                @pl.loop(low, high)
                def _(place):
                    pltpu.make_async_copy(window(source, place - begin), tiles_ref.at[place - base], tile_sem).start()

    @pl.loop(0, count)
    def _(number):
        pltpu.make_async_copy(flip_in.at[block_at[base + number]], blocks.at[number], block_sems.at[number]).start()

    def each_row(action):
        @pl.loop(0, PPD)
        def _(row):
            first, last = starts[row], starts[row + 1]

            @pl.when(((last > base) if base else True) & ((last <= stop) | (first < stop)))
            def _():
                action(row, last <= stop)

    def load(row):
        return pltpu.make_async_copy(sum_in.at[row], sums.at[row], row_sems.at[row])

    def store(row):
        return pltpu.make_async_copy(rounded.at[row], result.at[row], out_sems.at[row])

    def keep(row):
        return pltpu.make_async_copy(sums.at[row], sum_out.at[row], out_sems.at[row])

    each_row(lambda row, complete: load(row).start())
    pltpu.make_async_copy(tiles_ref, tiles_ref, tile_sem).wait()


    def add(row, complete):
        begin, end = jnp.maximum(starts[row], base), jnp.minimum(starts[row + 1], stop)
        load(row).wait()

        @pl.loop(0, end - begin)
        def _(number):
            block = blocks.at[begin - base + number]
            pltpu.make_async_copy(block, block, block_sems.at[begin - base + number]).wait()

        add_row(
            sums.at[row],
            begin,
            end,
            4,
            lambda place: tiles_ref[place - base],
            lambda place, window: blocks[place - base, :, window],
        )

        @pl.when(complete)
        def _():
            rounded[row] = sums[row].astype(rounded.dtype)
            store(row).start()

        @pl.when(jnp.logical_not(complete))
        def _():
            keep(row).start()

    def finish(row, complete):
        pl.when(complete)(lambda: store(row).wait())
        pl.when(jnp.logical_not(complete))(lambda: keep(row).wait())

    each_row(add)
    each_row(finish)


def far_part(base, count, far_tables, chosen, sources, flipped, total, result=None):
    starts, _, block_at, _ = far_tables
    whole = total.shape
    given = [] if result is None else [result]
    held = [array.size // (whole[1] * flipped.shape[1]) for _, _, array in sources]
    used = [
        (source[:2], source[2])
        for source, size in zip(sources, held)
        if source[1] < base + count and source[1] + size > base
    ]
    operand = 3 + len(used)
    aliases = {operand: 0, operand + 2: 1} if given else {operand: 0}
    return pl.pallas_call(
        functools.partial(far_kernel, base, [segment for segment, _ in used]),
        in_specs=[SMEM] * 3 + [ANY] * (len(used) + 2 + len(given)),
        out_specs=[ANY] * 2,
        out_shape=[jax.ShapeDtypeStruct(whole, jnp.float32), jax.ShapeDtypeStruct(whole, jnp.bfloat16)],
        input_output_aliases=aliases,
        scratch_shapes=[
            pltpu.VMEM((count, whole[1], flipped.shape[1]), jnp.bfloat16),
            pltpu.VMEM((count,) + flipped.shape[1:], jnp.bfloat16),
            pltpu.VMEM(whole, jnp.float32),
            pltpu.VMEM(whole, jnp.bfloat16),
            pltpu.SemaphoreType.DMA,
            pltpu.SemaphoreType.DMA((count,)),
            pltpu.SemaphoreType.DMA((PPD,)),
            pltpu.SemaphoreType.DMA((PPD,)),
        ],
        compiler_params=pltpu.CompilerParams(vmem_limit_bytes=40 * MIB),
        name="far_part",
    )(starts, block_at, chosen, *[array for _, array in used], total, flipped, *given)


def together(*values):
    return lax.optimization_barrier(values)


def send(value, pairs):
    return lax.ppermute(value, "tile", pairs)


def flipped_bit(bit):
    return [(i, i ^ bit) for i in range(16)]


def staged_part(tiles, rows, cols, shard):
    local = shard.shape[0]
    block_total = 16 * local
    centre = [i for i in range(16) if i // 4 in (1, 2)]
    across = [(i, i ^ 12) for i in centre]
    from_ends = [(i, i ^ 8) for i in range(16) if i not in centre]
    from_centre = [(i, i ^ 8) for i in centre]
    around = [(i, i ^ 4) for i in centre] + from_ends
    other_z, other_y, other_core, opposite = (flipped_bit(bit) for bit in (4, 2, 1, 8))
    me = lax.axis_index("tile")
    z = me // 4
    in_centre = (z == 1) | (z == 2)
    at_end = 1 - in_centre.astype(jnp.int32).reshape(1)
    zs = [z, z ^ 1, jnp.where(z < 2, 2, 1), jnp.where(z < 2, 3, 0)]

    def owner(k, bits):
        return 4 * zs[k] + ((me & 3) ^ bits)

    def first_blocks(firsts):
        return jnp.stack(firsts).astype(jnp.int32)

    col_owner = cols // local
    late = (col_owner // 4 == zs[3]) | (col_owner == owner(2, 3))
    keys = rows + PPD * late.astype(jnp.int32)

    near = send(shard, other_z)
    first = send(shard, across)
    notes = send(jnp.stack([rows, cols]), opposite)
    order = tables(rows, cols, block_total)[1]
    c_own = send(shard, other_core)
    y_own = send(shard, other_y)
    count = tiles.shape[0]
    step = shard.size // tiles[0].size
    sizes = tile_parts(count)
    shapes = [shard.shape] * 2 + [(size,) + tiles.shape[1:] for size in [count - 2 * step] + sizes]
    parts = sort_tiles(order, at_end, tiles, [1, 1, 1, 0, 0, 0], shapes)
    first, *parts = together(first, *parts)

    first = payload_of(at_end, parts[0], first)
    outer = send(first, around)
    near, c_own, y_own, *parts = together(near, c_own, y_own, *parts)
    second = send(near, across)
    y_near = send(near, other_y)
    c_near = send(near, other_core)
    own_tables = tables(keys, cols, block_total, 2 * PPD)
    far_tables = tables(notes[0], notes[1], block_total, cost=FAR_COST)
    perm = flip_matrix(W)
    far_ends = [outer]
    first = jnp.where(in_centre, first, outer)
    second, tiles_next = together(second, parts[1])
    second = payload_of(at_end, tiles_next, second)
    outer = send(second, around)
    first, y_own, y_near, c_near, perm, *rest = together(
        first, y_own, y_near, c_near, perm, *parts[2:], *own_tables, *far_tables
    )
    parts, own_tables, far_tables = rest[:4], rest[4:8], rest[8:]
    y_first = send(first, other_y)
    c_first = send(first, other_core)
    c_y_own = send(y_own, other_core)
    c_y_near = send(y_near, other_core)
    tiles_last, c_first = together(parts[0], c_first)
    far_ends += [outer, send(tiles_last, from_ends)]
    halves = (slice(0, local // 2), slice(local // 2, None))
    second = [jnp.where(in_centre, second[half], outer[half]) for half in halves]
    *second, y_first, c_first, c_y_own, c_y_near = together(*second, y_first, c_first, c_y_own, c_y_near)

    far_centre = [send(parts[1], from_centre)]
    y_second = [send(half, other_y) for half in second]
    pieces = [shard, c_own, near, c_near, first, c_first, y_own, c_y_own, y_near, c_y_near, y_first]
    firsts = [owner(k, y + core) * local for y in (0, 2) for k in range(3) for core in (0, 1)][:11]
    early = own_part(own_tables, far_tables[3], tiles, pieces, first_blocks(firsts), perm)
    y_second[0], y_second[1], second[0], second[1], y_first, total, flipped, *parts = together(
        *y_second, *second, y_first, *early, *parts[2:]
    )
    far_centre += [send(part, from_centre) for part in parts]
    *y_second, far_ends[2] = together(*y_second, far_ends[2])

    c_y_first = send(y_first, other_core)
    c_second = [send(half, other_core) for half in second]
    c_y_second = [send(half, other_core) for half in y_second]
    pieces = [c_y_first, *second, *c_second, *y_second, *c_y_second]
    firsts = [owner(2, 3) * local] + [owner(3, bits) * local + half for bits in range(4) for half in (0, local // 2)]
    total, flipped = own_part(own_tables, far_tables[3], tiles, pieces, first_blocks(firsts), perm, PPD, (total, flipped))

    sources = [(0, step * number, array) for number, array in enumerate(far_ends)]
    sources += [(1, sum(sizes[:number]), array) for number, array in enumerate(far_centre)]
    return far_products(far_tables, at_end, sources, sizes, flipped, total)


def tile_parts(count):
    sizes = [count * share // 48 for share in SHARES]
    return sizes + [count - sum(sizes)]


def far_products(far_tables, chosen, sources, sizes, flipped, total):
    base, result = 0, None
    for size in sizes:
        total, result = far_part(base, size, far_tables, chosen, sources, flipped, total, result)
        base += size
    return result


def per_device(t2_tiles, t2_row, t2_col, integrals):
    peers = lax.axis_size("tile")
    if peers == 16:
        return staged_part(t2_tiles, t2_row, t2_col, integrals)
    block_total = peers * integrals.shape[0]
    opposite = [(source, (source + peers // 2) % peers) for source in range(peers)]
    own_tables = tables(t2_row, t2_col, block_total)
    sizes = tile_parts(t2_tiles.shape[0])
    zero = jnp.zeros((1,), jnp.int32)
    parts = sort_tiles(own_tables[1], zero, t2_tiles, [0] * 3, [(size,) + t2_tiles.shape[1:] for size in sizes])
    notes = send(jnp.stack([t2_row, t2_col]), opposite)
    sources = [(0, sum(sizes[:number]), send(part, opposite)) for number, part in enumerate(parts)]
    blocks = lax.all_gather(integrals, "tile", axis=0, tiled=True)
    far_tables = tables(notes[0], notes[1], block_total)
    total, flipped = own_part(own_tables, far_tables[3], t2_tiles, [blocks], zero, flip_matrix(W))
    return far_products(far_tables, zero, sources, sizes, flipped, total)


def solution(mesh):
    in_specs = (
        P(("groups", "tile"), None, None),
        P(("groups", "tile")),
        P(("groups", "tile")),
        P(("groups", "tile"), None, None),
    )
    out_specs = P(("groups", "tile"), None, None)
    return jax.shard_map(
        per_device, mesh=mesh, in_specs=in_specs, out_specs=out_specs, check_vma=False
    )
```

```python
import functools

import jax
import jax.numpy as jnp
from jax import lax
from jax.experimental import pallas as pl
from jax.experimental.pallas import tpu as pltpu
from jax.sharding import PartitionSpec as P

W = 32
PPD = 16
REUSE = 3
SHARES = (30, 12)
COLUMNS = 256
MIB = 1024 * 1024
FAR_COST = 4 * 10**9
SMEM = pl.BlockSpec(memory_space=pltpu.SMEM)
VMEM = pl.BlockSpec(memory_space=pltpu.VMEM)
ANY = pl.BlockSpec(memory_space=pl.ANY)


def flip_matrix(columns):
    source = (columns % W) * W + columns // W
    return (columns[:, None] == source[None, :]).astype(jnp.bfloat16)


def tables_kernel(rows, cols, starts, tile_at, block_at, slots, cursor):
    count, total, groups = rows.shape[0], slots.shape[0], cursor.shape[0]

    @pl.loop(0, total)
    def _(block):
        slots[block] = 0

    for row in range(groups):
        cursor[row] = 0

    @pl.loop(0, count)
    def _(tile):
        cursor[rows[tile]] += 1
        slots[cols[tile]] = 1

    place = jnp.int32(0)
    for row in range(groups):
        size = cursor[row]
        starts[row] = place
        cursor[row] = place
        place += size
    starts[groups] = place

    def number(block, used):
        named = slots[block]
        slots[block] = jnp.where(named > 0, used, -1)
        return used + named

    lax.fori_loop(0, total, number, jnp.int32(0))

    @pl.loop(0, count)
    def _(tile):
        row = rows[tile]
        position = cursor[row]
        cursor[row] = position + 1
        tile_at[position] = tile
        block_at[position] = slots[cols[tile]]


def tables(rows, cols, total, groups=PPD, cost=0):
    count = rows.shape[0]
    return pl.pallas_call(
        tables_kernel,
        in_specs=[SMEM] * 2,
        out_specs=[SMEM] * 4,
        out_shape=[jax.ShapeDtypeStruct((size,), jnp.int32) for size in (groups + 1, count, count, total)],
        scratch_shapes=[pltpu.SMEM((groups,), jnp.int32)],
        cost_estimate=pl.CostEstimate(flops=cost, bytes_accessed=0, transcendentals=0) if cost else None,
        name="tables",
    )(rows, cols)


def window(ref, tile):
    depth = ref.shape[1]
    across = ref.shape[2] // depth
    if across == 1:
        return ref.at[tile]
    return ref.at[lax.div(tile, across), :, pl.ds(pl.multiple_of(lax.rem(tile, across) * depth, depth), depth)]


def sort_kernel(choices, tile_at, chosen, tiles_ref, *refs):
    parts, sems = refs[: len(refs) // 2], refs[len(refs) // 2 :]
    begin = {choice: 0 for choice in choices}
    for choice, part, sem in zip(choices, parts, sems):
        base = begin[choice]
        count = part.shape[0] * part.shape[2] // tiles_ref.shape[2]
        begin[choice] += count

        @pl.when(chosen[0] == choice)
        def _(part=part, sem=sem, base=base, count=count):
            @pl.loop(0, count)
            def _(number):
                pltpu.make_async_copy(tiles_ref.at[tile_at[base + number]], window(part, number), sem).start()

    for choice, part, sem in zip(choices, parts, sems):

        @pl.when(chosen[0] == choice)
        def _(part=part, sem=sem):
            pltpu.make_async_copy(part, part, sem).wait()


def sort_tiles(tile_at, chosen, tiles, choices, shapes):
    return pl.pallas_call(
        functools.partial(sort_kernel, choices),
        in_specs=[SMEM] * 2 + [ANY],
        out_specs=[VMEM] * len(shapes),
        out_shape=[jax.ShapeDtypeStruct(shape, tiles.dtype) for shape in shapes],
        scratch_shapes=[pltpu.SemaphoreType.DMA] * len(shapes),
        compiler_params=pltpu.CompilerParams(vmem_limit_bytes=16 * MIB),
        name="sort_tiles",
    )(tile_at, chosen, tiles)


def payload_kernel(at_end, tiles_ref, received, payload, sem):
    del received

    @pl.when(at_end[0] == 1)
    def _():
        copy = pltpu.make_async_copy(tiles_ref, payload, sem)
        copy.start()
        copy.wait()


def payload_of(at_end, tiles, received):
    return pl.pallas_call(
        payload_kernel,
        in_specs=[SMEM, ANY, ANY],
        out_specs=ANY,
        out_shape=jax.ShapeDtypeStruct(received.shape, received.dtype),
        input_output_aliases={2: 0},
        scratch_shapes=[pltpu.SemaphoreType.DMA],
        compiler_params=pltpu.CompilerParams(vmem_limit_bytes=4 * MIB),
        name="payload",
    )(at_end, tiles, received)


def add_row(sum_ref, begin, end, depth, tile_of, block_of):
    width = sum_ref.shape[1]

    @pl.loop(0, (end - begin + depth - 1) // depth)
    def _(turn):
        here = begin + turn * depth
        places = [jnp.minimum(here + part, end - 1) for part in range(depth)]
        left = [tile_of(places[0])]
        for part in range(1, depth):
            tile = tile_of(places[part])
            left.append(jnp.where(here + part < end, tile, jnp.zeros_like(tile)))
        left = jnp.concatenate(left, axis=1)
        for column in range(0, width, COLUMNS):
            window = pl.ds(column, COLUMNS)
            right = jnp.concatenate([block_of(place, window) for place in places], axis=0)
            sum_ref[:, window] += jnp.dot(left, right, preferred_element_type=jnp.float32)


def own_kernel(counts, group, fresh, starts, tile_at, block_at, own_slots, far_slots, firsts, tiles_ref, perm_ref, *refs):
    pieces = refs[: len(counts)]
    refs = refs[len(counts) :]
    if not fresh:
        sum_in, refs = refs[0], refs[2:]
    sum_out, flip_out, own_blocks, far_blocks, sums, own_list, far_list, own_sems, far_sems, row_sems = refs

    def fetch(slots, landing, sems, fetched):
        found = jnp.int32(0)
        for number, (piece, count) in enumerate(zip(pieces, counts)):

            def one(offset, found, piece=piece, number=number):
                slot = slots[firsts[number] + offset]

                @pl.when(slot >= 0)
                def _():
                    fetched[found] = slot
                    pltpu.make_async_copy(piece.at[offset], landing.at[slot], sems.at[slot]).start()

                return found + (slot >= 0).astype(jnp.int32)

            found = lax.fori_loop(0, count, one, found)
        return found

    far_found = fetch(far_slots, far_blocks, far_sems, far_list)
    own_found = fetch(own_slots, own_blocks, own_sems, own_list)
    if not fresh:
        for row in range(PPD):
            pltpu.make_async_copy(sum_in.at[row], sums.at[row], row_sems.at[row]).start()

    def arrived(landing, sems, slot):
        pltpu.make_async_copy(landing.at[slot], landing.at[slot], sems.at[slot]).wait()

    def flip_store(slot):
        return pltpu.make_async_copy(far_blocks.at[slot], flip_out.at[slot], far_sems.at[slot])

    @pl.loop(0, far_found)
    def _(number):
        slot = far_list[number]
        arrived(far_blocks, far_sems, slot)
        far_blocks[slot] = jnp.dot(
            far_blocks[slot], perm_ref[...], preferred_element_type=jnp.float32
        ).astype(jnp.bfloat16)
        flip_store(slot).start()

    @pl.loop(0, own_found)
    def _(number):
        arrived(own_blocks, own_sems, own_list[number])

    def store(row):
        return pltpu.make_async_copy(sums.at[row], sum_out.at[row], row_sems.at[row])

    @pl.loop(0, PPD)
    def _(row):
        if fresh:
            sums[row] = jnp.zeros(sums.shape[1:], jnp.float32)
        else:
            arrived(sums, row_sems, row)
        add_row(
            sums.at[row],
            starts[group + row],
            starts[group + row + 1],
            4 if fresh else 2,
            lambda place: tiles_ref[tile_at[place]],
            lambda place, window: own_blocks[block_at[place], :, window],
        )
        store(row).start()

    @pl.loop(0, far_found)
    def _(number):
        flip_store(far_list[number]).wait()

    @pl.loop(0, PPD)
    def _(row):
        store(row).wait()


def own_part(own_tables, far_slots, tiles, pieces, firsts, perm, group=0, earlier=()):
    starts, tile_at, block_at, own_slots = own_tables
    count, height, _ = tiles.shape
    depth, width = pieces[0].shape[1:]
    need = count // REUSE
    counts = [piece.shape[0] for piece in pieces]
    operands = 8 + len(pieces)
    return pl.pallas_call(
        functools.partial(own_kernel, counts, group, not earlier),
        in_specs=[SMEM] * 6 + [VMEM] * 2 + [ANY] * (len(pieces) + len(earlier)),
        out_specs=[ANY] * 2,
        out_shape=[
            jax.ShapeDtypeStruct((PPD, height, width), jnp.float32),
            jax.ShapeDtypeStruct((need, depth, width), jnp.bfloat16),
        ],
        input_output_aliases={operands: 0, operands + 1: 1} if earlier else {},
        scratch_shapes=[
            pltpu.VMEM((need, depth, width), jnp.bfloat16),
            pltpu.VMEM((need, depth, width), jnp.bfloat16),
            pltpu.VMEM((PPD, height, width), jnp.float32),
            pltpu.SMEM((need,), jnp.int32),
            pltpu.SMEM((need,), jnp.int32),
            pltpu.SemaphoreType.DMA((need,)),
            pltpu.SemaphoreType.DMA((need,)),
            pltpu.SemaphoreType.DMA((PPD,)),
        ],
        compiler_params=pltpu.CompilerParams(vmem_limit_bytes=56 * MIB),
        name="own_part",
    )(starts, tile_at, block_at, own_slots, far_slots, firsts, tiles, perm, *pieces, *earlier)


def far_kernel(base, segments, starts, block_at, chosen, *refs):
    tile_refs, refs = refs[: len(segments)], refs[len(segments) :]
    sum_in, flip_in = refs[:2]
    refs = refs[3:] if base else refs[2:]
    sum_out, result, tiles_ref, blocks, sums, rounded, tile_sem, block_sems, row_sems, out_sems = refs
    count = tiles_ref.shape[0]
    stop = base + count

    for source, (choice, begin) in zip(tile_refs, segments):
        held = source.shape[0] * source.shape[2] // tiles_ref.shape[2]
        low, high = max(begin, base), min(begin + held, stop)

        @pl.when(chosen[0] == choice)
        def _(source=source, begin=begin, low=low, high=high):
            if source.shape[2] == tiles_ref.shape[2]:
                here, there = source.at[pl.ds(low - begin, high - low)], tiles_ref.at[pl.ds(low - base, high - low)]
                pltpu.make_async_copy(here, there, tile_sem).start()
            else:

                @pl.loop(low, high)
                def _(place):
                    pltpu.make_async_copy(window(source, place - begin), tiles_ref.at[place - base], tile_sem).start()

    @pl.loop(0, count)
    def _(number):
        pltpu.make_async_copy(flip_in.at[block_at[base + number]], blocks.at[number], block_sems.at[number]).start()

    def each_row(action):
        @pl.loop(0, PPD)
        def _(row):
            first, last = starts[row], starts[row + 1]

            @pl.when(((last > base) if base else True) & ((last <= stop) | (first < stop)))
            def _():
                action(row, last <= stop)

    def load(row):
        return pltpu.make_async_copy(sum_in.at[row], sums.at[row], row_sems.at[row])

    def store(row):
        return pltpu.make_async_copy(rounded.at[row], result.at[row], out_sems.at[row])

    def keep(row):
        return pltpu.make_async_copy(sums.at[row], sum_out.at[row], out_sems.at[row])

    each_row(lambda row, complete: load(row).start())
    pltpu.make_async_copy(tiles_ref, tiles_ref, tile_sem).wait()


    def add(row, complete):
        begin, end = jnp.maximum(starts[row], base), jnp.minimum(starts[row + 1], stop)
        load(row).wait()

        @pl.loop(0, end - begin)
        def _(number):
            block = blocks.at[begin - base + number]
            pltpu.make_async_copy(block, block, block_sems.at[begin - base + number]).wait()

        add_row(
            sums.at[row],
            begin,
            end,
            4,
            lambda place: tiles_ref[place - base],
            lambda place, window: blocks[place - base, :, window],
        )

        @pl.when(complete)
        def _():
            rounded[row] = sums[row].astype(rounded.dtype)
            store(row).start()

        @pl.when(jnp.logical_not(complete))
        def _():
            keep(row).start()

    def finish(row, complete):
        pl.when(complete)(lambda: store(row).wait())
        pl.when(jnp.logical_not(complete))(lambda: keep(row).wait())

    each_row(add)
    each_row(finish)


def far_part(base, count, far_tables, chosen, sources, flipped, total, result=None):
    starts, _, block_at, _ = far_tables
    whole = total.shape
    given = [] if result is None else [result]
    held = [array.size // (whole[1] * flipped.shape[1]) for _, _, array in sources]
    used = [
        (source[:2], source[2])
        for source, size in zip(sources, held)
        if source[1] < base + count and source[1] + size > base
    ]
    operand = 3 + len(used)
    aliases = {operand: 0, operand + 2: 1} if given else {operand: 0}
    return pl.pallas_call(
        functools.partial(far_kernel, base, [segment for segment, _ in used]),
        in_specs=[SMEM] * 3 + [ANY] * (len(used) + 2 + len(given)),
        out_specs=[ANY] * 2,
        out_shape=[jax.ShapeDtypeStruct(whole, jnp.float32), jax.ShapeDtypeStruct(whole, jnp.bfloat16)],
        input_output_aliases=aliases,
        scratch_shapes=[
            pltpu.VMEM((count, whole[1], flipped.shape[1]), jnp.bfloat16),
            pltpu.VMEM((count,) + flipped.shape[1:], jnp.bfloat16),
            pltpu.VMEM(whole, jnp.float32),
            pltpu.VMEM(whole, jnp.bfloat16),
            pltpu.SemaphoreType.DMA,
            pltpu.SemaphoreType.DMA((count,)),
            pltpu.SemaphoreType.DMA((PPD,)),
            pltpu.SemaphoreType.DMA((PPD,)),
        ],
        compiler_params=pltpu.CompilerParams(vmem_limit_bytes=40 * MIB),
        name="far_part",
    )(starts, block_at, chosen, *[array for _, array in used], total, flipped, *given)


def together(*values):
    return lax.optimization_barrier(values)


def send(value, pairs):
    return lax.ppermute(value, "tile", pairs)


def flipped_bit(bit):
    return [(i, i ^ bit) for i in range(16)]


def staged_part(tiles, rows, cols, shard):
    local = shard.shape[0]
    block_total = 16 * local
    centre = [i for i in range(16) if i // 4 in (1, 2)]
    across = [(i, i ^ 12) for i in centre]
    from_ends = [(i, i ^ 8) for i in range(16) if i not in centre]
    from_centre = [(i, i ^ 8) for i in centre]
    around = [(i, i ^ 4) for i in centre] + from_ends
    other_z, other_y, other_core, opposite = (flipped_bit(bit) for bit in (4, 2, 1, 8))
    me = lax.axis_index("tile")
    z = me // 4
    in_centre = (z == 1) | (z == 2)
    at_end = 1 - in_centre.astype(jnp.int32).reshape(1)
    zs = [z, z ^ 1, jnp.where(z < 2, 2, 1), jnp.where(z < 2, 3, 0)]

    def owner(k, bits):
        return 4 * zs[k] + ((me & 3) ^ bits)

    def first_blocks(firsts):
        return jnp.stack(firsts).astype(jnp.int32)

    col_owner = cols // local
    late = (col_owner // 4 == zs[3]) | (col_owner == owner(2, 3))
    keys = rows + PPD * late.astype(jnp.int32)
    columns = jnp.arange(shard.shape[2], dtype=jnp.int32)

    near = send(shard, other_z)
    first = send(shard, across)
    notes = send(jnp.stack([rows, cols]), opposite)
    order = tables(rows, cols, block_total)[1]
    c_own = send(shard, other_core)
    y_own = send(shard, other_y)
    count = tiles.shape[0]
    step = shard.size // tiles[0].size
    sizes = tile_parts(count)
    shapes = [shard.shape] * 2 + [(size,) + tiles.shape[1:] for size in [count - 2 * step] + sizes]
    parts = sort_tiles(order, at_end, tiles, [1, 1, 1, 0, 0, 0], shapes)
    first, *parts = together(first, *parts)

    first = payload_of(at_end, parts[0], first)
    outer = send(first, around)
    near, c_own, y_own, keys, columns, *parts = together(near, c_own, y_own, keys, columns, *parts)
    second = send(near, across)
    y_near = send(near, other_y)
    c_near = send(near, other_core)
    own_tables = tables(keys, cols, block_total, 2 * PPD)
    far_tables = tables(notes[0], notes[1], block_total, cost=FAR_COST)
    perm = flip_matrix(columns)
    far_ends = [outer]
    first = jnp.where(in_centre, first, outer)
    second = payload_of(at_end, parts[1], second)
    outer = send(second, around)
    first, y_own, y_near, c_near, perm, *rest = together(
        first, y_own, y_near, c_near, perm, *parts[2:], *own_tables, *far_tables
    )
    parts, own_tables, far_tables = rest[:4], rest[4:8], rest[8:]
    y_first = send(first, other_y)
    c_first = send(first, other_core)
    c_y_own = send(y_own, other_core)
    c_y_near = send(y_near, other_core)
    tiles_last, c_first = together(parts[0], c_first)
    far_ends += [outer, send(tiles_last, from_ends)]
    halves = (slice(0, local // 2), slice(local // 2, None))
    second = [jnp.where(in_centre, second[half], outer[half]) for half in halves]
    *second, y_first, c_first, c_y_own, c_y_near = together(*second, y_first, c_first, c_y_own, c_y_near)

    far_centre = [send(parts[1], from_centre)]
    y_second = [send(half, other_y) for half in second]
    pieces = [shard, c_own, near, c_near, first, c_first, y_own, c_y_own, y_near, c_y_near, y_first]
    firsts = [owner(k, y + core) * local for y in (0, 2) for k in range(3) for core in (0, 1)][:11]
    early = own_part(own_tables, far_tables[3], tiles, pieces, first_blocks(firsts), perm)
    y_second[0], y_second[1], second[0], second[1], y_first, total, flipped, *parts = together(
        *y_second, *second, y_first, *early, *parts[2:]
    )
    far_centre += [send(part, from_centre) for part in parts]
    *y_second, far_ends[2] = together(*y_second, far_ends[2])

    c_y_first = send(y_first, other_core)
    c_second = [send(half, other_core) for half in second]
    c_y_second = [send(half, other_core) for half in y_second]
    pieces = [c_y_first, *second, *c_second, *y_second, *c_y_second]
    firsts = [owner(2, 3) * local] + [owner(3, bits) * local + half for bits in range(4) for half in (0, local // 2)]
    total, flipped = own_part(own_tables, far_tables[3], tiles, pieces, first_blocks(firsts), perm, PPD, (total, flipped))

    sources = [(0, step * number, array) for number, array in enumerate(far_ends)]
    sources += [(1, sum(sizes[:number]), array) for number, array in enumerate(far_centre)]
    return far_products(far_tables, at_end, sources, sizes, flipped, total)


def tile_parts(count):
    sizes = [count * share // 48 for share in SHARES]
    return sizes + [count - sum(sizes)]


def far_products(far_tables, chosen, sources, sizes, flipped, total):
    base, result = 0, None
    for size in sizes:
        total, result = far_part(base, size, far_tables, chosen, sources, flipped, total, result)
        base += size
    return result


def per_device(t2_tiles, t2_row, t2_col, integrals):
    peers = lax.axis_size("tile")
    if peers == 16:
        return staged_part(t2_tiles, t2_row, t2_col, integrals)
    block_total = peers * integrals.shape[0]
    opposite = [(source, (source + peers // 2) % peers) for source in range(peers)]
    own_tables = tables(t2_row, t2_col, block_total)
    sizes = tile_parts(t2_tiles.shape[0])
    zero = jnp.zeros((1,), jnp.int32)
    parts = sort_tiles(own_tables[1], zero, t2_tiles, [0] * 3, [(size,) + t2_tiles.shape[1:] for size in sizes])
    notes = send(jnp.stack([t2_row, t2_col]), opposite)
    sources = [(0, sum(sizes[:number]), send(part, opposite)) for number, part in enumerate(parts)]
    blocks = lax.all_gather(integrals, "tile", axis=0, tiled=True)
    far_tables = tables(notes[0], notes[1], block_total)
    columns = jnp.arange(integrals.shape[2], dtype=jnp.int32)
    total, flipped = own_part(own_tables, far_tables[3], t2_tiles, [blocks], zero, flip_matrix(columns))
    return far_products(far_tables, zero, sources, sizes, flipped, total)


def solution(mesh):
    in_specs = (
        P(("groups", "tile"), None, None),
        P(("groups", "tile")),
        P(("groups", "tile")),
        P(("groups", "tile"), None, None),
    )
    out_specs = P(("groups", "tile"), None, None)
    return jax.shard_map(
        per_device, mesh=mesh, in_specs=in_specs, out_specs=out_specs, check_vma=False
    )
```

```python
import functools

import jax
import jax.numpy as jnp
from jax import lax
from jax.experimental import pallas as pl
from jax.experimental.pallas import tpu as pltpu
from jax.sharding import PartitionSpec as P

W = 32
PPD = 16
REUSE = 3
SHARES = (30, 9, 6)
COLUMNS = 256
MIB = 1024 * 1024
FAR_COST = 4 * 10**9
SMEM = pl.BlockSpec(memory_space=pltpu.SMEM)
VMEM = pl.BlockSpec(memory_space=pltpu.VMEM)
ANY = pl.BlockSpec(memory_space=pl.ANY)


def flip_matrix(columns):
    source = (columns % W) * W + columns // W
    return (columns[:, None] == source[None, :]).astype(jnp.bfloat16)


class View:
    def __init__(self, ref, offset):
        self.ref, self.offset = ref, offset

    def __getitem__(self, index):
        return self.ref[self.offset + index]

    def __setitem__(self, index, value):
        self.ref[self.offset + index] = value


def table_views(table, count, groups):
    places = [0, groups + 1, groups + 1 + count, groups + 1 + 2 * count]
    return [View(table, place) for place in places]


def tables_kernel(rows, cols, table, cursor):
    count, groups = rows.shape[0], cursor.shape[0]
    total = table.shape[0] - (groups + 1 + 2 * count)
    starts, tile_at, block_at, slots = table_views(table, count, groups)

    @pl.loop(0, total)
    def _(block):
        slots[block] = 0

    for row in range(groups):
        cursor[row] = 0

    @pl.loop(0, count)
    def _(tile):
        cursor[rows[tile]] += 1
        slots[cols[tile]] = 1

    place = jnp.int32(0)
    for row in range(groups):
        size = cursor[row]
        starts[row] = place
        cursor[row] = place
        place += size
    starts[groups] = place

    def number(block, used):
        named = slots[block]
        slots[block] = jnp.where(named > 0, used, -1)
        return used + named

    lax.fori_loop(0, total, number, jnp.int32(0))

    @pl.loop(0, count)
    def _(tile):
        row = rows[tile]
        position = cursor[row]
        cursor[row] = position + 1
        tile_at[position] = tile
        block_at[position] = slots[cols[tile]]


def tables(rows, cols, total, groups=PPD, cost=0):
    count = rows.shape[0]
    return pl.pallas_call(
        tables_kernel,
        in_specs=[SMEM] * 2,
        out_specs=SMEM,
        out_shape=jax.ShapeDtypeStruct((groups + 1 + 2 * count + total,), jnp.int32),
        scratch_shapes=[pltpu.SMEM((groups,), jnp.int32)],
        cost_estimate=pl.CostEstimate(flops=cost, bytes_accessed=0, transcendentals=0) if cost else None,
        name="tables",
    )(rows, cols)


def window(ref, tile):
    depth = ref.shape[1]
    across = ref.shape[2] // depth
    if across == 1:
        return ref.at[tile]
    return ref.at[lax.div(tile, across), :, pl.ds(pl.multiple_of(lax.rem(tile, across) * depth, depth), depth)]


def sort_kernel(choices, table, chosen, tiles_ref, *refs):
    tile_at = table_views(table, tiles_ref.shape[0], PPD)[1]
    parts, sems = refs[: len(refs) // 2], refs[len(refs) // 2 :]
    begin = {choice: 0 for choice in choices}
    for choice, part, sem in zip(choices, parts, sems):
        base = begin[choice]
        count = part.shape[0] * part.shape[2] // tiles_ref.shape[2]
        begin[choice] += count

        @pl.when(chosen[0] == choice)
        def _(part=part, sem=sem, base=base, count=count):
            @pl.loop(0, count)
            def _(number):
                pltpu.make_async_copy(tiles_ref.at[tile_at[base + number]], window(part, number), sem).start()

    for choice, part, sem in zip(choices, parts, sems):

        @pl.when(chosen[0] == choice)
        def _(part=part, sem=sem):
            pltpu.make_async_copy(part, part, sem).wait()


def sort_tiles(table, chosen, tiles, choices, shapes):
    return pl.pallas_call(
        functools.partial(sort_kernel, choices),
        in_specs=[SMEM] * 2 + [ANY],
        out_specs=[VMEM] * len(shapes),
        out_shape=[jax.ShapeDtypeStruct(shape, tiles.dtype) for shape in shapes],
        scratch_shapes=[pltpu.SemaphoreType.DMA] * len(shapes),
        compiler_params=pltpu.CompilerParams(vmem_limit_bytes=16 * MIB),
        name="sort_tiles",
    )(table, chosen, tiles)


def payload_kernel(at_end, tiles_ref, received, payload, sem):
    del received

    @pl.when(at_end[0] == 1)
    def _():
        copy = pltpu.make_async_copy(tiles_ref, payload, sem)
        copy.start()
        copy.wait()


def payload_of(at_end, tiles, received):
    return pl.pallas_call(
        payload_kernel,
        in_specs=[SMEM, ANY, ANY],
        out_specs=ANY,
        out_shape=jax.ShapeDtypeStruct(received.shape, received.dtype),
        input_output_aliases={2: 0},
        scratch_shapes=[pltpu.SemaphoreType.DMA],
        compiler_params=pltpu.CompilerParams(vmem_limit_bytes=4 * MIB),
        name="payload",
    )(at_end, tiles, received)


def add_row(sum_ref, begin, end, depth, tile_of, block_of):
    width = sum_ref.shape[1]

    @pl.loop(0, (end - begin + depth - 1) // depth)
    def _(turn):
        here = begin + turn * depth
        places = [jnp.minimum(here + part, end - 1) for part in range(depth)]
        left = [tile_of(places[0])]
        for part in range(1, depth):
            tile = tile_of(places[part])
            left.append(jnp.where(here + part < end, tile, jnp.zeros_like(tile)))
        left = jnp.concatenate(left, axis=1)
        for column in range(0, width, COLUMNS):
            window = pl.ds(column, COLUMNS)
            right = jnp.concatenate([block_of(place, window) for place in places], axis=0)
            sum_ref[:, window] += jnp.dot(left, right, preferred_element_type=jnp.float32)


def own_kernel(counts, groups, group, fresh, own_table, far_table, firsts, tiles_ref, perm_ref, *refs):
    starts, tile_at, block_at, own_slots = table_views(own_table, tiles_ref.shape[0], groups)
    far_slots = table_views(far_table, tiles_ref.shape[0], PPD)[3]
    pieces = refs[: len(counts)]
    refs = refs[len(counts) :]
    if not fresh:
        sum_in, refs = refs[0], refs[2:]
    sum_out, flip_out, own_blocks, far_blocks, sums, own_list, far_list, own_sems, far_sems, row_sems = refs

    def fetch(slots, landing, sems, fetched):
        found = jnp.int32(0)
        for number, (piece, count) in enumerate(zip(pieces, counts)):

            def one(offset, found, piece=piece, number=number):
                slot = slots[firsts[number] + offset]

                @pl.when(slot >= 0)
                def _():
                    fetched[found] = slot
                    pltpu.make_async_copy(piece.at[offset], landing.at[slot], sems.at[slot]).start()

                return found + (slot >= 0).astype(jnp.int32)

            found = lax.fori_loop(0, count, one, found)
        return found

    far_found = fetch(far_slots, far_blocks, far_sems, far_list)
    own_found = fetch(own_slots, own_blocks, own_sems, own_list)
    if not fresh:
        for row in range(PPD):
            pltpu.make_async_copy(sum_in.at[row], sums.at[row], row_sems.at[row]).start()

    def arrived(landing, sems, slot):
        pltpu.make_async_copy(landing.at[slot], landing.at[slot], sems.at[slot]).wait()

    def flip_store(slot):
        return pltpu.make_async_copy(far_blocks.at[slot], flip_out.at[slot], far_sems.at[slot])

    @pl.loop(0, far_found)
    def _(number):
        slot = far_list[number]
        arrived(far_blocks, far_sems, slot)
        far_blocks[slot] = jnp.dot(
            far_blocks[slot], perm_ref[...], preferred_element_type=jnp.float32
        ).astype(jnp.bfloat16)
        flip_store(slot).start()

    @pl.loop(0, own_found)
    def _(number):
        arrived(own_blocks, own_sems, own_list[number])

    def store(row):
        return pltpu.make_async_copy(sums.at[row], sum_out.at[row], row_sems.at[row])

    @pl.loop(0, PPD)
    def _(row):
        if fresh:
            sums[row] = jnp.zeros(sums.shape[1:], jnp.float32)
        else:
            arrived(sums, row_sems, row)
        add_row(
            sums.at[row],
            starts[group + row],
            starts[group + row + 1],
            4 if fresh else 2,
            lambda place: tiles_ref[tile_at[place]],
            lambda place, window: own_blocks[block_at[place], :, window],
        )
        store(row).start()

    @pl.loop(0, far_found)
    def _(number):
        flip_store(far_list[number]).wait()

    @pl.loop(0, PPD)
    def _(row):
        store(row).wait()


def own_part(own_table, far_table, tiles, pieces, firsts, perm, groups=PPD, group=0, earlier=()):
    count, height, _ = tiles.shape
    depth, width = pieces[0].shape[1:]
    need = count // REUSE
    counts = [piece.shape[0] for piece in pieces]
    operands = 5 + len(pieces)
    return pl.pallas_call(
        functools.partial(own_kernel, counts, groups, group, not earlier),
        in_specs=[SMEM] * 3 + [VMEM] * 2 + [ANY] * (len(pieces) + len(earlier)),
        out_specs=[ANY] * 2,
        out_shape=[
            jax.ShapeDtypeStruct((PPD, height, width), jnp.float32),
            jax.ShapeDtypeStruct((need, depth, width), jnp.bfloat16),
        ],
        input_output_aliases={operands: 0, operands + 1: 1} if earlier else {},
        scratch_shapes=[
            pltpu.VMEM((need, depth, width), jnp.bfloat16),
            pltpu.VMEM((need, depth, width), jnp.bfloat16),
            pltpu.VMEM((PPD, height, width), jnp.float32),
            pltpu.SMEM((need,), jnp.int32),
            pltpu.SMEM((need,), jnp.int32),
            pltpu.SemaphoreType.DMA((need,)),
            pltpu.SemaphoreType.DMA((need,)),
            pltpu.SemaphoreType.DMA((PPD,)),
        ],
        compiler_params=pltpu.CompilerParams(vmem_limit_bytes=56 * MIB),
        name="own_part",
    )(own_table, far_table, firsts, tiles, perm, *pieces, *earlier)


def far_kernel(base, total_count, segments, table, chosen, *refs):
    starts, _, block_at, _ = table_views(table, total_count, PPD)
    tile_refs, refs = refs[: len(segments)], refs[len(segments) :]
    sum_in, flip_in = refs[:2]
    refs = refs[3:] if base else refs[2:]
    sum_out, result, tiles_ref, blocks, sums, rounded, tile_sem, block_sems, row_sems, out_sems = refs
    count = tiles_ref.shape[0]
    stop = base + count

    for source, (choice, begin) in zip(tile_refs, segments):
        held = source.shape[0] * source.shape[2] // tiles_ref.shape[2]
        low, high = max(begin, base), min(begin + held, stop)

        @pl.when(chosen[0] == choice)
        def _(source=source, begin=begin, low=low, high=high):
            if source.shape[2] == tiles_ref.shape[2]:
                here, there = source.at[pl.ds(low - begin, high - low)], tiles_ref.at[pl.ds(low - base, high - low)]
                pltpu.make_async_copy(here, there, tile_sem).start()
            else:

                @pl.loop(low, high)
                def _(place):
                    pltpu.make_async_copy(window(source, place - begin), tiles_ref.at[place - base], tile_sem).start()

    @pl.loop(0, count)
    def _(number):
        pltpu.make_async_copy(flip_in.at[block_at[base + number]], blocks.at[number], block_sems.at[number]).start()

    def each_row(action):
        @pl.loop(0, PPD)
        def _(row):
            first, last = starts[row], starts[row + 1]

            @pl.when(((last > base) if base else True) & ((last <= stop) | (first < stop)))
            def _():
                action(row, last <= stop)

    def load(row):
        return pltpu.make_async_copy(sum_in.at[row], sums.at[row], row_sems.at[row])

    def store(row):
        return pltpu.make_async_copy(rounded.at[row], result.at[row], out_sems.at[row])

    def keep(row):
        return pltpu.make_async_copy(sums.at[row], sum_out.at[row], out_sems.at[row])

    each_row(lambda row, complete: load(row).start())
    pltpu.make_async_copy(tiles_ref, tiles_ref, tile_sem).wait()


    def add(row, complete):
        begin, end = jnp.maximum(starts[row], base), jnp.minimum(starts[row + 1], stop)
        load(row).wait()

        @pl.loop(0, end - begin)
        def _(number):
            block = blocks.at[begin - base + number]
            pltpu.make_async_copy(block, block, block_sems.at[begin - base + number]).wait()

        add_row(
            sums.at[row],
            begin,
            end,
            4,
            lambda place: tiles_ref[place - base],
            lambda place, window: blocks[place - base, :, window],
        )

        @pl.when(complete)
        def _():
            rounded[row] = sums[row].astype(rounded.dtype)
            store(row).start()

        @pl.when(jnp.logical_not(complete))
        def _():
            keep(row).start()

    def finish(row, complete):
        pl.when(complete)(lambda: store(row).wait())
        pl.when(jnp.logical_not(complete))(lambda: keep(row).wait())

    each_row(add)
    each_row(finish)


def far_part(base, count, total_count, far_table, chosen, sources, flipped, total, result=None):
    whole = total.shape
    given = [] if result is None else [result]
    held = [array.size // (whole[1] * flipped.shape[1]) for _, _, array in sources]
    used = [
        (source[:2], source[2])
        for source, size in zip(sources, held)
        if source[1] < base + count and source[1] + size > base
    ]
    operand = 2 + len(used)
    aliases = {operand: 0, operand + 2: 1} if given else {operand: 0}
    return pl.pallas_call(
        functools.partial(far_kernel, base, total_count, [segment for segment, _ in used]),
        in_specs=[SMEM] * 2 + [ANY] * (len(used) + 2 + len(given)),
        out_specs=[ANY] * 2,
        out_shape=[jax.ShapeDtypeStruct(whole, jnp.float32), jax.ShapeDtypeStruct(whole, jnp.bfloat16)],
        input_output_aliases=aliases,
        scratch_shapes=[
            pltpu.VMEM((count, whole[1], flipped.shape[1]), jnp.bfloat16),
            pltpu.VMEM((count,) + flipped.shape[1:], jnp.bfloat16),
            pltpu.VMEM(whole, jnp.float32),
            pltpu.VMEM(whole, jnp.bfloat16),
            pltpu.SemaphoreType.DMA,
            pltpu.SemaphoreType.DMA((count,)),
            pltpu.SemaphoreType.DMA((PPD,)),
            pltpu.SemaphoreType.DMA((PPD,)),
        ],
        compiler_params=pltpu.CompilerParams(vmem_limit_bytes=40 * MIB),
        name="far_part",
    )(far_table, chosen, *[array for _, array in used], total, flipped, *given)


def together(*values):
    return lax.optimization_barrier(values)


def send(value, pairs):
    return lax.ppermute(value, "tile", pairs)


def flipped_bit(bit):
    return [(i, i ^ bit) for i in range(16)]


def staged_part(tiles, rows, cols, shard):
    local = shard.shape[0]
    block_total = 16 * local
    centre = [i for i in range(16) if i // 4 in (1, 2)]
    across = [(i, i ^ 12) for i in centre]
    from_ends = [(i, i ^ 8) for i in range(16) if i not in centre]
    from_centre = [(i, i ^ 8) for i in centre]
    around = [(i, i ^ 4) for i in centre] + from_ends
    other_z, other_y, other_core, opposite = (flipped_bit(bit) for bit in (4, 2, 1, 8))
    me = lax.axis_index("tile")
    z = me // 4
    in_centre = (z == 1) | (z == 2)
    at_end = 1 - in_centre.astype(jnp.int32).reshape(1)
    zs = [z, z ^ 1, jnp.where(z < 2, 2, 1), jnp.where(z < 2, 3, 0)]

    def owner(k, bits):
        return 4 * zs[k] + ((me & 3) ^ bits)

    def first_blocks(firsts):
        return jnp.stack(firsts).astype(jnp.int32)

    col_owner = cols // local
    late = (col_owner // 4 == zs[3]) | (col_owner == owner(2, 3))
    keys = rows + PPD * late.astype(jnp.int32)
    columns = jnp.arange(shard.shape[2], dtype=jnp.int32)

    near = send(shard, other_z)
    first = send(shard, across)
    notes = send(jnp.stack([rows, cols]), opposite)
    order = tables(rows, cols, block_total)
    c_own = send(shard, other_core)
    y_own = send(shard, other_y)
    count = tiles.shape[0]
    step = shard.size // tiles[0].size
    sizes = tile_parts(count)
    shapes = [shard.shape] * 2 + [(size,) + tiles.shape[1:] for size in [count - 2 * step] + sizes]
    parts = sort_tiles(order, at_end, tiles, [1] * 3 + [0] * len(sizes), shapes)
    first, *parts = together(first, *parts)

    first = payload_of(at_end, parts[0], first)
    outer = send(first, around)
    near, c_own, y_own, keys, columns, *parts = together(near, c_own, y_own, keys, columns, *parts)
    second = send(near, across)
    y_near = send(near, other_y)
    c_near = send(near, other_core)
    c_y_own = send(y_own, other_core)
    own_table = tables(keys, cols, block_total, 2 * PPD)
    far_table = tables(notes[0], notes[1], block_total, cost=FAR_COST)
    perm = flip_matrix(columns)
    far_ends = [outer]
    first = jnp.where(in_centre, first, outer)
    second = payload_of(at_end, parts[1], second)
    outer = send(second, around)
    first, c_y_own, y_near, c_near, perm, *rest = together(
        first, c_y_own, y_near, c_near, perm, own_table, far_table, *parts[2:]
    )
    own_table, far_table, *parts = rest
    y_first = send(first, other_y)
    c_first = send(first, other_core)
    c_y_near = send(y_near, other_core)
    tiles_last, c_first = together(parts[0], c_first)
    far_ends += [outer, send(tiles_last, from_ends)]
    halves = (slice(0, local // 2), slice(local // 2, None))
    second = [jnp.where(in_centre, second[half], outer[half]) for half in halves]
    *second, y_first, c_first, c_y_near = together(*second, y_first, c_first, c_y_near)

    far_centre = [send(parts[1], from_centre)]
    y_second = [send(half, other_y) for half in second]
    pieces = [shard, c_own, near, c_near, first, c_first, y_own, c_y_own, y_near, c_y_near, y_first]
    firsts = [owner(k, y + core) * local for y in (0, 2) for k in range(3) for core in (0, 1)][:11]
    early = own_part(own_table, far_table, tiles, pieces, first_blocks(firsts), perm, 2 * PPD)
    y_second[0], y_second[1], second[0], second[1], y_first, total, flipped, *parts = together(
        *y_second, *second, y_first, *early, *parts[2:]
    )
    far_centre += [send(part, from_centre) for part in parts]
    *y_second, far_ends[2] = together(*y_second, far_ends[2])

    c_y_first = send(y_first, other_core)
    c_second = [send(half, other_core) for half in second]
    c_y_second = [send(half, other_core) for half in y_second]
    pieces = [c_y_first, *second, *c_second, *y_second, *c_y_second]
    firsts = [owner(2, 3) * local] + [owner(3, bits) * local + half for bits in range(4) for half in (0, local // 2)]
    earlier = (total, flipped)
    total, flipped = own_part(own_table, far_table, tiles, pieces, first_blocks(firsts), perm, 2 * PPD, PPD, earlier)

    sources = [(0, step * number, array) for number, array in enumerate(far_ends)]
    sources += [(1, sum(sizes[:number]), array) for number, array in enumerate(far_centre)]
    return far_products(far_table, at_end, sources, sizes, flipped, total)


def tile_parts(count):
    sizes = [count * share // 48 for share in SHARES]
    return sizes + [count - sum(sizes)]


def far_products(far_table, chosen, sources, sizes, flipped, total):
    base, result = 0, None
    for size in sizes:
        total, result = far_part(base, size, sum(sizes), far_table, chosen, sources, flipped, total, result)
        base += size
    return result


def per_device(t2_tiles, t2_row, t2_col, integrals):
    peers = lax.axis_size("tile")
    if peers == 16:
        return staged_part(t2_tiles, t2_row, t2_col, integrals)
    block_total = peers * integrals.shape[0]
    opposite = [(source, (source + peers // 2) % peers) for source in range(peers)]
    own_table = tables(t2_row, t2_col, block_total)
    sizes = tile_parts(t2_tiles.shape[0])
    zero = jnp.zeros((1,), jnp.int32)
    parts = sort_tiles(own_table, zero, t2_tiles, [0] * len(sizes), [(size,) + t2_tiles.shape[1:] for size in sizes])
    notes = send(jnp.stack([t2_row, t2_col]), opposite)
    sources = [(0, sum(sizes[:number]), send(part, opposite)) for number, part in enumerate(parts)]
    blocks = lax.all_gather(integrals, "tile", axis=0, tiled=True)
    far_table = tables(notes[0], notes[1], block_total)
    columns = jnp.arange(integrals.shape[2], dtype=jnp.int32)
    total, flipped = own_part(own_table, far_table, t2_tiles, [blocks], zero, flip_matrix(columns))
    return far_products(far_table, zero, sources, sizes, flipped, total)


def solution(mesh):
    in_specs = (
        P(("groups", "tile"), None, None),
        P(("groups", "tile")),
        P(("groups", "tile")),
        P(("groups", "tile"), None, None),
    )
    out_specs = P(("groups", "tile"), None, None)
    return jax.shard_map(
        per_device, mesh=mesh, in_specs=in_specs, out_specs=out_specs, check_vma=False
    )
```

```python
import functools

import jax
import jax.numpy as jnp
from jax import lax
from jax.experimental import pallas as pl
from jax.experimental.pallas import tpu as pltpu
from jax.sharding import PartitionSpec as P

W = 32
PPD = 16
REUSE = 3
SHARES = (30, 9, 6)
COLUMNS = 256
MIB = 1024 * 1024
FAR_COST = 4 * 10**9
SMEM = pl.BlockSpec(memory_space=pltpu.SMEM)
VMEM = pl.BlockSpec(memory_space=pltpu.VMEM)
ANY = pl.BlockSpec(memory_space=pl.ANY)


def flip_matrix(columns):
    source = (columns % W) * W + columns // W
    return (columns[:, None] == source[None, :]).astype(jnp.bfloat16)


class View:
    def __init__(self, ref, offset):
        self.ref, self.offset = ref, offset

    def __getitem__(self, index):
        return self.ref[self.offset + index]

    def __setitem__(self, index, value):
        self.ref[self.offset + index] = value


def table_views(table, count, groups):
    places = [0, groups + 1, groups + 1 + count, groups + 1 + 2 * count]
    return [View(table, place) for place in places]


def tables_kernel(rows, cols, table, cursor):
    count, groups = rows.shape[0], cursor.shape[0]
    total = table.shape[0] - (groups + 1 + 2 * count)
    starts, tile_at, block_at, slots = table_views(table, count, groups)

    @pl.loop(0, total)
    def _(block):
        slots[block] = 0

    for row in range(groups):
        cursor[row] = 0

    @pl.loop(0, count)
    def _(tile):
        cursor[rows[tile]] += 1
        slots[cols[tile]] = 1

    place = jnp.int32(0)
    for row in range(groups):
        size = cursor[row]
        starts[row] = place
        cursor[row] = place
        place += size
    starts[groups] = place

    def number(block, used):
        named = slots[block]
        slots[block] = jnp.where(named > 0, used, -1)
        return used + named

    lax.fori_loop(0, total, number, jnp.int32(0))

    @pl.loop(0, count)
    def _(tile):
        row = rows[tile]
        position = cursor[row]
        cursor[row] = position + 1
        tile_at[position] = tile
        block_at[position] = slots[cols[tile]]


def tables(rows, cols, total, groups=PPD, cost=0):
    count = rows.shape[0]
    return pl.pallas_call(
        tables_kernel,
        in_specs=[SMEM] * 2,
        out_specs=SMEM,
        out_shape=jax.ShapeDtypeStruct((groups + 1 + 2 * count + total,), jnp.int32),
        scratch_shapes=[pltpu.SMEM((groups,), jnp.int32)],
        cost_estimate=pl.CostEstimate(flops=cost, bytes_accessed=0, transcendentals=0) if cost else None,
        name="tables",
    )(rows, cols)


def window(ref, tile):
    depth = ref.shape[1]
    across = ref.shape[2] // depth
    if across == 1:
        return ref.at[tile]
    return ref.at[lax.div(tile, across), :, pl.ds(pl.multiple_of(lax.rem(tile, across) * depth, depth), depth)]


def sort_kernel(choices, table, chosen, tiles_ref, *refs):
    tile_at = table_views(table, tiles_ref.shape[0], PPD)[1]
    parts, sems = refs[: len(refs) // 2], refs[len(refs) // 2 :]
    begin = {choice: 0 for choice in choices}
    for choice, part, sem in zip(choices, parts, sems):
        base = begin[choice]
        count = part.shape[0] * part.shape[2] // tiles_ref.shape[2]
        begin[choice] += count

        @pl.when(chosen[0] == choice)
        def _(part=part, sem=sem, base=base, count=count):
            @pl.loop(0, count)
            def _(number):
                pltpu.make_async_copy(tiles_ref.at[tile_at[base + number]], window(part, number), sem).start()

    for choice, part, sem in zip(choices, parts, sems):

        @pl.when(chosen[0] == choice)
        def _(part=part, sem=sem):
            pltpu.make_async_copy(part, part, sem).wait()


def sort_tiles(table, chosen, tiles, choices, shapes):
    return pl.pallas_call(
        functools.partial(sort_kernel, choices),
        in_specs=[SMEM] * 2 + [ANY],
        out_specs=[VMEM] * len(shapes),
        out_shape=[jax.ShapeDtypeStruct(shape, tiles.dtype) for shape in shapes],
        scratch_shapes=[pltpu.SemaphoreType.DMA] * len(shapes),
        compiler_params=pltpu.CompilerParams(vmem_limit_bytes=16 * MIB),
        name="sort_tiles",
    )(table, chosen, tiles)


def payload_kernel(at_end, tiles_ref, received, payload, sem):
    del received

    @pl.when(at_end[0] == 1)
    def _():
        copy = pltpu.make_async_copy(tiles_ref, payload, sem)
        copy.start()
        copy.wait()


def payload_of(at_end, tiles, received):
    return pl.pallas_call(
        payload_kernel,
        in_specs=[SMEM, ANY, ANY],
        out_specs=ANY,
        out_shape=jax.ShapeDtypeStruct(received.shape, received.dtype),
        input_output_aliases={2: 0},
        scratch_shapes=[pltpu.SemaphoreType.DMA],
        compiler_params=pltpu.CompilerParams(vmem_limit_bytes=4 * MIB),
        name="payload",
    )(at_end, tiles, received)


def add_row(sum_ref, begin, end, depth, tile_of, block_of):
    width = sum_ref.shape[1]

    @pl.loop(0, (end - begin + depth - 1) // depth)
    def _(turn):
        here = begin + turn * depth
        places = [jnp.minimum(here + part, end - 1) for part in range(depth)]
        left = [tile_of(places[0])]
        for part in range(1, depth):
            tile = tile_of(places[part])
            left.append(jnp.where(here + part < end, tile, jnp.zeros_like(tile)))
        left = jnp.concatenate(left, axis=1)
        for column in range(0, width, COLUMNS):
            window = pl.ds(column, COLUMNS)
            right = jnp.concatenate([block_of(place, window) for place in places], axis=0)
            sum_ref[:, window] += jnp.dot(left, right, preferred_element_type=jnp.float32)


def own_kernel(counts, groups, group, fresh, own_table, far_table, firsts, tiles_ref, perm_ref, *refs):
    starts, tile_at, block_at, own_slots = table_views(own_table, tiles_ref.shape[0], groups)
    far_slots = table_views(far_table, tiles_ref.shape[0], PPD)[3]
    pieces = refs[: len(counts)]
    refs = refs[len(counts) :]
    if not fresh:
        sum_in, refs = refs[0], refs[2:]
    sum_out, flip_out, own_blocks, far_blocks, sums, own_list, far_list, own_sems, far_sems, row_sems = refs

    def fetch(slots, landing, sems, fetched):
        found = jnp.int32(0)
        for number, (piece, count) in enumerate(zip(pieces, counts)):

            def one(offset, found, piece=piece, number=number):
                slot = slots[firsts[number] + offset]

                @pl.when(slot >= 0)
                def _():
                    fetched[found] = slot
                    pltpu.make_async_copy(piece.at[offset], landing.at[slot], sems.at[slot]).start()

                return found + (slot >= 0).astype(jnp.int32)

            found = lax.fori_loop(0, count, one, found)
        return found

    far_found = fetch(far_slots, far_blocks, far_sems, far_list)
    own_found = fetch(own_slots, own_blocks, own_sems, own_list)
    if not fresh:
        for row in range(PPD):
            pltpu.make_async_copy(sum_in.at[row], sums.at[row], row_sems.at[row]).start()

    def arrived(landing, sems, slot):
        pltpu.make_async_copy(landing.at[slot], landing.at[slot], sems.at[slot]).wait()

    def flip_store(slot):
        return pltpu.make_async_copy(far_blocks.at[slot], flip_out.at[slot], far_sems.at[slot])

    @pl.loop(0, far_found)
    def _(number):
        slot = far_list[number]
        arrived(far_blocks, far_sems, slot)
        far_blocks[slot] = jnp.dot(
            far_blocks[slot], perm_ref[...], preferred_element_type=jnp.float32
        ).astype(jnp.bfloat16)
        flip_store(slot).start()

    @pl.loop(0, own_found)
    def _(number):
        arrived(own_blocks, own_sems, own_list[number])

    def store(row):
        return pltpu.make_async_copy(sums.at[row], sum_out.at[row], row_sems.at[row])

    @pl.loop(0, PPD)
    def _(row):
        if fresh:
            sums[row] = jnp.zeros(sums.shape[1:], jnp.float32)
        else:
            arrived(sums, row_sems, row)
        add_row(
            sums.at[row],
            starts[group + row],
            starts[group + row + 1],
            4 if fresh else 2,
            lambda place: tiles_ref[tile_at[place]],
            lambda place, window: own_blocks[block_at[place], :, window],
        )
        store(row).start()

    @pl.loop(0, far_found)
    def _(number):
        flip_store(far_list[number]).wait()

    @pl.loop(0, PPD)
    def _(row):
        store(row).wait()


def own_part(own_table, far_table, tiles, pieces, firsts, perm, groups=PPD, group=0, earlier=()):
    count, height, _ = tiles.shape
    depth, width = pieces[0].shape[1:]
    need = count // REUSE
    counts = [piece.shape[0] for piece in pieces]
    operands = 5 + len(pieces)
    return pl.pallas_call(
        functools.partial(own_kernel, counts, groups, group, not earlier),
        in_specs=[SMEM] * 3 + [VMEM] * 2 + [ANY] * (len(pieces) + len(earlier)),
        out_specs=[ANY] * 2,
        out_shape=[
            jax.ShapeDtypeStruct((PPD, height, width), jnp.float32),
            jax.ShapeDtypeStruct((need, depth, width), jnp.bfloat16),
        ],
        input_output_aliases={operands: 0, operands + 1: 1} if earlier else {},
        scratch_shapes=[
            pltpu.VMEM((need, depth, width), jnp.bfloat16),
            pltpu.VMEM((need, depth, width), jnp.bfloat16),
            pltpu.VMEM((PPD, height, width), jnp.float32),
            pltpu.SMEM((need,), jnp.int32),
            pltpu.SMEM((need,), jnp.int32),
            pltpu.SemaphoreType.DMA((need,)),
            pltpu.SemaphoreType.DMA((need,)),
            pltpu.SemaphoreType.DMA((PPD,)),
        ],
        compiler_params=pltpu.CompilerParams(vmem_limit_bytes=36 * MIB),
        name="own_part",
    )(own_table, far_table, firsts, tiles, perm, *pieces, *earlier)


def far_kernel(base, total_count, segments, table, chosen, *refs):
    starts, _, block_at, _ = table_views(table, total_count, PPD)
    tile_refs, refs = refs[: len(segments)], refs[len(segments) :]
    sum_in, flip_in = refs[:2]
    refs = refs[3:] if base else refs[2:]
    sum_out, result, tiles_ref, sums, rounded, tile_sem, row_sems, out_sems = refs
    count = tiles_ref.shape[0]
    stop = base + count

    for source, (choice, begin) in zip(tile_refs, segments):
        held = source.shape[0] * source.shape[2] // tiles_ref.shape[2]
        low, high = max(begin, base), min(begin + held, stop)

        @pl.when(chosen[0] == choice)
        def _(source=source, begin=begin, low=low, high=high):
            if source.shape[2] == tiles_ref.shape[2]:
                here, there = source.at[pl.ds(low - begin, high - low)], tiles_ref.at[pl.ds(low - base, high - low)]
                pltpu.make_async_copy(here, there, tile_sem).start()
            else:

                @pl.loop(low, high)
                def _(place):
                    pltpu.make_async_copy(window(source, place - begin), tiles_ref.at[place - base], tile_sem).start()

    def each_row(action):
        @pl.loop(0, PPD)
        def _(row):
            first, last = starts[row], starts[row + 1]

            @pl.when(((last > base) if base else True) & ((last <= stop) | (first < stop)))
            def _():
                action(row, last <= stop)

    def load(row):
        return pltpu.make_async_copy(sum_in.at[row], sums.at[row], row_sems.at[row])

    def store(row):
        return pltpu.make_async_copy(rounded.at[row], result.at[row], out_sems.at[row])

    def keep(row):
        return pltpu.make_async_copy(sums.at[row], sum_out.at[row], out_sems.at[row])

    each_row(lambda row, complete: load(row).start())
    pltpu.make_async_copy(tiles_ref, tiles_ref, tile_sem).wait()

    def add(row, complete):
        begin, end = jnp.maximum(starts[row], base), jnp.minimum(starts[row + 1], stop)
        load(row).wait()

        add_row(
            sums.at[row],
            begin,
            end,
            4,
            lambda place: tiles_ref[place - base],
            lambda place, window: flip_in[block_at[place], :, window],
        )

        @pl.when(complete)
        def _():
            rounded[row] = sums[row].astype(rounded.dtype)
            store(row).start()

        @pl.when(jnp.logical_not(complete))
        def _():
            keep(row).start()

    def finish(row, complete):
        pl.when(complete)(lambda: store(row).wait())
        pl.when(jnp.logical_not(complete))(lambda: keep(row).wait())

    each_row(add)
    each_row(finish)


def far_part(base, count, total_count, far_table, chosen, sources, flipped, total, result=None):
    whole = total.shape
    given = [] if result is None else [result]
    held = [array.size // (whole[1] * flipped.shape[1]) for _, _, array in sources]
    used = [
        (source[:2], source[2])
        for source, size in zip(sources, held)
        if source[1] < base + count and source[1] + size > base
    ]
    operand = 2 + len(used)
    aliases = {operand: 0, operand + 2: 1} if given else {operand: 0}
    return pl.pallas_call(
        functools.partial(far_kernel, base, total_count, [segment for segment, _ in used]),
        in_specs=[SMEM] * 2 + [ANY] * (len(used) + 1) + [VMEM] + [ANY] * len(given),
        out_specs=[ANY] * 2,
        out_shape=[jax.ShapeDtypeStruct(whole, jnp.float32), jax.ShapeDtypeStruct(whole, jnp.bfloat16)],
        input_output_aliases=aliases,
        scratch_shapes=[
            pltpu.VMEM((count, whole[1], flipped.shape[1]), jnp.bfloat16),
            pltpu.VMEM(whole, jnp.float32),
            pltpu.VMEM(whole, jnp.bfloat16),
            pltpu.SemaphoreType.DMA,
            pltpu.SemaphoreType.DMA((PPD,)),
            pltpu.SemaphoreType.DMA((PPD,)),
        ],
        compiler_params=pltpu.CompilerParams(vmem_limit_bytes=26 * MIB),
        name="far_part",
    )(far_table, chosen, *[array for _, array in used], total, flipped, *given)


def together(*values):
    return lax.optimization_barrier(values)


def send(value, pairs):
    return lax.ppermute(value, "tile", pairs)


def flipped_bit(bit):
    return [(i, i ^ bit) for i in range(16)]


def staged_part(tiles, rows, cols, shard):
    local = shard.shape[0]
    block_total = 16 * local
    centre = [i for i in range(16) if i // 4 in (1, 2)]
    across = [(i, i ^ 12) for i in centre]
    from_ends = [(i, i ^ 8) for i in range(16) if i not in centre]
    from_centre = [(i, i ^ 8) for i in centre]
    around = [(i, i ^ 4) for i in centre] + from_ends
    other_z, other_y, other_core, opposite = (flipped_bit(bit) for bit in (4, 2, 1, 8))
    me = lax.axis_index("tile")
    z = me // 4
    in_centre = (z == 1) | (z == 2)
    at_end = 1 - in_centre.astype(jnp.int32).reshape(1)
    zs = [z, z ^ 1, jnp.where(z < 2, 2, 1), jnp.where(z < 2, 3, 0)]

    def owner(k, bits):
        return 4 * zs[k] + ((me & 3) ^ bits)

    def first_blocks(firsts):
        return jnp.stack(firsts).astype(jnp.int32)

    col_owner = cols // local
    late = (col_owner // 4 == zs[3]) | (col_owner == owner(2, 3))
    keys = rows + PPD * late.astype(jnp.int32)
    columns = jnp.arange(shard.shape[2], dtype=jnp.int32)

    near = send(shard, other_z)
    first = send(shard, across)
    notes = send(jnp.stack([rows, cols]), opposite)
    order = tables(rows, cols, block_total)
    c_own = send(shard, other_core)
    y_own = send(shard, other_y)
    count = tiles.shape[0]
    step = shard.size // tiles[0].size
    sizes = tile_parts(count)
    shapes = [shard.shape] * 2 + [(size,) + tiles.shape[1:] for size in [count - 2 * step] + sizes]
    parts = sort_tiles(order, at_end, tiles, [1] * 3 + [0] * len(sizes), shapes)
    first, *parts = together(first, *parts)

    first = payload_of(at_end, parts[0], first)
    outer = send(first, around)
    near, c_own, y_own, keys, columns, *parts = together(near, c_own, y_own, keys, columns, *parts)
    second = send(near, across)
    y_near = send(near, other_y)
    c_near = send(near, other_core)
    c_y_own = send(y_own, other_core)
    own_table = tables(keys, cols, block_total, 2 * PPD)
    far_table = tables(notes[0], notes[1], block_total, cost=FAR_COST)
    perm = flip_matrix(columns)
    far_ends = [outer]
    first = jnp.where(in_centre, first, outer)
    second = payload_of(at_end, parts[1], second)
    outer = send(second, around)
    first, c_y_own, y_near, c_near, perm, *rest = together(
        first, c_y_own, y_near, c_near, perm, own_table, far_table, *parts[2:]
    )
    own_table, far_table, *parts = rest
    y_first = send(first, other_y)
    c_first = send(first, other_core)
    c_y_near = send(y_near, other_core)
    tiles_last, c_first = together(parts[0], c_first)
    far_ends += [outer, send(tiles_last, from_ends)]
    halves = (slice(0, local // 2), slice(local // 2, None))
    second = [jnp.where(in_centre, second[half], outer[half]) for half in halves]
    *second, y_first, c_first, c_y_near = together(*second, y_first, c_first, c_y_near)

    far_centre = [send(parts[1], from_centre)]
    y_second = [send(half, other_y) for half in second]
    pieces = [shard, c_own, near, c_near, first, c_first, y_own, c_y_own, y_near, c_y_near, y_first]
    firsts = [owner(k, y + core) * local for y in (0, 2) for k in range(3) for core in (0, 1)][:11]
    early = own_part(own_table, far_table, tiles, pieces, first_blocks(firsts), perm, 2 * PPD)
    y_second[0], y_second[1], second[0], second[1], y_first, total, flipped, *parts = together(
        *y_second, *second, y_first, *early, *parts[2:]
    )
    far_centre += [send(part, from_centre) for part in parts]
    *y_second, far_ends[2] = together(*y_second, far_ends[2])

    c_y_first = send(y_first, other_core)
    c_second = [send(half, other_core) for half in second]
    c_y_second = [send(half, other_core) for half in y_second]
    pieces = [c_y_first, *second, *c_second, *y_second, *c_y_second]
    firsts = [owner(2, 3) * local] + [owner(3, bits) * local + half for bits in range(4) for half in (0, local // 2)]
    earlier = (total, flipped)
    total, flipped = own_part(own_table, far_table, tiles, pieces, first_blocks(firsts), perm, 2 * PPD, PPD, earlier)

    sources = [(0, step * number, array) for number, array in enumerate(far_ends)]
    sources += [(1, sum(sizes[:number]), array) for number, array in enumerate(far_centre)]
    return far_products(far_table, at_end, sources, sizes, flipped, total)


def tile_parts(count):
    sizes = [count * share // 48 for share in SHARES]
    return sizes + [count - sum(sizes)]


def far_products(far_table, chosen, sources, sizes, flipped, total):
    base, result = 0, None
    for size in sizes:
        total, result = far_part(base, size, sum(sizes), far_table, chosen, sources, flipped, total, result)
        base += size
    return result


def per_device(t2_tiles, t2_row, t2_col, integrals):
    peers = lax.axis_size("tile")
    if peers == 16:
        return staged_part(t2_tiles, t2_row, t2_col, integrals)
    block_total = peers * integrals.shape[0]
    opposite = [(source, (source + peers // 2) % peers) for source in range(peers)]
    own_table = tables(t2_row, t2_col, block_total)
    sizes = tile_parts(t2_tiles.shape[0])
    zero = jnp.zeros((1,), jnp.int32)
    parts = sort_tiles(own_table, zero, t2_tiles, [0] * len(sizes), [(size,) + t2_tiles.shape[1:] for size in sizes])
    notes = send(jnp.stack([t2_row, t2_col]), opposite)
    sources = [(0, sum(sizes[:number]), send(part, opposite)) for number, part in enumerate(parts)]
    blocks = lax.all_gather(integrals, "tile", axis=0, tiled=True)
    far_table = tables(notes[0], notes[1], block_total)
    columns = jnp.arange(integrals.shape[2], dtype=jnp.int32)
    total, flipped = own_part(own_table, far_table, t2_tiles, [blocks], zero, flip_matrix(columns))
    return far_products(far_table, zero, sources, sizes, flipped, total)


def solution(mesh):
    in_specs = (
        P(("groups", "tile"), None, None),
        P(("groups", "tile")),
        P(("groups", "tile")),
        P(("groups", "tile"), None, None),
    )
    out_specs = P(("groups", "tile"), None, None)
    return jax.shard_map(
        per_device, mesh=mesh, in_specs=in_specs, out_specs=out_specs, check_vma=False
    )
```

```python
import functools

import jax
import jax.numpy as jnp
from jax import lax
from jax.experimental import pallas as pl
from jax.experimental.pallas import tpu as pltpu
from jax.sharding import PartitionSpec as P

W = 32
PPD = 16
REUSE = 3
SHARES = (30, 9, 6)
COLUMNS = 256
MIB = 1024 * 1024
FAR_COST = 4 * 10**9
SMEM = pl.BlockSpec(memory_space=pltpu.SMEM)
VMEM = pl.BlockSpec(memory_space=pltpu.VMEM)
ANY = pl.BlockSpec(memory_space=pl.ANY)


def flip_matrix(columns):
    source = (columns % W) * W + columns // W
    return (columns[:, None] == source[None, :]).astype(jnp.bfloat16)


class View:
    def __init__(self, ref, offset):
        self.ref, self.offset = ref, offset

    def __getitem__(self, index):
        return self.ref[self.offset + index]

    def __setitem__(self, index, value):
        self.ref[self.offset + index] = value


def table_views(table, count, groups):
    places = [0, groups + 1, groups + 1 + count, groups + 1 + 2 * count]
    return [View(table, place) for place in places]


def tables_kernel(rows, cols, table, cursor):
    count, groups = rows.shape[0], cursor.shape[0]
    total = table.shape[0] - (groups + 1 + 2 * count)
    starts, tile_at, block_at, slots = table_views(table, count, groups)

    @pl.loop(0, total)
    def _(block):
        slots[block] = 0

    for row in range(groups):
        cursor[row] = 0

    @pl.loop(0, count)
    def _(tile):
        cursor[rows[tile]] += 1
        slots[cols[tile]] = 1

    place = jnp.int32(0)
    for row in range(groups):
        size = cursor[row]
        starts[row] = place
        cursor[row] = place
        place += size
    starts[groups] = place

    def number(block, used):
        named = slots[block]
        slots[block] = jnp.where(named > 0, used, -1)
        return used + named

    lax.fori_loop(0, total, number, jnp.int32(0))

    @pl.loop(0, count)
    def _(tile):
        row = rows[tile]
        position = cursor[row]
        cursor[row] = position + 1
        tile_at[position] = tile
        block_at[position] = slots[cols[tile]]


def tables(rows, cols, total, groups=PPD, cost=0):
    count = rows.shape[0]
    return pl.pallas_call(
        tables_kernel,
        in_specs=[SMEM] * 2,
        out_specs=SMEM,
        out_shape=jax.ShapeDtypeStruct((groups + 1 + 2 * count + total,), jnp.int32),
        scratch_shapes=[pltpu.SMEM((groups,), jnp.int32)],
        cost_estimate=pl.CostEstimate(flops=cost, bytes_accessed=0, transcendentals=0) if cost else None,
        name="tables",
    )(rows, cols)


def window(ref, tile):
    depth = ref.shape[1]
    across = ref.shape[2] // depth
    if across == 1:
        return ref.at[tile]
    return ref.at[lax.div(tile, across), :, pl.ds(pl.multiple_of(lax.rem(tile, across) * depth, depth), depth)]


def sort_kernel(choices, table, chosen, tiles_ref, *refs):
    tile_at = table_views(table, tiles_ref.shape[0], PPD)[1]
    parts, sems = refs[: len(refs) // 2], refs[len(refs) // 2 :]
    begin = {choice: 0 for choice in choices}
    for choice, part, sem in zip(choices, parts, sems):
        base = begin[choice]
        count = part.shape[0] * part.shape[2] // tiles_ref.shape[2]
        begin[choice] += count

        @pl.when(chosen[0] == choice)
        def _(part=part, sem=sem, base=base, count=count):
            @pl.loop(0, count)
            def _(number):
                pltpu.make_async_copy(tiles_ref.at[tile_at[base + number]], window(part, number), sem).start()

    for choice, part, sem in zip(choices, parts, sems):

        @pl.when(chosen[0] == choice)
        def _(part=part, sem=sem):
            pltpu.make_async_copy(part, part, sem).wait()


def sort_tiles(table, chosen, tiles, choices, shapes):
    return pl.pallas_call(
        functools.partial(sort_kernel, choices),
        in_specs=[SMEM] * 2 + [ANY],
        out_specs=[VMEM] * len(shapes),
        out_shape=[jax.ShapeDtypeStruct(shape, tiles.dtype) for shape in shapes],
        scratch_shapes=[pltpu.SemaphoreType.DMA] * len(shapes),
        compiler_params=pltpu.CompilerParams(vmem_limit_bytes=16 * MIB),
        name="sort_tiles",
    )(table, chosen, tiles)


def payload_kernel(at_end, tiles_ref, received, payload, sem):
    del received

    @pl.when(at_end[0] == 1)
    def _():
        copy = pltpu.make_async_copy(tiles_ref, payload, sem)
        copy.start()
        copy.wait()


def payload_of(at_end, tiles, received):
    return pl.pallas_call(
        payload_kernel,
        in_specs=[SMEM, ANY, ANY],
        out_specs=ANY,
        out_shape=jax.ShapeDtypeStruct(received.shape, received.dtype),
        input_output_aliases={2: 0},
        scratch_shapes=[pltpu.SemaphoreType.DMA],
        compiler_params=pltpu.CompilerParams(vmem_limit_bytes=4 * MIB),
        name="payload",
    )(at_end, tiles, received)


def add_row(sum_ref, begin, end, depth, tile_of, block_of):
    width = sum_ref.shape[1]

    @pl.loop(0, (end - begin + depth - 1) // depth)
    def _(turn):
        here = begin + turn * depth
        places = [jnp.minimum(here + part, end - 1) for part in range(depth)]
        left = [tile_of(places[0])]
        for part in range(1, depth):
            tile = tile_of(places[part])
            left.append(jnp.where(here + part < end, tile, jnp.zeros_like(tile)))
        left = jnp.concatenate(left, axis=1)
        for column in range(0, width, COLUMNS):
            window = pl.ds(column, COLUMNS)
            right = jnp.concatenate([block_of(place, window) for place in places], axis=0)
            sum_ref[:, window] += jnp.dot(left, right, preferred_element_type=jnp.float32)


def own_kernel(counts, groups, group, fresh, own_table, far_table, firsts, tiles_ref, perm_ref, *refs):
    starts, tile_at, block_at, own_slots = table_views(own_table, tiles_ref.shape[0], groups)
    far_slots = table_views(far_table, tiles_ref.shape[0], PPD)[3]
    pieces = refs[: len(counts)]
    refs = refs[len(counts) :]
    if not fresh:
        sum_in, refs = refs[0], refs[2:]
    sum_out, flip_out, own_blocks, far_blocks, sums, own_list, far_list, own_sems, far_sems, row_sems = refs

    def fetch(slots, landing, sems, fetched):
        found = jnp.int32(0)
        for number, (piece, count) in enumerate(zip(pieces, counts)):

            def one(offset, found, piece=piece, number=number):
                slot = slots[firsts[number] + offset]

                @pl.when(slot >= 0)
                def _():
                    fetched[found] = slot
                    pltpu.make_async_copy(piece.at[offset], landing.at[slot], sems.at[slot]).start()

                return found + (slot >= 0).astype(jnp.int32)

            found = lax.fori_loop(0, count, one, found)
        return found

    far_found = fetch(far_slots, far_blocks, far_sems, far_list)
    own_found = fetch(own_slots, own_blocks, own_sems, own_list)
    if not fresh:
        for row in range(PPD):
            pltpu.make_async_copy(sum_in.at[row], sums.at[row], row_sems.at[row]).start()

    def arrived(landing, sems, slot):
        pltpu.make_async_copy(landing.at[slot], landing.at[slot], sems.at[slot]).wait()

    def flip_store(slot):
        return pltpu.make_async_copy(far_blocks.at[slot], flip_out.at[slot], far_sems.at[slot])

    @pl.loop(0, far_found)
    def _(number):
        slot = far_list[number]
        arrived(far_blocks, far_sems, slot)
        far_blocks[slot] = jnp.dot(
            far_blocks[slot], perm_ref[...], preferred_element_type=jnp.float32
        ).astype(jnp.bfloat16)
        flip_store(slot).start()

    @pl.loop(0, own_found)
    def _(number):
        arrived(own_blocks, own_sems, own_list[number])

    def store(row):
        return pltpu.make_async_copy(sums.at[row], sum_out.at[row], row_sems.at[row])

    @pl.loop(0, PPD)
    def _(row):
        if fresh:
            sums[row] = jnp.zeros(sums.shape[1:], jnp.float32)
        else:
            arrived(sums, row_sems, row)
        add_row(
            sums.at[row],
            starts[group + row],
            starts[group + row + 1],
            4 if fresh else 2,
            lambda place: tiles_ref[tile_at[place]],
            lambda place, window: own_blocks[block_at[place], :, window],
        )
        store(row).start()

    @pl.loop(0, far_found)
    def _(number):
        flip_store(far_list[number]).wait()

    @pl.loop(0, PPD)
    def _(row):
        store(row).wait()


def own_part(own_table, far_table, tiles, pieces, firsts, perm, groups=PPD, group=0, earlier=()):
    count, height, _ = tiles.shape
    depth, width = pieces[0].shape[1:]
    need = count // REUSE
    counts = [piece.shape[0] for piece in pieces]
    operands = 5 + len(pieces)
    return pl.pallas_call(
        functools.partial(own_kernel, counts, groups, group, not earlier),
        in_specs=[SMEM] * 3 + [VMEM] * 2 + [ANY] * (len(pieces) + len(earlier)),
        out_specs=[ANY] * 2,
        out_shape=[
            jax.ShapeDtypeStruct((PPD, height, width), jnp.float32),
            jax.ShapeDtypeStruct((need, depth, width), jnp.bfloat16),
        ],
        input_output_aliases={operands: 0, operands + 1: 1} if earlier else {},
        scratch_shapes=[
            pltpu.VMEM((need, depth, width), jnp.bfloat16),
            pltpu.VMEM((need, depth, width), jnp.bfloat16),
            pltpu.VMEM((PPD, height, width), jnp.float32),
            pltpu.SMEM((need,), jnp.int32),
            pltpu.SMEM((need,), jnp.int32),
            pltpu.SemaphoreType.DMA((need,)),
            pltpu.SemaphoreType.DMA((need,)),
            pltpu.SemaphoreType.DMA((PPD,)),
        ],
        compiler_params=pltpu.CompilerParams(vmem_limit_bytes=56 * MIB),
        name="own_part",
    )(own_table, far_table, firsts, tiles, perm, *pieces, *earlier)


def far_kernel(base, total_count, segments, table, chosen, *refs):
    starts, _, block_at, _ = table_views(table, total_count, PPD)
    tile_refs, refs = refs[: len(segments)], refs[len(segments) :]
    sum_in, flip_in = refs[:2]
    refs = refs[3:] if base else refs[2:]
    sum_out, result, tiles_ref, sums, rounded, tile_sem, row_sems, out_sems = refs
    count = tiles_ref.shape[0]
    stop = base + count

    for source, (choice, begin) in zip(tile_refs, segments):
        held = source.shape[0] * source.shape[2] // tiles_ref.shape[2]
        low, high = max(begin, base), min(begin + held, stop)

        @pl.when(chosen[0] == choice)
        def _(source=source, begin=begin, low=low, high=high):
            if source.shape[2] == tiles_ref.shape[2]:
                here, there = source.at[pl.ds(low - begin, high - low)], tiles_ref.at[pl.ds(low - base, high - low)]
                pltpu.make_async_copy(here, there, tile_sem).start()
            else:

                @pl.loop(low, high)
                def _(place):
                    pltpu.make_async_copy(window(source, place - begin), tiles_ref.at[place - base], tile_sem).start()

    def each_row(action):
        @pl.loop(0, PPD)
        def _(row):
            first, last = starts[row], starts[row + 1]

            @pl.when(((last > base) if base else True) & ((last <= stop) | (first < stop)))
            def _():
                action(row, last <= stop)

    def load(row):
        return pltpu.make_async_copy(sum_in.at[row], sums.at[row], row_sems.at[row])

    def store(row):
        return pltpu.make_async_copy(rounded.at[row], result.at[row], out_sems.at[row])

    def keep(row):
        return pltpu.make_async_copy(sums.at[row], sum_out.at[row], out_sems.at[row])

    each_row(lambda row, complete: load(row).start())
    pltpu.make_async_copy(tiles_ref, tiles_ref, tile_sem).wait()

    def add(row, complete):
        begin, end = jnp.maximum(starts[row], base), jnp.minimum(starts[row + 1], stop)
        load(row).wait()

        add_row(
            sums.at[row],
            begin,
            end,
            4,
            lambda place: tiles_ref[place - base],
            lambda place, window: flip_in[block_at[place], :, window],
        )

        @pl.when(complete)
        def _():
            rounded[row] = sums[row].astype(rounded.dtype)
            store(row).start()

        @pl.when(jnp.logical_not(complete))
        def _():
            keep(row).start()

    def finish(row, complete):
        pl.when(complete)(lambda: store(row).wait())
        pl.when(jnp.logical_not(complete))(lambda: keep(row).wait())

    each_row(add)
    each_row(finish)


def far_part(base, count, total_count, far_table, chosen, sources, flipped, total, result=None):
    whole = total.shape
    given = [] if result is None else [result]
    held = [array.size // (whole[1] * flipped.shape[1]) for _, _, array in sources]
    used = [
        (source[:2], source[2])
        for source, size in zip(sources, held)
        if source[1] < base + count and source[1] + size > base
    ]
    operand = 2 + len(used)
    aliases = {operand: 0, operand + 2: 1} if given else {operand: 0}
    return pl.pallas_call(
        functools.partial(far_kernel, base, total_count, [segment for segment, _ in used]),
        in_specs=[SMEM] * 2 + [ANY] * (len(used) + 1) + [VMEM] + [ANY] * len(given),
        out_specs=[ANY] * 2,
        out_shape=[jax.ShapeDtypeStruct(whole, jnp.float32), jax.ShapeDtypeStruct(whole, jnp.bfloat16)],
        input_output_aliases=aliases,
        scratch_shapes=[
            pltpu.VMEM((count, whole[1], flipped.shape[1]), jnp.bfloat16),
            pltpu.VMEM(whole, jnp.float32),
            pltpu.VMEM(whole, jnp.bfloat16),
            pltpu.SemaphoreType.DMA,
            pltpu.SemaphoreType.DMA((PPD,)),
            pltpu.SemaphoreType.DMA((PPD,)),
        ],
        compiler_params=pltpu.CompilerParams(vmem_limit_bytes=26 * MIB),
        name="far_part",
    )(far_table, chosen, *[array for _, array in used], total, flipped, *given)


def together(*values):
    return lax.optimization_barrier(values)


def send(value, pairs):
    return lax.ppermute(value, "tile", pairs)


def flipped_bit(bit):
    return [(i, i ^ bit) for i in range(16)]


def staged_part(tiles, rows, cols, shard):
    local = shard.shape[0]
    block_total = 16 * local
    centre = [i for i in range(16) if i // 4 in (1, 2)]
    across = [(i, i ^ 12) for i in centre]
    from_ends = [(i, i ^ 8) for i in range(16) if i not in centre]
    from_centre = [(i, i ^ 8) for i in centre]
    around = [(i, i ^ 4) for i in centre] + from_ends
    other_z, other_y, other_core, opposite = (flipped_bit(bit) for bit in (4, 2, 1, 8))
    me = lax.axis_index("tile")
    z = me // 4
    in_centre = (z == 1) | (z == 2)
    at_end = 1 - in_centre.astype(jnp.int32).reshape(1)
    zs = [z, z ^ 1, jnp.where(z < 2, 2, 1), jnp.where(z < 2, 3, 0)]

    def owner(k, bits):
        return 4 * zs[k] + ((me & 3) ^ bits)

    def first_blocks(firsts):
        return jnp.stack(firsts).astype(jnp.int32)

    col_owner = cols // local
    late = (col_owner // 4 == zs[3]) | (col_owner == owner(2, 3))
    keys = rows + PPD * late.astype(jnp.int32)
    columns = jnp.arange(shard.shape[2], dtype=jnp.int32)

    near = send(shard, other_z)
    first = send(shard, across)
    notes = send(jnp.stack([rows, cols]), opposite)
    order = tables(rows, cols, block_total)
    c_own = send(shard, other_core)
    y_own = send(shard, other_y)
    count = tiles.shape[0]
    step = shard.size // tiles[0].size
    sizes = tile_parts(count)
    shapes = [shard.shape] * 2 + [(size,) + tiles.shape[1:] for size in [count - 2 * step] + sizes]
    parts = sort_tiles(order, at_end, tiles, [1] * 3 + [0] * len(sizes), shapes)
    first, *parts = together(first, *parts)

    first = payload_of(at_end, parts[0], first)
    outer = send(first, around)
    near, c_own, y_own, keys, columns, *parts = together(near, c_own, y_own, keys, columns, *parts)
    second = send(near, across)
    y_near = send(near, other_y)
    c_near = send(near, other_core)
    c_y_own = send(y_own, other_core)
    own_table = tables(keys, cols, block_total, 2 * PPD)
    far_table = tables(notes[0], notes[1], block_total, cost=FAR_COST)
    perm = flip_matrix(columns)
    far_ends = [outer]
    first = jnp.where(in_centre, first, outer)
    second = payload_of(at_end, parts[1], second)
    outer = send(second, around)
    first, c_y_own, y_near, c_near, perm, *rest = together(
        first, c_y_own, y_near, c_near, perm, own_table, far_table, *parts[2:]
    )
    own_table, far_table, *parts = rest
    y_first = send(first, other_y)
    c_first = send(first, other_core)
    c_y_near = send(y_near, other_core)
    tiles_last, c_first = together(parts[0], c_first)
    far_ends += [outer, send(tiles_last, from_ends)]
    halves = (slice(0, local // 2), slice(local // 2, None))
    second = [jnp.where(in_centre, second[half], outer[half]) for half in halves]
    *second, y_first, c_first, c_y_near = together(*second, y_first, c_first, c_y_near)

    far_centre = [send(parts[1], from_centre)]
    y_second = [send(half, other_y) for half in second]
    pieces = [shard, c_own, near, c_near, first, c_first, y_own, c_y_own, y_near, c_y_near, y_first]
    firsts = [owner(k, y + core) * local for y in (0, 2) for k in range(3) for core in (0, 1)][:11]
    early = own_part(own_table, far_table, tiles, pieces, first_blocks(firsts), perm, 2 * PPD)
    y_second[0], y_second[1], second[0], second[1], y_first, total, flipped, *parts = together(
        *y_second, *second, y_first, *early, *parts[2:]
    )
    far_centre += [send(part, from_centre) for part in parts]
    *y_second, far_ends[2] = together(*y_second, far_ends[2])

    c_y_first = send(y_first, other_core)
    c_second = [send(half, other_core) for half in second]
    c_y_second = [send(half, other_core) for half in y_second]
    pieces = [c_y_first, *second, *c_second, *y_second, *c_y_second]
    firsts = [owner(2, 3) * local] + [owner(3, bits) * local + half for bits in range(4) for half in (0, local // 2)]
    earlier = (total, flipped)
    total, flipped = own_part(own_table, far_table, tiles, pieces, first_blocks(firsts), perm, 2 * PPD, PPD, earlier)

    sources = [(0, step * number, array) for number, array in enumerate(far_ends)]
    sources += [(1, sum(sizes[:number]), array) for number, array in enumerate(far_centre)]
    return far_products(far_table, at_end, sources, sizes, flipped, total)


def tile_parts(count):
    sizes = [count * share // 48 for share in SHARES]
    return sizes + [count - sum(sizes)]


def far_products(far_table, chosen, sources, sizes, flipped, total):
    base, result = 0, None
    for size in sizes:
        total, result = far_part(base, size, sum(sizes), far_table, chosen, sources, flipped, total, result)
        base += size
    return result


def per_device(t2_tiles, t2_row, t2_col, integrals):
    peers = lax.axis_size("tile")
    if peers == 16:
        return staged_part(t2_tiles, t2_row, t2_col, integrals)
    block_total = peers * integrals.shape[0]
    opposite = [(source, (source + peers // 2) % peers) for source in range(peers)]
    own_table = tables(t2_row, t2_col, block_total)
    sizes = tile_parts(t2_tiles.shape[0])
    zero = jnp.zeros((1,), jnp.int32)
    parts = sort_tiles(own_table, zero, t2_tiles, [0] * len(sizes), [(size,) + t2_tiles.shape[1:] for size in sizes])
    notes = send(jnp.stack([t2_row, t2_col]), opposite)
    sources = [(0, sum(sizes[:number]), send(part, opposite)) for number, part in enumerate(parts)]
    blocks = lax.all_gather(integrals, "tile", axis=0, tiled=True)
    far_table = tables(notes[0], notes[1], block_total)
    columns = jnp.arange(integrals.shape[2], dtype=jnp.int32)
    total, flipped = own_part(own_table, far_table, t2_tiles, [blocks], zero, flip_matrix(columns))
    return far_products(far_table, zero, sources, sizes, flipped, total)


def solution(mesh):
    in_specs = (
        P(("groups", "tile"), None, None),
        P(("groups", "tile")),
        P(("groups", "tile")),
        P(("groups", "tile"), None, None),
    )
    out_specs = P(("groups", "tile"), None, None)
    return jax.shard_map(
        per_device, mesh=mesh, in_specs=in_specs, out_specs=out_specs, check_vma=False
    )
```

```python
import functools

import jax
import jax.numpy as jnp
from jax import lax
from jax.experimental import pallas as pl
from jax.experimental.pallas import tpu as pltpu
from jax.sharding import PartitionSpec as P

W = 32
PPD = 16
REUSE = 3
SHARES = (30, 9, 6)
COLUMNS = 256
MIB = 1024 * 1024
FAR_COST = 4 * 10**9
SMEM = pl.BlockSpec(memory_space=pltpu.SMEM)
VMEM = pl.BlockSpec(memory_space=pltpu.VMEM)
ANY = pl.BlockSpec(memory_space=pl.ANY)


def flip_matrix(columns):
    source = (columns % W) * W + columns // W
    return (columns[:, None] == source[None, :]).astype(jnp.bfloat16)


class View:
    def __init__(self, ref, offset):
        self.ref, self.offset = ref, offset

    def __getitem__(self, index):
        return self.ref[self.offset + index]

    def __setitem__(self, index, value):
        self.ref[self.offset + index] = value


def table_views(table, count, groups):
    places = [0, groups + 1, groups + 1 + count, groups + 1 + 2 * count]
    return [View(table, place) for place in places]


def tables_kernel(rows, cols, table, cursor):
    count, groups = rows.shape[0], cursor.shape[0]
    total = table.shape[0] - (groups + 1 + 2 * count)
    starts, tile_at, block_at, slots = table_views(table, count, groups)

    @pl.loop(0, total)
    def _(block):
        slots[block] = 0

    for row in range(groups):
        cursor[row] = 0

    @pl.loop(0, count)
    def _(tile):
        cursor[rows[tile]] += 1
        slots[cols[tile]] = 1

    place = jnp.int32(0)
    for row in range(groups):
        size = cursor[row]
        starts[row] = place
        cursor[row] = place
        place += size
    starts[groups] = place

    def number(block, used):
        named = slots[block]
        slots[block] = jnp.where(named > 0, used, -1)
        return used + named

    lax.fori_loop(0, total, number, jnp.int32(0))

    @pl.loop(0, count)
    def _(tile):
        row = rows[tile]
        position = cursor[row]
        cursor[row] = position + 1
        tile_at[position] = tile
        block_at[position] = slots[cols[tile]]


def tables(rows, cols, total, groups=PPD, cost=0):
    count = rows.shape[0]
    return pl.pallas_call(
        tables_kernel,
        in_specs=[SMEM] * 2,
        out_specs=SMEM,
        out_shape=jax.ShapeDtypeStruct((groups + 1 + 2 * count + total,), jnp.int32),
        scratch_shapes=[pltpu.SMEM((groups,), jnp.int32)],
        cost_estimate=pl.CostEstimate(flops=cost, bytes_accessed=0, transcendentals=0) if cost else None,
        name="tables",
    )(rows, cols)


def window(ref, tile):
    depth = ref.shape[1]
    across = ref.shape[2] // depth
    if across == 1:
        return ref.at[tile]
    return ref.at[lax.div(tile, across), :, pl.ds(pl.multiple_of(lax.rem(tile, across) * depth, depth), depth)]


def sort_kernel(choices, table, chosen, tiles_ref, *refs):
    tile_at = table_views(table, tiles_ref.shape[0], PPD)[1]
    parts, sems = refs[: len(refs) // 2], refs[len(refs) // 2 :]
    begin = {choice: 0 for choice in choices}
    for choice, part, sem in zip(choices, parts, sems):
        base = begin[choice]
        count = part.shape[0] * part.shape[2] // tiles_ref.shape[2]
        begin[choice] += count

        @pl.when(chosen[0] == choice)
        def _(part=part, sem=sem, base=base, count=count):
            @pl.loop(0, count)
            def _(number):
                pltpu.make_async_copy(tiles_ref.at[tile_at[base + number]], window(part, number), sem).start()

    for choice, part, sem in zip(choices, parts, sems):

        @pl.when(chosen[0] == choice)
        def _(part=part, sem=sem):
            pltpu.make_async_copy(part, part, sem).wait()


def sort_tiles(table, chosen, tiles, choices, shapes):
    return pl.pallas_call(
        functools.partial(sort_kernel, choices),
        in_specs=[SMEM] * 2 + [ANY],
        out_specs=[VMEM] * len(shapes),
        out_shape=[jax.ShapeDtypeStruct(shape, tiles.dtype) for shape in shapes],
        scratch_shapes=[pltpu.SemaphoreType.DMA] * len(shapes),
        compiler_params=pltpu.CompilerParams(vmem_limit_bytes=16 * MIB),
        name="sort_tiles",
    )(table, chosen, tiles)


def payload_kernel(at_end, tiles_ref, received, payload, sem):
    del received

    @pl.when(at_end[0] == 1)
    def _():
        copy = pltpu.make_async_copy(tiles_ref, payload, sem)
        copy.start()
        copy.wait()


def payload_of(at_end, tiles, received):
    return pl.pallas_call(
        payload_kernel,
        in_specs=[SMEM, ANY, ANY],
        out_specs=ANY,
        out_shape=jax.ShapeDtypeStruct(received.shape, received.dtype),
        input_output_aliases={2: 0},
        scratch_shapes=[pltpu.SemaphoreType.DMA],
        compiler_params=pltpu.CompilerParams(vmem_limit_bytes=4 * MIB),
        name="payload",
    )(at_end, tiles, received)


def add_row(sum_ref, begin, end, depth, tile_of, block_of):
    width = sum_ref.shape[1]

    @pl.loop(0, (end - begin + depth - 1) // depth)
    def _(turn):
        here = begin + turn * depth
        places = [jnp.minimum(here + part, end - 1) for part in range(depth)]
        left = [tile_of(places[0])]
        for part in range(1, depth):
            tile = tile_of(places[part])
            left.append(jnp.where(here + part < end, tile, jnp.zeros_like(tile)))
        left = jnp.concatenate(left, axis=1)
        for column in range(0, width, COLUMNS):
            window = pl.ds(column, COLUMNS)
            right = jnp.concatenate([block_of(place, window) for place in places], axis=0)
            sum_ref[:, window] += jnp.dot(left, right, preferred_element_type=jnp.float32)


def own_kernel(counts, groups, group, fresh, own_table, far_table, firsts, tiles_ref, perm_ref, *refs):
    starts, tile_at, block_at, own_slots = table_views(own_table, tiles_ref.shape[0], groups)
    far_slots = table_views(far_table, tiles_ref.shape[0], PPD)[3]
    pieces = refs[: len(counts)]
    refs = refs[len(counts) :]
    if not fresh:
        sum_in, refs = refs[0], refs[2:]
    sum_out, flip_out, own_blocks, far_blocks, sums, own_list, far_list, own_sems, far_sems, row_sems = refs

    def fetch(slots, landing, sems, fetched):
        found = jnp.int32(0)
        for number, (piece, count) in enumerate(zip(pieces, counts)):

            def one(offset, found, piece=piece, number=number):
                slot = slots[firsts[number] + offset]

                @pl.when(slot >= 0)
                def _():
                    fetched[found] = slot
                    pltpu.make_async_copy(piece.at[offset], landing.at[slot], sems.at[slot]).start()

                return found + (slot >= 0).astype(jnp.int32)

            found = lax.fori_loop(0, count, one, found)
        return found

    far_found = fetch(far_slots, far_blocks, far_sems, far_list)
    own_found = fetch(own_slots, own_blocks, own_sems, own_list)
    if not fresh:
        for row in range(PPD):
            pltpu.make_async_copy(sum_in.at[row], sums.at[row], row_sems.at[row]).start()

    def arrived(landing, sems, slot):
        pltpu.make_async_copy(landing.at[slot], landing.at[slot], sems.at[slot]).wait()

    def flip_store(slot):
        return pltpu.make_async_copy(far_blocks.at[slot], flip_out.at[slot], far_sems.at[slot])

    @pl.loop(0, far_found)
    def _(number):
        slot = far_list[number]
        arrived(far_blocks, far_sems, slot)
        far_blocks[slot] = jnp.dot(
            far_blocks[slot], perm_ref[...], preferred_element_type=jnp.float32
        ).astype(jnp.bfloat16)
        flip_store(slot).start()

    @pl.loop(0, own_found)
    def _(number):
        arrived(own_blocks, own_sems, own_list[number])

    def store(row):
        return pltpu.make_async_copy(sums.at[row], sum_out.at[row], row_sems.at[row])

    @pl.loop(0, PPD)
    def _(row):
        if fresh:
            sums[row] = jnp.zeros(sums.shape[1:], jnp.float32)
        else:
            arrived(sums, row_sems, row)
        add_row(
            sums.at[row],
            starts[group + row],
            starts[group + row + 1],
            4 if fresh else 2,
            lambda place: tiles_ref[tile_at[place]],
            lambda place, window: own_blocks[block_at[place], :, window],
        )
        store(row).start()

    @pl.loop(0, far_found)
    def _(number):
        flip_store(far_list[number]).wait()

    @pl.loop(0, PPD)
    def _(row):
        store(row).wait()


def own_part(own_table, far_table, tiles, pieces, firsts, perm, groups=PPD, group=0, earlier=()):
    count, height, _ = tiles.shape
    depth, width = pieces[0].shape[1:]
    need = count // REUSE
    counts = [piece.shape[0] for piece in pieces]
    operands = 5 + len(pieces)
    return pl.pallas_call(
        functools.partial(own_kernel, counts, groups, group, not earlier),
        in_specs=[SMEM] * 3 + [VMEM] * 2 + [ANY] * (len(pieces) + len(earlier)),
        out_specs=[ANY] * 2,
        out_shape=[
            jax.ShapeDtypeStruct((PPD, height, width), jnp.float32),
            jax.ShapeDtypeStruct((need, depth, width), jnp.bfloat16),
        ],
        input_output_aliases={operands: 0, operands + 1: 1} if earlier else {},
        scratch_shapes=[
            pltpu.VMEM((need, depth, width), jnp.bfloat16),
            pltpu.VMEM((need, depth, width), jnp.bfloat16),
            pltpu.VMEM((PPD, height, width), jnp.float32),
            pltpu.SMEM((need,), jnp.int32),
            pltpu.SMEM((need,), jnp.int32),
            pltpu.SemaphoreType.DMA((need,)),
            pltpu.SemaphoreType.DMA((need,)),
            pltpu.SemaphoreType.DMA((PPD,)),
        ],
        compiler_params=pltpu.CompilerParams(vmem_limit_bytes=56 * MIB),
        name="own_part",
    )(own_table, far_table, firsts, tiles, perm, *pieces, *earlier)


def far_kernel(base, total_count, segments, table, chosen, *refs):
    starts, _, block_at, _ = table_views(table, total_count, PPD)
    tile_refs, refs = refs[: len(segments)], refs[len(segments) :]
    sum_in, flip_in = refs[:2]
    refs = refs[3:] if base else refs[2:]
    sum_out, result, tiles_ref, sums, rounded, tile_sem, row_sems, out_sems = refs
    count = tiles_ref.shape[0]
    stop = base + count

    for source, (choice, begin) in zip(tile_refs, segments):
        held = source.shape[0] * source.shape[2] // tiles_ref.shape[2]
        low, high = max(begin, base), min(begin + held, stop)

        @pl.when(chosen[0] == choice)
        def _(source=source, begin=begin, low=low, high=high):
            if source.shape[2] == tiles_ref.shape[2]:
                here, there = source.at[pl.ds(low - begin, high - low)], tiles_ref.at[pl.ds(low - base, high - low)]
                pltpu.make_async_copy(here, there, tile_sem).start()
            else:

                @pl.loop(low, high)
                def _(place):
                    pltpu.make_async_copy(window(source, place - begin), tiles_ref.at[place - base], tile_sem).start()

    def each_row(action):
        @pl.loop(0, PPD)
        def _(row):
            first, last = starts[row], starts[row + 1]

            @pl.when(((last > base) if base else True) & ((last <= stop) | (first < stop)))
            def _():
                action(row, last <= stop)

    def load(row):
        return pltpu.make_async_copy(sum_in.at[row], sums.at[row], row_sems.at[row])

    def store(row):
        return pltpu.make_async_copy(rounded.at[row], result.at[row], out_sems.at[row])

    def keep(row):
        return pltpu.make_async_copy(sums.at[row], sum_out.at[row], out_sems.at[row])

    each_row(lambda row, complete: load(row).start())
    pltpu.make_async_copy(tiles_ref, tiles_ref, tile_sem).wait()

    def add(row, complete):
        begin, end = jnp.maximum(starts[row], base), jnp.minimum(starts[row + 1], stop)
        load(row).wait()

        add_row(
            sums.at[row],
            begin,
            end,
            4,
            lambda place: tiles_ref[place - base],
            lambda place, window: flip_in[block_at[place], :, window],
        )

        @pl.when(complete)
        def _():
            rounded[row] = sums[row].astype(rounded.dtype)
            store(row).start()

        @pl.when(jnp.logical_not(complete))
        def _():
            keep(row).start()

    def finish(row, complete):
        pl.when(complete)(lambda: store(row).wait())
        pl.when(jnp.logical_not(complete))(lambda: keep(row).wait())

    each_row(add)
    each_row(finish)


def far_part(base, count, total_count, far_table, chosen, sources, flipped, total, result=None):
    whole = total.shape
    given = [] if result is None else [result]
    held = [array.size // (whole[1] * flipped.shape[1]) for _, _, array in sources]
    used = [
        (source[:2], source[2])
        for source, size in zip(sources, held)
        if source[1] < base + count and source[1] + size > base
    ]
    operand = 2 + len(used)
    aliases = {operand: 0, operand + 2: 1} if given else {operand: 0}
    return pl.pallas_call(
        functools.partial(far_kernel, base, total_count, [segment for segment, _ in used]),
        in_specs=[SMEM] * 2 + [ANY] * (len(used) + 1) + [VMEM] + [ANY] * len(given),
        out_specs=[ANY] * 2,
        out_shape=[jax.ShapeDtypeStruct(whole, jnp.float32), jax.ShapeDtypeStruct(whole, jnp.bfloat16)],
        input_output_aliases=aliases,
        scratch_shapes=[
            pltpu.VMEM((count, whole[1], flipped.shape[1]), jnp.bfloat16),
            pltpu.VMEM(whole, jnp.float32),
            pltpu.VMEM(whole, jnp.bfloat16),
            pltpu.SemaphoreType.DMA,
            pltpu.SemaphoreType.DMA((PPD,)),
            pltpu.SemaphoreType.DMA((PPD,)),
        ],
        compiler_params=pltpu.CompilerParams(vmem_limit_bytes=26 * MIB),
        name="far_part",
    )(far_table, chosen, *[array for _, array in used], total, flipped, *given)


def together(*values):
    return lax.optimization_barrier(values)


def send(value, pairs):
    return lax.ppermute(value, "tile", pairs)


def flipped_bit(bit):
    return [(i, i ^ bit) for i in range(16)]


def staged_part(tiles, rows, cols, shard):
    local = shard.shape[0]
    block_total = 16 * local
    centre = [i for i in range(16) if i // 4 in (1, 2)]
    across = [(i, i ^ 12) for i in centre]
    from_ends = [(i, i ^ 8) for i in range(16) if i not in centre]
    from_centre = [(i, i ^ 8) for i in centre]
    around = [(i, i ^ 4) for i in centre] + from_ends
    other_z, other_y, other_core, opposite = (flipped_bit(bit) for bit in (4, 2, 1, 8))
    me = lax.axis_index("tile")
    z = me // 4
    in_centre = (z == 1) | (z == 2)
    at_end = 1 - in_centre.astype(jnp.int32).reshape(1)
    zs = [z, z ^ 1, jnp.where(z < 2, 2, 1), jnp.where(z < 2, 3, 0)]

    def owner(k, bits):
        return 4 * zs[k] + ((me & 3) ^ bits)

    def first_blocks(firsts):
        return jnp.stack(firsts).astype(jnp.int32)

    col_owner = cols // local
    late = (col_owner // 4 == zs[3]) | (col_owner == owner(2, 3))
    keys = rows + PPD * late.astype(jnp.int32)
    columns = jnp.arange(shard.shape[2], dtype=jnp.int32)

    near = send(shard, other_z)
    first = send(shard, across)
    notes = send(jnp.stack([rows, cols]), opposite)
    order = tables(rows, cols, block_total)
    c_own = send(shard, other_core)
    y_own = send(shard, other_y)
    count = tiles.shape[0]
    step = shard.size // tiles[0].size
    sizes = tile_parts(count)
    shapes = [shard.shape] * 2 + [(size,) + tiles.shape[1:] for size in [count - 2 * step] + sizes]
    parts = sort_tiles(order, at_end, tiles, [1] * 3 + [0] * len(sizes), shapes)
    first, *parts = together(first, *parts)

    first = payload_of(at_end, parts[0], first)
    outer = send(first, around)
    near, c_own, y_own, keys, columns, *parts = together(near, c_own, y_own, keys, columns, *parts)
    second = send(near, across)
    y_near = send(near, other_y)
    c_near = send(near, other_core)
    own_table = tables(keys, cols, block_total, 2 * PPD)
    far_table = tables(notes[0], notes[1], block_total, cost=FAR_COST)
    perm = flip_matrix(columns)
    far_ends = [outer]
    first = jnp.where(in_centre, first, outer)
    second = payload_of(at_end, parts[1], second)
    outer = send(second, around)
    first, y_own, y_near, c_near, perm, *rest = together(
        first, y_own, y_near, c_near, perm, own_table, far_table, *parts[2:]
    )
    own_table, far_table, *parts = rest
    y_first = send(first, other_y)
    c_first = send(first, other_core)
    c_y_own = send(y_own, other_core)
    c_y_near = send(y_near, other_core)
    tiles_last, c_first = together(parts[0], c_first)
    far_ends += [outer, send(tiles_last, from_ends)]
    halves = (slice(0, local // 2), slice(local // 2, None))
    second = [jnp.where(in_centre, second[half], outer[half]) for half in halves]
    *second, y_first, c_first, c_y_own, c_y_near = together(*second, y_first, c_first, c_y_own, c_y_near)

    far_centre = [send(parts[1], from_centre)]
    y_second = [send(half, other_y) for half in second]
    pieces = [shard, c_own, near, c_near, first, c_first, y_own, c_y_own, y_near, c_y_near, y_first]
    firsts = [owner(k, y + core) * local for y in (0, 2) for k in range(3) for core in (0, 1)][:11]
    early = own_part(own_table, far_table, tiles, pieces, first_blocks(firsts), perm, 2 * PPD)
    y_second[0], y_second[1], second[0], second[1], y_first, total, flipped, *parts = together(
        *y_second, *second, y_first, *early, *parts[2:]
    )
    far_centre += [send(part, from_centre) for part in parts]
    *y_second, far_ends[2] = together(*y_second, far_ends[2])

    c_y_first = send(y_first, other_core)
    c_second = [send(half, other_core) for half in second]
    c_y_second = [send(half, other_core) for half in y_second]
    pieces = [c_y_first, *second, *c_second, *y_second, *c_y_second]
    firsts = [owner(2, 3) * local] + [owner(3, bits) * local + half for bits in range(4) for half in (0, local // 2)]
    earlier = (total, flipped)
    total, flipped = own_part(own_table, far_table, tiles, pieces, first_blocks(firsts), perm, 2 * PPD, PPD, earlier)

    sources = [(0, step * number, array) for number, array in enumerate(far_ends)]
    sources += [(1, sum(sizes[:number]), array) for number, array in enumerate(far_centre)]
    return far_products(far_table, at_end, sources, sizes, flipped, total)


def tile_parts(count):
    sizes = [count * share // 48 for share in SHARES]
    return sizes + [count - sum(sizes)]


def far_products(far_table, chosen, sources, sizes, flipped, total):
    base, result = 0, None
    for size in sizes:
        total, result = far_part(base, size, sum(sizes), far_table, chosen, sources, flipped, total, result)
        base += size
    return result


def per_device(t2_tiles, t2_row, t2_col, integrals):
    peers = lax.axis_size("tile")
    if peers == 16:
        return staged_part(t2_tiles, t2_row, t2_col, integrals)
    block_total = peers * integrals.shape[0]
    opposite = [(source, (source + peers // 2) % peers) for source in range(peers)]
    own_table = tables(t2_row, t2_col, block_total)
    sizes = tile_parts(t2_tiles.shape[0])
    zero = jnp.zeros((1,), jnp.int32)
    parts = sort_tiles(own_table, zero, t2_tiles, [0] * len(sizes), [(size,) + t2_tiles.shape[1:] for size in sizes])
    notes = send(jnp.stack([t2_row, t2_col]), opposite)
    sources = [(0, sum(sizes[:number]), send(part, opposite)) for number, part in enumerate(parts)]
    blocks = lax.all_gather(integrals, "tile", axis=0, tiled=True)
    far_table = tables(notes[0], notes[1], block_total)
    columns = jnp.arange(integrals.shape[2], dtype=jnp.int32)
    total, flipped = own_part(own_table, far_table, t2_tiles, [blocks], zero, flip_matrix(columns))
    return far_products(far_table, zero, sources, sizes, flipped, total)


def solution(mesh):
    in_specs = (
        P(("groups", "tile"), None, None),
        P(("groups", "tile")),
        P(("groups", "tile")),
        P(("groups", "tile"), None, None),
    )
    out_specs = P(("groups", "tile"), None, None)
    return jax.shard_map(
        per_device, mesh=mesh, in_specs=in_specs, out_specs=out_specs, check_vma=False
    )
```

```python
import functools

import jax
import jax.numpy as jnp
from jax import lax
from jax.experimental import pallas as pl
from jax.experimental.pallas import tpu as pltpu
from jax.sharding import PartitionSpec as P

W = 32
PPD = 16
REUSE = 3
SHARES = (30, 9, 6)
COLUMNS = 256
MIB = 1024 * 1024
GRANT = 36
FAR_COST = 4 * 10**9
SMEM = pl.BlockSpec(memory_space=pltpu.SMEM)
VMEM = pl.BlockSpec(memory_space=pltpu.VMEM)
ANY = pl.BlockSpec(memory_space=pl.ANY)
HBM = pl.BlockSpec(memory_space=pltpu.HBM)


def flip_matrix(columns):
    source = (columns % W) * W + columns // W
    return (columns[:, None] == source[None, :]).astype(jnp.bfloat16)


class View:
    def __init__(self, ref, offset):
        self.ref, self.offset = ref, offset

    def __getitem__(self, index):
        return self.ref[self.offset + index]

    def __setitem__(self, index, value):
        self.ref[self.offset + index] = value


def table_views(table, count, groups):
    places = [0, groups + 1, groups + 1 + count, groups + 1 + 2 * count]
    return [View(table, place) for place in places]


def tables_kernel(rows, cols, table, cursor):
    count, groups = rows.shape[0], cursor.shape[0]
    total = table.shape[0] - (groups + 1 + 2 * count)
    starts, tile_at, block_at, slots = table_views(table, count, groups)

    @pl.loop(0, total)
    def _(block):
        slots[block] = 0

    for row in range(groups):
        cursor[row] = 0

    @pl.loop(0, count)
    def _(tile):
        cursor[rows[tile]] += 1
        slots[cols[tile]] = 1

    place = jnp.int32(0)
    for row in range(groups):
        size = cursor[row]
        starts[row] = place
        cursor[row] = place
        place += size
    starts[groups] = place

    def number(block, used):
        named = slots[block]
        slots[block] = jnp.where(named > 0, used, -1)
        return used + named

    lax.fori_loop(0, total, number, jnp.int32(0))

    @pl.loop(0, count)
    def _(tile):
        row = rows[tile]
        position = cursor[row]
        cursor[row] = position + 1
        tile_at[position] = tile
        block_at[position] = slots[cols[tile]]


def tables(rows, cols, total, groups=PPD, cost=0):
    count = rows.shape[0]
    return pl.pallas_call(
        tables_kernel,
        in_specs=[SMEM] * 2,
        out_specs=SMEM,
        out_shape=jax.ShapeDtypeStruct((groups + 1 + 2 * count + total,), jnp.int32),
        scratch_shapes=[pltpu.SMEM((groups,), jnp.int32)],
        cost_estimate=pl.CostEstimate(flops=cost, bytes_accessed=0, transcendentals=0) if cost else None,
        name="tables",
    )(rows, cols)


def window(ref, tile):
    depth = ref.shape[1]
    across = ref.shape[2] // depth
    if across == 1:
        return ref.at[tile]
    return ref.at[lax.div(tile, across), :, pl.ds(pl.multiple_of(lax.rem(tile, across) * depth, depth), depth)]


def sort_kernel(choices, table, chosen, tiles_ref, *refs):
    tile_at = table_views(table, tiles_ref.shape[0], PPD)[1]
    parts, sems = refs[: len(refs) // 2], refs[len(refs) // 2 :]
    begin = {choice: 0 for choice in choices}
    for choice, part, sem in zip(choices, parts, sems):
        base = begin[choice]
        count = part.shape[0] * part.shape[2] // tiles_ref.shape[2]
        begin[choice] += count

        @pl.when(chosen[0] == choice)
        def _(part=part, sem=sem, base=base, count=count):
            @pl.loop(0, count)
            def _(number):
                pltpu.make_async_copy(tiles_ref.at[tile_at[base + number]], window(part, number), sem).start()

    for choice, part, sem in zip(choices, parts, sems):

        @pl.when(chosen[0] == choice)
        def _(part=part, sem=sem):
            pltpu.make_async_copy(part, part, sem).wait()


def sort_tiles(table, chosen, tiles, choices, shapes):
    return pl.pallas_call(
        functools.partial(sort_kernel, choices),
        in_specs=[SMEM] * 2 + [ANY],
        out_specs=[VMEM] * len(shapes),
        out_shape=[jax.ShapeDtypeStruct(shape, tiles.dtype) for shape in shapes],
        scratch_shapes=[pltpu.SemaphoreType.DMA] * len(shapes),
        compiler_params=pltpu.CompilerParams(vmem_limit_bytes=16 * MIB),
        name="sort_tiles",
    )(table, chosen, tiles)


def payload_kernel(at_end, tiles_ref, received, payload, sem):
    del received

    @pl.when(at_end[0] == 1)
    def _():
        copy = pltpu.make_async_copy(tiles_ref, payload, sem)
        copy.start()
        copy.wait()


def payload_of(at_end, tiles, received):
    return pl.pallas_call(
        payload_kernel,
        in_specs=[SMEM, HBM, ANY],
        out_specs=ANY,
        out_shape=jax.ShapeDtypeStruct(received.shape, received.dtype),
        input_output_aliases={2: 0},
        scratch_shapes=[pltpu.SemaphoreType.DMA],
        compiler_params=pltpu.CompilerParams(vmem_limit_bytes=4 * MIB),
        name="payload",
    )(at_end, tiles, received)


def add_row(sum_ref, begin, end, depth, tile_of, block_of):
    width = sum_ref.shape[1]

    @pl.loop(0, (end - begin + depth - 1) // depth)
    def _(turn):
        here = begin + turn * depth
        places = [jnp.minimum(here + part, end - 1) for part in range(depth)]
        left = [tile_of(places[0])]
        for part in range(1, depth):
            tile = tile_of(places[part])
            left.append(jnp.where(here + part < end, tile, jnp.zeros_like(tile)))
        left = jnp.concatenate(left, axis=1)
        for column in range(0, width, COLUMNS):
            window = pl.ds(column, COLUMNS)
            right = jnp.concatenate([block_of(place, window) for place in places], axis=0)
            sum_ref[:, window] += jnp.dot(left, right, preferred_element_type=jnp.float32)


def own_kernel(counts, groups, group, fresh, own_table, far_table, firsts, tiles_ref, perm_ref, *refs):
    starts, tile_at, block_at, own_slots = table_views(own_table, tiles_ref.shape[0], groups)
    far_slots = table_views(far_table, tiles_ref.shape[0], PPD)[3]
    pieces = refs[: len(counts)]
    refs = refs[len(counts) :]
    if fresh:
        sum_out, flip_out, sums, *refs = refs
    else:
        sum_in, flip_in, sums, flip_out, flip_sem, *refs = refs
    own_blocks, far_blocks, own_list, far_list, own_sems, far_sems, row_sems = refs

    def fetch(slots, landing, sems, fetched):
        found = jnp.int32(0)
        for number, (piece, count) in enumerate(zip(pieces, counts)):

            def one(offset, found, piece=piece, number=number):
                slot = slots[firsts[number] + offset]

                @pl.when(slot >= 0)
                def _():
                    fetched[found] = slot
                    pltpu.make_async_copy(piece.at[offset], landing.at[slot], sems.at[slot]).start()

                return found + (slot >= 0).astype(jnp.int32)

            found = lax.fori_loop(0, count, one, found)
        return found

    far_found = fetch(far_slots, far_blocks, far_sems, far_list)
    own_found = fetch(own_slots, own_blocks, own_sems, own_list)
    if not fresh:
        pltpu.make_async_copy(flip_in, flip_out, flip_sem).start()
        for row in range(PPD):
            pltpu.make_async_copy(sum_in.at[row], sums.at[row], row_sems.at[row]).start()
        pltpu.make_async_copy(flip_in, flip_out, flip_sem).wait()

    def arrived(landing, sems, slot):
        pltpu.make_async_copy(landing.at[slot], landing.at[slot], sems.at[slot]).wait()

    def flip_store(slot):
        return pltpu.make_async_copy(far_blocks.at[slot], flip_out.at[slot], far_sems.at[slot])

    @pl.loop(0, far_found)
    def _(number):
        slot = far_list[number]
        arrived(far_blocks, far_sems, slot)
        turned = jnp.dot(far_blocks[slot], perm_ref[...], preferred_element_type=jnp.float32).astype(jnp.bfloat16)
        if fresh:
            far_blocks[slot] = turned
            flip_store(slot).start()
        else:
            flip_out[slot] = turned

    @pl.loop(0, own_found)
    def _(number):
        arrived(own_blocks, own_sems, own_list[number])

    def store(row):
        return pltpu.make_async_copy(sums.at[row], sum_out.at[row], row_sems.at[row])

    @pl.loop(0, PPD)
    def _(row):
        if fresh:
            sums[row] = jnp.zeros(sums.shape[1:], jnp.float32)
        else:
            arrived(sums, row_sems, row)
        add_row(
            sums.at[row],
            starts[group + row],
            starts[group + row + 1],
            4 if fresh else 2,
            lambda place: tiles_ref[tile_at[place]],
            lambda place, window: own_blocks[block_at[place], :, window],
        )
        if fresh:
            store(row).start()

    if fresh:

        @pl.loop(0, far_found)
        def _(number):
            flip_store(far_list[number]).wait()

        @pl.loop(0, PPD)
        def _(row):
            store(row).wait()


def own_part(own_table, far_table, tiles, pieces, firsts, perm, groups=PPD, group=0, earlier=()):
    count, height, _ = tiles.shape
    depth, width = pieces[0].shape[1:]
    need = count // REUSE
    counts = [piece.shape[0] for piece in pieces]
    whole = (PPD, height, width)
    flips = (need, depth, width)
    if earlier:
        out_specs = [VMEM] * 2
        out_shape = [pltpu.VMEM(whole, jnp.float32), pltpu.VMEM(flips, jnp.bfloat16)]
        first_scratch = pltpu.SemaphoreType.DMA
    else:
        out_specs = [ANY] * 2
        out_shape = [jax.ShapeDtypeStruct(whole, jnp.float32), jax.ShapeDtypeStruct(flips, jnp.bfloat16)]
        first_scratch = pltpu.VMEM(whole, jnp.float32)
    return pl.pallas_call(
        functools.partial(own_kernel, counts, groups, group, not earlier),
        in_specs=[SMEM] * 3 + [VMEM] * 2 + [ANY] * (len(pieces) + len(earlier)),
        out_specs=out_specs,
        out_shape=out_shape,
        scratch_shapes=[
            first_scratch,
            pltpu.VMEM(flips, jnp.bfloat16),
            pltpu.VMEM(flips, jnp.bfloat16),
            pltpu.SMEM((need,), jnp.int32),
            pltpu.SMEM((need,), jnp.int32),
            pltpu.SemaphoreType.DMA((need,)),
            pltpu.SemaphoreType.DMA((need,)),
            pltpu.SemaphoreType.DMA((PPD,)),
        ],
        compiler_params=pltpu.CompilerParams(vmem_limit_bytes=(GRANT if earlier else 56) * MIB),
        name="own_part",
    )(own_table, far_table, firsts, tiles, perm, *pieces, *earlier)


def far_kernel(base, total_count, segments, table, chosen, *refs):
    starts, _, block_at, _ = table_views(table, total_count, PPD)
    tile_refs, refs = refs[: len(segments)], refs[len(segments) :]
    sum_in, flip_in = refs[:2]
    carry_in = refs[2] if base else None
    carry_out, result, tiles_ref, sums, rounded, tile_sem, row_sems, out_sems = refs[4:] if base else refs[2:]
    count = tiles_ref.shape[0]
    stop = base + count

    for source, (choice, begin) in zip(tile_refs, segments):
        held = source.shape[0] * source.shape[2] // tiles_ref.shape[2]
        low, high = max(begin, base), min(begin + held, stop)

        @pl.when(chosen[0] == choice)
        def _(source=source, begin=begin, low=low, high=high):
            if source.shape[2] == tiles_ref.shape[2]:
                here, there = source.at[pl.ds(low - begin, high - low)], tiles_ref.at[pl.ds(low - base, high - low)]
                pltpu.make_async_copy(here, there, tile_sem).start()
            else:

                @pl.loop(low, high)
                def _(place):
                    pltpu.make_async_copy(window(source, place - begin), tiles_ref.at[place - base], tile_sem).start()

    def each_row(action):
        @pl.loop(0, PPD)
        def _(row):
            first, last = starts[row], starts[row + 1]

            @pl.when(((last > base) if base else True) & ((last <= stop) | (first < stop)))
            def _():
                action(row, last <= stop)

    def load(row):
        if base:
            goes_on = starts[row] < base

            @pl.when(goes_on)
            def _():
                pltpu.make_async_copy(carry_in, sums.at[row], row_sems.at[row]).start()

            @pl.when(jnp.logical_not(goes_on))
            def _():
                pltpu.make_async_copy(sum_in.at[row], sums.at[row], row_sems.at[row]).start()
        else:
            pltpu.make_async_copy(sum_in.at[row], sums.at[row], row_sems.at[row]).start()

    def store(row):
        return pltpu.make_async_copy(rounded.at[row], result.at[row], out_sems.at[row])

    def keep(row):
        return pltpu.make_async_copy(sums.at[row], carry_out, out_sems.at[row])

    each_row(lambda row, complete: load(row))
    pltpu.make_async_copy(tiles_ref, tiles_ref, tile_sem).wait()

    def add(row, complete):
        begin, end = jnp.maximum(starts[row], base), jnp.minimum(starts[row + 1], stop)
        pltpu.make_async_copy(sums.at[row], sums.at[row], row_sems.at[row]).wait()

        add_row(
            sums.at[row],
            begin,
            end,
            4,
            lambda place: tiles_ref[place - base],
            lambda place, window: flip_in[block_at[place], :, window],
        )

        @pl.when(complete)
        def _():
            rounded[row] = sums[row].astype(rounded.dtype)
            store(row).start()

        @pl.when(jnp.logical_not(complete))
        def _():
            keep(row).start()

    def finish(row, complete):
        pl.when(complete)(lambda: store(row).wait())
        pl.when(jnp.logical_not(complete))(lambda: keep(row).wait())

    each_row(add)
    each_row(finish)


def far_part(base, count, total_count, far_table, chosen, sources, flipped, total, earlier=()):
    whole = total.shape
    held = [array.size // (whole[1] * flipped.shape[1]) for _, _, array in sources]
    used = [
        (source[:2], source[2])
        for source, size in zip(sources, held)
        if source[1] < base + count and source[1] + size > base
    ]
    return pl.pallas_call(
        functools.partial(far_kernel, base, total_count, [segment for segment, _ in used]),
        in_specs=[SMEM] * 2 + [ANY] * len(used) + [VMEM] * 2 + [ANY] * len(earlier),
        out_specs=[ANY] * 2,
        out_shape=[jax.ShapeDtypeStruct(whole[1:], jnp.float32), jax.ShapeDtypeStruct(whole, jnp.bfloat16)],
        input_output_aliases={5 + len(used): 1} if earlier else {},
        scratch_shapes=[
            pltpu.VMEM((count, whole[1], flipped.shape[1]), jnp.bfloat16),
            pltpu.VMEM(whole, jnp.float32),
            pltpu.VMEM(whole, jnp.bfloat16),
            pltpu.SemaphoreType.DMA,
            pltpu.SemaphoreType.DMA((PPD,)),
            pltpu.SemaphoreType.DMA((PPD,)),
        ],
        compiler_params=pltpu.CompilerParams(vmem_limit_bytes=24 * MIB),
        name="far_part",
    )(far_table, chosen, *[array for _, array in used], total, flipped, *earlier)


def together(*values):
    return lax.optimization_barrier(values)


def send(value, pairs):
    return lax.ppermute(value, "tile", pairs)


def flipped_bit(bit):
    return [(i, i ^ bit) for i in range(16)]


def staged_part(tiles, rows, cols, shard):
    local = shard.shape[0]
    block_total = 16 * local
    centre = [i for i in range(16) if i // 4 in (1, 2)]
    across = [(i, i ^ 12) for i in centre]
    from_ends = [(i, i ^ 8) for i in range(16) if i not in centre]
    from_centre = [(i, i ^ 8) for i in centre]
    around = [(i, i ^ 4) for i in centre] + from_ends
    other_z, other_y, other_core, opposite = (flipped_bit(bit) for bit in (4, 2, 1, 8))
    me = lax.axis_index("tile")
    z = me // 4
    in_centre = (z == 1) | (z == 2)
    at_end = 1 - in_centre.astype(jnp.int32).reshape(1)
    zs = [z, z ^ 1, jnp.where(z < 2, 2, 1), jnp.where(z < 2, 3, 0)]

    def owner(k, bits):
        return 4 * zs[k] + ((me & 3) ^ bits)

    def first_blocks(firsts):
        return jnp.stack(firsts).astype(jnp.int32)

    col_owner = cols // local
    late = (col_owner // 4 == zs[3]) | (col_owner == owner(2, 3))
    keys = rows + PPD * late.astype(jnp.int32)
    columns = jnp.arange(shard.shape[2], dtype=jnp.int32)

    near = send(shard, other_z)
    first = send(shard, across)
    notes = send(jnp.stack([rows, cols]), opposite)
    order = tables(rows, cols, block_total)
    c_own = send(shard, other_core)
    y_own = send(shard, other_y)
    count = tiles.shape[0]
    step = shard.size // tiles[0].size
    sizes = tile_parts(count)
    shapes = [shard.shape] * 2 + [(size,) + tiles.shape[1:] for size in [count - 2 * step] + sizes]
    parts = sort_tiles(order, at_end, tiles, [1] * 3 + [0] * len(sizes), shapes)
    first, *parts = together(first, *parts)

    first = payload_of(at_end, parts[0], first)
    outer = send(first, around)
    near, c_own, y_own, keys, columns, *parts = together(near, c_own, y_own, keys, columns, *parts)
    second = send(near, across)
    y_near = send(near, other_y)
    c_near = send(near, other_core)
    own_table = tables(keys, cols, block_total, 2 * PPD)
    far_table = tables(notes[0], notes[1], block_total, cost=FAR_COST)
    perm = flip_matrix(columns)
    far_ends = [outer]
    first = jnp.where(in_centre, first, outer)
    second = payload_of(at_end, parts[1], second)
    outer = send(second, around)
    first, y_own, y_near, c_near, perm, *rest = together(
        first, y_own, y_near, c_near, perm, own_table, far_table, *parts[2:]
    )
    own_table, far_table, *parts = rest
    y_first = send(first, other_y)
    c_first = send(first, other_core)
    c_y_own = send(y_own, other_core)
    c_y_near = send(y_near, other_core)
    tiles_last, c_first = together(parts[0], c_first)
    far_ends += [outer, send(tiles_last, from_ends)]
    halves = (slice(0, local // 2), slice(local // 2, None))
    second = [jnp.where(in_centre, second[half], outer[half]) for half in halves]
    *second, y_first, c_first, c_y_own, c_y_near = together(*second, y_first, c_first, c_y_own, c_y_near)

    far_centre = [send(parts[1], from_centre)]
    y_second = [send(half, other_y) for half in second]
    pieces = [shard, c_own, near, c_near, first, c_first, y_own, c_y_own, y_near, c_y_near, y_first]
    firsts = [owner(k, y + core) * local for y in (0, 2) for k in range(3) for core in (0, 1)][:11]
    early = own_part(own_table, far_table, tiles, pieces, first_blocks(firsts), perm, 2 * PPD)
    y_second[0], y_second[1], second[0], second[1], y_first, total, flipped, *parts = together(
        *y_second, *second, y_first, *early, *parts[2:]
    )
    far_centre += [send(part, from_centre) for part in parts]
    *y_second, far_ends[2] = together(*y_second, far_ends[2])

    c_y_first = send(y_first, other_core)
    c_second = [send(half, other_core) for half in second]
    c_y_second = [send(half, other_core) for half in y_second]
    pieces = [c_y_first, *second, *c_second, *y_second, *c_y_second]
    firsts = [owner(2, 3) * local] + [owner(3, bits) * local + half for bits in range(4) for half in (0, local // 2)]
    earlier = (total, flipped)
    total, flipped = own_part(own_table, far_table, tiles, pieces, first_blocks(firsts), perm, 2 * PPD, PPD, earlier)

    sources = [(0, step * number, array) for number, array in enumerate(far_ends)]
    sources += [(1, sum(sizes[:number]), array) for number, array in enumerate(far_centre)]
    return far_products(far_table, at_end, sources, sizes, flipped, total)


def tile_parts(count):
    sizes = [count * share // 48 for share in SHARES]
    return sizes + [count - sum(sizes)]


def far_products(far_table, chosen, sources, sizes, flipped, total):
    base, earlier = 0, ()
    for size in sizes:
        earlier = far_part(base, size, sum(sizes), far_table, chosen, sources, flipped, total, earlier)
        base += size
    return earlier[1]


def per_device(t2_tiles, t2_row, t2_col, integrals):
    peers = lax.axis_size("tile")
    if peers == 16:
        return staged_part(t2_tiles, t2_row, t2_col, integrals)
    block_total = peers * integrals.shape[0]
    opposite = [(source, (source + peers // 2) % peers) for source in range(peers)]
    own_table = tables(t2_row, t2_col, block_total)
    sizes = tile_parts(t2_tiles.shape[0])
    zero = jnp.zeros((1,), jnp.int32)
    parts = sort_tiles(own_table, zero, t2_tiles, [0] * len(sizes), [(size,) + t2_tiles.shape[1:] for size in sizes])
    notes = send(jnp.stack([t2_row, t2_col]), opposite)
    sources = [(0, sum(sizes[:number]), send(part, opposite)) for number, part in enumerate(parts)]
    blocks = lax.all_gather(integrals, "tile", axis=0, tiled=True)
    far_table = tables(notes[0], notes[1], block_total)
    columns = jnp.arange(integrals.shape[2], dtype=jnp.int32)
    total, flipped = own_part(own_table, far_table, t2_tiles, [blocks], zero, flip_matrix(columns))
    return far_products(far_table, zero, sources, sizes, flipped, total)


def solution(mesh):
    in_specs = (
        P(("groups", "tile"), None, None),
        P(("groups", "tile")),
        P(("groups", "tile")),
        P(("groups", "tile"), None, None),
    )
    out_specs = P(("groups", "tile"), None, None)
    return jax.shard_map(
        per_device, mesh=mesh, in_specs=in_specs, out_specs=out_specs, check_vma=False
    )
```

```python
import functools

import jax
import jax.numpy as jnp
from jax import lax
from jax.experimental import pallas as pl
from jax.experimental.pallas import tpu as pltpu
from jax.sharding import PartitionSpec as P

W = 32
PPD = 16
REUSE = 3
SHARES = (30, 9, 6)
COLUMNS = 256
MIB = 1024 * 1024
GRANT = 36
FAR_COST = 4 * 10**9
SMEM = pl.BlockSpec(memory_space=pltpu.SMEM)
VMEM = pl.BlockSpec(memory_space=pltpu.VMEM)
ANY = pl.BlockSpec(memory_space=pl.ANY)
HBM = pl.BlockSpec(memory_space=pltpu.HBM)


def flip_matrix(columns):
    source = (columns % W) * W + columns // W
    return (columns[:, None] == source[None, :]).astype(jnp.bfloat16)


class View:
    def __init__(self, ref, offset):
        self.ref, self.offset = ref, offset

    def __getitem__(self, index):
        return self.ref[self.offset + index]

    def __setitem__(self, index, value):
        self.ref[self.offset + index] = value


def table_views(table, count, groups):
    places = [0, groups + 1, groups + 1 + count, groups + 1 + 2 * count]
    return [View(table, place) for place in places]


def tables_kernel(rows, cols, table, cursor):
    count, groups = rows.shape[0], cursor.shape[0]
    total = table.shape[0] - (groups + 1 + 2 * count)
    starts, tile_at, block_at, slots = table_views(table, count, groups)

    @pl.loop(0, total)
    def _(block):
        slots[block] = 0

    for row in range(groups):
        cursor[row] = 0

    @pl.loop(0, count)
    def _(tile):
        cursor[rows[tile]] += 1
        slots[cols[tile]] = 1

    place = jnp.int32(0)
    for row in range(groups):
        size = cursor[row]
        starts[row] = place
        cursor[row] = place
        place += size
    starts[groups] = place

    def number(block, used):
        named = slots[block]
        slots[block] = jnp.where(named > 0, used, -1)
        return used + named

    lax.fori_loop(0, total, number, jnp.int32(0))

    @pl.loop(0, count)
    def _(tile):
        row = rows[tile]
        position = cursor[row]
        cursor[row] = position + 1
        tile_at[position] = tile
        block_at[position] = slots[cols[tile]]


def tables(rows, cols, total, groups=PPD, cost=0):
    count = rows.shape[0]
    return pl.pallas_call(
        tables_kernel,
        in_specs=[SMEM] * 2,
        out_specs=SMEM,
        out_shape=jax.ShapeDtypeStruct((groups + 1 + 2 * count + total,), jnp.int32),
        scratch_shapes=[pltpu.SMEM((groups,), jnp.int32)],
        cost_estimate=pl.CostEstimate(flops=cost, bytes_accessed=0, transcendentals=0) if cost else None,
        name="tables",
    )(rows, cols)


def window(ref, tile):
    depth = ref.shape[1]
    across = ref.shape[2] // depth
    if across == 1:
        return ref.at[tile]
    return ref.at[lax.div(tile, across), :, pl.ds(pl.multiple_of(lax.rem(tile, across) * depth, depth), depth)]


def sort_kernel(choices, table, chosen, tiles_ref, *refs):
    tile_at = table_views(table, tiles_ref.shape[0], PPD)[1]
    parts, sems = refs[: len(refs) // 2], refs[len(refs) // 2 :]
    begin = {choice: 0 for choice in choices}
    for choice, part, sem in zip(choices, parts, sems):
        base = begin[choice]
        count = part.shape[0] * part.shape[2] // tiles_ref.shape[2]
        begin[choice] += count

        @pl.when(chosen[0] == choice)
        def _(part=part, sem=sem, base=base, count=count):
            @pl.loop(0, count)
            def _(number):
                pltpu.make_async_copy(tiles_ref.at[tile_at[base + number]], window(part, number), sem).start()

    for choice, part, sem in zip(choices, parts, sems):

        @pl.when(chosen[0] == choice)
        def _(part=part, sem=sem):
            pltpu.make_async_copy(part, part, sem).wait()


def sort_tiles(table, chosen, tiles, choices, shapes):
    return pl.pallas_call(
        functools.partial(sort_kernel, choices),
        in_specs=[SMEM] * 2 + [ANY],
        out_specs=[VMEM] * len(shapes),
        out_shape=[jax.ShapeDtypeStruct(shape, tiles.dtype) for shape in shapes],
        scratch_shapes=[pltpu.SemaphoreType.DMA] * len(shapes),
        compiler_params=pltpu.CompilerParams(vmem_limit_bytes=16 * MIB),
        name="sort_tiles",
    )(table, chosen, tiles)


def payload_kernel(at_end, tiles_ref, received, payload, sem):
    del received

    @pl.when(at_end[0] == 1)
    def _():
        copy = pltpu.make_async_copy(tiles_ref, payload, sem)
        copy.start()
        copy.wait()


def payload_of(at_end, tiles, received):
    return pl.pallas_call(
        payload_kernel,
        in_specs=[SMEM, HBM, ANY],
        out_specs=ANY,
        out_shape=jax.ShapeDtypeStruct(received.shape, received.dtype),
        input_output_aliases={2: 0},
        scratch_shapes=[pltpu.SemaphoreType.DMA],
        compiler_params=pltpu.CompilerParams(vmem_limit_bytes=4 * MIB),
        name="payload",
    )(at_end, tiles, received)


def add_row(sum_ref, begin, end, depth, tile_of, block_of):
    width = sum_ref.shape[1]

    @pl.loop(0, (end - begin + depth - 1) // depth)
    def _(turn):
        here = begin + turn * depth
        places = [jnp.minimum(here + part, end - 1) for part in range(depth)]
        left = [tile_of(places[0])]
        for part in range(1, depth):
            tile = tile_of(places[part])
            left.append(jnp.where(here + part < end, tile, jnp.zeros_like(tile)))
        left = jnp.concatenate(left, axis=1)
        for column in range(0, width, COLUMNS):
            window = pl.ds(column, COLUMNS)
            right = jnp.concatenate([block_of(place, window) for place in places], axis=0)
            sum_ref[:, window] += jnp.dot(left, right, preferred_element_type=jnp.float32)


def own_kernel(counts, groups, group, fresh, own_table, far_table, firsts, tiles_ref, perm_ref, *refs):
    starts, tile_at, block_at, own_slots = table_views(own_table, tiles_ref.shape[0], groups)
    far_slots = table_views(far_table, tiles_ref.shape[0], PPD)[3]
    pieces = refs[: len(counts)]
    refs = refs[len(counts) :]
    if fresh:
        sum_out, flip_out, sums, *refs = refs
    else:
        sum_in, flip_in, sums, flip_out, flip_sem, *refs = refs
    own_blocks, far_blocks, own_list, far_list, own_sems, far_sems, row_sems = refs

    def fetch(slots, landing, sems, fetched):
        found = jnp.int32(0)
        for number, (piece, count) in enumerate(zip(pieces, counts)):

            def one(offset, found, piece=piece, number=number):
                slot = slots[firsts[number] + offset]

                @pl.when(slot >= 0)
                def _():
                    fetched[found] = slot
                    pltpu.make_async_copy(piece.at[offset], landing.at[slot], sems.at[slot]).start()

                return found + (slot >= 0).astype(jnp.int32)

            found = lax.fori_loop(0, count, one, found)
        return found

    far_found = fetch(far_slots, far_blocks, far_sems, far_list)
    own_found = fetch(own_slots, own_blocks, own_sems, own_list)
    if not fresh:
        pltpu.make_async_copy(flip_in, flip_out, flip_sem).start()
        for row in range(PPD):
            pltpu.make_async_copy(sum_in.at[row], sums.at[row], row_sems.at[row]).start()
        pltpu.make_async_copy(flip_in, flip_out, flip_sem).wait()

    def arrived(landing, sems, slot):
        pltpu.make_async_copy(landing.at[slot], landing.at[slot], sems.at[slot]).wait()

    def flip_store(slot):
        return pltpu.make_async_copy(far_blocks.at[slot], flip_out.at[slot], far_sems.at[slot])

    @pl.loop(0, far_found)
    def _(number):
        slot = far_list[number]
        arrived(far_blocks, far_sems, slot)
        turned = jnp.dot(far_blocks[slot], perm_ref[...], preferred_element_type=jnp.float32).astype(jnp.bfloat16)
        if fresh:
            far_blocks[slot] = turned
            flip_store(slot).start()
        else:
            flip_out[slot] = turned

    @pl.loop(0, own_found)
    def _(number):
        arrived(own_blocks, own_sems, own_list[number])

    def store(row):
        return pltpu.make_async_copy(sums.at[row], sum_out.at[row], row_sems.at[row])

    @pl.loop(0, PPD)
    def _(row):
        if fresh:
            sums[row] = jnp.zeros(sums.shape[1:], jnp.float32)
        else:
            arrived(sums, row_sems, row)
        add_row(
            sums.at[row],
            starts[group + row],
            starts[group + row + 1],
            4 if fresh else 2,
            lambda place: tiles_ref[tile_at[place]],
            lambda place, window: own_blocks[block_at[place], :, window],
        )
        if fresh:
            store(row).start()

    if fresh:

        @pl.loop(0, far_found)
        def _(number):
            flip_store(far_list[number]).wait()

        @pl.loop(0, PPD)
        def _(row):
            store(row).wait()


def own_part(own_table, far_table, tiles, pieces, firsts, perm, groups=PPD, group=0, earlier=()):
    count, height, _ = tiles.shape
    depth, width = pieces[0].shape[1:]
    need = count // REUSE
    counts = [piece.shape[0] for piece in pieces]
    whole = (PPD, height, width)
    flips = (need, depth, width)
    if earlier:
        out_specs = [VMEM] * 2
        out_shape = [pltpu.VMEM(whole, jnp.float32), pltpu.VMEM(flips, jnp.bfloat16)]
        first_scratch = pltpu.SemaphoreType.DMA
    else:
        out_specs = [ANY] * 2
        out_shape = [jax.ShapeDtypeStruct(whole, jnp.float32), jax.ShapeDtypeStruct(flips, jnp.bfloat16)]
        first_scratch = pltpu.VMEM(whole, jnp.float32)
    return pl.pallas_call(
        functools.partial(own_kernel, counts, groups, group, not earlier),
        in_specs=[SMEM] * 3 + [VMEM] * 2 + [ANY] * (len(pieces) + len(earlier)),
        out_specs=out_specs,
        out_shape=out_shape,
        scratch_shapes=[
            first_scratch,
            pltpu.VMEM(flips, jnp.bfloat16),
            pltpu.VMEM(flips, jnp.bfloat16),
            pltpu.SMEM((need,), jnp.int32),
            pltpu.SMEM((need,), jnp.int32),
            pltpu.SemaphoreType.DMA((need,)),
            pltpu.SemaphoreType.DMA((need,)),
            pltpu.SemaphoreType.DMA((PPD,)),
        ],
        compiler_params=pltpu.CompilerParams(vmem_limit_bytes=(GRANT if earlier else 56) * MIB),
        name="own_part",
    )(own_table, far_table, firsts, tiles, perm, *pieces, *earlier)


def far_kernel(base, total_count, segments, table, chosen, *refs):
    starts, _, block_at, _ = table_views(table, total_count, PPD)
    tile_refs, refs = refs[: len(segments)], refs[len(segments) :]
    sum_in, flip_in = refs[:2]
    carry_in = refs[2] if base else None
    carry_out, result, tiles_ref, sums, rounded, tile_sem, row_sems, out_sems = refs[4:] if base else refs[2:]
    count = tiles_ref.shape[0]
    stop = base + count

    direct, direct_choice = tile_refs[-1], segments[-1][0]
    copied = list(zip(tile_refs, segments))[:-1]
    for source, (choice, begin) in copied:
        held = source.shape[0] * source.shape[2] // tiles_ref.shape[2]
        low, high = max(begin, base), min(begin + held, stop)

        @pl.when(chosen[0] == choice)
        def _(source=source, begin=begin, low=low, high=high):
            if source.shape[2] == tiles_ref.shape[2]:
                here, there = source.at[pl.ds(low - begin, high - low)], tiles_ref.at[pl.ds(low - base, high - low)]
                pltpu.make_async_copy(here, there, tile_sem).start()
            else:

                @pl.loop(low, high)
                def _(place):
                    pltpu.make_async_copy(window(source, place - begin), tiles_ref.at[place - base], tile_sem).start()

    def each_row(action):
        @pl.loop(0, PPD)
        def _(row):
            first, last = starts[row], starts[row + 1]

            @pl.when(((last > base) if base else True) & ((last <= stop) | (first < stop)))
            def _():
                action(row, last <= stop)

    def load(row):
        if base:
            goes_on = starts[row] < base

            @pl.when(goes_on)
            def _():
                pltpu.make_async_copy(carry_in, sums.at[row], row_sems.at[row]).start()

            @pl.when(jnp.logical_not(goes_on))
            def _():
                pltpu.make_async_copy(sum_in.at[row], sums.at[row], row_sems.at[row]).start()
        else:
            pltpu.make_async_copy(sum_in.at[row], sums.at[row], row_sems.at[row]).start()

    def store(row):
        return pltpu.make_async_copy(rounded.at[row], result.at[row], out_sems.at[row])

    def keep(row):
        return pltpu.make_async_copy(sums.at[row], carry_out, out_sems.at[row])

    each_row(lambda row, complete: load(row))
    if copied:

        @pl.when(chosen[0] != direct_choice)
        def _():
            pltpu.make_async_copy(tiles_ref, tiles_ref, tile_sem).wait()

    def tile_of(place):
        if not copied:
            return direct[place - base]
        return jnp.where(chosen[0] == direct_choice, direct[place - base], tiles_ref[place - base])

    def add(row, complete):
        begin, end = jnp.maximum(starts[row], base), jnp.minimum(starts[row + 1], stop)
        pltpu.make_async_copy(sums.at[row], sums.at[row], row_sems.at[row]).wait()

        add_row(
            sums.at[row],
            begin,
            end,
            4,
            tile_of,
            lambda place, window: flip_in[block_at[place], :, window],
        )

        @pl.when(complete)
        def _():
            rounded[row] = sums[row].astype(rounded.dtype)
            store(row).start()

        @pl.when(jnp.logical_not(complete))
        def _():
            keep(row).start()

    def finish(row, complete):
        pl.when(complete)(lambda: store(row).wait())
        pl.when(jnp.logical_not(complete))(lambda: keep(row).wait())

    each_row(add)
    each_row(finish)


def far_part(base, count, total_count, far_table, chosen, sources, flipped, total, earlier=()):
    whole = total.shape
    held = [array.size // (whole[1] * flipped.shape[1]) for _, _, array in sources]
    used = [
        (source[:2], source[2])
        for source, size in zip(sources, held)
        if source[1] < base + count and source[1] + size > base
    ]
    return pl.pallas_call(
        functools.partial(far_kernel, base, total_count, [segment for segment, _ in used]),
        in_specs=[SMEM] * 2 + [ANY] * (len(used) - 1) + [VMEM] * 3 + [ANY] * len(earlier),
        out_specs=[ANY] * 2,
        out_shape=[jax.ShapeDtypeStruct(whole[1:], jnp.float32), jax.ShapeDtypeStruct(whole, jnp.bfloat16)],
        input_output_aliases={5 + len(used): 1} if earlier else {},
        scratch_shapes=[
            pltpu.VMEM((count, whole[1], flipped.shape[1]), jnp.bfloat16),
            pltpu.VMEM(whole, jnp.float32),
            pltpu.VMEM(whole, jnp.bfloat16),
            pltpu.SemaphoreType.DMA,
            pltpu.SemaphoreType.DMA((PPD,)),
            pltpu.SemaphoreType.DMA((PPD,)),
        ],
        compiler_params=pltpu.CompilerParams(vmem_limit_bytes=24 * MIB),
        name="far_part",
    )(far_table, chosen, *[array for _, array in used], total, flipped, *earlier)


def together(*values):
    return lax.optimization_barrier(values)


def send(value, pairs):
    return lax.ppermute(value, "tile", pairs)


def flipped_bit(bit):
    return [(i, i ^ bit) for i in range(16)]


def staged_part(tiles, rows, cols, shard):
    local = shard.shape[0]
    block_total = 16 * local
    centre = [i for i in range(16) if i // 4 in (1, 2)]
    across = [(i, i ^ 12) for i in centre]
    from_ends = [(i, i ^ 8) for i in range(16) if i not in centre]
    from_centre = [(i, i ^ 8) for i in centre]
    around = [(i, i ^ 4) for i in centre] + from_ends
    other_z, other_y, other_core, opposite = (flipped_bit(bit) for bit in (4, 2, 1, 8))
    me = lax.axis_index("tile")
    z = me // 4
    in_centre = (z == 1) | (z == 2)
    at_end = 1 - in_centre.astype(jnp.int32).reshape(1)
    zs = [z, z ^ 1, jnp.where(z < 2, 2, 1), jnp.where(z < 2, 3, 0)]

    def owner(k, bits):
        return 4 * zs[k] + ((me & 3) ^ bits)

    def first_blocks(firsts):
        return jnp.stack(firsts).astype(jnp.int32)

    col_owner = cols // local
    late = (col_owner // 4 == zs[3]) | (col_owner == owner(2, 3))
    keys = rows + PPD * late.astype(jnp.int32)
    columns = jnp.arange(shard.shape[2], dtype=jnp.int32)

    near = send(shard, other_z)
    first = send(shard, across)
    notes = send(jnp.stack([rows, cols]), opposite)
    order = tables(rows, cols, block_total)
    c_own = send(shard, other_core)
    y_own = send(shard, other_y)
    count = tiles.shape[0]
    step = shard.size // tiles[0].size
    sizes = tile_parts(count)
    shapes = [shard.shape] * 2 + [(size,) + tiles.shape[1:] for size in [count - 2 * step] + sizes]
    parts = sort_tiles(order, at_end, tiles, [1] * 3 + [0] * len(sizes), shapes)
    first, *parts = together(first, *parts)

    first = payload_of(at_end, parts[0], first)
    outer = send(first, around)
    near, c_own, y_own, keys, columns, *parts = together(near, c_own, y_own, keys, columns, *parts)
    second = send(near, across)
    y_near = send(near, other_y)
    c_near = send(near, other_core)
    own_table = tables(keys, cols, block_total, 2 * PPD)
    far_table = tables(notes[0], notes[1], block_total, cost=FAR_COST)
    perm = flip_matrix(columns)
    far_ends = [outer]
    first = jnp.where(in_centre, first, outer)
    second = payload_of(at_end, parts[1], second)
    outer = send(second, around)
    first, y_own, y_near, c_near, perm, *rest = together(
        first, y_own, y_near, c_near, perm, own_table, far_table, *parts[2:]
    )
    own_table, far_table, *parts = rest
    y_first = send(first, other_y)
    c_first = send(first, other_core)
    c_y_own = send(y_own, other_core)
    c_y_near = send(y_near, other_core)
    tiles_last, c_first = together(parts[0], c_first)
    far_ends += [outer, send(tiles_last, from_ends)]
    halves = (slice(0, local // 2), slice(local // 2, None))
    second = [jnp.where(in_centre, second[half], outer[half]) for half in halves]
    *second, y_first, c_first, c_y_own, c_y_near = together(*second, y_first, c_first, c_y_own, c_y_near)

    far_centre = [send(parts[1], from_centre)]
    y_second = [send(half, other_y) for half in second]
    pieces = [shard, c_own, near, c_near, first, c_first, y_own, c_y_own, y_near, c_y_near, y_first]
    firsts = [owner(k, y + core) * local for y in (0, 2) for k in range(3) for core in (0, 1)][:11]
    early = own_part(own_table, far_table, tiles, pieces, first_blocks(firsts), perm, 2 * PPD)
    y_second[0], y_second[1], second[0], second[1], y_first, total, flipped, *parts = together(
        *y_second, *second, y_first, *early, *parts[2:]
    )
    far_centre += [send(part, from_centre) for part in parts]
    *y_second, far_ends[2] = together(*y_second, far_ends[2])

    c_y_first = send(y_first, other_core)
    c_second = [send(half, other_core) for half in second]
    c_y_second = [send(half, other_core) for half in y_second]
    pieces = [c_y_first, *second, *c_second, *y_second, *c_y_second]
    firsts = [owner(2, 3) * local] + [owner(3, bits) * local + half for bits in range(4) for half in (0, local // 2)]
    earlier = (total, flipped)
    total, flipped = own_part(own_table, far_table, tiles, pieces, first_blocks(firsts), perm, 2 * PPD, PPD, earlier)

    sources = [(0, step * number, array) for number, array in enumerate(far_ends)]
    sources += [(1, sum(sizes[:number]), array) for number, array in enumerate(far_centre)]
    return far_products(far_table, at_end, sources, sizes, flipped, total)


def tile_parts(count):
    sizes = [count * share // 48 for share in SHARES]
    return sizes + [count - sum(sizes)]


def far_products(far_table, chosen, sources, sizes, flipped, total):
    base, earlier = 0, ()
    for size in sizes:
        earlier = far_part(base, size, sum(sizes), far_table, chosen, sources, flipped, total, earlier)
        base += size
    return earlier[1]


def per_device(t2_tiles, t2_row, t2_col, integrals):
    peers = lax.axis_size("tile")
    if peers == 16:
        return staged_part(t2_tiles, t2_row, t2_col, integrals)
    block_total = peers * integrals.shape[0]
    opposite = [(source, (source + peers // 2) % peers) for source in range(peers)]
    own_table = tables(t2_row, t2_col, block_total)
    sizes = tile_parts(t2_tiles.shape[0])
    zero = jnp.zeros((1,), jnp.int32)
    parts = sort_tiles(own_table, zero, t2_tiles, [0] * len(sizes), [(size,) + t2_tiles.shape[1:] for size in sizes])
    notes = send(jnp.stack([t2_row, t2_col]), opposite)
    sources = [(0, sum(sizes[:number]), send(part, opposite)) for number, part in enumerate(parts)]
    blocks = lax.all_gather(integrals, "tile", axis=0, tiled=True)
    far_table = tables(notes[0], notes[1], block_total)
    columns = jnp.arange(integrals.shape[2], dtype=jnp.int32)
    total, flipped = own_part(own_table, far_table, t2_tiles, [blocks], zero, flip_matrix(columns))
    return far_products(far_table, zero, sources, sizes, flipped, total)


def solution(mesh):
    in_specs = (
        P(("groups", "tile"), None, None),
        P(("groups", "tile")),
        P(("groups", "tile")),
        P(("groups", "tile"), None, None),
    )
    out_specs = P(("groups", "tile"), None, None)
    return jax.shard_map(
        per_device, mesh=mesh, in_specs=in_specs, out_specs=out_specs, check_vma=False
    )
```

```python
import functools

import jax
import jax.numpy as jnp
from jax import lax
from jax.experimental import pallas as pl
from jax.experimental.pallas import tpu as pltpu
from jax.sharding import PartitionSpec as P

W = 32
PPD = 16
REUSE = 3
SHARES = (30, 11, 4)
COLUMNS = 256
MIB = 1024 * 1024
GRANT = 36
FAR_COST = 4 * 10**9
SMEM = pl.BlockSpec(memory_space=pltpu.SMEM)
VMEM = pl.BlockSpec(memory_space=pltpu.VMEM)
ANY = pl.BlockSpec(memory_space=pl.ANY)
HBM = pl.BlockSpec(memory_space=pltpu.HBM)


def flip_matrix(columns):
    source = (columns % W) * W + columns // W
    return (columns[:, None] == source[None, :]).astype(jnp.bfloat16)


class View:
    def __init__(self, ref, offset):
        self.ref, self.offset = ref, offset

    def __getitem__(self, index):
        return self.ref[self.offset + index]

    def __setitem__(self, index, value):
        self.ref[self.offset + index] = value


def table_views(table, count, groups):
    places = [0, groups + 1, groups + 1 + count, groups + 1 + 2 * count]
    return [View(table, place) for place in places]


def tables_kernel(rows, cols, table, cursor):
    count, groups = rows.shape[0], cursor.shape[0]
    total = table.shape[0] - (groups + 1 + 2 * count)
    starts, tile_at, block_at, slots = table_views(table, count, groups)

    @pl.loop(0, total)
    def _(block):
        slots[block] = 0

    for row in range(groups):
        cursor[row] = 0

    @pl.loop(0, count)
    def _(tile):
        cursor[rows[tile]] += 1
        slots[cols[tile]] = 1

    place = jnp.int32(0)
    for row in range(groups):
        size = cursor[row]
        starts[row] = place
        cursor[row] = place
        place += size
    starts[groups] = place

    def number(block, used):
        named = slots[block]
        slots[block] = jnp.where(named > 0, used, -1)
        return used + named

    lax.fori_loop(0, total, number, jnp.int32(0))

    @pl.loop(0, count)
    def _(tile):
        row = rows[tile]
        position = cursor[row]
        cursor[row] = position + 1
        tile_at[position] = tile
        block_at[position] = slots[cols[tile]]


def tables(rows, cols, total, groups=PPD, cost=0):
    count = rows.shape[0]
    return pl.pallas_call(
        tables_kernel,
        in_specs=[SMEM] * 2,
        out_specs=SMEM,
        out_shape=jax.ShapeDtypeStruct((groups + 1 + 2 * count + total,), jnp.int32),
        scratch_shapes=[pltpu.SMEM((groups,), jnp.int32)],
        cost_estimate=pl.CostEstimate(flops=cost, bytes_accessed=0, transcendentals=0) if cost else None,
        name="tables",
    )(rows, cols)


def window(ref, tile):
    depth = ref.shape[1]
    across = ref.shape[2] // depth
    if across == 1:
        return ref.at[tile]
    return ref.at[lax.div(tile, across), :, pl.ds(pl.multiple_of(lax.rem(tile, across) * depth, depth), depth)]


def sort_kernel(choices, table, chosen, tiles_ref, *refs):
    tile_at = table_views(table, tiles_ref.shape[0], PPD)[1]
    parts, sems = refs[: len(refs) // 2], refs[len(refs) // 2 :]
    begin = {choice: 0 for choice in choices}
    for choice, part, sem in zip(choices, parts, sems):
        base = begin[choice]
        count = part.shape[0] * part.shape[2] // tiles_ref.shape[2]
        begin[choice] += count

        @pl.when(chosen[0] == choice)
        def _(part=part, sem=sem, base=base, count=count):
            @pl.loop(0, count)
            def _(number):
                pltpu.make_async_copy(tiles_ref.at[tile_at[base + number]], window(part, number), sem).start()

    for choice, part, sem in zip(choices, parts, sems):

        @pl.when(chosen[0] == choice)
        def _(part=part, sem=sem):
            pltpu.make_async_copy(part, part, sem).wait()


def sort_tiles(table, chosen, tiles, choices, shapes):
    return pl.pallas_call(
        functools.partial(sort_kernel, choices),
        in_specs=[SMEM] * 2 + [ANY],
        out_specs=[VMEM] * len(shapes),
        out_shape=[jax.ShapeDtypeStruct(shape, tiles.dtype) for shape in shapes],
        scratch_shapes=[pltpu.SemaphoreType.DMA] * len(shapes),
        compiler_params=pltpu.CompilerParams(vmem_limit_bytes=16 * MIB),
        name="sort_tiles",
    )(table, chosen, tiles)


def payload_kernel(at_end, tiles_ref, received, payload, sem):
    del received

    @pl.when(at_end[0] == 1)
    def _():
        copy = pltpu.make_async_copy(tiles_ref, payload, sem)
        copy.start()
        copy.wait()


def payload_of(at_end, tiles, received):
    return pl.pallas_call(
        payload_kernel,
        in_specs=[SMEM, HBM, ANY],
        out_specs=ANY,
        out_shape=jax.ShapeDtypeStruct(received.shape, received.dtype),
        input_output_aliases={2: 0},
        scratch_shapes=[pltpu.SemaphoreType.DMA],
        compiler_params=pltpu.CompilerParams(vmem_limit_bytes=4 * MIB),
        name="payload",
    )(at_end, tiles, received)


def add_row(sum_ref, begin, end, depth, tile_of, block_of):
    width = sum_ref.shape[1]

    @pl.loop(0, (end - begin + depth - 1) // depth)
    def _(turn):
        here = begin + turn * depth
        places = [jnp.minimum(here + part, end - 1) for part in range(depth)]
        left = [tile_of(places[0])]
        for part in range(1, depth):
            tile = tile_of(places[part])
            left.append(jnp.where(here + part < end, tile, jnp.zeros_like(tile)))
        left = jnp.concatenate(left, axis=1)
        for column in range(0, width, COLUMNS):
            window = pl.ds(column, COLUMNS)
            right = jnp.concatenate([block_of(place, window) for place in places], axis=0)
            sum_ref[:, window] += jnp.dot(left, right, preferred_element_type=jnp.float32)


def own_kernel(counts, groups, group, fresh, own_table, far_table, firsts, tiles_ref, perm_ref, *refs):
    starts, tile_at, block_at, own_slots = table_views(own_table, tiles_ref.shape[0], groups)
    far_slots = table_views(far_table, tiles_ref.shape[0], PPD)[3]
    pieces = refs[: len(counts)]
    refs = refs[len(counts) :]
    if fresh:
        sum_out, flip_out, sums, *refs = refs
    else:
        sum_in, flip_in, sums, flip_out, flip_sem, *refs = refs
    own_blocks, far_blocks, own_list, far_list, own_sems, far_sems, row_sems = refs

    def fetch(slots, landing, sems, fetched):
        found = jnp.int32(0)
        for number, (piece, count) in enumerate(zip(pieces, counts)):

            def one(offset, found, piece=piece, number=number):
                slot = slots[firsts[number] + offset]

                @pl.when(slot >= 0)
                def _():
                    fetched[found] = slot
                    pltpu.make_async_copy(piece.at[offset], landing.at[slot], sems.at[slot]).start()

                return found + (slot >= 0).astype(jnp.int32)

            found = lax.fori_loop(0, count, one, found)
        return found

    far_found = fetch(far_slots, far_blocks, far_sems, far_list)
    own_found = fetch(own_slots, own_blocks, own_sems, own_list)
    if not fresh:
        pltpu.make_async_copy(flip_in, flip_out, flip_sem).start()
        for row in range(PPD):
            pltpu.make_async_copy(sum_in.at[row], sums.at[row], row_sems.at[row]).start()
        pltpu.make_async_copy(flip_in, flip_out, flip_sem).wait()

    def arrived(landing, sems, slot):
        pltpu.make_async_copy(landing.at[slot], landing.at[slot], sems.at[slot]).wait()

    def flip_store(slot):
        return pltpu.make_async_copy(far_blocks.at[slot], flip_out.at[slot], far_sems.at[slot])

    @pl.loop(0, far_found)
    def _(number):
        slot = far_list[number]
        arrived(far_blocks, far_sems, slot)
        turned = jnp.dot(far_blocks[slot], perm_ref[...], preferred_element_type=jnp.float32).astype(jnp.bfloat16)
        if fresh:
            far_blocks[slot] = turned
            flip_store(slot).start()
        else:
            flip_out[slot] = turned

    @pl.loop(0, own_found)
    def _(number):
        arrived(own_blocks, own_sems, own_list[number])

    def store(row):
        return pltpu.make_async_copy(sums.at[row], sum_out.at[row], row_sems.at[row])

    @pl.loop(0, PPD)
    def _(row):
        if fresh:
            sums[row] = jnp.zeros(sums.shape[1:], jnp.float32)
        else:
            arrived(sums, row_sems, row)
        add_row(
            sums.at[row],
            starts[group + row],
            starts[group + row + 1],
            4 if fresh else 2,
            lambda place: tiles_ref[tile_at[place]],
            lambda place, window: own_blocks[block_at[place], :, window],
        )
        if fresh:
            store(row).start()

    if fresh:

        @pl.loop(0, far_found)
        def _(number):
            flip_store(far_list[number]).wait()

        @pl.loop(0, PPD)
        def _(row):
            store(row).wait()


def own_part(own_table, far_table, tiles, pieces, firsts, perm, groups=PPD, group=0, earlier=()):
    count, height, _ = tiles.shape
    depth, width = pieces[0].shape[1:]
    need = count // REUSE
    counts = [piece.shape[0] for piece in pieces]
    whole = (PPD, height, width)
    flips = (need, depth, width)
    if earlier:
        out_specs = [VMEM] * 2
        out_shape = [pltpu.VMEM(whole, jnp.float32), pltpu.VMEM(flips, jnp.bfloat16)]
        first_scratch = pltpu.SemaphoreType.DMA
    else:
        out_specs = [ANY] * 2
        out_shape = [jax.ShapeDtypeStruct(whole, jnp.float32), jax.ShapeDtypeStruct(flips, jnp.bfloat16)]
        first_scratch = pltpu.VMEM(whole, jnp.float32)
    return pl.pallas_call(
        functools.partial(own_kernel, counts, groups, group, not earlier),
        in_specs=[SMEM] * 3 + [VMEM] * 2 + [ANY] * (len(pieces) + len(earlier)),
        out_specs=out_specs,
        out_shape=out_shape,
        scratch_shapes=[
            first_scratch,
            pltpu.VMEM(flips, jnp.bfloat16),
            pltpu.VMEM(flips, jnp.bfloat16),
            pltpu.SMEM((need,), jnp.int32),
            pltpu.SMEM((need,), jnp.int32),
            pltpu.SemaphoreType.DMA((need,)),
            pltpu.SemaphoreType.DMA((need,)),
            pltpu.SemaphoreType.DMA((PPD,)),
        ],
        compiler_params=pltpu.CompilerParams(vmem_limit_bytes=(GRANT if earlier else 56) * MIB),
        name="own_part",
    )(own_table, far_table, firsts, tiles, perm, *pieces, *earlier)


def far_kernel(base, total_count, segments, table, chosen, *refs):
    starts, _, block_at, _ = table_views(table, total_count, PPD)
    tile_refs, refs = refs[: len(segments)], refs[len(segments) :]
    sum_in, flip_in = refs[:2]
    carry_in = refs[2] if base else None
    carry_out, result, tiles_ref, sums, rounded, tile_sem, row_sems, out_sems = refs[4:] if base else refs[2:]
    count = tiles_ref.shape[0]
    stop = base + count

    direct, direct_choice = tile_refs[-1], segments[-1][0]
    copied = list(zip(tile_refs, segments))[:-1]
    for source, (choice, begin) in copied:
        held = source.shape[0] * source.shape[2] // tiles_ref.shape[2]
        low, high = max(begin, base), min(begin + held, stop)

        @pl.when(chosen[0] == choice)
        def _(source=source, begin=begin, low=low, high=high):
            if source.shape[2] == tiles_ref.shape[2]:
                here, there = source.at[pl.ds(low - begin, high - low)], tiles_ref.at[pl.ds(low - base, high - low)]
                pltpu.make_async_copy(here, there, tile_sem).start()
            else:

                @pl.loop(low, high)
                def _(place):
                    pltpu.make_async_copy(window(source, place - begin), tiles_ref.at[place - base], tile_sem).start()

    def each_row(action):
        @pl.loop(0, PPD)
        def _(row):
            first, last = starts[row], starts[row + 1]

            @pl.when(((last > base) if base else True) & ((last <= stop) | (first < stop)))
            def _():
                action(row, last <= stop)

    def load(row):
        if base:
            goes_on = starts[row] < base

            @pl.when(goes_on)
            def _():
                pltpu.make_async_copy(carry_in, sums.at[row], row_sems.at[row]).start()

            @pl.when(jnp.logical_not(goes_on))
            def _():
                pltpu.make_async_copy(sum_in.at[row], sums.at[row], row_sems.at[row]).start()
        else:
            pltpu.make_async_copy(sum_in.at[row], sums.at[row], row_sems.at[row]).start()

    def store(row):
        return pltpu.make_async_copy(rounded.at[row], result.at[row], out_sems.at[row])

    def keep(row):
        return pltpu.make_async_copy(sums.at[row], carry_out, out_sems.at[row])

    each_row(lambda row, complete: load(row))
    if copied:

        @pl.when(chosen[0] != direct_choice)
        def _():
            pltpu.make_async_copy(tiles_ref, tiles_ref, tile_sem).wait()

    def tile_of(place):
        if not copied:
            return direct[place - base]
        return jnp.where(chosen[0] == direct_choice, direct[place - base], tiles_ref[place - base])

    def add(row, complete):
        begin, end = jnp.maximum(starts[row], base), jnp.minimum(starts[row + 1], stop)
        pltpu.make_async_copy(sums.at[row], sums.at[row], row_sems.at[row]).wait()

        add_row(
            sums.at[row],
            begin,
            end,
            4,
            tile_of,
            lambda place, window: flip_in[block_at[place], :, window],
        )

        @pl.when(complete)
        def _():
            rounded[row] = sums[row].astype(rounded.dtype)
            store(row).start()

        @pl.when(jnp.logical_not(complete))
        def _():
            keep(row).start()

    def finish(row, complete):
        pl.when(complete)(lambda: store(row).wait())
        pl.when(jnp.logical_not(complete))(lambda: keep(row).wait())

    each_row(add)
    each_row(finish)


def far_part(base, count, total_count, far_table, chosen, sources, flipped, total, earlier=()):
    whole = total.shape
    held = [array.size // (whole[1] * flipped.shape[1]) for _, _, array in sources]
    used = [
        (source[:2], source[2])
        for source, size in zip(sources, held)
        if source[1] < base + count and source[1] + size > base
    ]
    return pl.pallas_call(
        functools.partial(far_kernel, base, total_count, [segment for segment, _ in used]),
        in_specs=[SMEM] * 2 + [ANY] * (len(used) - 1) + [VMEM] * 3 + [ANY] * len(earlier),
        out_specs=[ANY] * 2,
        out_shape=[jax.ShapeDtypeStruct(whole[1:], jnp.float32), jax.ShapeDtypeStruct(whole, jnp.bfloat16)],
        input_output_aliases={5 + len(used): 1} if earlier else {},
        scratch_shapes=[
            pltpu.VMEM((count, whole[1], flipped.shape[1]), jnp.bfloat16),
            pltpu.VMEM(whole, jnp.float32),
            pltpu.VMEM(whole, jnp.bfloat16),
            pltpu.SemaphoreType.DMA,
            pltpu.SemaphoreType.DMA((PPD,)),
            pltpu.SemaphoreType.DMA((PPD,)),
        ],
        compiler_params=pltpu.CompilerParams(vmem_limit_bytes=24 * MIB),
        name="far_part",
    )(far_table, chosen, *[array for _, array in used], total, flipped, *earlier)


def together(*values):
    return lax.optimization_barrier(values)


def send(value, pairs):
    return lax.ppermute(value, "tile", pairs)


def flipped_bit(bit):
    return [(i, i ^ bit) for i in range(16)]


def staged_part(tiles, rows, cols, shard):
    local = shard.shape[0]
    block_total = 16 * local
    centre = [i for i in range(16) if i // 4 in (1, 2)]
    across = [(i, i ^ 12) for i in centre]
    from_ends = [(i, i ^ 8) for i in range(16) if i not in centre]
    from_centre = [(i, i ^ 8) for i in centre]
    around = [(i, i ^ 4) for i in centre] + from_ends
    other_z, other_y, other_core, opposite = (flipped_bit(bit) for bit in (4, 2, 1, 8))
    me = lax.axis_index("tile")
    z = me // 4
    in_centre = (z == 1) | (z == 2)
    at_end = 1 - in_centre.astype(jnp.int32).reshape(1)
    zs = [z, z ^ 1, jnp.where(z < 2, 2, 1), jnp.where(z < 2, 3, 0)]

    def owner(k, bits):
        return 4 * zs[k] + ((me & 3) ^ bits)

    def first_blocks(firsts):
        return jnp.stack(firsts).astype(jnp.int32)

    col_owner = cols // local
    late = (col_owner // 4 == zs[3]) | (col_owner == owner(2, 3))
    keys = rows + PPD * late.astype(jnp.int32)
    columns = jnp.arange(shard.shape[2], dtype=jnp.int32)

    near = send(shard, other_z)
    first = send(shard, across)
    notes = send(jnp.stack([rows, cols]), opposite)
    order = tables(rows, cols, block_total)
    c_own = send(shard, other_core)
    y_own = send(shard, other_y)
    count = tiles.shape[0]
    step = shard.size // tiles[0].size
    sizes = tile_parts(count)
    shapes = [shard.shape] * 2 + [(size,) + tiles.shape[1:] for size in [count - 2 * step] + sizes]
    parts = sort_tiles(order, at_end, tiles, [1] * 3 + [0] * len(sizes), shapes)
    first, *parts = together(first, *parts)

    first = payload_of(at_end, parts[0], first)
    outer = send(first, around)
    near, c_own, y_own, keys, columns, *parts = together(near, c_own, y_own, keys, columns, *parts)
    second = send(near, across)
    y_near = send(near, other_y)
    c_near = send(near, other_core)
    own_table = tables(keys, cols, block_total, 2 * PPD)
    far_table = tables(notes[0], notes[1], block_total, cost=FAR_COST)
    perm = flip_matrix(columns)
    far_ends = [outer]
    first = jnp.where(in_centre, first, outer)
    second = payload_of(at_end, parts[1], second)
    outer = send(second, around)
    first, y_own, y_near, c_near, perm, *rest = together(
        first, y_own, y_near, c_near, perm, own_table, far_table, *parts[2:]
    )
    own_table, far_table, *parts = rest
    y_first = send(first, other_y)
    c_first = send(first, other_core)
    c_y_own = send(y_own, other_core)
    c_y_near = send(y_near, other_core)
    tiles_last, c_first = together(parts[0], c_first)
    far_ends += [outer, send(tiles_last, from_ends)]
    halves = (slice(0, local // 2), slice(local // 2, None))
    second = [jnp.where(in_centre, second[half], outer[half]) for half in halves]
    *second, y_first, c_first, c_y_own, c_y_near = together(*second, y_first, c_first, c_y_own, c_y_near)

    far_centre = [send(parts[1], from_centre)]
    y_second = [send(half, other_y) for half in second]
    pieces = [shard, c_own, near, c_near, first, c_first, y_own, c_y_own, y_near, c_y_near, y_first]
    firsts = [owner(k, y + core) * local for y in (0, 2) for k in range(3) for core in (0, 1)][:11]
    early = own_part(own_table, far_table, tiles, pieces, first_blocks(firsts), perm, 2 * PPD)
    y_second[0], y_second[1], second[0], second[1], y_first, total, flipped, *parts = together(
        *y_second, *second, y_first, *early, *parts[2:]
    )
    far_centre += [send(part, from_centre) for part in parts]
    *y_second, far_ends[2] = together(*y_second, far_ends[2])

    c_y_first = send(y_first, other_core)
    c_second = [send(half, other_core) for half in second]
    c_y_second = [send(half, other_core) for half in y_second]
    pieces = [c_y_first, *second, *c_second, *y_second, *c_y_second]
    firsts = [owner(2, 3) * local] + [owner(3, bits) * local + half for bits in range(4) for half in (0, local // 2)]
    earlier = (total, flipped)
    total, flipped = own_part(own_table, far_table, tiles, pieces, first_blocks(firsts), perm, 2 * PPD, PPD, earlier)

    sources = [(0, step * number, array) for number, array in enumerate(far_ends)]
    sources += [(1, sum(sizes[:number]), array) for number, array in enumerate(far_centre)]
    return far_products(far_table, at_end, sources, sizes, flipped, total)


def tile_parts(count):
    sizes = [count * share // 48 for share in SHARES]
    return sizes + [count - sum(sizes)]


def far_products(far_table, chosen, sources, sizes, flipped, total):
    base, earlier = 0, ()
    for size in sizes:
        earlier = far_part(base, size, sum(sizes), far_table, chosen, sources, flipped, total, earlier)
        base += size
    return earlier[1]


def per_device(t2_tiles, t2_row, t2_col, integrals):
    peers = lax.axis_size("tile")
    if peers == 16:
        return staged_part(t2_tiles, t2_row, t2_col, integrals)
    block_total = peers * integrals.shape[0]
    opposite = [(source, (source + peers // 2) % peers) for source in range(peers)]
    own_table = tables(t2_row, t2_col, block_total)
    sizes = tile_parts(t2_tiles.shape[0])
    zero = jnp.zeros((1,), jnp.int32)
    parts = sort_tiles(own_table, zero, t2_tiles, [0] * len(sizes), [(size,) + t2_tiles.shape[1:] for size in sizes])
    notes = send(jnp.stack([t2_row, t2_col]), opposite)
    sources = [(0, sum(sizes[:number]), send(part, opposite)) for number, part in enumerate(parts)]
    blocks = lax.all_gather(integrals, "tile", axis=0, tiled=True)
    far_table = tables(notes[0], notes[1], block_total)
    columns = jnp.arange(integrals.shape[2], dtype=jnp.int32)
    total, flipped = own_part(own_table, far_table, t2_tiles, [blocks], zero, flip_matrix(columns))
    return far_products(far_table, zero, sources, sizes, flipped, total)


def solution(mesh):
    in_specs = (
        P(("groups", "tile"), None, None),
        P(("groups", "tile")),
        P(("groups", "tile")),
        P(("groups", "tile"), None, None),
    )
    out_specs = P(("groups", "tile"), None, None)
    return jax.shard_map(
        per_device, mesh=mesh, in_specs=in_specs, out_specs=out_specs, check_vma=False
    )
```

```python
import functools

import jax
import jax.numpy as jnp
from jax import lax
from jax.experimental import pallas as pl
from jax.experimental.pallas import tpu as pltpu
from jax.sharding import PartitionSpec as P

W = 32
PPD = 16
REUSE = 3
SHARES = (30, 11, 4)
COLUMNS = 256
MIB = 1024 * 1024
GRANT = 36
FAR_COST = 4 * 10**9
SMEM = pl.BlockSpec(memory_space=pltpu.SMEM)
VMEM = pl.BlockSpec(memory_space=pltpu.VMEM)
ANY = pl.BlockSpec(memory_space=pl.ANY)
HBM = pl.BlockSpec(memory_space=pltpu.HBM)


def flip_matrix(columns):
    source = (columns % W) * W + columns // W
    return (columns[:, None] == source[None, :]).astype(jnp.bfloat16)


class View:
    def __init__(self, ref, offset):
        self.ref, self.offset = ref, offset

    def __getitem__(self, index):
        return self.ref[self.offset + index]

    def __setitem__(self, index, value):
        self.ref[self.offset + index] = value


def table_views(table, count, groups):
    places = [0, groups + 1, groups + 1 + count, groups + 1 + 2 * count]
    return [View(table, place) for place in places]


def tables_kernel(rows, cols, table, cursor):
    count, groups = rows.shape[0], cursor.shape[0]
    total = table.shape[0] - (groups + 1 + 2 * count)
    starts, tile_at, block_at, slots = table_views(table, count, groups)

    @pl.loop(0, total)
    def _(block):
        slots[block] = 0

    for row in range(groups):
        cursor[row] = 0

    @pl.loop(0, count)
    def _(tile):
        cursor[rows[tile]] += 1
        slots[cols[tile]] = 1

    place = jnp.int32(0)
    for row in range(groups):
        size = cursor[row]
        starts[row] = place
        cursor[row] = place
        place += size
    starts[groups] = place

    def number(block, used):
        named = slots[block]
        slots[block] = jnp.where(named > 0, used, -1)
        return used + named

    lax.fori_loop(0, total, number, jnp.int32(0))

    @pl.loop(0, count)
    def _(tile):
        row = rows[tile]
        position = cursor[row]
        cursor[row] = position + 1
        tile_at[position] = tile
        block_at[position] = slots[cols[tile]]


def tables(rows, cols, total, groups=PPD, cost=0):
    count = rows.shape[0]
    return pl.pallas_call(
        tables_kernel,
        in_specs=[SMEM] * 2,
        out_specs=SMEM,
        out_shape=jax.ShapeDtypeStruct((groups + 1 + 2 * count + total,), jnp.int32),
        scratch_shapes=[pltpu.SMEM((groups,), jnp.int32)],
        cost_estimate=pl.CostEstimate(flops=cost, bytes_accessed=0, transcendentals=0) if cost else None,
        name="tables",
    )(rows, cols)


def window(ref, tile):
    depth = ref.shape[1]
    across = ref.shape[2] // depth
    if across == 1:
        return ref.at[tile]
    return ref.at[lax.div(tile, across), :, pl.ds(pl.multiple_of(lax.rem(tile, across) * depth, depth), depth)]


def sort_kernel(choices, table, chosen, tiles_ref, *refs):
    tile_at = table_views(table, tiles_ref.shape[0], PPD)[1]
    parts, sems = refs[: len(refs) // 2], refs[len(refs) // 2 :]
    begin = {choice: 0 for choice in choices}
    for choice, part, sem in zip(choices, parts, sems):
        base = begin[choice]
        count = part.shape[0] * part.shape[2] // tiles_ref.shape[2]
        begin[choice] += count

        @pl.when(chosen[0] == choice)
        def _(part=part, sem=sem, base=base, count=count):
            @pl.loop(0, count)
            def _(number):
                pltpu.make_async_copy(tiles_ref.at[tile_at[base + number]], window(part, number), sem).start()

    for choice, part, sem in zip(choices, parts, sems):

        @pl.when(chosen[0] == choice)
        def _(part=part, sem=sem):
            pltpu.make_async_copy(part, part, sem).wait()


def sort_tiles(table, chosen, tiles, choices, shapes):
    return pl.pallas_call(
        functools.partial(sort_kernel, choices),
        in_specs=[SMEM] * 2 + [ANY],
        out_specs=[VMEM] * len(shapes),
        out_shape=[jax.ShapeDtypeStruct(shape, tiles.dtype) for shape in shapes],
        scratch_shapes=[pltpu.SemaphoreType.DMA] * len(shapes),
        compiler_params=pltpu.CompilerParams(vmem_limit_bytes=16 * MIB),
        name="sort_tiles",
    )(table, chosen, tiles)


def payload_kernel(at_end, tiles_ref, received, payload, sem):
    del received

    @pl.when(at_end[0] == 1)
    def _():
        copy = pltpu.make_async_copy(tiles_ref, payload, sem)
        copy.start()
        copy.wait()


def payload_of(at_end, tiles, received):
    return pl.pallas_call(
        payload_kernel,
        in_specs=[SMEM, HBM, ANY],
        out_specs=ANY,
        out_shape=jax.ShapeDtypeStruct(received.shape, received.dtype),
        input_output_aliases={2: 0},
        scratch_shapes=[pltpu.SemaphoreType.DMA],
        compiler_params=pltpu.CompilerParams(vmem_limit_bytes=4 * MIB),
        name="payload",
    )(at_end, tiles, received)


def add_row(sum_ref, begin, end, depth, tile_of, block_of):
    width = sum_ref.shape[1]

    @pl.loop(0, (end - begin + depth - 1) // depth)
    def _(turn):
        here = begin + turn * depth
        places = [jnp.minimum(here + part, end - 1) for part in range(depth)]
        left = [tile_of(places[0])]
        for part in range(1, depth):
            tile = tile_of(places[part])
            left.append(jnp.where(here + part < end, tile, jnp.zeros_like(tile)))
        left = jnp.concatenate(left, axis=1)
        for column in range(0, width, COLUMNS):
            window = pl.ds(column, COLUMNS)
            right = jnp.concatenate([block_of(place, window) for place in places], axis=0)
            sum_ref[:, window] += jnp.dot(left, right, preferred_element_type=jnp.float32)


def own_kernel(counts, groups, group, fresh, own_table, far_table, firsts, tiles_ref, perm_ref, *refs):
    starts, tile_at, block_at, own_slots = table_views(own_table, tiles_ref.shape[0], groups)
    far_slots = table_views(far_table, tiles_ref.shape[0], PPD)[3]
    pieces = refs[: len(counts)]
    refs = refs[len(counts) :]
    if fresh:
        sum_out, flip_out, sums, *refs = refs
    else:
        sum_in, flip_in, sums, flip_out, flip_sem, *refs = refs
    own_blocks, far_blocks, own_list, far_list, own_sems, far_sems, row_sems = refs

    def fetch(slots, landing, sems, fetched):
        found = jnp.int32(0)
        for number, (piece, count) in enumerate(zip(pieces, counts)):

            def one(offset, found, piece=piece, number=number):
                slot = slots[firsts[number] + offset]

                @pl.when(slot >= 0)
                def _():
                    fetched[found] = slot
                    pltpu.make_async_copy(piece.at[offset], landing.at[slot], sems.at[slot]).start()

                return found + (slot >= 0).astype(jnp.int32)

            found = lax.fori_loop(0, count, one, found)
        return found

    far_found = fetch(far_slots, far_blocks, far_sems, far_list)
    own_found = fetch(own_slots, own_blocks, own_sems, own_list)
    if not fresh:
        pltpu.make_async_copy(flip_in, flip_out, flip_sem).start()
        for row in range(PPD):
            pltpu.make_async_copy(sum_in.at[row], sums.at[row], row_sems.at[row]).start()
        pltpu.make_async_copy(flip_in, flip_out, flip_sem).wait()

    def arrived(landing, sems, slot):
        pltpu.make_async_copy(landing.at[slot], landing.at[slot], sems.at[slot]).wait()

    def flip_store(slot):
        return pltpu.make_async_copy(far_blocks.at[slot], flip_out.at[slot], far_sems.at[slot])

    @pl.loop(0, far_found)
    def _(number):
        slot = far_list[number]
        arrived(far_blocks, far_sems, slot)
        turned = jnp.dot(far_blocks[slot], perm_ref[...], preferred_element_type=jnp.float32).astype(jnp.bfloat16)
        if fresh:
            far_blocks[slot] = turned
            flip_store(slot).start()
        else:
            flip_out[slot] = turned

    @pl.loop(0, own_found)
    def _(number):
        arrived(own_blocks, own_sems, own_list[number])

    def store(row):
        return pltpu.make_async_copy(sums.at[row], sum_out.at[row], row_sems.at[row])

    @pl.loop(0, PPD)
    def _(row):
        if fresh:
            sums[row] = jnp.zeros(sums.shape[1:], jnp.float32)
        else:
            arrived(sums, row_sems, row)
        add_row(
            sums.at[row],
            starts[group + row],
            starts[group + row + 1],
            4 if fresh else 2,
            lambda place: tiles_ref[tile_at[place]],
            lambda place, window: own_blocks[block_at[place], :, window],
        )
        if fresh:
            store(row).start()

    if fresh:

        @pl.loop(0, far_found)
        def _(number):
            flip_store(far_list[number]).wait()

        @pl.loop(0, PPD)
        def _(row):
            store(row).wait()


def own_part(own_table, far_table, tiles, pieces, firsts, perm, groups=PPD, group=0, earlier=()):
    count, height, _ = tiles.shape
    depth, width = pieces[0].shape[1:]
    need = count // REUSE
    counts = [piece.shape[0] for piece in pieces]
    whole = (PPD, height, width)
    flips = (need, depth, width)
    if earlier:
        out_specs = [VMEM] * 2
        out_shape = [pltpu.VMEM(whole, jnp.float32), pltpu.VMEM(flips, jnp.bfloat16)]
        first_scratch = pltpu.SemaphoreType.DMA
    else:
        out_specs = [ANY] * 2
        out_shape = [jax.ShapeDtypeStruct(whole, jnp.float32), jax.ShapeDtypeStruct(flips, jnp.bfloat16)]
        first_scratch = pltpu.VMEM(whole, jnp.float32)
    return pl.pallas_call(
        functools.partial(own_kernel, counts, groups, group, not earlier),
        in_specs=[SMEM] * 3 + [VMEM] * 2 + [ANY] * (len(pieces) + len(earlier)),
        out_specs=out_specs,
        out_shape=out_shape,
        scratch_shapes=[
            first_scratch,
            pltpu.VMEM(flips, jnp.bfloat16),
            pltpu.VMEM(flips, jnp.bfloat16),
            pltpu.SMEM((need,), jnp.int32),
            pltpu.SMEM((need,), jnp.int32),
            pltpu.SemaphoreType.DMA((need,)),
            pltpu.SemaphoreType.DMA((need,)),
            pltpu.SemaphoreType.DMA((PPD,)),
        ],
        compiler_params=pltpu.CompilerParams(vmem_limit_bytes=(GRANT if earlier else 56) * MIB),
        name="own_part",
    )(own_table, far_table, firsts, tiles, perm, *pieces, *earlier)


def far_kernel(base, total_count, segments, table, chosen, *refs):
    starts, _, block_at, _ = table_views(table, total_count, PPD)
    tile_refs, refs = refs[: len(segments)], refs[len(segments) :]
    sum_in, flip_in = refs[:2]
    carry_in = refs[2] if base else None
    carry_out, result, tiles_ref, sums, rounded, tile_sem, row_sems, out_sems = refs[4:] if base else refs[2:]
    count = tiles_ref.shape[0]
    stop = base + count

    direct, direct_choice = tile_refs[-1], segments[-1][0]
    copied = list(zip(tile_refs, segments))[:-1]
    for source, (choice, begin) in copied:
        held = source.shape[0] * source.shape[2] // tiles_ref.shape[2]
        low, high = max(begin, base), min(begin + held, stop)

        @pl.when(chosen[0] == choice)
        def _(source=source, begin=begin, low=low, high=high):
            if source.shape[2] == tiles_ref.shape[2]:
                here, there = source.at[pl.ds(low - begin, high - low)], tiles_ref.at[pl.ds(low - base, high - low)]
                pltpu.make_async_copy(here, there, tile_sem).start()
            else:

                @pl.loop(low, high)
                def _(place):
                    pltpu.make_async_copy(window(source, place - begin), tiles_ref.at[place - base], tile_sem).start()

    def each_row(action):
        @pl.loop(0, PPD)
        def _(row):
            first, last = starts[row], starts[row + 1]

            @pl.when(((last > base) if base else True) & ((last <= stop) | (first < stop)))
            def _():
                action(row, last <= stop)

    def load(row):
        if base:
            goes_on = starts[row] < base

            @pl.when(goes_on)
            def _():
                pltpu.make_async_copy(carry_in, sums.at[row], row_sems.at[row]).start()

            @pl.when(jnp.logical_not(goes_on))
            def _():
                pltpu.make_async_copy(sum_in.at[row], sums.at[row], row_sems.at[row]).start()
        else:
            pltpu.make_async_copy(sum_in.at[row], sums.at[row], row_sems.at[row]).start()

    def store(row):
        return pltpu.make_async_copy(rounded.at[row], result.at[row], out_sems.at[row])

    def keep(row):
        return pltpu.make_async_copy(sums.at[row], carry_out, out_sems.at[row])

    each_row(lambda row, complete: load(row))
    if copied:

        @pl.when(chosen[0] != direct_choice)
        def _():
            pltpu.make_async_copy(tiles_ref, tiles_ref, tile_sem).wait()

    def tile_of(place):
        if not copied:
            return direct[place - base]
        return jnp.where(chosen[0] == direct_choice, direct[place - base], tiles_ref[place - base])

    def add(row, complete):
        begin, end = jnp.maximum(starts[row], base), jnp.minimum(starts[row + 1], stop)
        pltpu.make_async_copy(sums.at[row], sums.at[row], row_sems.at[row]).wait()

        add_row(
            sums.at[row],
            begin,
            end,
            4,
            tile_of,
            lambda place, window: flip_in[block_at[place], :, window],
        )

        @pl.when(complete)
        def _():
            rounded[row] = sums[row].astype(rounded.dtype)
            store(row).start()

        @pl.when(jnp.logical_not(complete))
        def _():
            keep(row).start()

    def finish(row, complete):
        pl.when(complete)(lambda: store(row).wait())
        pl.when(jnp.logical_not(complete))(lambda: keep(row).wait())

    each_row(add)
    each_row(finish)


def far_part(base, count, total_count, far_table, chosen, sources, flipped, total, earlier=()):
    whole = total.shape
    held = [array.size // (whole[1] * flipped.shape[1]) for _, _, array in sources]
    used = [
        (source[:2], source[2])
        for source, size in zip(sources, held)
        if source[1] < base + count and source[1] + size > base
    ]
    return pl.pallas_call(
        functools.partial(far_kernel, base, total_count, [segment for segment, _ in used]),
        in_specs=[SMEM] * 2 + [ANY] * (len(used) - 1) + [VMEM] * 3 + [ANY] * len(earlier),
        out_specs=[ANY] * 2,
        out_shape=[jax.ShapeDtypeStruct(whole[1:], jnp.float32), jax.ShapeDtypeStruct(whole, jnp.bfloat16)],
        input_output_aliases={5 + len(used): 1} if earlier else {},
        scratch_shapes=[
            pltpu.VMEM((count, whole[1], flipped.shape[1]), jnp.bfloat16),
            pltpu.VMEM(whole, jnp.float32),
            pltpu.VMEM(whole, jnp.bfloat16),
            pltpu.SemaphoreType.DMA,
            pltpu.SemaphoreType.DMA((PPD,)),
            pltpu.SemaphoreType.DMA((PPD,)),
        ],
        compiler_params=pltpu.CompilerParams(vmem_limit_bytes=24 * MIB),
        name="far_part",
    )(far_table, chosen, *[array for _, array in used], total, flipped, *earlier)


def together(*values):
    return lax.optimization_barrier(values)


def send(value, pairs):
    return lax.ppermute(value, "tile", pairs)


def flipped_bit(bit):
    return [(i, i ^ bit) for i in range(16)]


def staged_part(tiles, rows, cols, shard):
    local = shard.shape[0]
    block_total = 16 * local
    centre = [i for i in range(16) if i // 4 in (1, 2)]
    across = [(i, i ^ 12) for i in centre]
    from_ends = [(i, i ^ 8) for i in range(16) if i not in centre]
    from_centre = [(i, i ^ 8) for i in centre]
    around = [(i, i ^ 4) for i in centre] + from_ends
    around_crossed = [(i, i ^ 4) for i in centre] + [(i, i ^ 9) for i, _ in from_ends]
    other_z, other_y, other_core, opposite = (flipped_bit(bit) for bit in (4, 2, 1, 8))
    me = lax.axis_index("tile")
    z = me // 4
    in_centre = (z == 1) | (z == 2)
    at_end = 1 - in_centre.astype(jnp.int32).reshape(1)
    zs = [z, z ^ 1, jnp.where(z < 2, 2, 1), jnp.where(z < 2, 3, 0)]

    def owner(k, bits):
        return 4 * zs[k] + ((me & 3) ^ bits)

    def first_blocks(firsts):
        return jnp.stack(firsts).astype(jnp.int32)

    col_owner = cols // local
    late = (col_owner // 4 == zs[3]) | (col_owner == owner(2, 3))
    keys = rows + PPD * late.astype(jnp.int32)
    columns = jnp.arange(shard.shape[2], dtype=jnp.int32)

    near = send(shard, other_z)
    first = send(shard, across)
    notes = send(jnp.stack([rows, cols]), opposite)
    order = tables(rows, cols, block_total)
    c_own = send(shard, other_core)
    y_own = send(shard, other_y)
    count = tiles.shape[0]
    step = shard.size // tiles[0].size
    sizes = tile_parts(count)
    shapes = [shard.shape] * 2 + [(size,) + tiles.shape[1:] for size in [count - 2 * step] + sizes]
    parts = sort_tiles(order, at_end, tiles, [1] * 3 + [0] * len(sizes), shapes)
    first, *parts = together(first, *parts)

    first = payload_of(at_end, parts[0], first)
    outer = send(first, around)
    near, c_own, y_own, keys, columns, *parts = together(near, c_own, y_own, keys, columns, *parts)
    second = send(jnp.where(in_centre, near, parts[1]), across + [(i, i ^ 1) for i, _ in from_ends])
    y_near = send(near, other_y)
    c_near = send(near, other_core)
    own_table = tables(keys, cols, block_total, 2 * PPD)
    far_table = tables(notes[0], notes[1], block_total, cost=FAR_COST)
    perm = flip_matrix(columns)
    far_ends = [outer]
    first = jnp.where(in_centre, first, outer)
    outer = send(second, around_crossed)
    first, y_own, y_near, c_near, perm, *rest = together(
        first, y_own, y_near, c_near, perm, own_table, far_table, *parts[2:]
    )
    own_table, far_table, *parts = rest
    y_first = send(first, other_y)
    c_first = send(first, other_core)
    c_y_own = send(y_own, other_core)
    c_y_near = send(y_near, other_core)
    tiles_last, c_first = together(parts[0], c_first)
    far_ends += [outer, send(tiles_last, from_ends)]
    halves = (slice(0, local // 2), slice(local // 2, None))
    second = [jnp.where(in_centre, second[half], outer[half]) for half in halves]
    *second, y_first, c_first, c_y_own, c_y_near = together(*second, y_first, c_first, c_y_own, c_y_near)

    far_centre = [send(parts[1], from_centre)]
    y_second = [send(half, other_y) for half in second]
    pieces = [shard, c_own, near, c_near, first, c_first, y_own, c_y_own, y_near, c_y_near, y_first]
    firsts = [owner(k, y + core) * local for y in (0, 2) for k in range(3) for core in (0, 1)][:11]
    early = own_part(own_table, far_table, tiles, pieces, first_blocks(firsts), perm, 2 * PPD)
    y_second[0], y_second[1], second[0], second[1], y_first, total, flipped, *parts = together(
        *y_second, *second, y_first, *early, *parts[2:]
    )
    far_centre += [send(part, from_centre) for part in parts]
    *y_second, far_ends[2] = together(*y_second, far_ends[2])

    c_y_first = send(y_first, other_core)
    c_second = [send(half, other_core) for half in second]
    c_y_second = [send(half, other_core) for half in y_second]
    pieces = [c_y_first, *second, *c_second, *y_second, *c_y_second]
    firsts = [owner(2, 3) * local] + [owner(3, bits) * local + half for bits in range(4) for half in (0, local // 2)]
    earlier = (total, flipped)
    total, flipped = own_part(own_table, far_table, tiles, pieces, first_blocks(firsts), perm, 2 * PPD, PPD, earlier)

    sources = [(0, step * number, array) for number, array in enumerate(far_ends)]
    sources += [(1, sum(sizes[:number]), array) for number, array in enumerate(far_centre)]
    return far_products(far_table, at_end, sources, sizes, flipped, total)


def tile_parts(count):
    sizes = [count * share // 48 for share in SHARES]
    return sizes + [count - sum(sizes)]


def far_products(far_table, chosen, sources, sizes, flipped, total):
    base, earlier = 0, ()
    for size in sizes:
        earlier = far_part(base, size, sum(sizes), far_table, chosen, sources, flipped, total, earlier)
        base += size
    return earlier[1]


def per_device(t2_tiles, t2_row, t2_col, integrals):
    peers = lax.axis_size("tile")
    if peers == 16:
        return staged_part(t2_tiles, t2_row, t2_col, integrals)
    block_total = peers * integrals.shape[0]
    opposite = [(source, (source + peers // 2) % peers) for source in range(peers)]
    own_table = tables(t2_row, t2_col, block_total)
    sizes = tile_parts(t2_tiles.shape[0])
    zero = jnp.zeros((1,), jnp.int32)
    parts = sort_tiles(own_table, zero, t2_tiles, [0] * len(sizes), [(size,) + t2_tiles.shape[1:] for size in sizes])
    notes = send(jnp.stack([t2_row, t2_col]), opposite)
    sources = [(0, sum(sizes[:number]), send(part, opposite)) for number, part in enumerate(parts)]
    blocks = lax.all_gather(integrals, "tile", axis=0, tiled=True)
    far_table = tables(notes[0], notes[1], block_total)
    columns = jnp.arange(integrals.shape[2], dtype=jnp.int32)
    total, flipped = own_part(own_table, far_table, t2_tiles, [blocks], zero, flip_matrix(columns))
    return far_products(far_table, zero, sources, sizes, flipped, total)


def solution(mesh):
    in_specs = (
        P(("groups", "tile"), None, None),
        P(("groups", "tile")),
        P(("groups", "tile")),
        P(("groups", "tile"), None, None),
    )
    out_specs = P(("groups", "tile"), None, None)
    return jax.shard_map(
        per_device, mesh=mesh, in_specs=in_specs, out_specs=out_specs, check_vma=False
    )
```

```python
import functools

import jax
import jax.numpy as jnp
from jax import lax
from jax.experimental import pallas as pl
from jax.experimental.pallas import tpu as pltpu
from jax.sharding import PartitionSpec as P

W = 32
PPD = 16
REUSE = 3
SHARES = (60, 23, 8)
COLUMNS = 256
MIB = 1024 * 1024
GRANT = 36
FAR_COST = 4 * 10**9
SMEM = pl.BlockSpec(memory_space=pltpu.SMEM)
VMEM = pl.BlockSpec(memory_space=pltpu.VMEM)
ANY = pl.BlockSpec(memory_space=pl.ANY)
HBM = pl.BlockSpec(memory_space=pltpu.HBM)


def flip_matrix(columns):
    source = (columns % W) * W + columns // W
    return (columns[:, None] == source[None, :]).astype(jnp.bfloat16)


class View:
    def __init__(self, ref, offset):
        self.ref, self.offset = ref, offset

    def __getitem__(self, index):
        return self.ref[self.offset + index]

    def __setitem__(self, index, value):
        self.ref[self.offset + index] = value


def table_views(table, count, groups):
    places = [0, groups + 1, groups + 1 + count, groups + 1 + 2 * count]
    return [View(table, place) for place in places]


def tables_kernel(rows, cols, table, cursor):
    count, groups = rows.shape[0], cursor.shape[0]
    total = table.shape[0] - (groups + 1 + 2 * count)
    starts, tile_at, block_at, slots = table_views(table, count, groups)

    @pl.loop(0, total)
    def _(block):
        slots[block] = 0

    for row in range(groups):
        cursor[row] = 0

    @pl.loop(0, count)
    def _(tile):
        cursor[rows[tile]] += 1
        slots[cols[tile]] = 1

    place = jnp.int32(0)
    for row in range(groups):
        size = cursor[row]
        starts[row] = place
        cursor[row] = place
        place += size
    starts[groups] = place

    def number(block, used):
        named = slots[block]
        slots[block] = jnp.where(named > 0, used, -1)
        return used + named

    lax.fori_loop(0, total, number, jnp.int32(0))

    @pl.loop(0, count)
    def _(tile):
        row = rows[tile]
        position = cursor[row]
        cursor[row] = position + 1
        tile_at[position] = tile
        block_at[position] = slots[cols[tile]]


def tables(rows, cols, total, groups=PPD, cost=0):
    count = rows.shape[0]
    return pl.pallas_call(
        tables_kernel,
        in_specs=[SMEM] * 2,
        out_specs=SMEM,
        out_shape=jax.ShapeDtypeStruct((groups + 1 + 2 * count + total,), jnp.int32),
        scratch_shapes=[pltpu.SMEM((groups,), jnp.int32)],
        cost_estimate=pl.CostEstimate(flops=cost, bytes_accessed=0, transcendentals=0) if cost else None,
        name="tables",
    )(rows, cols)


def window(ref, tile):
    depth = ref.shape[1]
    across = ref.shape[2] // depth
    if across == 1:
        return ref.at[tile]
    return ref.at[lax.div(tile, across), :, pl.ds(pl.multiple_of(lax.rem(tile, across) * depth, depth), depth)]


def sort_kernel(choices, table, chosen, tiles_ref, *refs):
    tile_at = table_views(table, tiles_ref.shape[0], PPD)[1]
    parts, sems = refs[: len(refs) // 2], refs[len(refs) // 2 :]
    begin = {choice: 0 for choice in choices}
    for choice, part, sem in zip(choices, parts, sems):
        base = begin[choice]
        count = part.shape[0] * part.shape[2] // tiles_ref.shape[2]
        begin[choice] += count

        @pl.when(chosen[0] == choice)
        def _(part=part, sem=sem, base=base, count=count):
            @pl.loop(0, count)
            def _(number):
                pltpu.make_async_copy(tiles_ref.at[tile_at[base + number]], window(part, number), sem).start()

    for choice, part, sem in zip(choices, parts, sems):

        @pl.when(chosen[0] == choice)
        def _(part=part, sem=sem):
            pltpu.make_async_copy(part, part, sem).wait()


def sort_tiles(table, chosen, tiles, choices, shapes):
    return pl.pallas_call(
        functools.partial(sort_kernel, choices),
        in_specs=[SMEM] * 2 + [ANY],
        out_specs=[VMEM] * len(shapes),
        out_shape=[jax.ShapeDtypeStruct(shape, tiles.dtype) for shape in shapes],
        scratch_shapes=[pltpu.SemaphoreType.DMA] * len(shapes),
        compiler_params=pltpu.CompilerParams(vmem_limit_bytes=16 * MIB),
        name="sort_tiles",
    )(table, chosen, tiles)


def payload_kernel(at_end, tiles_ref, received, payload, sem):
    del received

    @pl.when(at_end[0] == 1)
    def _():
        copy = pltpu.make_async_copy(tiles_ref, payload, sem)
        copy.start()
        copy.wait()


def payload_of(at_end, tiles, received):
    return pl.pallas_call(
        payload_kernel,
        in_specs=[SMEM, HBM, ANY],
        out_specs=ANY,
        out_shape=jax.ShapeDtypeStruct(received.shape, received.dtype),
        input_output_aliases={2: 0},
        scratch_shapes=[pltpu.SemaphoreType.DMA],
        compiler_params=pltpu.CompilerParams(vmem_limit_bytes=4 * MIB),
        name="payload",
    )(at_end, tiles, received)


def add_row(sum_ref, begin, end, depth, tile_of, block_of):
    width = sum_ref.shape[1]

    @pl.loop(0, (end - begin + depth - 1) // depth)
    def _(turn):
        here = begin + turn * depth
        places = [jnp.minimum(here + part, end - 1) for part in range(depth)]
        left = [tile_of(places[0])]
        for part in range(1, depth):
            tile = tile_of(places[part])
            left.append(jnp.where(here + part < end, tile, jnp.zeros_like(tile)))
        left = jnp.concatenate(left, axis=1)
        for column in range(0, width, COLUMNS):
            window = pl.ds(column, COLUMNS)
            right = jnp.concatenate([block_of(place, window) for place in places], axis=0)
            sum_ref[:, window] += jnp.dot(left, right, preferred_element_type=jnp.float32)


def own_kernel(counts, groups, group, fresh, own_table, far_table, firsts, tiles_ref, perm_ref, *refs):
    starts, tile_at, block_at, own_slots = table_views(own_table, tiles_ref.shape[0], groups)
    far_slots = table_views(far_table, tiles_ref.shape[0], PPD)[3]
    pieces = refs[: len(counts)]
    refs = refs[len(counts) :]
    if fresh:
        sum_out, flip_out, sums, *refs = refs
    else:
        sum_in, flip_in, sums, flip_out, flip_sem, *refs = refs
    own_blocks, far_blocks, own_list, far_list, own_sems, far_sems, row_sems = refs

    def fetch(slots, landing, sems, fetched):
        found = jnp.int32(0)
        for number, (piece, count) in enumerate(zip(pieces, counts)):

            def one(offset, found, piece=piece, number=number):
                slot = slots[firsts[number] + offset]

                @pl.when(slot >= 0)
                def _():
                    fetched[found] = slot
                    pltpu.make_async_copy(piece.at[offset], landing.at[slot], sems.at[slot]).start()

                return found + (slot >= 0).astype(jnp.int32)

            found = lax.fori_loop(0, count, one, found)
        return found

    far_found = fetch(far_slots, far_blocks, far_sems, far_list)
    own_found = fetch(own_slots, own_blocks, own_sems, own_list)
    if not fresh:
        pltpu.make_async_copy(flip_in, flip_out, flip_sem).start()
        for row in range(PPD):
            pltpu.make_async_copy(sum_in.at[row], sums.at[row], row_sems.at[row]).start()
        pltpu.make_async_copy(flip_in, flip_out, flip_sem).wait()

    def arrived(landing, sems, slot):
        pltpu.make_async_copy(landing.at[slot], landing.at[slot], sems.at[slot]).wait()

    def flip_store(slot):
        return pltpu.make_async_copy(far_blocks.at[slot], flip_out.at[slot], far_sems.at[slot])

    @pl.loop(0, far_found)
    def _(number):
        slot = far_list[number]
        arrived(far_blocks, far_sems, slot)
        turned = jnp.dot(far_blocks[slot], perm_ref[...], preferred_element_type=jnp.float32).astype(jnp.bfloat16)
        if fresh:
            far_blocks[slot] = turned
            flip_store(slot).start()
        else:
            flip_out[slot] = turned

    @pl.loop(0, own_found)
    def _(number):
        arrived(own_blocks, own_sems, own_list[number])

    def store(row):
        return pltpu.make_async_copy(sums.at[row], sum_out.at[row], row_sems.at[row])

    @pl.loop(0, PPD)
    def _(row):
        if fresh:
            sums[row] = jnp.zeros(sums.shape[1:], jnp.float32)
        else:
            arrived(sums, row_sems, row)
        add_row(
            sums.at[row],
            starts[group + row],
            starts[group + row + 1],
            4 if fresh else 2,
            lambda place: tiles_ref[tile_at[place]],
            lambda place, window: own_blocks[block_at[place], :, window],
        )
        if fresh:
            store(row).start()

    if fresh:

        @pl.loop(0, far_found)
        def _(number):
            flip_store(far_list[number]).wait()

        @pl.loop(0, PPD)
        def _(row):
            store(row).wait()


def own_part(own_table, far_table, tiles, pieces, firsts, perm, groups=PPD, group=0, earlier=()):
    count, height, _ = tiles.shape
    depth, width = pieces[0].shape[1:]
    need = count // REUSE
    counts = [piece.shape[0] for piece in pieces]
    whole = (PPD, height, width)
    flips = (need, depth, width)
    if earlier:
        out_specs = [VMEM] * 2
        out_shape = [pltpu.VMEM(whole, jnp.float32), pltpu.VMEM(flips, jnp.bfloat16)]
        first_scratch = pltpu.SemaphoreType.DMA
    else:
        out_specs = [ANY] * 2
        out_shape = [jax.ShapeDtypeStruct(whole, jnp.float32), jax.ShapeDtypeStruct(flips, jnp.bfloat16)]
        first_scratch = pltpu.VMEM(whole, jnp.float32)
    return pl.pallas_call(
        functools.partial(own_kernel, counts, groups, group, not earlier),
        in_specs=[SMEM] * 3 + [VMEM] * 2 + [ANY] * (len(pieces) + len(earlier)),
        out_specs=out_specs,
        out_shape=out_shape,
        scratch_shapes=[
            first_scratch,
            pltpu.VMEM(flips, jnp.bfloat16),
            pltpu.VMEM(flips, jnp.bfloat16),
            pltpu.SMEM((need,), jnp.int32),
            pltpu.SMEM((need,), jnp.int32),
            pltpu.SemaphoreType.DMA((need,)),
            pltpu.SemaphoreType.DMA((need,)),
            pltpu.SemaphoreType.DMA((PPD,)),
        ],
        compiler_params=pltpu.CompilerParams(vmem_limit_bytes=(GRANT if earlier else 56) * MIB),
        name="own_part",
    )(own_table, far_table, firsts, tiles, perm, *pieces, *earlier)


def far_kernel(base, total_count, segments, table, chosen, *refs):
    starts, _, block_at, _ = table_views(table, total_count, PPD)
    tile_refs, refs = refs[: len(segments)], refs[len(segments) :]
    sum_in, flip_in = refs[:2]
    carry_in = refs[2] if base else None
    carry_out, result, tiles_ref, sums, rounded, tile_sem, row_sems, out_sems = refs[4:] if base else refs[2:]
    count = tiles_ref.shape[0]
    stop = base + count

    direct, direct_choice = tile_refs[-1], segments[-1][0]
    copied = list(zip(tile_refs, segments))[:-1]
    for source, (choice, begin) in copied:
        held = source.shape[0] * source.shape[2] // tiles_ref.shape[2]
        low, high = max(begin, base), min(begin + held, stop)

        @pl.when(chosen[0] == choice)
        def _(source=source, begin=begin, low=low, high=high):
            if source.shape[2] == tiles_ref.shape[2]:
                here, there = source.at[pl.ds(low - begin, high - low)], tiles_ref.at[pl.ds(low - base, high - low)]
                pltpu.make_async_copy(here, there, tile_sem).start()
            else:

                @pl.loop(low, high)
                def _(place):
                    pltpu.make_async_copy(window(source, place - begin), tiles_ref.at[place - base], tile_sem).start()

    def each_row(action):
        @pl.loop(0, PPD)
        def _(row):
            first, last = starts[row], starts[row + 1]

            @pl.when(((last > base) if base else True) & ((last <= stop) | (first < stop)))
            def _():
                action(row, last <= stop)

    def load(row):
        if base:
            goes_on = starts[row] < base

            @pl.when(goes_on)
            def _():
                pltpu.make_async_copy(carry_in, sums.at[row], row_sems.at[row]).start()

            @pl.when(jnp.logical_not(goes_on))
            def _():
                pltpu.make_async_copy(sum_in.at[row], sums.at[row], row_sems.at[row]).start()
        else:
            pltpu.make_async_copy(sum_in.at[row], sums.at[row], row_sems.at[row]).start()

    def store(row):
        return pltpu.make_async_copy(rounded.at[row], result.at[row], out_sems.at[row])

    def keep(row):
        return pltpu.make_async_copy(sums.at[row], carry_out, out_sems.at[row])

    each_row(lambda row, complete: load(row))
    if copied:

        @pl.when(chosen[0] != direct_choice)
        def _():
            pltpu.make_async_copy(tiles_ref, tiles_ref, tile_sem).wait()

    def tile_of(place):
        if not copied:
            return direct[place - base]
        return jnp.where(chosen[0] == direct_choice, direct[place - base], tiles_ref[place - base])

    def add(row, complete):
        begin, end = jnp.maximum(starts[row], base), jnp.minimum(starts[row + 1], stop)
        pltpu.make_async_copy(sums.at[row], sums.at[row], row_sems.at[row]).wait()

        add_row(
            sums.at[row],
            begin,
            end,
            4,
            tile_of,
            lambda place, window: flip_in[block_at[place], :, window],
        )

        @pl.when(complete)
        def _():
            rounded[row] = sums[row].astype(rounded.dtype)
            store(row).start()

        @pl.when(jnp.logical_not(complete))
        def _():
            keep(row).start()

    def finish(row, complete):
        pl.when(complete)(lambda: store(row).wait())
        pl.when(jnp.logical_not(complete))(lambda: keep(row).wait())

    each_row(add)
    each_row(finish)


def far_part(base, count, total_count, far_table, chosen, sources, flipped, total, earlier=()):
    whole = total.shape
    held = [array.size // (whole[1] * flipped.shape[1]) for _, _, array in sources]
    used = [
        (source[:2], source[2])
        for source, size in zip(sources, held)
        if source[1] < base + count and source[1] + size > base
    ]
    return pl.pallas_call(
        functools.partial(far_kernel, base, total_count, [segment for segment, _ in used]),
        in_specs=[SMEM] * 2 + [ANY] * (len(used) - 1) + [VMEM] * 3 + [ANY] * len(earlier),
        out_specs=[ANY] * 2,
        out_shape=[jax.ShapeDtypeStruct(whole[1:], jnp.float32), jax.ShapeDtypeStruct(whole, jnp.bfloat16)],
        input_output_aliases={5 + len(used): 1} if earlier else {},
        scratch_shapes=[
            pltpu.VMEM((count, whole[1], flipped.shape[1]), jnp.bfloat16),
            pltpu.VMEM(whole, jnp.float32),
            pltpu.VMEM(whole, jnp.bfloat16),
            pltpu.SemaphoreType.DMA,
            pltpu.SemaphoreType.DMA((PPD,)),
            pltpu.SemaphoreType.DMA((PPD,)),
        ],
        compiler_params=pltpu.CompilerParams(vmem_limit_bytes=24 * MIB),
        name="far_part",
    )(far_table, chosen, *[array for _, array in used], total, flipped, *earlier)


def together(*values):
    return lax.optimization_barrier(values)


def send(value, pairs):
    return lax.ppermute(value, "tile", pairs)


def flipped_bit(bit):
    return [(i, i ^ bit) for i in range(16)]


def staged_part(tiles, rows, cols, shard):
    local = shard.shape[0]
    block_total = 16 * local
    centre = [i for i in range(16) if i // 4 in (1, 2)]
    across = [(i, i ^ 12) for i in centre]
    from_ends = [(i, i ^ 8) for i in range(16) if i not in centre]
    from_centre = [(i, i ^ 8) for i in centre]
    around = [(i, i ^ 4) for i in centre] + from_ends
    other_z, other_y, other_core, opposite = (flipped_bit(bit) for bit in (4, 2, 1, 8))
    me = lax.axis_index("tile")
    z = me // 4
    in_centre = (z == 1) | (z == 2)
    at_end = 1 - in_centre.astype(jnp.int32).reshape(1)
    zs = [z, z ^ 1, jnp.where(z < 2, 2, 1), jnp.where(z < 2, 3, 0)]

    def owner(k, bits):
        return 4 * zs[k] + ((me & 3) ^ bits)

    def first_blocks(firsts):
        return jnp.stack(firsts).astype(jnp.int32)

    col_owner = cols // local
    late = (col_owner // 4 == zs[3]) | (col_owner == owner(2, 3))
    keys = rows + PPD * late.astype(jnp.int32)
    columns = jnp.arange(shard.shape[2], dtype=jnp.int32)

    near = send(shard, other_z)
    first = send(shard, across)
    notes = send(jnp.stack([rows, cols]), opposite)
    order = tables(rows, cols, block_total)
    c_own = send(shard, other_core)
    y_own = send(shard, other_y)
    count = tiles.shape[0]
    step = shard.size // tiles[0].size
    sizes = tile_parts(count)
    shapes = [shard.shape] * 2 + [(size,) + tiles.shape[1:] for size in [count - 2 * step] + sizes]
    parts = sort_tiles(order, at_end, tiles, [1] * 3 + [0] * len(sizes), shapes)
    first, *parts = together(first, *parts)

    first = payload_of(at_end, parts[0], first)
    outer = send(first, around)
    near, c_own, y_own, keys, columns, *parts = together(near, c_own, y_own, keys, columns, *parts)
    second = send(near, across)
    y_near = send(near, other_y)
    c_near = send(near, other_core)
    own_table = tables(keys, cols, block_total, 2 * PPD)
    far_table = tables(notes[0], notes[1], block_total, cost=FAR_COST)
    perm = flip_matrix(columns)
    far_ends = [outer]
    first = jnp.where(in_centre, first, outer)
    second = payload_of(at_end, parts[1], second)
    outer = send(second, around)
    first, y_own, y_near, c_near, perm, *rest = together(
        first, y_own, y_near, c_near, perm, own_table, far_table, *parts[2:]
    )
    own_table, far_table, *parts = rest
    y_first = send(first, other_y)
    c_first = send(first, other_core)
    c_y_own = send(y_own, other_core)
    c_y_near = send(y_near, other_core)
    tiles_last, c_first = together(parts[0], c_first)
    far_ends += [outer, send(tiles_last, from_ends)]
    halves = (slice(0, local // 2), slice(local // 2, None))
    second = [jnp.where(in_centre, second[half], outer[half]) for half in halves]
    *second, y_first, c_first, c_y_own, c_y_near = together(*second, y_first, c_first, c_y_own, c_y_near)

    far_centre = [send(parts[1], from_centre)]
    y_second = [send(half, other_y) for half in second]
    pieces = [shard, c_own, near, c_near, first, c_first, y_own, c_y_own, y_near, c_y_near, y_first]
    firsts = [owner(k, y + core) * local for y in (0, 2) for k in range(3) for core in (0, 1)][:11]
    early = own_part(own_table, far_table, tiles, pieces, first_blocks(firsts), perm, 2 * PPD)
    y_second[0], y_second[1], second[0], second[1], y_first, total, flipped, *parts = together(
        *y_second, *second, y_first, *early, *parts[2:]
    )
    far_centre += [send(part, from_centre) for part in parts]
    *y_second, far_ends[2] = together(*y_second, far_ends[2])

    c_y_first = send(y_first, other_core)
    c_second = [send(half, other_core) for half in second]
    c_y_second = [send(half, other_core) for half in y_second]
    pieces = [c_y_first, *second, *c_second, *y_second, *c_y_second]
    firsts = [owner(2, 3) * local] + [owner(3, bits) * local + half for bits in range(4) for half in (0, local // 2)]
    earlier = (total, flipped)
    total, flipped = own_part(own_table, far_table, tiles, pieces, first_blocks(firsts), perm, 2 * PPD, PPD, earlier)

    sources = [(0, step * number, array) for number, array in enumerate(far_ends)]
    sources += [(1, sum(sizes[:number]), array) for number, array in enumerate(far_centre)]
    return far_products(far_table, at_end, sources, sizes, flipped, total)


def tile_parts(count):
    sizes = [count * share // 96 for share in SHARES]
    return sizes + [count - sum(sizes)]


def far_products(far_table, chosen, sources, sizes, flipped, total):
    base, earlier = 0, ()
    for size in sizes:
        earlier = far_part(base, size, sum(sizes), far_table, chosen, sources, flipped, total, earlier)
        base += size
    return earlier[1]


def per_device(t2_tiles, t2_row, t2_col, integrals):
    peers = lax.axis_size("tile")
    if peers == 16:
        return staged_part(t2_tiles, t2_row, t2_col, integrals)
    block_total = peers * integrals.shape[0]
    opposite = [(source, (source + peers // 2) % peers) for source in range(peers)]
    own_table = tables(t2_row, t2_col, block_total)
    sizes = tile_parts(t2_tiles.shape[0])
    zero = jnp.zeros((1,), jnp.int32)
    parts = sort_tiles(own_table, zero, t2_tiles, [0] * len(sizes), [(size,) + t2_tiles.shape[1:] for size in sizes])
    notes = send(jnp.stack([t2_row, t2_col]), opposite)
    sources = [(0, sum(sizes[:number]), send(part, opposite)) for number, part in enumerate(parts)]
    blocks = lax.all_gather(integrals, "tile", axis=0, tiled=True)
    far_table = tables(notes[0], notes[1], block_total)
    columns = jnp.arange(integrals.shape[2], dtype=jnp.int32)
    total, flipped = own_part(own_table, far_table, t2_tiles, [blocks], zero, flip_matrix(columns))
    return far_products(far_table, zero, sources, sizes, flipped, total)


def solution(mesh):
    in_specs = (
        P(("groups", "tile"), None, None),
        P(("groups", "tile")),
        P(("groups", "tile")),
        P(("groups", "tile"), None, None),
    )
    out_specs = P(("groups", "tile"), None, None)
    return jax.shard_map(
        per_device, mesh=mesh, in_specs=in_specs, out_specs=out_specs, check_vma=False
    )
```
